32 devices in a mesh: grp: 4 (over y, x), seq: 8 (over z, core).
Axes of the slice: x: 2, y: 2, z: 4, core: 2. Of those that a mesh axis runs over, the one named last changes fastest.
Arguments:
- block_input: bfloat16 [8192, 768], P(('grp', 'seq')), may hold values from -18 to 18
- out_grad: bfloat16 [8192, 768], P(('grp', 'seq')), may hold values from -6 to 6
- seq_span: int32 [4, 2], P('grp'), may hold values from 0 to 2048, as said below
- ln1_gain: float32 [768], replicated, may hold values from 0.5 to 1.5
- ln1_bias: float32 [768], replicated, may hold values from -2 to 2
- w_qkv: bfloat16 [768, 2304], replicated, may hold values from -0.21875 to 0.21875
- w_out: bfloat16 [768, 768], replicated, may hold values from -3 to 3
- ln2_gain: float32 [768], replicated, may hold values from 0.5 to 1.5
- ln2_bias: float32 [768], replicated, may hold values from -2 to 2
- w_up: bfloat16 [768, 3072], replicated, may hold values from -0.21875 to 0.21875
- w_down: bfloat16 [3072, 768], replicated, may hold values from -0.109375 to 0.109375
Outputs:
- block_output: bfloat16 [8192, 768], P(('grp', 'seq'))
- input_grad: bfloat16 [8192, 768], P(('grp', 'seq'))
- ln1_gain_grad: float32 [768], P(('grp', 'seq'))
- ln1_bias_grad: float32 [768], P(('grp', 'seq'))
- w_qkv_grad: float32 [768, 2304], P(('grp', 'seq'))
- w_out_grad: float32 [768, 768], P(('grp', 'seq'))
- ln2_gain_grad: float32 [768], P(('grp', 'seq'))
- ln2_bias_grad: float32 [768], P(('grp', 'seq'))
- w_up_grad: float32 [768, 3072], P(('grp', 'seq'))
- w_down_grad: float32 [3072, 768], P(('grp', 'seq'))
- rms_stats: float32 [3], replicated
The draws below stay inside these ranges and needn't reach their ends.
Inputs may be any that keep to these rules, and one draw needn't show every extreme that they name: seq_span[g, 0] is at most 128 and seq_span[g, 1] at least 1920, so each group's sequence runs from its first device to its last.
All inputs are finite; a program needn't handle non-finite values.
Results may differ from the reference program's by a relative error of at most 0.012.
Values may be sent and summed in bfloat16 or wider, within the bound.
A program may use at most 128 MiB of HBM per device.

```python
import math
import jax
import jax.numpy as jnp
from jax import lax

D = 768
HEADS = 12
HEAD_DIM = 64
FF = 3072
TOK_DEV = 256
GROUPS = 4
GTOK = 2048
TOKENS = 8192


def draw_block_input(key, part):
    key = jax.random.fold_in(key, 3)
    key_one = jax.random.fold_in(key, 0)
    row_index = jnp.arange(TOKENS, dtype=jnp.float32)
    row_scale = jnp.exp(jnp.log(3.0) * (2.0 * row_index / TOKENS - 1.0))
    base_draw = jnp.clip(jax.random.normal(key_one, (TOKENS, D), dtype=jnp.float32), -6.0, 6.0)
    return (base_draw * row_scale[:, None]).astype(jnp.bfloat16)


def draw_seq_span(key, part):
    key = jax.random.fold_in(key, 5)
    key_one, key_two, key_three, key_four = jax.random.split(key, 4)
    gap_most = TOK_DEV // 2
    lead_gap = jax.random.randint(key_one, (GROUPS,), 0, gap_most + 1)
    tail_gap = jax.random.randint(key_two, (GROUPS,), 0, gap_most + 1)
    order_one = jax.random.permutation(key_three, GROUPS)
    order_two = jax.random.permutation(key_four, GROUPS)
    lead_gap = jnp.where(order_one == 0, 0, jnp.where(order_one == 1, gap_most, lead_gap))
    tail_gap = jnp.where(order_two == 0, 0, jnp.where(order_two == 1, gap_most, tail_gap))
    return jnp.stack([lead_gap, GTOK - tail_gap], axis=1).astype(jnp.int32)


def steps_of(own_key, dims, pieces, low, top_value):
    def one(dim, parts):
        draws = jax.random.uniform(jax.random.fold_in(jax.random.fold_in(own_key, 6), dim), (parts,), jnp.float32, low / len(pieces), top_value / len(pieces))
        return jnp.repeat(jnp.exp(draws), dims[dim] // parts).reshape((-1,) + (1,) * (len(dims) - dim - 1))

    factor_of = one(*pieces[0])
    for cut in pieces[1:]:
        factor_of = factor_of * one(*cut)
    return factor_of


def scatter_about(rng, dims, deviation, limit, cuts=(), kind=jnp.bfloat16):
    values = deviation * jax.random.normal(rng, dims, jnp.float32)
    if cuts:
        values = values * steps_of(rng, dims, cuts, -0.22, 0.18)
    return jnp.clip(values, -limit, limit).astype(kind)


def setup_inputs(seed: int = 0) -> dict:
    splits = jax.random.split(jax.random.key(seed), 12)
    return {
        "block_input": draw_block_input(jax.random.fold_in(splits[11], 71), 0),
        "out_grad": scatter_about(splits[1], (TOKENS, D), 1.0, 6.0, ((0, 32),)),
        "seq_span": draw_seq_span(jax.random.fold_in(splits[11], 71), 0),
        "ln1_gain": jnp.clip(1.0 + 0.1 * jax.random.normal(splits[3], (D,), jnp.float32), 0.5, 1.5),
        "ln1_bias": scatter_about(splits[4], (D,), 0.3, 2.0, (), jnp.float32),
        "w_qkv": scatter_about(splits[5], (D, 3 * D), D ** -0.5, 0.21875),
        "w_out": scatter_about(splits[6], (D, D), 4 ** -0.5, 3.0),
        "ln2_gain": jnp.clip(1.0 + 0.1 * jax.random.normal(splits[7], (D,), jnp.float32), 0.5, 1.5),
        "ln2_bias": scatter_about(splits[8], (D,), 0.3, 2.0, (), jnp.float32),
        "w_up": scatter_about(splits[9], (D, FF), D ** -0.5, 0.21875),
        "w_down": scatter_about(splits[10], (FF, D), FF ** -0.5, 0.109375),
    }


@jax.custom_vjp
def low(v):
    return lax.optimization_barrier(v.astype(jnp.bfloat16)).astype(jnp.float32)

@jax.custom_vjp
def low_back(v):
    return v

def low_keep(v):
    return (low(v), None)

def low_pass(kept, grad):
    return (grad,)

def back_keep(v):
    return (v, None)

def back_low(kept, grad):
    return (low(grad),)
low.defvjp(low_keep, low_pass)
low_back.defvjp(back_keep, back_low)
epsilon = 1e-05
highest = lax.Precision.HIGHEST

def layer_norm(vector, scale_vec, shift_vec):
    row_mean = lax.optimization_barrier(jnp.mean(vector, axis=-1, keepdims=True))
    centered = vector - row_mean
    variance = lax.optimization_barrier(jnp.mean(centered * centered, axis=-1, keepdims=True))
    return centered * lax.rsqrt(variance + epsilon) * scale_vec + shift_vec

def matmul_high(left, right):
    return jnp.dot(left, right, precision=highest, preferred_element_type=jnp.float32)

def attend_group(queries, key_block, value_block, seq_first, seq_limit):
    query_block = math.gcd(GTOK, 512)
    key_pos = jnp.arange(GTOK, dtype=jnp.int32)
    key_valid = (key_pos >= seq_first) & (key_pos < seq_limit)

    def one_block(block_index):
        query_pos = block_index * query_block + jnp.arange(query_block, dtype=jnp.int32)
        query_valid = (query_pos >= seq_first) & (query_pos < seq_limit)
        query_rows = lax.dynamic_slice_in_dim(queries, block_index * query_block, query_block, 0)
        scores = jnp.einsum('qhd,khd->qhk', query_rows, key_block, precision=highest) * 0.125
        scores = low_back(scores)
        allowed = (key_pos[None, :] <= query_pos[:, None]) & (query_valid[:, None] & key_valid[None, :] | (key_pos[None, :] == query_pos[:, None]))
        magnitude = jnp.sqrt(scores * scores + 1.0)
        signed_part = scores / magnitude
        exp_terms = jnp.where(allowed[:, None, :], jnp.exp(magnitude), 0.0)
        totals = lax.optimization_barrier(jnp.sum(exp_terms, axis=-1))
        weights = low(signed_part * exp_terms)
        unnorm = low_back(jnp.einsum('qhk,khd->qhd', weights, value_block, precision=highest))
        return unnorm / totals[:, :, None]
    blocks = lax.map(jax.checkpoint(one_block), jnp.arange(GTOK // query_block, dtype=jnp.int32))
    return blocks.reshape(GTOK, HEADS, HEAD_DIM)

def forward(block_input, ln1_gain, ln1_bias, w_qkv, w_out, ln2_gain, ln2_bias, w_up, w_down, seq_span):
    normed = low(layer_norm(block_input, ln1_gain, ln1_bias))
    proj_qkv = low_back(low(matmul_high(normed, w_qkv)))
    proj_qkv = proj_qkv.reshape(GROUPS, GTOK, 3, HEADS, HEAD_DIM)

    def per_group(group_item):
        group_qkv, group_span = group_item
        return attend_group(group_qkv[:, 0], group_qkv[:, 1], group_qkv[:, 2], group_span[0], group_span[1])
    mixed_heads = lax.map(per_group, (proj_qkv, seq_span)).reshape(TOKENS, D)
    attn_out = low_back(matmul_high(low(mixed_heads), w_out))
    middle = block_input + attn_out
    normed_two = low(layer_norm(middle, ln2_gain, ln2_bias))
    up_proj = low_back(matmul_high(normed_two, w_up))
    mlp_out = matmul_high(low(jax.nn.gelu(up_proj, approximate=True)), w_down)
    return (middle + mlp_out, attn_out, mlp_out)

def reference(block_input, out_grad, seq_span, ln1_gain, ln1_bias, w_qkv, w_out, ln2_gain, ln2_bias, w_up, w_down):
    floats = (block_input.astype(jnp.float32), ln1_gain.astype(jnp.float32), ln1_bias.astype(jnp.float32), w_qkv.astype(jnp.float32), w_out.astype(jnp.float32), ln2_gain.astype(jnp.float32), ln2_bias.astype(jnp.float32), w_up.astype(jnp.float32), w_down.astype(jnp.float32))

    def run_layer(*values):
        return forward(*values, seq_span)
    (output, attn_out, mlp_out), pull_back = jax.vjp(run_layer, *floats)
    grads = pull_back((out_grad.astype(jnp.float32), jnp.zeros_like(attn_out), jnp.zeros_like(mlp_out)))
    positions = jnp.arange(GTOK, dtype=jnp.int32)
    valid = (positions[None, :] >= seq_span[:, 0:1]) & (positions[None, :] < seq_span[:, 1:2])
    valid_rows = valid.reshape(TOKENS).astype(jnp.float32)[:, None]
    count = jnp.sum(valid_rows) * D
    squares = jnp.stack([jnp.sum(valid_rows * output * output), jnp.sum(valid_rows * attn_out * attn_out), jnp.sum(valid_rows * mlp_out * mlp_out)])
    rms_stats = jnp.sqrt(squares / count)
    return (output.astype(jnp.bfloat16), grads[0].astype(jnp.bfloat16), grads[1], grads[2], grads[3], grads[4], grads[5], grads[6], grads[7], grads[8], rms_stats)
```

```python
import functools

import jax
import jax.numpy as jnp
from jax import lax
from jax.experimental import pallas as pl
from jax.experimental.pallas import tpu as pltpu
from jax.sharding import PartitionSpec as P

D = 768
HEADS = 12
HEAD_DIM = 64
MESH = pl.DeviceIdType.MESH


epsilon = 1e-05


def passed_along(array, axis, by):
    devices = lax.axis_size(axis)
    pairs = [(i, i + by) for i in range(devices) if 0 <= i + by < devices]
    return lax.ppermute(array, axis, pairs)


def shifted(array, axis, by):
    devices = lax.axis_size(axis)
    return lax.ppermute(array, axis, [(i, (i + by) % devices) for i in range(devices)])


def layer_norm(vector, scale_vec, shift_vec):
    row_mean = jnp.mean(vector, axis=-1, keepdims=True)
    centered = vector - row_mean
    variance = jnp.mean(centered * centered, axis=-1, keepdims=True)
    return centered * lax.rsqrt(variance + epsilon) * scale_vec + shift_vec


def contract_rows(left, right):
    return lax.dot_general(
        left, right, (((0,), (0,)), ((), ())), preferred_element_type=jnp.float32
    )


def contract_cols(left, right):
    return lax.dot_general(
        left, right, (((1,), (1,)), ((), ())), preferred_element_type=jnp.float32
    )


def score_terms(queries, key_block, query_pos, key_pos, seq_first, seq_limit):
    scores = (
        jnp.einsum("qhd,khd->qhk", queries, key_block, preferred_element_type=jnp.float32) * 0.125
    )
    query_valid = (query_pos >= seq_first) & (query_pos < seq_limit)
    key_valid = (key_pos >= seq_first) & (key_pos < seq_limit)
    allowed = (key_pos[None, :] <= query_pos[:, None]) & (
        query_valid[:, None] & key_valid[None, :] | (key_pos[None, :] == query_pos[:, None])
    )
    magnitude = jnp.sqrt(scores * scores + 1.0)
    signed_part = scores / magnitude
    exp_terms = jnp.where(allowed[:, None, :], jnp.exp(magnitude), 0.0)
    return (magnitude, signed_part, exp_terms)


def split_pair(kv_pair):
    count_rows = kv_pair.shape[0]
    key_block = kv_pair[:, :D].reshape(count_rows, HEADS, HEAD_DIM)
    value_block = kv_pair[:, D:].reshape(count_rows, HEADS, HEAD_DIM)
    return (key_block, value_block)


def forward_block(running, kv_pair, key_start, queries, query_pos, seq_first, seq_limit):
    totals, unnorm = running
    key_block, value_block = split_pair(kv_pair)
    key_pos = key_start + jnp.arange(kv_pair.shape[0], dtype=jnp.int32)
    magnitude, signed_part, exp_terms = score_terms(
        queries, key_block, query_pos, key_pos, seq_first, seq_limit
    )
    weights = (signed_part * exp_terms).astype(jnp.bfloat16)
    totals = totals + jnp.sum(exp_terms, axis=-1)
    unnorm = unnorm + jnp.einsum(
        "qhk,khd->qhd", weights, value_block, preferred_element_type=jnp.float32
    )
    return (totals, unnorm)


def grad_core(
    kv_pair, key_start, queries, query_pos, seq_first, seq_limit, grad_unnorm, grad_totals
):
    key_block, value_block = split_pair(kv_pair)
    key_pos = key_start + jnp.arange(kv_pair.shape[0], dtype=jnp.int32)
    magnitude, signed_part, exp_terms = score_terms(
        queries, key_block, query_pos, key_pos, seq_first, seq_limit
    )
    weights = (signed_part * exp_terms).astype(jnp.bfloat16)
    grad_weights = jnp.einsum(
        "qhd,khd->qhk", grad_unnorm, value_block, preferred_element_type=jnp.float32
    )
    grad_scores = (
        grad_weights * exp_terms / (magnitude * magnitude * magnitude)
        + (grad_weights * signed_part + grad_totals[:, :, None]) * exp_terms * signed_part
    )
    return (key_block, weights, grad_scores.astype(jnp.bfloat16))


def backward_block(
    kv_pair, key_start, queries, query_pos, seq_first, seq_limit, grad_unnorm, grad_totals
):
    key_block, weights, grad_scores = grad_core(
        kv_pair, key_start, queries, query_pos, seq_first, seq_limit, grad_unnorm, grad_totals
    )
    count_rows = kv_pair.shape[0]
    grad_query = (
        jnp.einsum("qhk,khd->qhd", grad_scores, key_block, preferred_element_type=jnp.float32)
        * 0.125
    )
    grad_key = (
        jnp.einsum("qhk,qhd->khd", grad_scores, queries, preferred_element_type=jnp.float32) * 0.125
    )
    grad_value = jnp.einsum(
        "qhk,qhd->khd", weights, grad_unnorm, preferred_element_type=jnp.float32
    )
    grad_pair = jnp.concatenate(
        [grad_key.reshape(count_rows, D), grad_value.reshape(count_rows, D)], axis=1
    )
    return (grad_query, grad_pair)


def rs_kernel(shapes, *refs):
    n = len(shapes)
    ins, small_in = refs[:n], refs[n]
    outs, small_out = refs[n + 1 : 2 * n + 1], refs[2 * n + 1]
    scratch = refs[2 * n + 2 :]
    first, held, second, mine, third = (scratch[i * n : (i + 1) * n] for i in range(5))
    small_a, small_b, small_c = scratch[5 * n : 5 * n + 3]
    send_sems, recv_sems = scratch[5 * n + 3 :]

    grp, seq = lax.axis_index("grp"), lax.axis_index("seq")
    zed, core = seq // 2, seq % 2
    sibling = (grp, zed * 2 + 1 - core)
    across = [((grp // 2 + k // 2) % 2) * 2 + (grp % 2 + k % 2) % 2 for k in range(4)]
    along = [(zed + k) % 4 for k in range(4)]
    back = [(zed + 4 - k) % 4 for k in range(4)]

    barrier = pltpu.get_barrier_semaphore()
    partners = [sibling]
    partners += [(across[k], seq) for k in (1, 2, 3)]
    partners += [(grp, along[k] * 2 + core) for k in (1, 2, 3)]
    for partner in partners:
        pl.semaphore_signal(barrier, inc=1, device_id=partner, device_id_type=MESH)
    pl.semaphore_wait(barrier, len(partners))

    def send(src, dst, slot, target):
        copy = pltpu.make_async_remote_copy(
            src_ref=src, dst_ref=dst, send_sem=send_sems.at[slot], recv_sem=recv_sems.at[slot],
            device_id=target, device_id_type=MESH,
        )
        copy.start()
        return copy

    def rows(start, count):
        return pl.ds(pl.multiple_of(start, 16), count)

    copies = {}
    slot = 0
    copies["s0"] = send(small_in, small_a.at[1 - 0], slot, sibling)
    slot += 1
    for a, (r, c) in enumerate(shapes):
        for k in (1, 2, 3, 0):
            at = rows(across[k] * (r // 4), r // 4)
            cols = pl.ds(pl.multiple_of((1 - core) * (c // 2), 128), c // 2)
            copies["a", a, k] = send(ins[a].at[at, cols], first[a].at[at, :], slot, sibling)
            slot += 1

    copies["s0"].wait()
    small_a[0] = small_in[...] + small_a[1]
    small_b[pl.ds(grp, 1)] = small_a[0:1]
    for k in (1, 2, 3):
        copies["s1", k] = send(small_a.at[0], small_b.at[grp], slot, (across[k], seq))
        slot += 1

    for a, (r, c) in enumerate(shapes):
        half = pl.ds(pl.multiple_of(core * (c // 2), 128), c // 2)
        for k in (1, 2, 3):
            base = across[k] * (r // 4)
            copies["a", a, k].wait_recv()

            def add(i, _):
                at = rows(base + i * 16, 16)
                first[a][at, :] = (
                    ins[a][at, half].astype(jnp.float32) + first[a][at, :].astype(jnp.float32)
                ).astype(jnp.bfloat16)
                return 0

            lax.fori_loop(0, r // 64, add, 0)
            copies["b", a, k] = send(
                first[a].at[rows(base, r // 4), :], second[a].at[k - 1], slot, (across[k], seq)
            )
            slot += 1

    for k in (1, 2, 3):
        copies["s1", k].wait()
    small_c[pl.ds(zed, 1)] = (small_b[0:1] + small_b[1:2]) + (small_b[2:3] + small_b[3:4])
    for k in (1, 2, 3):
        copies["s2", k] = send(small_c.at[zed], small_c.at[zed], slot, (grp, along[k] * 2 + core))
        slot += 1

    for a, (r, c) in enumerate(shapes):
        half = pl.ds(pl.multiple_of(core * (c // 2), 128), c // 2)
        base = across[0] * (r // 4)
        copies["a", a, 0].wait_recv()
        for k in (1, 2, 3):
            copies["b", a, k].wait_recv()

        def gather(i, _):
            at = rows(base + i * 16, 16)
            here = rows(i * 16, 16)
            total = ins[a][at, half].astype(jnp.float32) + first[a][at, :].astype(jnp.float32)
            for j in range(3):
                total = total + second[a][j, here, :].astype(jnp.float32)
            held[a][here, :] = total.astype(jnp.bfloat16)
            return 0

        lax.fori_loop(0, r // 64, gather, 0)
        for k in (1, 2, 3):
            copies["c", a, k] = send(
                held[a].at[rows(along[k] * (r // 16), r // 16), :],
                third[a].at[k - 1],
                slot,
                (grp, along[k] * 2 + core),
            )
            slot += 1

    for k in (1, 2, 3):
        copies["s2", k].wait()
    small_out[...] = (small_c[0] + small_c[1]) + (small_c[2] + small_c[3])

    for a, (r, c) in enumerate(shapes):
        half = pl.ds(pl.multiple_of(core * (c // 2), 128), c // 2)
        for k in (1, 2, 3):
            copies["c", a, k].wait_recv()
        for part in range(2):
            total = held[a][rows(zed * (r // 16), r // 16), :].astype(jnp.float32)
            for j in range(3):
                total = total + third[a][j].astype(jnp.float32)
        mine[a][...] = total
        count = r // 32
        copies["d", a] = send(
            mine[a].at[pl.ds(pl.multiple_of((1 - core) * count, 8), count), :],
            outs[a].at[:, half], slot, sibling,
        )
        slot += 1
        outs[a][:, half] = mine[a][pl.ds(pl.multiple_of(core * count, 8), count), :]
    for key, copy in copies.items():
        if key == "s0" or key[0] in ("s1", "s2"):
            continue
        copy.wait_send()
        if key[0] == "d":
            copy.wait_recv()


def reduce_scatter(grads, small):
    shapes = tuple(g.shape for g in grads)
    vmem = pl.BlockSpec(memory_space=pltpu.VMEM)
    bf16, f32 = jnp.bfloat16, jnp.float32
    copies = 1 + 3 + 3 + len(shapes) * (4 + 3 + 3 + 1)
    scratch = [pltpu.VMEM((r, c // 2), bf16) for r, c in shapes]
    scratch += [pltpu.VMEM((r // 4, c // 2), bf16) for r, c in shapes]
    scratch += [pltpu.VMEM((3, r // 4, c // 2), bf16) for r, c in shapes]
    scratch += [pltpu.VMEM((r // 16, c // 2), f32) for r, c in shapes]
    scratch += [pltpu.VMEM((3, r // 16, c // 2), bf16) for r, c in shapes]
    scratch += [pltpu.VMEM((count,) + small.shape, f32) for count in (2, 4, 4)]
    scratch += [pltpu.SemaphoreType.DMA((copies,)), pltpu.SemaphoreType.DMA((copies,))]
    return pl.pallas_call(
        functools.partial(rs_kernel, shapes),
        out_shape=[jax.ShapeDtypeStruct((r // 32, c), f32) for r, c in shapes]
        + [jax.ShapeDtypeStruct(small.shape, f32)],
        in_specs=[vmem] * (len(shapes) + 1),
        out_specs=[vmem] * (len(shapes) + 1),
        scratch_shapes=scratch,
        compiler_params=pltpu.CompilerParams(
            collective_id=0, has_side_effects=True, vmem_limit_bytes=60 * 2**20
        ),
    )(*grads, small)


def per_device(
    planned,
    block_input,
    out_grad,
    seq_span,
    ln1_gain,
    ln1_bias,
    w_qkv,
    w_out,
    ln2_gain,
    ln2_bias,
    w_up,
    w_down,
):
    tok_rows = block_input.shape[0]
    feat_width = block_input.shape[1]
    seq_count = lax.axis_size("seq")
    seq_index = lax.axis_index("seq")
    query_pos = seq_index * tok_rows + jnp.arange(tok_rows, dtype=jnp.int32)
    query_last = query_pos[tok_rows - 1]
    seq_first = seq_span[0, 0]
    seq_limit = seq_span[0, 1]
    inputs = block_input.astype(jnp.float32)
    normed = layer_norm(inputs, ln1_gain, ln1_bias).astype(jnp.bfloat16)
    proj_qkv = jnp.dot(normed, w_qkv, preferred_element_type=jnp.float32).astype(jnp.bfloat16)
    queries = proj_qkv[:, :feat_width].reshape(tok_rows, HEADS, HEAD_DIM)
    kv_pair = proj_qkv[:, feat_width:]

    def visit_block(running, shard_rows, key_start):
        return lax.cond(
            key_start <= query_last,
            lambda state_in: forward_block(
                state_in, shard_rows, key_start, queries, query_pos, seq_first, seq_limit
            ),
            lambda state_in: state_in,
            running,
        )

    empty = (
        jnp.zeros((tok_rows, HEADS), jnp.float32),
        jnp.zeros((tok_rows, HEADS, HEAD_DIM), jnp.float32),
    )
    first_state = visit_block(empty, kv_pair, seq_index * tok_rows)

    def forward_hop(hop_count, loop_state):
        moving, running = loop_state
        moving = passed_along(moving, "seq", 1)
        source = (seq_index - hop_count) % seq_count
        return (moving, visit_block(running, moving, source * tok_rows))

    _, (totals, unnorm) = lax.fori_loop(1, seq_count, forward_hop, (kv_pair, first_state))
    mixed_heads = (unnorm / totals[:, :, None]).reshape(tok_rows, feat_width).astype(jnp.bfloat16)
    attn_out = jnp.dot(mixed_heads, w_out, preferred_element_type=jnp.float32)
    middle = inputs + attn_out
    normed_two = layer_norm(middle, ln2_gain, ln2_bias).astype(jnp.bfloat16)
    up_proj = jnp.dot(normed_two, w_up, preferred_element_type=jnp.float32)
    activated = jax.nn.gelu(up_proj, approximate=True).astype(jnp.bfloat16)
    mlp_out = jnp.dot(activated, w_down, preferred_element_type=jnp.float32)
    output = middle + mlp_out
    valid_rows = ((query_pos >= seq_first) & (query_pos < seq_limit)).astype(jnp.float32)[:, None]
    rms_terms = (
        jnp.sum(valid_rows * output * output),
        jnp.sum(valid_rows * attn_out * attn_out),
        jnp.sum(valid_rows * mlp_out * mlp_out),
        jnp.sum(valid_rows) * feat_width,
    )
    grad_w_down = contract_rows(activated, out_grad)
    grad_activated = contract_cols(out_grad, w_down)
    _, gelu_pull = jax.vjp(lambda pre_act: jax.nn.gelu(pre_act, approximate=True), up_proj)
    grad_up = gelu_pull(grad_activated)[0].astype(jnp.bfloat16)
    grad_w_up = contract_rows(normed_two, grad_up)
    grad_norm_two = contract_cols(grad_up, w_up)
    _, norm_pull_two = jax.vjp(layer_norm, middle, ln2_gain, ln2_bias)
    grad_mid_norm, grad_gain_two, grad_bias_two = norm_pull_two(grad_norm_two)
    grad_middle = out_grad.astype(jnp.float32) + grad_mid_norm
    grad_attn = grad_middle.astype(jnp.bfloat16)
    grad_w_out = contract_rows(mixed_heads, grad_attn)
    grad_mixed = contract_cols(grad_attn, w_out).reshape(tok_rows, HEADS, HEAD_DIM)
    grad_unnorm = (grad_mixed / totals[:, :, None]).astype(jnp.bfloat16)
    grad_totals = -jnp.sum(grad_mixed * unnorm, axis=-1) / (totals * totals)

    def back_block(grad_run, shard_rows, key_start):

        def compute_block(grad_in):
            grad_query, grad_pair = backward_block(
                shard_rows,
                key_start,
                queries,
                query_pos,
                seq_first,
                seq_limit,
                grad_unnorm,
                grad_totals,
            )
            return (grad_in + grad_query, grad_pair)

        def skip_block(grad_in):
            return (grad_in, jnp.zeros((shard_rows.shape[0], 2 * feat_width), jnp.float32))

        return lax.cond(key_start <= query_last, compute_block, skip_block, grad_run)

    grad_start = jnp.zeros((tok_rows, HEADS, HEAD_DIM), jnp.float32)
    grad_queries, local_terms = back_block(grad_start, kv_pair, seq_index * tok_rows)

    def backward_hop(hop_count, loop_state):
        moving, grad_acc, grad_run = loop_state
        moving = passed_along(moving, "seq", 1)
        grad_acc = shifted(grad_acc.astype(jnp.bfloat16), "seq", 1).astype(grad_acc.dtype)
        source = (seq_index - hop_count) % seq_count
        grad_run, new_terms = back_block(grad_run, moving, source * tok_rows)
        return (moving, grad_acc + new_terms, grad_run)

    _, grad_acc, grad_queries = lax.fori_loop(
        1, seq_count, backward_hop, (kv_pair, local_terms, grad_queries)
    )
    grad_kv = shifted(grad_acc.astype(jnp.bfloat16), "seq", 1).astype(grad_acc.dtype)
    grad_qkv = jnp.concatenate(
        [grad_queries.reshape(tok_rows, feat_width), grad_kv], axis=1
    ).astype(jnp.bfloat16)
    grad_w_qkv = contract_rows(normed, grad_qkv)
    grad_norm_one = contract_cols(grad_qkv, w_qkv)
    _, norm_pull_one = jax.vjp(layer_norm, inputs, ln1_gain, ln1_bias)
    grad_in_norm, grad_gain_one, grad_bias_one = norm_pull_one(grad_norm_one)
    input_grad = (grad_middle + grad_in_norm).astype(jnp.bfloat16)
    if planned:
        bf16 = jnp.bfloat16
        grads = [g.astype(bf16) for g in (grad_w_qkv, grad_w_out, grad_w_up, grad_w_down)]
        rms_row = jnp.pad(jnp.stack(rms_terms), (0, feat_width - 4))
        small = jnp.stack(
            [grad_gain_one, grad_bias_one, grad_gain_two, grad_bias_two, rms_row] + [rms_row] * 3
        )
        *sums, small = reduce_scatter(grads, small)
        rms_stats = jnp.sqrt(small[4, :3] / small[4, 3])
        count = feat_width // (seq_count * lax.axis_size("grp"))
        place = (lax.axis_index("grp") * seq_count + seq_index) * count
        vecs = [lax.dynamic_slice(small[i], (place,), (count,)) for i in range(4)]
        summed = (vecs[0], vecs[1], sums[0], sums[1], vecs[2], vecs[3], sums[2], sums[3])
    else:
        rms_parts = lax.psum(rms_terms, ("grp", "seq"))
        rms_stats = jnp.sqrt(jnp.stack(rms_parts[:3]) / rms_parts[3])
        summed = (
            lax.psum_scatter(grad_gain_one, ("grp", "seq"), scatter_dimension=0, tiled=True),
            lax.psum_scatter(grad_bias_one, ("grp", "seq"), scatter_dimension=0, tiled=True),
            lax.psum_scatter(grad_w_qkv, ("grp", "seq"), scatter_dimension=0, tiled=True),
            lax.psum_scatter(grad_w_out, ("grp", "seq"), scatter_dimension=0, tiled=True),
            lax.psum_scatter(grad_gain_two, ("grp", "seq"), scatter_dimension=0, tiled=True),
            lax.psum_scatter(grad_bias_two, ("grp", "seq"), scatter_dimension=0, tiled=True),
            lax.psum_scatter(grad_w_up, ("grp", "seq"), scatter_dimension=0, tiled=True),
            lax.psum_scatter(grad_w_down, ("grp", "seq"), scatter_dimension=0, tiled=True),
        )
    return (
        output.astype(jnp.bfloat16),
        input_grad,
        summed[0],
        summed[1],
        summed[2],
        summed[3],
        summed[4],
        summed[5],
        summed[6],
        summed[7],
        rms_stats,
    )


def solution(mesh):
    placed = (
        P(("grp", "seq"), None),
        P(("grp", "seq"), None),
        P("grp", None),
        P(),
        P(),
        P(),
        P(),
        P(),
        P(),
        P(),
        P(),
    )
    planned = mesh.shape["grp"] == 4 and mesh.shape["seq"] == 8
    return jax.shard_map(
        functools.partial(per_device, planned),
        mesh=mesh,
        in_specs=placed,
        out_specs=(
            P(("grp", "seq"), None),
            P(("grp", "seq"), None),
            P(("grp", "seq")),
            P(("grp", "seq")),
            P(("grp", "seq"), None),
            P(("grp", "seq"), None),
            P(("grp", "seq")),
            P(("grp", "seq")),
            P(("grp", "seq"), None),
            P(("grp", "seq"), None),
            P(),
        ),
        check_vma=False,
    )
```

```python
import functools

import jax
import jax.numpy as jnp
from jax import lax
from jax.experimental import pallas as pl
from jax.experimental.pallas import tpu as pltpu
from jax.sharding import PartitionSpec as P

D = 768
HEADS = 12
HEAD_DIM = 64
MESH = pl.DeviceIdType.MESH


epsilon = 1e-05


def passed_along(array, axis, by):
    devices = lax.axis_size(axis)
    pairs = [(i, i + by) for i in range(devices) if 0 <= i + by < devices]
    return lax.ppermute(array, axis, pairs)


def shifted(array, axis, by):
    devices = lax.axis_size(axis)
    return lax.ppermute(array, axis, [(i, (i + by) % devices) for i in range(devices)])


def layer_norm(vector, scale_vec, shift_vec):
    row_mean = jnp.mean(vector, axis=-1, keepdims=True)
    centered = vector - row_mean
    variance = jnp.mean(centered * centered, axis=-1, keepdims=True)
    return centered * lax.rsqrt(variance + epsilon) * scale_vec + shift_vec


def contract_rows(left, right):
    return lax.dot_general(
        left, right, (((0,), (0,)), ((), ())), preferred_element_type=jnp.float32
    )


def contract_cols(left, right):
    return lax.dot_general(
        left, right, (((1,), (1,)), ((), ())), preferred_element_type=jnp.float32
    )


def score_terms(queries, key_block, query_pos, key_pos, seq_first, seq_limit):
    scores = (
        jnp.einsum("qhd,khd->qhk", queries, key_block, preferred_element_type=jnp.float32) * 0.125
    )
    query_valid = (query_pos >= seq_first) & (query_pos < seq_limit)
    key_valid = (key_pos >= seq_first) & (key_pos < seq_limit)
    allowed = (key_pos[None, :] <= query_pos[:, None]) & (
        query_valid[:, None] & key_valid[None, :] | (key_pos[None, :] == query_pos[:, None])
    )
    magnitude = jnp.sqrt(scores * scores + 1.0)
    signed_part = scores / magnitude
    exp_terms = jnp.where(allowed[:, None, :], jnp.exp(magnitude), 0.0)
    return (magnitude, signed_part, exp_terms)


def split_pair(kv_pair):
    count_rows = kv_pair.shape[0]
    key_block = kv_pair[:, :D].reshape(count_rows, HEADS, HEAD_DIM)
    value_block = kv_pair[:, D:].reshape(count_rows, HEADS, HEAD_DIM)
    return (key_block, value_block)


def forward_block(running, kv_pair, key_start, queries, query_pos, seq_first, seq_limit):
    totals, unnorm = running
    key_block, value_block = split_pair(kv_pair)
    key_pos = key_start + jnp.arange(kv_pair.shape[0], dtype=jnp.int32)
    magnitude, signed_part, exp_terms = score_terms(
        queries, key_block, query_pos, key_pos, seq_first, seq_limit
    )
    weights = (signed_part * exp_terms).astype(jnp.bfloat16)
    totals = totals + jnp.sum(exp_terms, axis=-1)
    unnorm = unnorm + jnp.einsum(
        "qhk,khd->qhd", weights, value_block, preferred_element_type=jnp.float32
    )
    return (totals, unnorm)


def grad_core(
    kv_pair, key_start, queries, query_pos, seq_first, seq_limit, grad_unnorm, grad_totals
):
    key_block, value_block = split_pair(kv_pair)
    key_pos = key_start + jnp.arange(kv_pair.shape[0], dtype=jnp.int32)
    magnitude, signed_part, exp_terms = score_terms(
        queries, key_block, query_pos, key_pos, seq_first, seq_limit
    )
    weights = (signed_part * exp_terms).astype(jnp.bfloat16)
    grad_weights = jnp.einsum(
        "qhd,khd->qhk", grad_unnorm, value_block, preferred_element_type=jnp.float32
    )
    grad_scores = (
        grad_weights * exp_terms / (magnitude * magnitude * magnitude)
        + (grad_weights * signed_part + grad_totals[:, :, None]) * exp_terms * signed_part
    )
    return (key_block, weights, grad_scores.astype(jnp.bfloat16))


def backward_block(
    kv_pair, key_start, queries, query_pos, seq_first, seq_limit, grad_unnorm, grad_totals
):
    key_block, weights, grad_scores = grad_core(
        kv_pair, key_start, queries, query_pos, seq_first, seq_limit, grad_unnorm, grad_totals
    )
    count_rows = kv_pair.shape[0]
    grad_query = (
        jnp.einsum("qhk,khd->qhd", grad_scores, key_block, preferred_element_type=jnp.float32)
        * 0.125
    )
    grad_key = (
        jnp.einsum("qhk,qhd->khd", grad_scores, queries, preferred_element_type=jnp.float32) * 0.125
    )
    grad_value = jnp.einsum(
        "qhk,qhd->khd", weights, grad_unnorm, preferred_element_type=jnp.float32
    )
    grad_pair = jnp.concatenate(
        [grad_key.reshape(count_rows, D), grad_value.reshape(count_rows, D)], axis=1
    )
    return (grad_query, grad_pair)


def per_device(
    block_input,
    out_grad,
    seq_span,
    ln1_gain,
    ln1_bias,
    w_qkv,
    w_out,
    ln2_gain,
    ln2_bias,
    w_up,
    w_down,
):
    tok_rows = block_input.shape[0]
    feat_width = block_input.shape[1]
    seq_count = lax.axis_size("seq")
    seq_index = lax.axis_index("seq")
    query_pos = seq_index * tok_rows + jnp.arange(tok_rows, dtype=jnp.int32)
    query_last = query_pos[tok_rows - 1]
    seq_first = seq_span[0, 0]
    seq_limit = seq_span[0, 1]
    inputs = block_input.astype(jnp.float32)
    normed = layer_norm(inputs, ln1_gain, ln1_bias).astype(jnp.bfloat16)
    proj_qkv = jnp.dot(normed, w_qkv, preferred_element_type=jnp.float32).astype(jnp.bfloat16)
    queries = proj_qkv[:, :feat_width].reshape(tok_rows, HEADS, HEAD_DIM)
    kv_pair = proj_qkv[:, feat_width:]

    def visit_block(running, shard_rows, key_start):
        return lax.cond(
            key_start <= query_last,
            lambda state_in: forward_block(
                state_in, shard_rows, key_start, queries, query_pos, seq_first, seq_limit
            ),
            lambda state_in: state_in,
            running,
        )

    empty = (
        jnp.zeros((tok_rows, HEADS), jnp.float32),
        jnp.zeros((tok_rows, HEADS, HEAD_DIM), jnp.float32),
    )
    first_state = visit_block(empty, kv_pair, seq_index * tok_rows)

    def forward_hop(hop_count, loop_state):
        moving, running = loop_state
        moving = passed_along(moving, "seq", 1)
        source = (seq_index - hop_count) % seq_count
        return (moving, visit_block(running, moving, source * tok_rows))

    _, (totals, unnorm) = lax.fori_loop(1, seq_count, forward_hop, (kv_pair, first_state))
    mixed_heads = (unnorm / totals[:, :, None]).reshape(tok_rows, feat_width).astype(jnp.bfloat16)
    attn_out = jnp.dot(mixed_heads, w_out, preferred_element_type=jnp.float32)
    middle = inputs + attn_out
    normed_two = layer_norm(middle, ln2_gain, ln2_bias).astype(jnp.bfloat16)
    up_proj = jnp.dot(normed_two, w_up, preferred_element_type=jnp.float32)
    activated = jax.nn.gelu(up_proj, approximate=True).astype(jnp.bfloat16)
    mlp_out = jnp.dot(activated, w_down, preferred_element_type=jnp.float32)
    output = middle + mlp_out
    valid_rows = ((query_pos >= seq_first) & (query_pos < seq_limit)).astype(jnp.float32)[:, None]
    rms_parts = lax.psum(
        (
            jnp.sum(valid_rows * output * output),
            jnp.sum(valid_rows * attn_out * attn_out),
            jnp.sum(valid_rows * mlp_out * mlp_out),
            jnp.sum(valid_rows) * feat_width,
        ),
        ("grp", "seq"),
    )
    rms_stats = jnp.sqrt(jnp.stack([rms_parts[0], rms_parts[1], rms_parts[2]]) / rms_parts[3])
    grad_w_down = contract_rows(activated, out_grad)
    grad_activated = contract_cols(out_grad, w_down)
    _, gelu_pull = jax.vjp(lambda pre_act: jax.nn.gelu(pre_act, approximate=True), up_proj)
    grad_up = gelu_pull(grad_activated)[0].astype(jnp.bfloat16)
    grad_w_up = contract_rows(normed_two, grad_up)
    grad_norm_two = contract_cols(grad_up, w_up)
    _, norm_pull_two = jax.vjp(layer_norm, middle, ln2_gain, ln2_bias)
    grad_mid_norm, grad_gain_two, grad_bias_two = norm_pull_two(grad_norm_two)
    grad_middle = out_grad.astype(jnp.float32) + grad_mid_norm
    grad_attn = grad_middle.astype(jnp.bfloat16)
    grad_w_out = contract_rows(mixed_heads, grad_attn)
    grad_mixed = contract_cols(grad_attn, w_out).reshape(tok_rows, HEADS, HEAD_DIM)
    grad_unnorm = (grad_mixed / totals[:, :, None]).astype(jnp.bfloat16)
    grad_totals = -jnp.sum(grad_mixed * unnorm, axis=-1) / (totals * totals)

    def back_block(grad_run, shard_rows, key_start):

        def compute_block(grad_in):
            grad_query, grad_pair = backward_block(
                shard_rows,
                key_start,
                queries,
                query_pos,
                seq_first,
                seq_limit,
                grad_unnorm,
                grad_totals,
            )
            return (grad_in + grad_query, grad_pair)

        def skip_block(grad_in):
            return (grad_in, jnp.zeros((shard_rows.shape[0], 2 * feat_width), jnp.float32))

        return lax.cond(key_start <= query_last, compute_block, skip_block, grad_run)

    grad_start = jnp.zeros((tok_rows, HEADS, HEAD_DIM), jnp.float32)
    grad_queries, local_terms = back_block(grad_start, kv_pair, seq_index * tok_rows)

    def backward_hop(hop_count, loop_state):
        moving, grad_acc, grad_run = loop_state
        moving = passed_along(moving, "seq", 1)
        grad_acc = shifted(grad_acc.astype(jnp.bfloat16), "seq", 1).astype(grad_acc.dtype)
        source = (seq_index - hop_count) % seq_count
        grad_run, new_terms = back_block(grad_run, moving, source * tok_rows)
        return (moving, grad_acc + new_terms, grad_run)

    _, grad_acc, grad_queries = lax.fori_loop(
        1, seq_count, backward_hop, (kv_pair, local_terms, grad_queries)
    )
    grad_kv = shifted(grad_acc.astype(jnp.bfloat16), "seq", 1).astype(grad_acc.dtype)
    grad_qkv = jnp.concatenate(
        [grad_queries.reshape(tok_rows, feat_width), grad_kv], axis=1
    ).astype(jnp.bfloat16)
    grad_w_qkv = contract_rows(normed, grad_qkv)
    grad_norm_one = contract_cols(grad_qkv, w_qkv)
    _, norm_pull_one = jax.vjp(layer_norm, inputs, ln1_gain, ln1_bias)
    grad_in_norm, grad_gain_one, grad_bias_one = norm_pull_one(grad_norm_one)
    input_grad = (grad_middle + grad_in_norm).astype(jnp.bfloat16)
    summed = (
        lax.psum_scatter(grad_gain_one, ("grp", "seq"), scatter_dimension=0, tiled=True),
        lax.psum_scatter(grad_bias_one, ("grp", "seq"), scatter_dimension=0, tiled=True),
        lax.psum_scatter(grad_w_qkv, ("grp", "seq"), scatter_dimension=0, tiled=True),
        lax.psum_scatter(grad_w_out, ("grp", "seq"), scatter_dimension=0, tiled=True),
        lax.psum_scatter(grad_gain_two, ("grp", "seq"), scatter_dimension=0, tiled=True),
        lax.psum_scatter(grad_bias_two, ("grp", "seq"), scatter_dimension=0, tiled=True),
        lax.psum_scatter(grad_w_up, ("grp", "seq"), scatter_dimension=0, tiled=True),
        lax.psum_scatter(grad_w_down, ("grp", "seq"), scatter_dimension=0, tiled=True),
    )
    return (
        output.astype(jnp.bfloat16),
        input_grad,
        summed[0],
        summed[1],
        summed[2],
        summed[3],
        summed[4],
        summed[5],
        summed[6],
        summed[7],
        rms_stats,
    )


def rows_of(start, count):
    return pl.ds(pl.multiple_of(start, 16), count)


def matmul(left, right):
    return jnp.dot(left, right, preferred_element_type=jnp.float32)


def signed_terms(scores):
    square = scores * scores + 1.0
    inverse = lax.rsqrt(square)
    return inverse, scores * inverse, jnp.exp(square * inverse)


def valid_columns(span, start, count):
    pos = start + lax.broadcasted_iota(jnp.int32, (1, count), 1)
    return (pos >= span[0, 0]) & (pos < span[0, 1])


def greet(partners):
    barrier = pltpu.get_barrier_semaphore()
    for partner in partners:
        pl.semaphore_signal(barrier, inc=1, device_id=partner, device_id_type=MESH)
    pl.semaphore_wait(barrier, len(partners))


def sender(send_sems, recv_sems):
    count = [0]

    def send(src, dst, target):
        slot = count[0]
        count[0] += 1
        copy = pltpu.make_async_remote_copy(
            src_ref=src, dst_ref=dst, send_sem=send_sems.at[slot], recv_sem=recv_sems.at[slot],
            device_id=target, device_id_type=MESH,
        )
        copy.start()
        return copy

    return send


def place():
    grp, seq = lax.axis_index("grp"), lax.axis_index("seq")
    zed, core = seq // 2, seq % 2
    sibling = (grp, zed * 2 + 1 - core)
    along = [(zed + k) % 4 for k in range(4)]
    return grp, seq, zed, core, sibling, along


def attend_kernel(
    proj, span, mixed_out, q_all, kv_all, mix_all, tot_all,
    masked, arrived, leaving, own, keys, send_sems, recv_sems,
):
    tokens = proj.shape[-1]
    f32, bf16 = jnp.float32, jnp.bfloat16
    grp, seq, zed, core, sibling, along = place()
    line = [(grp, along[k] * 2 + core) for k in (1, 2, 3)]
    valid_here = valid_columns(span, seq * tokens, tokens)
    keep = valid_here.astype(f32)

    def mask_head(head, _):
        for part in range(3):
            masked[part, head] = (proj[part, head].astype(f32) * keep).astype(bf16)
        return 0

    lax.fori_loop(0, HEADS, mask_head, 0)
    greet([sibling] + line)
    send = sender(send_sems, recv_sems)
    going = []
    for h in range(3):
        for k in (1, 2, 3):
            head = along[k] * 3 + h
            going.append(send(masked.at[0, head], q_all.at[h, zed], line[k - 1]))
            going.append(
                send(masked.at[pl.ds(1, 2), head], kv_all.at[h, zed, core], line[k - 1])
            )
    for h in range(3):
        head = zed * 3 + h
        q_all[h, zed] = masked[0, head]
        for part in range(2):
            kv_all[h, zed, core, part] = masked[1 + part, head]

    def alone(head, _):
        q, k, v = (proj[part, head].astype(f32) for part in range(3))
        _, signed, terms = signed_terms(jnp.sum(q * k, axis=0, keepdims=True))
        weight = (signed * terms).astype(bf16).astype(f32)
        own[head] = (weight * v / terms).astype(bf16)
        return 0

    lax.fori_loop(0, HEADS, alone, 0)
    extra = span[0, 0].astype(f32) * signed_terms(jnp.zeros((1, tokens), f32))[2]

    returning = []
    for h in range(3):
        for copy in going[h * 6 : h * 6 + 6]:
            copy.wait_recv()
        relay = send(kv_all.at[h, :, core], kv_all.at[h, :, core], sibling)

        def turn(side):
            def one(z, _):
                keys[z, rows_of(side * tokens, tokens), :] = kv_all[h, z, side, 0].T
                return 0

            lax.fori_loop(0, 4, one, 0)

        turn(core)
        relay.wait()
        turn(1 - core)

        def query_block(z, _):
            queries = q_all[h, z]

            def pair(other, carry, last=False):
                total, mixed = carry
                for side in range(2):
                    scores = matmul(keys[other, pl.ds(side * tokens, tokens), :], queries)
                    _, signed, terms = signed_terms(scores)
                    if last:
                        key_pos = lax.broadcasted_iota(jnp.int32, scores.shape, 0)
                        query_pos = lax.broadcasted_iota(jnp.int32, scores.shape, 1)
                        seen = key_pos + side * tokens <= query_pos + core * tokens
                        terms = jnp.where(seen, terms, 0.0)
                    total = total + jnp.sum(terms.reshape(tokens // 8, 8, tokens), axis=0)
                    weights = (signed * terms).astype(bf16)
                    mixed = mixed + matmul(kv_all[h, other, side, 1], weights)
                return total, mixed

            zero = (jnp.zeros((8, tokens), f32), jnp.zeros((HEAD_DIM, tokens), f32))
            total, mixed = pair(z, lax.fori_loop(0, z, pair, zero), True)
            total = jnp.sum(total, axis=0, keepdims=True) - extra
            fine = valid_columns(span, (2 * z + core) * tokens, tokens)
            total = jnp.where(fine, total, 1.0)
            mixed = mixed / total
            mix_all[h, z] = mixed
            tot_all[h, z] = total
            leaving[h, z] = mixed.astype(bf16)
            return 0

        lax.fori_loop(0, 4, query_block, 0)
        for k in (1, 2, 3):
            returning.append(
                send(leaving.at[h, along[k]], arrived.at[zed * 3 + h], line[k - 1])
            )
        arrived[zed * 3 + h] = leaving[h, zed]
    for copy in returning:
        copy.wait_recv()

    def join(head, _):
        mixed_out[head] = jnp.where(
            valid_here, arrived[head].astype(f32), own[head].astype(f32)
        ).astype(bf16)
        return 0

    lax.fori_loop(0, HEADS, join, 0)
    for copy in going + returning:
        copy.wait_send()


def attend(proj, span):
    f32, bf16 = jnp.float32, jnp.bfloat16
    tokens = proj.shape[-1]
    vmem, smem = pl.BlockSpec(memory_space=pltpu.VMEM), pl.BlockSpec(memory_space=pltpu.SMEM)
    block = (HEAD_DIM, tokens)
    copies = 18 + 3 + 9
    return pl.pallas_call(
        attend_kernel,
        out_shape=[
            jax.ShapeDtypeStruct((HEADS,) + block, bf16),
            jax.ShapeDtypeStruct((3, 4) + block, bf16),
            jax.ShapeDtypeStruct((3, 4, 2, 2) + block, bf16),
            jax.ShapeDtypeStruct((3, 4) + block, f32),
            jax.ShapeDtypeStruct((3, 4, 1, tokens), f32),
        ],
        in_specs=[vmem, smem],
        out_specs=[vmem] * 5,
        scratch_shapes=[
            pltpu.VMEM((3, HEADS) + block, bf16),
            pltpu.VMEM((HEADS,) + block, bf16),
            pltpu.VMEM((3, 4) + block, bf16),
            pltpu.VMEM((HEADS,) + block, bf16),
            pltpu.VMEM((4, 2 * tokens, HEAD_DIM), bf16),
            pltpu.SemaphoreType.DMA((copies,)),
            pltpu.SemaphoreType.DMA((copies,)),
        ],
        compiler_params=pltpu.CompilerParams(
            collective_id=1, has_side_effects=True, vmem_limit_bytes=48 * 2**20
        ),
    )(proj, span)


def add_halves(term, first, column, base, count):
    def add(i, _):
        at = rows_of(base + i * 16, 16)
        first[at, :] = (
            term[at, column].astype(jnp.float32) + first[at, :].astype(jnp.float32)
        ).astype(jnp.bfloat16)
        return 0

    lax.fori_loop(0, count // 16, add, 0)


def add_groups(term, first, second, held, column, base, count):
    def add(i, _):
        at, here = rows_of(base + i * 16, 16), rows_of(i * 16, 16)
        total = term[at, column].astype(jnp.float32) + first[at, :].astype(jnp.float32)
        for j in range(3):
            total = total + second[j, here, :].astype(jnp.float32)
        held[here, :] = total.astype(jnp.bfloat16)
        return 0

    lax.fori_loop(0, count // 16, add, 0)


def across_groups(grp):
    return [((grp // 2 + k // 2) % 2) * 2 + (grp % 2 + k % 2) % 2 for k in range(4)]


def send_halves(send, term, first, core, across, sibling):
    rows, columns = term.shape[0] // 4, term.shape[1] // 2
    away = pl.ds(pl.multiple_of((1 - core) * columns, 128), columns)
    copies = {}
    for k in (1, 2, 3, 0):
        at = rows_of(across[k] * rows, rows)
        copies[k] = send(term.at[at, away], first.at[at, :], sibling)
    return copies


def send_quarters(send, copies, term, first, second, core, across, seq):
    rows, columns = term.shape[0] // 4, term.shape[1] // 2
    column = pl.ds(pl.multiple_of(core * columns, 128), columns)
    going = []
    for k in (1, 2, 3):
        base = across[k] * rows
        copies[k].wait_recv()
        add_halves(term, first, column, base, rows)
        going.append(send(first.at[rows_of(base, rows), :], second.at[k - 1], (across[k], seq)))
    return going


def sum_quarters(copies, going, term, first, second, held, core, across):
    rows, columns = term.shape[0] // 4, term.shape[1] // 2
    column = pl.ds(pl.multiple_of(core * columns, 128), columns)
    copies[0].wait_recv()
    for copy in going:
        copy.wait_recv()
    add_groups(term, first, second, held, column, across[0] * rows, rows)


def attend_back_kernel(many, *refs):
    gmix, proj, q_all, kv_all, mix_all, tot_all, span = refs[:7]
    terms_in = refs[7 : 7 + many]
    grad_out = refs[7 + many]
    held = refs[8 + many : 8 + 2 * many]
    rest = refs[8 + 2 * many :]
    first, second = rest[:many], rest[many : 2 * many]
    (gm_in, own, keys, values, g_all, gt_all, grad_kv, part_out, part_in, leaving, arrived,
     send_sems, recv_sems) = rest[2 * many :]
    tokens = proj.shape[-1]
    f32, bf16 = jnp.float32, jnp.bfloat16
    grp, seq, zed, core, sibling, along = place()
    line = [(grp, along[k] * 2 + core) for k in (1, 2, 3)]
    across = across_groups(grp)
    valid_here = valid_columns(span, seq * tokens, tokens)

    greet([sibling] + line + [(across[k], seq) for k in (1, 2, 3)])
    send = sender(send_sems, recv_sems)
    coming = []
    for h in range(3):
        for k in (1, 2, 3):
            coming.append(send(gmix.at[along[k] * 3 + h], gm_in.at[h, zed], line[k - 1]))
    halves = [send_halves(send, terms_in[a], first[a], core, across, sibling) for a in range(many)]
    for h in range(3):
        gm_in[h, zed] = gmix[zed * 3 + h]

    def alone(head, _):
        q, k, v = (proj[part, head].astype(f32) for part in range(3))
        g = gmix[head].astype(f32)
        inverse, signed, terms = signed_terms(jnp.sum(q * k, axis=0, keepdims=True))
        weight = (signed * terms).astype(bf16).astype(f32)
        total = 1.0 / terms
        grad_total = -jnp.sum(g * (weight * v), axis=0, keepdims=True) * total * total
        g = (g * total).astype(bf16).astype(f32)
        grad_weight = jnp.sum(g * v, axis=0, keepdims=True)
        square = inverse * inverse
        grad_score = terms * (grad_weight * (1.0 + square * (inverse - 1.0)) + grad_total * signed)
        grad_score = grad_score.astype(bf16).astype(f32)
        own[0, head] = (grad_score * k * 0.125).astype(bf16)
        own[1, head] = (grad_score * q).astype(bf16)
        own[2, head] = (weight * g).astype(bf16)
        return 0

    lax.fori_loop(0, HEADS, alone, 0)

    def turn(i, _):
        h, z = i // 4, i % 4
        for side in range(2):
            at = pl.ds(side * tokens, tokens)
            keys[h, z, at, :] = kv_all[h, z, side, 0].T
            values[h, z, at, :] = kv_all[h, z, side, 1].T
        return 0

    lax.fori_loop(0, 12, turn, 0)
    quarters = [
        send_quarters(send, halves[a], terms_in[a], first[a], second[a], core, across, seq)
        for a in range(many)
    ]

    swaps, sends = [], []

    def finish(h):
        swaps[h].wait_recv()

        def merge(z, _):
            for part in range(2):
                total = grad_kv[h, z, core, part] + part_in[h, z, part].astype(f32)
                leaving[h, z, 1 + part] = total.astype(bf16)
            return 0

        lax.fori_loop(0, 4, merge, 0)
        for k in (1, 2, 3):
            sends.append(send(leaving.at[h, along[k]], arrived.at[zed * 3 + h], line[k - 1]))
        arrived[zed * 3 + h] = leaving[h, zed]

    for h in range(3):
        for copy in coming[h * 3 : h * 3 + 3]:
            copy.wait_recv()

        def prepare(z, _):
            g = gm_in[h, z].astype(f32)
            total = 1.0 / tot_all[h, z]
            g_all[z] = (g * total).astype(bf16)
            gt_all[z] = -jnp.sum(g * mix_all[h, z], axis=0, keepdims=True) * total
            for side in range(2):
                for part in range(2):
                    grad_kv[h, z, side, part] = jnp.zeros((HEAD_DIM, tokens), f32)
            return 0

        lax.fori_loop(0, 4, prepare, 0)

        def query_block(z, _):
            queries, grads, grad_total = q_all[h, z], g_all[z], gt_all[z]

            def pair(other, grad_query, last=False):
                for side in range(2):
                    at = pl.ds(side * tokens, tokens)
                    scores = matmul(keys[h, other, at, :], queries)
                    grad_weights = matmul(values[h, other, at, :], grads)
                    inverse, signed, terms = signed_terms(scores)
                    if last:
                        key_pos = lax.broadcasted_iota(jnp.int32, scores.shape, 0)
                        query_pos = lax.broadcasted_iota(jnp.int32, scores.shape, 1)
                        seen = key_pos + side * tokens <= query_pos + core * tokens
                        terms = jnp.where(seen, terms, 0.0)
                    weights = (signed * terms).astype(bf16)
                    slope = 1.0 + (inverse * inverse) * (inverse - 1.0)
                    grad_scores = terms * (grad_weights * slope + grad_total * signed)
                    grad_scores = grad_scores.astype(bf16)
                    grad_query = grad_query + matmul(kv_all[h, other, side, 0], grad_scores)
                    grad_kv[h, other, side, 0] += contract_cols(queries, grad_scores)
                    grad_kv[h, other, side, 1] += contract_cols(grads, weights)
                return grad_query

            zero = jnp.zeros((HEAD_DIM, tokens), f32)
            grad_query = pair(z, lax.fori_loop(0, z, pair, zero), True)
            leaving[h, z, 0] = (grad_query * 0.125).astype(bf16)
            return 0

        lax.fori_loop(0, 4, query_block, 0)

        def pack(z, _):
            for part in range(2):
                part_out[h, z, part] = grad_kv[h, z, 1 - core, part].astype(bf16)
            return 0

        lax.fori_loop(0, 4, pack, 0)
        swaps.append(send(part_out.at[h], part_in.at[h], sibling))
        if h > 0:
            finish(h - 1)
    finish(2)
    for a in range(many):
        sum_quarters(
            halves[a], quarters[a], terms_in[a], first[a], second[a], held[a], core, across
        )
    for copy in sends:
        copy.wait_recv()

    def join(head, _):
        for part in range(3):
            grad_out[part, head] = jnp.where(
                valid_here, arrived[head, part].astype(f32), own[part, head].astype(f32)
            ).astype(bf16)
        return 0

    lax.fori_loop(0, HEADS, join, 0)
    for copy in coming + swaps + sends:
        copy.wait_send()
    for a in range(many):
        for copy in list(halves[a].values()) + quarters[a]:
            copy.wait_send()


def attend_back(gmix, proj, saved, span, terms):
    f32, bf16 = jnp.float32, jnp.bfloat16
    tokens = proj.shape[-1]
    many = len(terms)
    vmem, smem = pl.BlockSpec(memory_space=pltpu.VMEM), pl.BlockSpec(memory_space=pltpu.SMEM)
    block = (HEAD_DIM, tokens)
    copies = 9 + 7 * many + 3 + 9
    shapes = [t.shape for t in terms]
    return pl.pallas_call(
        functools.partial(attend_back_kernel, many),
        out_shape=[jax.ShapeDtypeStruct((3, HEADS) + block, bf16)]
        + [jax.ShapeDtypeStruct((r // 4, c // 2), bf16) for r, c in shapes],
        in_specs=[vmem] * 6 + [smem] + [vmem] * many,
        out_specs=[vmem] * (1 + many),
        scratch_shapes=[pltpu.VMEM((r, c // 2), bf16) for r, c in shapes]
        + [pltpu.VMEM((3, r // 4, c // 2), bf16) for r, c in shapes]
        + [
            pltpu.VMEM((3, 4) + block, bf16),
            pltpu.VMEM((3, HEADS) + block, bf16),
            pltpu.VMEM((3, 4, 2 * tokens, HEAD_DIM), bf16),
            pltpu.VMEM((3, 4, 2 * tokens, HEAD_DIM), bf16),
            pltpu.VMEM((4,) + block, bf16),
            pltpu.VMEM((4, 1, tokens), f32),
            pltpu.VMEM((3, 4, 2, 2) + block, f32),
            pltpu.VMEM((3, 4, 2) + block, bf16),
            pltpu.VMEM((3, 4, 2) + block, bf16),
            pltpu.VMEM((3, 4, 3) + block, bf16),
            pltpu.VMEM((HEADS, 3) + block, bf16),
            pltpu.SemaphoreType.DMA((copies,)),
            pltpu.SemaphoreType.DMA((copies,)),
        ],
        compiler_params=pltpu.CompilerParams(
            collective_id=2, has_side_effects=True, vmem_limit_bytes=60 * 2**20
        ),
    )(gmix, proj, *saved, span, *terms)


def send_line(send, held, third, along, line):
    rows = held.shape[0] // 4
    return [
        send(held.at[rows_of(along[k] * rows, rows), :], third.at[k - 1], line[k - 1])
        for k in (1, 2, 3)
    ]


def sum_line(send, copies, held, third, mine, out, zed, core, sibling):
    rows, columns = held.shape[0] // 4, held.shape[1]
    for copy in copies:
        copy.wait_recv()
    total = held[rows_of(zed * rows, rows), :].astype(jnp.float32)
    for j in range(3):
        total = total + third[j].astype(jnp.float32)
    mine[...] = total
    column = pl.ds(pl.multiple_of(core * columns, 128), columns)
    half = rows // 2
    away = pl.ds(pl.multiple_of((1 - core) * half, 8), half)
    out[:, column] = mine[pl.ds(pl.multiple_of(core * half, 8), half), :]
    return send(mine.at[away, :], out.at[:, column], sibling)


def finish_kernel(many, *refs):
    term, small_in = refs[:2]
    early = refs[2 : 2 + many]
    outs = refs[2 + many : 3 + 2 * many]
    small_out = refs[3 + 2 * many]
    rest = refs[4 + 2 * many :]
    third, mine = rest[: many + 1], rest[many + 1 : 2 * many + 2]
    first, second, held, small_a, small_b, small_c, send_sems, recv_sems = rest[2 * many + 2 :]
    grp, seq, zed, core, sibling, along = place()
    line = [(grp, along[k] * 2 + core) for k in (1, 2, 3)]
    across = across_groups(grp)
    greet([sibling] + line + [(across[k], seq) for k in (1, 2, 3)])
    send = sender(send_sems, recv_sems)
    swap = send(small_in, small_a.at[1], sibling)
    halves = send_halves(send, term, first, core, across, sibling)
    lines = [send_line(send, early[a], third[1 + a], along, line) for a in range(many)]
    swap.wait_recv()
    small_a[0] = small_in[...] + small_a[1]
    small_b[pl.ds(grp, 1)] = small_a[0:1]
    planes = [send(small_a.at[0], small_b.at[grp], (across[k], seq)) for k in (1, 2, 3)]
    quarters = send_quarters(send, halves, term, first, second, core, across, seq)
    for copy in planes:
        copy.wait_recv()
    small_c[pl.ds(zed, 1)] = (small_b[0:1] + small_b[1:2]) + (small_b[2:3] + small_b[3:4])
    columns = [send(small_c.at[zed], small_c.at[zed], line[k - 1]) for k in (1, 2, 3)]
    swaps = []
    for a in range(many):
        swaps.append(
            sum_line(
                send, lines[a], early[a], third[1 + a], mine[1 + a], outs[1 + a], zed, core, sibling
            )
        )
    for copy in columns:
        copy.wait_recv()
    small_out[...] = (small_c[0] + small_c[1]) + (small_c[2] + small_c[3])
    sum_quarters(halves, quarters, term, first, second, held, core, across)
    last = send_line(send, held, third[0], along, line)
    swaps.append(sum_line(send, last, held, third[0], mine[0], outs[0], zed, core, sibling))
    for copy in swaps:
        copy.wait_recv()
    for copy in [swap] + planes + columns + swaps + quarters + last + list(halves.values()):
        copy.wait_send()
    for copies in lines:
        for copy in copies:
            copy.wait_send()


def finish(term, small, early):
    f32, bf16 = jnp.float32, jnp.bfloat16
    many = len(early)
    vmem = pl.BlockSpec(memory_space=pltpu.VMEM)
    r, c = term.shape
    helds = [(r // 4, c // 2)] + [e.shape for e in early]
    copies = 1 + 4 + 3 * many + 3 + 3 + 3 + many + 3 + 1
    return pl.pallas_call(
        functools.partial(finish_kernel, many),
        out_shape=[jax.ShapeDtypeStruct((hr // 8, 2 * hc), f32) for hr, hc in helds]
        + [jax.ShapeDtypeStruct(small.shape, f32)],
        in_specs=[vmem] * (2 + many),
        out_specs=[vmem] * (2 + many),
        scratch_shapes=[pltpu.VMEM((3, hr // 4, hc), bf16) for hr, hc in helds]
        + [pltpu.VMEM((hr // 4, hc), f32) for hr, hc in helds]
        + [
            pltpu.VMEM((r, c // 2), bf16),
            pltpu.VMEM((3, r // 4, c // 2), bf16),
            pltpu.VMEM((r // 4, c // 2), bf16),
            pltpu.VMEM((2,) + small.shape, f32),
            pltpu.VMEM((4,) + small.shape, f32),
            pltpu.VMEM((4,) + small.shape, f32),
            pltpu.SemaphoreType.DMA((copies,)),
            pltpu.SemaphoreType.DMA((copies,)),
        ],
        compiler_params=pltpu.CompilerParams(
            collective_id=0, has_side_effects=True, vmem_limit_bytes=48 * 2**20
        ),
    )(term, small, *early)


def per_device_planned(
    block_input,
    out_grad,
    seq_span,
    ln1_gain,
    ln1_bias,
    w_qkv,
    w_out,
    ln2_gain,
    ln2_bias,
    w_up,
    w_down,
):
    f32, bf16 = jnp.float32, jnp.bfloat16
    tokens, width = block_input.shape
    seq_count = lax.axis_size("seq")
    seq_index = lax.axis_index("seq")
    token_pos = seq_index * tokens + jnp.arange(tokens, dtype=jnp.int32)
    valid = (token_pos >= seq_span[0, 0]) & (token_pos < seq_span[0, 1])
    inputs = block_input.astype(f32)
    normed = layer_norm(inputs, ln1_gain, ln1_bias).astype(bf16)
    proj = lax.dot_general(w_qkv, normed, (((0,), (1,)), ((), ())), preferred_element_type=f32)
    scale = jnp.where(jnp.arange(3 * width) < width, 0.125, 1.0).astype(f32)
    proj = (proj * scale[:, None]).astype(bf16).reshape(3, HEADS, HEAD_DIM, tokens)
    mixed, *saved = attend(proj, seq_span)
    mixed = mixed.reshape(width, tokens)

    attn_out = contract_rows(mixed, w_out)
    middle = inputs + attn_out
    normed_two = layer_norm(middle, ln2_gain, ln2_bias).astype(bf16)
    up_proj = jnp.dot(normed_two, w_up, preferred_element_type=f32)
    activated, gelu_pull = jax.vjp(lambda u: jax.nn.gelu(u, approximate=True), up_proj)
    activated = activated.astype(bf16)
    mlp_out = jnp.dot(activated, w_down, preferred_element_type=f32)
    output = middle + mlp_out
    valid_rows = valid.astype(f32)[:, None]
    rms_terms = (
        jnp.sum(valid_rows * output * output),
        jnp.sum(valid_rows * attn_out * attn_out),
        jnp.sum(valid_rows * mlp_out * mlp_out),
        jnp.sum(valid_rows) * width,
    )
    term_down = contract_rows(activated, out_grad).astype(bf16)
    grad_up = gelu_pull(contract_cols(out_grad, w_down))[0].astype(bf16)
    term_up = contract_rows(normed_two, grad_up).astype(bf16)
    grad_norm_two = contract_cols(grad_up, w_up)
    _, norm_pull_two = jax.vjp(layer_norm, middle, ln2_gain, ln2_bias)
    grad_mid_norm, grad_gain_two, grad_bias_two = norm_pull_two(grad_norm_two)
    grad_middle = out_grad.astype(f32) + grad_mid_norm
    grad_attn = grad_middle.astype(bf16)
    term_out = jnp.dot(mixed, grad_attn, preferred_element_type=f32).astype(bf16)
    grad_mixed = contract_cols(w_out, grad_attn).astype(bf16)
    grad_qkv, *early = attend_back(
        grad_mixed.reshape(HEADS, HEAD_DIM, tokens),
        proj,
        saved,
        seq_span,
        (term_down, term_up, term_out),
    )
    grad_qkv = grad_qkv.reshape(3 * width, tokens)
    term_qkv = lax.dot_general(
        normed, grad_qkv, (((0,), (1,)), ((), ())), preferred_element_type=f32
    ).astype(bf16)
    grad_norm_one = lax.dot_general(
        grad_qkv, w_qkv, (((0,), (1,)), ((), ())), preferred_element_type=f32
    )
    _, norm_pull_one = jax.vjp(layer_norm, inputs, ln1_gain, ln1_bias)
    grad_in_norm, grad_gain_one, grad_bias_one = norm_pull_one(grad_norm_one)
    input_grad = (grad_middle + grad_in_norm).astype(bf16)

    rms_row = jnp.pad(jnp.stack(rms_terms), (0, width - 4))
    small = jnp.stack(
        [grad_gain_one, grad_bias_one, grad_gain_two, grad_bias_two, rms_row] + [rms_row] * 3
    )
    sum_qkv, sum_down, sum_up, sum_out, small = finish(term_qkv, small, early)
    rms_stats = jnp.sqrt(small[4, :3] / small[4, 3])
    count = width // (seq_count * lax.axis_size("grp"))
    start = (lax.axis_index("grp") * seq_count + seq_index) * count
    vecs = [lax.dynamic_slice(small[i], (start,), (count,)) for i in range(4)]
    return (
        output.astype(bf16),
        input_grad,
        vecs[0],
        vecs[1],
        sum_qkv,
        sum_out,
        vecs[2],
        vecs[3],
        sum_up,
        sum_down,
        rms_stats,
    )


def solution(mesh):
    placed = (
        P(("grp", "seq"), None),
        P(("grp", "seq"), None),
        P("grp", None),
        P(),
        P(),
        P(),
        P(),
        P(),
        P(),
        P(),
        P(),
    )
    planned = mesh.shape["grp"] == 4 and mesh.shape["seq"] == 8
    return jax.shard_map(
        per_device_planned if planned else per_device,
        mesh=mesh,
        in_specs=placed,
        out_specs=(
            P(("grp", "seq"), None),
            P(("grp", "seq"), None),
            P(("grp", "seq")),
            P(("grp", "seq")),
            P(("grp", "seq"), None),
            P(("grp", "seq"), None),
            P(("grp", "seq")),
            P(("grp", "seq")),
            P(("grp", "seq"), None),
            P(("grp", "seq"), None),
            P(),
        ),
        check_vma=False,
    )
```

```python
import functools

import jax
import jax.numpy as jnp
from jax import lax
from jax.experimental import pallas as pl
from jax.experimental.pallas import tpu as pltpu
from jax.sharding import PartitionSpec as P

D = 768
HEADS = 12
HEAD_DIM = 64
MESH = pl.DeviceIdType.MESH


epsilon = 1e-05


def passed_along(array, axis, by):
    devices = lax.axis_size(axis)
    pairs = [(i, i + by) for i in range(devices) if 0 <= i + by < devices]
    return lax.ppermute(array, axis, pairs)


def shifted(array, axis, by):
    devices = lax.axis_size(axis)
    return lax.ppermute(array, axis, [(i, (i + by) % devices) for i in range(devices)])


def layer_norm(vector, scale_vec, shift_vec):
    row_mean = jnp.mean(vector, axis=-1, keepdims=True)
    centered = vector - row_mean
    variance = jnp.mean(centered * centered, axis=-1, keepdims=True)
    return centered * lax.rsqrt(variance + epsilon) * scale_vec + shift_vec


def contract_rows(left, right):
    return lax.dot_general(
        left, right, (((0,), (0,)), ((), ())), preferred_element_type=jnp.float32
    )


def contract_cols(left, right):
    return lax.dot_general(
        left, right, (((1,), (1,)), ((), ())), preferred_element_type=jnp.float32
    )


def score_terms(queries, key_block, query_pos, key_pos, seq_first, seq_limit):
    scores = (
        jnp.einsum("qhd,khd->qhk", queries, key_block, preferred_element_type=jnp.float32) * 0.125
    )
    query_valid = (query_pos >= seq_first) & (query_pos < seq_limit)
    key_valid = (key_pos >= seq_first) & (key_pos < seq_limit)
    allowed = (key_pos[None, :] <= query_pos[:, None]) & (
        query_valid[:, None] & key_valid[None, :] | (key_pos[None, :] == query_pos[:, None])
    )
    magnitude = jnp.sqrt(scores * scores + 1.0)
    signed_part = scores / magnitude
    exp_terms = jnp.where(allowed[:, None, :], jnp.exp(magnitude), 0.0)
    return (magnitude, signed_part, exp_terms)


def split_pair(kv_pair):
    count_rows = kv_pair.shape[0]
    key_block = kv_pair[:, :D].reshape(count_rows, HEADS, HEAD_DIM)
    value_block = kv_pair[:, D:].reshape(count_rows, HEADS, HEAD_DIM)
    return (key_block, value_block)


def forward_block(running, kv_pair, key_start, queries, query_pos, seq_first, seq_limit):
    totals, unnorm = running
    key_block, value_block = split_pair(kv_pair)
    key_pos = key_start + jnp.arange(kv_pair.shape[0], dtype=jnp.int32)
    magnitude, signed_part, exp_terms = score_terms(
        queries, key_block, query_pos, key_pos, seq_first, seq_limit
    )
    weights = (signed_part * exp_terms).astype(jnp.bfloat16)
    totals = totals + jnp.sum(exp_terms, axis=-1)
    unnorm = unnorm + jnp.einsum(
        "qhk,khd->qhd", weights, value_block, preferred_element_type=jnp.float32
    )
    return (totals, unnorm)


def grad_core(
    kv_pair, key_start, queries, query_pos, seq_first, seq_limit, grad_unnorm, grad_totals
):
    key_block, value_block = split_pair(kv_pair)
    key_pos = key_start + jnp.arange(kv_pair.shape[0], dtype=jnp.int32)
    magnitude, signed_part, exp_terms = score_terms(
        queries, key_block, query_pos, key_pos, seq_first, seq_limit
    )
    weights = (signed_part * exp_terms).astype(jnp.bfloat16)
    grad_weights = jnp.einsum(
        "qhd,khd->qhk", grad_unnorm, value_block, preferred_element_type=jnp.float32
    )
    grad_scores = (
        grad_weights * exp_terms / (magnitude * magnitude * magnitude)
        + (grad_weights * signed_part + grad_totals[:, :, None]) * exp_terms * signed_part
    )
    return (key_block, weights, grad_scores.astype(jnp.bfloat16))


def backward_block(
    kv_pair, key_start, queries, query_pos, seq_first, seq_limit, grad_unnorm, grad_totals
):
    key_block, weights, grad_scores = grad_core(
        kv_pair, key_start, queries, query_pos, seq_first, seq_limit, grad_unnorm, grad_totals
    )
    count_rows = kv_pair.shape[0]
    grad_query = (
        jnp.einsum("qhk,khd->qhd", grad_scores, key_block, preferred_element_type=jnp.float32)
        * 0.125
    )
    grad_key = (
        jnp.einsum("qhk,qhd->khd", grad_scores, queries, preferred_element_type=jnp.float32) * 0.125
    )
    grad_value = jnp.einsum(
        "qhk,qhd->khd", weights, grad_unnorm, preferred_element_type=jnp.float32
    )
    grad_pair = jnp.concatenate(
        [grad_key.reshape(count_rows, D), grad_value.reshape(count_rows, D)], axis=1
    )
    return (grad_query, grad_pair)


def per_device(
    block_input,
    out_grad,
    seq_span,
    ln1_gain,
    ln1_bias,
    w_qkv,
    w_out,
    ln2_gain,
    ln2_bias,
    w_up,
    w_down,
):
    tok_rows = block_input.shape[0]
    feat_width = block_input.shape[1]
    seq_count = lax.axis_size("seq")
    seq_index = lax.axis_index("seq")
    query_pos = seq_index * tok_rows + jnp.arange(tok_rows, dtype=jnp.int32)
    query_last = query_pos[tok_rows - 1]
    seq_first = seq_span[0, 0]
    seq_limit = seq_span[0, 1]
    inputs = block_input.astype(jnp.float32)
    normed = layer_norm(inputs, ln1_gain, ln1_bias).astype(jnp.bfloat16)
    proj_qkv = jnp.dot(normed, w_qkv, preferred_element_type=jnp.float32).astype(jnp.bfloat16)
    queries = proj_qkv[:, :feat_width].reshape(tok_rows, HEADS, HEAD_DIM)
    kv_pair = proj_qkv[:, feat_width:]

    def visit_block(running, shard_rows, key_start):
        return lax.cond(
            key_start <= query_last,
            lambda state_in: forward_block(
                state_in, shard_rows, key_start, queries, query_pos, seq_first, seq_limit
            ),
            lambda state_in: state_in,
            running,
        )

    empty = (
        jnp.zeros((tok_rows, HEADS), jnp.float32),
        jnp.zeros((tok_rows, HEADS, HEAD_DIM), jnp.float32),
    )
    first_state = visit_block(empty, kv_pair, seq_index * tok_rows)

    def forward_hop(hop_count, loop_state):
        moving, running = loop_state
        moving = passed_along(moving, "seq", 1)
        source = (seq_index - hop_count) % seq_count
        return (moving, visit_block(running, moving, source * tok_rows))

    _, (totals, unnorm) = lax.fori_loop(1, seq_count, forward_hop, (kv_pair, first_state))
    mixed_heads = (unnorm / totals[:, :, None]).reshape(tok_rows, feat_width).astype(jnp.bfloat16)
    attn_out = jnp.dot(mixed_heads, w_out, preferred_element_type=jnp.float32)
    middle = inputs + attn_out
    normed_two = layer_norm(middle, ln2_gain, ln2_bias).astype(jnp.bfloat16)
    up_proj = jnp.dot(normed_two, w_up, preferred_element_type=jnp.float32)
    activated = jax.nn.gelu(up_proj, approximate=True).astype(jnp.bfloat16)
    mlp_out = jnp.dot(activated, w_down, preferred_element_type=jnp.float32)
    output = middle + mlp_out
    valid_rows = ((query_pos >= seq_first) & (query_pos < seq_limit)).astype(jnp.float32)[:, None]
    rms_parts = lax.psum(
        (
            jnp.sum(valid_rows * output * output),
            jnp.sum(valid_rows * attn_out * attn_out),
            jnp.sum(valid_rows * mlp_out * mlp_out),
            jnp.sum(valid_rows) * feat_width,
        ),
        ("grp", "seq"),
    )
    rms_stats = jnp.sqrt(jnp.stack([rms_parts[0], rms_parts[1], rms_parts[2]]) / rms_parts[3])
    grad_w_down = contract_rows(activated, out_grad)
    grad_activated = contract_cols(out_grad, w_down)
    _, gelu_pull = jax.vjp(lambda pre_act: jax.nn.gelu(pre_act, approximate=True), up_proj)
    grad_up = gelu_pull(grad_activated)[0].astype(jnp.bfloat16)
    grad_w_up = contract_rows(normed_two, grad_up)
    grad_norm_two = contract_cols(grad_up, w_up)
    _, norm_pull_two = jax.vjp(layer_norm, middle, ln2_gain, ln2_bias)
    grad_mid_norm, grad_gain_two, grad_bias_two = norm_pull_two(grad_norm_two)
    grad_middle = out_grad.astype(jnp.float32) + grad_mid_norm
    grad_attn = grad_middle.astype(jnp.bfloat16)
    grad_w_out = contract_rows(mixed_heads, grad_attn)
    grad_mixed = contract_cols(grad_attn, w_out).reshape(tok_rows, HEADS, HEAD_DIM)
    grad_unnorm = (grad_mixed / totals[:, :, None]).astype(jnp.bfloat16)
    grad_totals = -jnp.sum(grad_mixed * unnorm, axis=-1) / (totals * totals)

    def back_block(grad_run, shard_rows, key_start):

        def compute_block(grad_in):
            grad_query, grad_pair = backward_block(
                shard_rows,
                key_start,
                queries,
                query_pos,
                seq_first,
                seq_limit,
                grad_unnorm,
                grad_totals,
            )
            return (grad_in + grad_query, grad_pair)

        def skip_block(grad_in):
            return (grad_in, jnp.zeros((shard_rows.shape[0], 2 * feat_width), jnp.float32))

        return lax.cond(key_start <= query_last, compute_block, skip_block, grad_run)

    grad_start = jnp.zeros((tok_rows, HEADS, HEAD_DIM), jnp.float32)
    grad_queries, local_terms = back_block(grad_start, kv_pair, seq_index * tok_rows)

    def backward_hop(hop_count, loop_state):
        moving, grad_acc, grad_run = loop_state
        moving = passed_along(moving, "seq", 1)
        grad_acc = shifted(grad_acc.astype(jnp.bfloat16), "seq", 1).astype(grad_acc.dtype)
        source = (seq_index - hop_count) % seq_count
        grad_run, new_terms = back_block(grad_run, moving, source * tok_rows)
        return (moving, grad_acc + new_terms, grad_run)

    _, grad_acc, grad_queries = lax.fori_loop(
        1, seq_count, backward_hop, (kv_pair, local_terms, grad_queries)
    )
    grad_kv = shifted(grad_acc.astype(jnp.bfloat16), "seq", 1).astype(grad_acc.dtype)
    grad_qkv = jnp.concatenate(
        [grad_queries.reshape(tok_rows, feat_width), grad_kv], axis=1
    ).astype(jnp.bfloat16)
    grad_w_qkv = contract_rows(normed, grad_qkv)
    grad_norm_one = contract_cols(grad_qkv, w_qkv)
    _, norm_pull_one = jax.vjp(layer_norm, inputs, ln1_gain, ln1_bias)
    grad_in_norm, grad_gain_one, grad_bias_one = norm_pull_one(grad_norm_one)
    input_grad = (grad_middle + grad_in_norm).astype(jnp.bfloat16)
    summed = (
        lax.psum_scatter(grad_gain_one, ("grp", "seq"), scatter_dimension=0, tiled=True),
        lax.psum_scatter(grad_bias_one, ("grp", "seq"), scatter_dimension=0, tiled=True),
        lax.psum_scatter(grad_w_qkv, ("grp", "seq"), scatter_dimension=0, tiled=True),
        lax.psum_scatter(grad_w_out, ("grp", "seq"), scatter_dimension=0, tiled=True),
        lax.psum_scatter(grad_gain_two, ("grp", "seq"), scatter_dimension=0, tiled=True),
        lax.psum_scatter(grad_bias_two, ("grp", "seq"), scatter_dimension=0, tiled=True),
        lax.psum_scatter(grad_w_up, ("grp", "seq"), scatter_dimension=0, tiled=True),
        lax.psum_scatter(grad_w_down, ("grp", "seq"), scatter_dimension=0, tiled=True),
    )
    return (
        output.astype(jnp.bfloat16),
        input_grad,
        summed[0],
        summed[1],
        summed[2],
        summed[3],
        summed[4],
        summed[5],
        summed[6],
        summed[7],
        rms_stats,
    )


def rows_of(start, count):
    return pl.ds(pl.multiple_of(start, 16), count)


def matmul(left, right):
    return jnp.dot(left, right, preferred_element_type=jnp.float32)


def signed_terms(scores):
    square = scores * scores + 1.0
    inverse = lax.rsqrt(square)
    return inverse, scores * inverse, jnp.exp(square * inverse)


def valid_columns(span, start, count):
    pos = start + lax.broadcasted_iota(jnp.int32, (1, count), 1)
    return (pos >= span[0, 0]) & (pos < span[0, 1])


def greet(partners):
    barrier = pltpu.get_barrier_semaphore()
    for partner in partners:
        pl.semaphore_signal(barrier, inc=1, device_id=partner, device_id_type=MESH)
    pl.semaphore_wait(barrier, len(partners))


def sender(send_sems, recv_sems):
    count = [0]

    def send(src, dst, target):
        slot = count[0]
        count[0] += 1
        copy = pltpu.make_async_remote_copy(
            src_ref=src, dst_ref=dst, send_sem=send_sems.at[slot], recv_sem=recv_sems.at[slot],
            device_id=target, device_id_type=MESH,
        )
        copy.start()
        return copy

    return send


def place():
    grp, seq = lax.axis_index("grp"), lax.axis_index("seq")
    zed, core = seq // 2, seq % 2
    sibling = (grp, zed * 2 + 1 - core)
    along = [(zed + k) % 4 for k in range(4)]
    return grp, seq, zed, core, sibling, along


def alone_terms(raw):
    q, k, v = (raw[part].astype(jnp.float32) for part in range(3))
    inverse, signed, terms = signed_terms(jnp.sum(q * k, axis=0, keepdims=True))
    weight = (signed * terms).astype(jnp.bfloat16).astype(jnp.float32)
    return q, k, v, inverse, signed, terms, weight


def attend_kernel(
    x, gain, bias, w_qkv, span, mixed_out, q_all, kv_all, raw, mix_all, tot_all, norm_all,
    windows, weights, keys, mixes, totals, leaving, load, hop_send, hop_recv, swap_send, swap_recv, back_send, back_recv,
):
    tokens, width = x.shape
    f32, bf16 = jnp.float32, jnp.bfloat16
    grp, seq, zed, core, sibling, along = place()

    start = pl.multiple_of(zed * 192 // 128 * 128, 128)
    inside = pl.ds(pl.multiple_of(zed % 2 * HEAD_DIM, HEAD_DIM), 3 * HEAD_DIM)
    loads = []
    for part in range(3):
        window = w_qkv.at[:, pl.ds(pl.multiple_of(part * width + start, 128), 256)]
        loads.append(pltpu.make_async_copy(window, windows.at[part], load.at[part]))
        loads[-1].start()
    greet_line(grp, zed, core)
    vector = x[...].astype(f32)
    centered = vector - jnp.mean(vector, axis=-1, keepdims=True)
    variance = jnp.mean(centered * centered, axis=-1, keepdims=True)
    normed = (
        centered * lax.rsqrt(variance + epsilon) * gain[...].reshape(1, width)
        + bias[...].reshape(1, width)
    ).astype(bf16)
    norm_all[zed] = normed.T

    def hop(step, side):
        towards = 1 - 2 * side
        block = zed - towards * step
        runs = (block >= 0) & (block < 4) & (zed + towards >= 0) & (zed + towards < 4)
        copy = pltpu.make_async_remote_copy(
            src_ref=norm_all.at[block], dst_ref=norm_all.at[block],
            send_sem=hop_send.at[side, step], recv_sem=hop_recv.at[side, step],
            device_id=(grp, (zed + towards) * 2 + core), device_id_type=MESH,
        )
        return runs, copy

    def hop_on(step):
        for side in range(2):
            runs, copy = hop(step, side)
            pl.when(runs)(copy.start)

    hop_on(0)
    for part in range(3):
        loads[part].wait()
        weights[part] = windows[part].T
    no_score = signed_terms(jnp.zeros((1, tokens), f32))[2]
    extra = span[0, 0].astype(f32) * no_score
    mixes[...] = jnp.zeros(mixes.shape, f32)
    totals[...] = jnp.zeros(totals.shape, f32)

    def swap(block, slot):
        return pltpu.make_async_remote_copy(
            src_ref=kv_all.at[:, block, core], dst_ref=kv_all.at[:, block, core],
            send_sem=swap_send.at[slot], recv_sem=swap_recv.at[slot],
            device_id=sibling, device_id_type=MESH,
        )

    def project(block, slot):
        keep = valid_columns(span, (2 * block + core) * tokens, tokens).astype(f32)
        for part in range(3):
            heads = matmul(weights[part, inside, :], norm_all[block])
            if part == 0:
                heads = heads * 0.125
            for h in range(3):
                one = heads[h * HEAD_DIM : (h + 1) * HEAD_DIM]
                raw[block, 3 * h + part] = one.astype(bf16)
                if part == 0:
                    q_all[h, block] = (one * keep).astype(bf16)
                else:
                    kv_all[h, block, core, part - 1] = (one * keep).astype(bf16)
        swap(block, slot).start()

    def turn(block, slot):
        swap(block, slot).wait_recv()
        for h in range(3):
            for side in range(2):
                keys[h, block, side * tokens : (side + 1) * tokens, :] = kv_all[h, block, side, 0].T

    def pair(block, other, last):
        results = []
        for h in range(3):
            queries = q_all[h, block]
            total, mixed = totals[h, block], mixes[h, block]
            for side in range(2):
                scores = matmul(keys[h, other, side * tokens : (side + 1) * tokens, :], queries)
                _, signed, terms = signed_terms(scores)
                if last:
                    key_pos = lax.broadcasted_iota(jnp.int32, scores.shape, 0)
                    query_pos = lax.broadcasted_iota(jnp.int32, scores.shape, 1)
                    seen = key_pos + side * tokens <= query_pos + core * tokens
                    terms = jnp.where(seen, terms, 0.0)
                total = total + jnp.sum(terms.reshape(tokens // 8, 8, tokens), axis=0)
                mixed = mixed + matmul(kv_all[h, other, side, 1], (signed * terms).astype(bf16))
            results.append((total, mixed))
        for h, (total, mixed) in enumerate(results):
            totals[h, block], mixes[h, block] = total, mixed

    def back(block):
        return pltpu.make_async_remote_copy(
            src_ref=leaving.at[block], dst_ref=mixed_out.at[pl.ds(3 * zed, 3)],
            send_sem=back_send.at[block], recv_sem=back_recv.at[zed],
            device_id=(grp, block * 2 + core), device_id_type=MESH,
        )

    def complete(block):
        fine = valid_columns(span, (2 * block + core) * tokens, tokens)
        for h in range(3):
            total = jnp.sum(totals[h, block], axis=0, keepdims=True) - extra
            total = jnp.where(fine, total, 1.0)
            mixed = mixes[h, block] / total
            mix_all[h, block] = mixed
            tot_all[h, block] = total
            _, _, v, _, _, terms, weight = alone_terms(raw.at[block, pl.ds(3 * h, 3)])
            leaving[block, h] = jnp.where(fine, mixed, weight * v / terms).astype(bf16)

        @pl.when(block != zed)
        def _():
            back(block).start()

        @pl.when(block == zed)
        def _():
            mixed_out[pl.ds(3 * zed, 3)] = leaving[zed]

    project(zed, 0)
    turn(zed, 0)
    pair(zed, zed, True)

    @pl.when(zed == 0)
    def _():
        complete(0)

    def step(d, _):
        low, high = zed - d, zed + d
        for side, block in ((0, low), (1, high)):

            @pl.when((block >= 0) & (block < 4))
            def _():
                towards = 1 - 2 * side
                pltpu.make_async_remote_copy(
                    src_ref=norm_all.at[block], dst_ref=norm_all.at[block],
                    send_sem=hop_send.at[side, d - 1], recv_sem=hop_recv.at[side, d - 1],
                    device_id=(grp, (zed - towards) * 2 + core), device_id_type=MESH,
                ).wait_recv()
                runs, copy = hop(d, side)
                pl.when(runs)(copy.start)
                project(block, 2 * d + side)

        @pl.when(high < 4)
        def _():
            lax.fori_loop(jnp.maximum(low + 1, 0), high, lambda j, _: (pair(high, j, False), 0)[1], 0)
            turn(high, 2 * d + 1)
            pair(high, high, True)

        @pl.when(low >= 0)
        def _():
            turn(low, 2 * d)
            pair(low, low, True)

            @pl.when(high < 4)
            def _():
                pair(high, low, False)

            pl.when(low == 0)(lambda: complete(low))

            def later(i, _):
                pair(i, low, False)
                pl.when(low == 0)(lambda: complete(i))
                return 0

            lax.fori_loop(low + 1, jnp.minimum(high, 4), later, 0)

        @pl.when((high < 4) & (low <= 0))
        def _():
            complete(high)

        return 0

    lax.fori_loop(1, 4, step, 0)

    for k in (1, 2, 3):
        back(along[k]).wait_send()
        pltpu.make_async_remote_copy(
            src_ref=leaving.at[zed], dst_ref=mixed_out.at[pl.ds(3 * along[k], 3)],
            send_sem=back_send.at[zed], recv_sem=back_recv.at[along[k]],
            device_id=(grp, along[k] * 2 + core), device_id_type=MESH,
        ).wait_recv()
    for d in range(4):
        for side in range(2):
            runs, copy = hop(d, side)
            pl.when(runs)(copy.wait_send)
            if d > 0 or side == 0:
                block = zed + (2 * side - 1) * d
                pl.when((block >= 0) & (block < 4))(swap(block, 2 * d + side).wait_send)


def greet_line(grp, zed, core):
    partners = [(grp, zed * 2 + 1 - core)]
    partners += [(grp, (zed + k) % 4 * 2 + core) for k in (1, 2, 3)]
    greet(partners)


def attend(block_input, gain, bias, w_qkv, span):
    f32, bf16 = jnp.float32, jnp.bfloat16
    tokens, width = block_input.shape
    vmem, smem = pl.BlockSpec(memory_space=pltpu.VMEM), pl.BlockSpec(memory_space=pltpu.SMEM)
    block = (HEAD_DIM, tokens)
    dma = pltpu.SemaphoreType.DMA
    return pl.pallas_call(
        attend_kernel,
        out_shape=[
            jax.ShapeDtypeStruct((HEADS,) + block, bf16),
            jax.ShapeDtypeStruct((3, 4) + block, bf16),
            jax.ShapeDtypeStruct((3, 4, 2, 2) + block, bf16),
            jax.ShapeDtypeStruct((4, 9) + block, bf16),
            jax.ShapeDtypeStruct((3, 4) + block, f32),
            jax.ShapeDtypeStruct((3, 4, 1, tokens), f32),
            jax.ShapeDtypeStruct((4, width, tokens), bf16),
        ],
        in_specs=[vmem] * 3 + [pl.BlockSpec(memory_space=pl.ANY), smem],
        out_specs=[vmem] * 7,
        scratch_shapes=[
            pltpu.VMEM((3, width, 256), bf16),
            pltpu.VMEM((3, 256, width), bf16),
            pltpu.VMEM((3, 4, 2 * tokens, HEAD_DIM), bf16),
            pltpu.VMEM((3, 4) + block, f32),
            pltpu.VMEM((3, 4, 8, tokens), f32),
            pltpu.VMEM((4, 3) + block, bf16),
            dma((3,)),
            dma((2, 4)),
            dma((2, 4)),
            dma((8,)),
            dma((8,)),
            dma((4,)),
            dma((4,)),
        ],
        compiler_params=pltpu.CompilerParams(
            collective_id=1, has_side_effects=True, vmem_limit_bytes=48 * 2**20
        ),
    )(block_input, gain, bias, w_qkv, span)


def gelu_and_slope(u):
    root = 0.7978845608028654
    square = u * u
    bent = jnp.tanh(root * (u + 0.044715 * (square * u)))
    half = 0.5 * (1.0 + bent)
    slope = half + 0.5 * u * (1.0 - bent * bent) * (root * (1.0 + 0.134145 * square))
    return u * half, slope


def normal_parts(vector):
    centered = vector - jnp.mean(vector, axis=-1, keepdims=True)
    variance = jnp.mean(centered * centered, axis=-1, keepdims=True)
    inverse = lax.rsqrt(variance + epsilon)
    return centered * inverse, inverse


def norm_pull(normal, inverse, gain, grad):
    scaled = grad * gain
    along_normal = jnp.mean(scaled * normal, axis=-1, keepdims=True)
    return inverse * (scaled - jnp.mean(scaled, axis=-1, keepdims=True) - normal * along_normal)


def middle_kernel(
    chunk, mixed, x, out_grad, w_out, w_up, w_down, gain, bias, span,
    block_output, grad_middle, grad_mixed, term_down, term_up, term_out, small,
    middle, normed, normed_t, mlp_out, grad_norm,
):
    tokens, width = x.shape
    f32, bf16 = jnp.float32, jnp.bfloat16
    seq = lax.axis_index("seq")
    pos = seq * tokens + lax.broadcasted_iota(jnp.int32, (tokens, 1), 0)
    keep = ((pos >= span[0, 0]) & (pos < span[0, 1])).astype(f32)
    gain_row, bias_row = gain[...].reshape(1, width), bias[...].reshape(1, width)

    def squares(value):
        return jnp.sum(keep * value * value)

    attn_out = matmul(mixed[...].T, w_out[...])
    attn_squares = squares(attn_out)
    middle[...] = x[...].astype(f32) + attn_out
    normed[...] = (normal_parts(middle[...])[0] * gain_row + bias_row).astype(bf16)
    normed_t[...] = normed[...].T
    mlp_out[...] = jnp.zeros((tokens, width), f32)
    grad_norm[...] = jnp.zeros((tokens, width), f32)

    def hidden(i, _):
        at = pl.ds(pl.multiple_of(i * chunk, chunk), chunk)
        activated, slope = gelu_and_slope(matmul(normed[...], w_up[:, at]))
        activated = activated.astype(bf16)
        mlp_out[...] += matmul(activated, w_down[at, :])
        grad_up = (contract_cols(out_grad[...], w_down[at, :]) * slope).astype(bf16)
        grad_norm[...] += contract_cols(grad_up, w_up[:, at])
        term_up[:, at] = matmul(normed_t[...], grad_up).astype(bf16)
        term_down[at, :] = matmul(activated.T, out_grad[...]).astype(bf16)
        return 0

    lax.fori_loop(0, w_up.shape[1] // chunk, hidden, 0)
    output = middle[...] + mlp_out[...]
    block_output[...] = output.astype(bf16)
    sums = [squares(output), attn_squares, squares(mlp_out[...]), jnp.sum(keep) * width]
    normal, inverse = normal_parts(middle[...])
    grad = grad_norm[...]
    grad_middle[...] = out_grad[...].astype(f32) + norm_pull(normal, inverse, gain_row, grad)
    small[0:2] = jnp.zeros((2, width), f32)
    small[2:3] = jnp.sum(grad * normal, axis=0, keepdims=True)
    small[3:4] = jnp.sum(grad, axis=0, keepdims=True)
    lane = lax.broadcasted_iota(jnp.int32, (4, width), 1)
    row = jnp.zeros((4, width), f32)
    for i, value in enumerate(sums):
        row = jnp.where(lane == i, value, row)
    small[4:8] = row
    grad_attn = grad_middle[...].astype(bf16)
    grad_mixed[...] = contract_cols(w_out[...], grad_attn).astype(bf16)
    term_out[...] = matmul(mixed[...], grad_attn).astype(bf16)


def middle_part(mixed, block_input, out_grad, w_out, w_up, w_down, gain, bias, span):
    f32, bf16 = jnp.float32, jnp.bfloat16
    tokens, width = block_input.shape
    vmem, smem = pl.BlockSpec(memory_space=pltpu.VMEM), pl.BlockSpec(memory_space=pltpu.SMEM)
    return pl.pallas_call(
        functools.partial(middle_kernel, 512),
        out_shape=[
            jax.ShapeDtypeStruct((tokens, width), bf16),
            jax.ShapeDtypeStruct((tokens, width), f32),
            jax.ShapeDtypeStruct((width, tokens), bf16),
            jax.ShapeDtypeStruct(w_down.shape, bf16),
            jax.ShapeDtypeStruct(w_up.shape, bf16),
            jax.ShapeDtypeStruct(w_out.shape, bf16),
            jax.ShapeDtypeStruct((8, width), f32),
        ],
        in_specs=[vmem] * 8 + [smem],
        out_specs=[vmem] * 7,
        scratch_shapes=[
            pltpu.VMEM((tokens, width), f32),
            pltpu.VMEM((tokens, width), bf16),
            pltpu.VMEM((width, tokens), bf16),
            pltpu.VMEM((tokens, width), f32),
            pltpu.VMEM((tokens, width), f32),
        ],
        compiler_params=pltpu.CompilerParams(vmem_limit_bytes=48 * 2**20),
    )(mixed, block_input, out_grad, w_out, w_up, w_down, gain, bias, span)


def add_rows(into, base, count, *terms):
    def add(i, _):
        total = None
        for ref, start in terms:
            term = ref[rows_of(start + i * 16, 16), :].astype(jnp.float32)
            total = term if total is None else total + term
        into[rows_of(base + i * 16, 16), :] = total.astype(jnp.bfloat16)
        return 0

    lax.fori_loop(0, count // 16, add, 0)


class GroupSum:
    def __init__(self, term, first, near, held):
        self.term, self.first, self.near, self.held = term, first, near, held
        self.rows, self.columns = term.shape[0] // 4, term.shape[1] // 2
        grp, seq, zed, core, sibling, along = place()
        self.place_in_plane(grp, seq)
        self.sibling = sibling
        self.mine = term.at[:, pl.ds(pl.multiple_of(core * self.columns, 128), self.columns)]
        self.away = pl.ds(pl.multiple_of((1 - core) * self.columns, 128), self.columns)
        self.copies = []

    def place_in_plane(self, grp, seq):
        y, x = grp // 2, grp % 2
        self.own, self.beside, self.above = grp, y * 2 + 1 - x, (1 - y) * 2 + x
        self.across = (1 - y) * 2 + 1 - x
        self.to_x, self.to_y = (self.beside, seq), (self.above, seq)

    def swap(self, send):
        self.halves = []
        for quarter in (self.across, self.beside, self.above, self.own):
            at = rows_of(quarter * self.rows, self.rows)
            self.halves.append(
                send(self.term.at[at, self.away], self.first.at[at, :], self.sibling)
            )

    def part(self, quarter, half):
        return rows_of(quarter * self.rows + half * (self.rows // 2), self.rows // 2)

    def pass_on(self, send, quarter, half, slot, target):
        self.copies.append(
            send(self.first.at[self.part(quarter, half), :], self.near.at[slot], target)
        )

    def core_sum(self, quarter):
        base = quarter * self.rows
        add_rows(self.first, base, self.rows, (self.mine, base), (self.first, base))

    def step_one(self, send):
        steps = (
            (self.across, ((0, 0, self.to_x), (1, 2, self.to_y))),
            (self.beside, ((0, 1, self.to_x),)),
            (self.above, ((1, 3, self.to_y),)),
        )
        for copy, (quarter, passes) in zip(self.halves, steps):
            copy.wait_recv()
            self.core_sum(quarter)
            for half, slot, target in passes:
                self.pass_on(send, quarter, half, slot, target)
        self.copies = [self.copies[i] for i in (0, 2, 1, 3)]

    def step_two(self, send):
        half = self.rows // 2
        for slot, quarter, side, target in (
            (0, self.above, 0, self.to_y),
            (2, self.beside, 1, self.to_x),
        ):
            base = quarter * self.rows + side * half
            self.copies[slot].wait_recv()
            add_rows(self.first, base, half, (self.first, base), (self.near.at[slot], 0))
            self.pass_on(send, quarter, side, 4 + side, target)

    def total(self):
        half = self.rows // 2
        self.halves[3].wait_recv()
        for slot in (1, 3, 4, 5):
            self.copies[slot].wait_recv()
        for side, one, two in ((0, 1, 4), (1, 3, 5)):
            base = self.own * self.rows + side * half
            add_rows(
                self.held, side * half, half, (self.mine, base), (self.first, base),
                (self.near.at[one], 0), (self.near.at[two], 0),
            )

    def drain(self):
        for copy in self.halves + self.copies:
            copy.wait_send()


class HeadsSum(GroupSum):
    def __init__(self, term, other, first, near, final):
        self.term, self.other, self.first, self.near, self.final = term, other, first, near, final
        self.rows = 4 * term.shape[2]
        grp, seq, zed, self.core, self.sibling, along = place()
        self.place_in_plane(grp, seq)
        self.copies = []

    def swap_quarter(self, send, quarter):
        at = pl.ds(4 * quarter, 4)
        return send(self.term.at[at, 1 - self.core], self.other.at[at], self.sibling)

    def both_cores(self, quarter):
        at = pl.ds(4 * quarter, 4)
        return (self.term[at, self.core] + self.other[at]).reshape(self.rows, -1)

    def core_sum(self, quarter):
        self.first[rows_of(quarter * self.rows, self.rows), :] = self.both_cores(quarter).astype(
            jnp.bfloat16
        )

    def total(self):
        self.halves[3].wait_recv()
        for slot in (1, 3, 4, 5):
            self.copies[slot].wait_recv()
        near = [self.near[i].astype(jnp.float32) for i in range(6)]
        total = self.both_cores(self.own) + jnp.concatenate(
            [near[1] + near[4], near[3] + near[5]], axis=0
        )
        self.final[...] = total.reshape(self.final.shape)


def send_line(send, held, third, along, line):
    rows = held.shape[0] // 4
    return [
        send(held.at[rows_of(along[k] * rows, rows), :], third.at[k - 1], line[k - 1])
        for k in (1, 2, 3)
    ]


def sum_line(send, copies, held, third, mine, out, zed, core, sibling):
    rows, columns = held.shape[0] // 4, held.shape[1]
    for copy in copies:
        copy.wait_recv()
    total = held[rows_of(zed * rows, rows), :].astype(jnp.float32)
    for j in range(3):
        total = total + third[j].astype(jnp.float32)
    mine[...] = total
    column = pl.ds(pl.multiple_of(core * columns, 128), columns)
    half = rows // 2
    away = pl.ds(pl.multiple_of((1 - core) * half, 8), half)
    out[:, column] = mine[pl.ds(pl.multiple_of(core * half, 8), half), :]
    return send(mine.at[away, :], out.at[:, column], sibling)


def norm_back(x, gain, grad_norm, grad_out, into, chunk):
    f32 = jnp.float32
    tokens, width = x.shape
    gain_row = gain[...].reshape(1, width)

    def one(i, sums):
        at = rows_of(i * chunk, chunk)
        vector, grad = x[at, :].astype(f32), grad_norm[at, :]
        normal, inverse = normal_parts(vector)
        pulled = norm_pull(normal, inverse, gain_row, grad)
        into[at, :] = (grad_out[at, :] + pulled).astype(into.dtype)
        return (
            sums[0] + jnp.sum(grad * normal, axis=0, keepdims=True),
            sums[1] + jnp.sum(grad, axis=0, keepdims=True),
        )

    zero = jnp.zeros((1, width), f32)
    return lax.fori_loop(0, tokens // chunk, one, (zero, zero))


def settle_small(small, vecs, rms, owner):
    width, count = small.shape[-1], vecs.shape[-1]
    total = (small[0] + small[1]) + (small[2] + small[3])
    turned = pltpu.roll(total, (width - owner * count) % width, 1)
    for i in range(4):
        vecs[i] = turned[i : i + 1, :count]
    rms[...] = jnp.sqrt(total[4:5, :3] / total[4:5, 3:4])


def attend_back_kernel(many, *refs):
    (gmix, q_all, kv_all, raw, mix_all, tot_all, norm_all, span, x, gain, w_qkv, grad_middle,
     small_in) = refs[:13]
    terms_in = refs[13 : 13 + many]
    refs = refs[13 + many :]
    input_grad, sum_qkv, vecs, rms = refs[:4]
    outs = refs[4 : 4 + many]
    rest = refs[4 + many :]
    first, near, held, third, mine = (rest[i * many : (i + 1) * many] for i in range(5))
    (gm_in, keys, values, g_all, gt_all, grad_kv, part_out, part_in, leaving, arrived,
     term, other, first_qkv, near_qkv, final, gathered, grad_norm, small_a, small_b, small_c,
     send_sems, recv_sems) = rest[5 * many :]
    tokens, width = x.shape
    f32, bf16 = jnp.float32, jnp.bfloat16
    grp, seq, zed, core, sibling, along = place()
    line = [(grp, along[k] * 2 + core) for k in (1, 2, 3)]
    sums = [GroupSum(*refs_of) for refs_of in zip(terms_in, first, near, held)]
    heads_sum = HeadsSum(term, other, first_qkv, near_qkv, final)
    plane = [heads_sum.to_x, heads_sum.to_y, (heads_sum.across, seq)]

    greet([sibling] + line + plane)
    send = sender(send_sems, recv_sems)
    coming = []
    for h in range(3):
        for k in (1, 2, 3):
            coming.append(send(gmix.at[along[k] * 3 + h], gm_in.at[h, zed], line[k - 1]))
    for each in sums:
        each.swap(send)
    for h in range(3):
        gm_in[h, zed] = gmix[zed * 3 + h]

    def turn(i, _):
        h, z = i // 4, i % 4
        for side in range(2):
            at = pl.ds(side * tokens, tokens)
            keys[h, z, at, :] = kv_all[h, z, side, 0].T
            values[h, z, at, :] = kv_all[h, z, side, 1].T
        return 0

    lax.fori_loop(0, 12, turn, 0)
    for z in range(4):
        leaving[z, 9] = jnp.zeros((HEAD_DIM, tokens), bf16)
    sums[0].step_one(send)

    swaps, sends = [], []

    def finish(h):
        swaps[h].wait_recv()

        def merge(z, _):
            fine = valid_columns(span, (2 * z + core) * tokens, tokens)
            q, k, v, inverse, signed, terms, weight = alone_terms(raw.at[z, pl.ds(3 * h, 3)])
            g = gm_in[h, z].astype(f32)
            total = 1.0 / terms
            grad_total = -jnp.sum(g * (weight * v), axis=0, keepdims=True) * total * total
            g = (g * total).astype(bf16).astype(f32)
            grad_weight = jnp.sum(g * v, axis=0, keepdims=True)
            slope = 1.0 + (inverse * inverse) * (inverse - 1.0)
            grad_score = terms * (grad_weight * slope + grad_total * signed)
            grad_score = grad_score.astype(bf16).astype(f32)
            alone = (grad_score * k * 0.125, grad_score * q, weight * g)
            parts = [leaving[z, 3 * h].astype(f32)]
            for part in range(2):
                parts.append(grad_kv[h, z, core, part] + part_in[h, z, part].astype(f32))
            for part in range(3):
                leaving[z, 3 * h + part] = jnp.where(fine, parts[part], alone[part]).astype(bf16)
            return 0

        lax.fori_loop(0, 4, merge, 0)
        at = pl.ds(3 * h, 3)
        for k in (1, 2, 3):
            sends.append(
                send(leaving.at[along[k], at], arrived.at[:, zed * 3 + h], line[k - 1])
            )
        for part in range(3):
            arrived[part, zed * 3 + h] = leaving[zed, 3 * h + part]

    for h in range(3):
        for copy in coming[h * 3 : h * 3 + 3]:
            copy.wait_recv()

        def prepare(z, _):
            g = gm_in[h, z].astype(f32)
            total = 1.0 / tot_all[h, z]
            g_all[z] = (g * total).astype(bf16)
            gt_all[z] = -jnp.sum(g * mix_all[h, z], axis=0, keepdims=True) * total
            for side in range(2):
                for part in range(2):
                    grad_kv[h, z, side, part] = jnp.zeros((HEAD_DIM, tokens), f32)
            return 0

        lax.fori_loop(0, 4, prepare, 0)

        def query_block(z, _):
            queries, grads, grad_total = q_all[h, z], g_all[z], gt_all[z]

            def pair(other_z, grad_query, last=False):
                for side in range(2):
                    at = pl.ds(side * tokens, tokens)
                    scores = matmul(keys[h, other_z, at, :], queries)
                    grad_weights = matmul(values[h, other_z, at, :], grads)
                    inverse, signed, terms = signed_terms(scores)
                    if last:
                        key_pos = lax.broadcasted_iota(jnp.int32, scores.shape, 0)
                        query_pos = lax.broadcasted_iota(jnp.int32, scores.shape, 1)
                        seen = key_pos + side * tokens <= query_pos + core * tokens
                        terms = jnp.where(seen, terms, 0.0)
                    weights = (signed * terms).astype(bf16)
                    slope = 1.0 + (inverse * inverse) * (inverse - 1.0)
                    grad_scores = terms * (grad_weights * slope + grad_total * signed)
                    grad_scores = grad_scores.astype(bf16)
                    grad_query = grad_query + matmul(kv_all[h, other_z, side, 0], grad_scores)
                    grad_kv[h, other_z, side, 0] += contract_cols(queries, grad_scores)
                    grad_kv[h, other_z, side, 1] += contract_cols(grads, weights)
                return grad_query

            zero = jnp.zeros((HEAD_DIM, tokens), f32)
            grad_query = pair(z, lax.fori_loop(0, z, pair, zero), True)
            leaving[z, 3 * h] = (grad_query * 0.125).astype(bf16)
            return 0

        lax.fori_loop(0, 2, query_block, 0)
        if h > 0:
            finish(h - 1)
        if h == 2:
            sums[1].step_two(send)
        lax.fori_loop(2, 4, query_block, 0)

        def pack(z, _):
            for part in range(2):
                part_out[h, z, part] = grad_kv[h, z, 1 - core, part].astype(bf16)
            return 0

        lax.fori_loop(0, 4, pack, 0)
        swaps.append(send(part_out.at[h], part_in.at[h], sibling))
        if h == 0:
            sums[1].step_one(send)
        if h == 1:
            sums[0].step_two(send)
            sums[2].step_one(send)
    finish(2)
    sums[0].total()
    lines = [send_line(send, held[0], third[0], along, line)]

    heads_sum.halves = []
    for quarter in (heads_sum.across, heads_sum.beside, heads_sum.above, heads_sum.own):
        total = None
        for z in range(4):
            rows = norm_all[z, rows_of(quarter * (width // 4), width // 4), :]
            part = contract_cols(rows, leaving[z].reshape(10 * HEAD_DIM, tokens))
            total = part if total is None else total + part
        term[pl.ds(4 * quarter, 4)] = total.reshape((4,) + term.shape[1:])
        heads_sum.halves.append(heads_sum.swap_quarter(send, quarter))
    sums[2].step_two(send)
    heads_sum.step_one(send)
    for a in range(1, many):
        sums[a].total()
        lines.append(send_line(send, held[a], third[a], along, line))

    for copy in sends:
        copy.wait_recv()
    grads = arrived[...].reshape(3 * width, tokens)
    for i in range(width // 256):
        columns = slice(i * 256, (i + 1) * 256)
        grad_norm[:, columns] = matmul(w_qkv[columns, :], grads).T
    gain_grad, bias_grad = norm_back(x, gain, grad_norm, grad_middle, input_grad, 64)
    small_a[0] = small_in[...]
    small_a[0, 0:1] = gain_grad
    small_a[0, 1:2] = bias_grad
    swap = send(small_a.at[0], small_a.at[1], sibling)
    heads_sum.step_two(send)
    swap.wait()
    small_b[pl.ds(grp, 1)] = small_a[0:1] + small_a[1:2]
    across = [(k, seq) for k in (heads_sum.beside, heads_sum.above, heads_sum.across)]
    planes = [send(small_b.at[grp], small_b.at[grp], target) for target in across]
    heads_sum.total()
    gathered[pl.ds(zed, 1)] = final[pl.ds(zed, 1)]
    blocks = [send(final.at[along[k]], gathered.at[zed], line[k - 1]) for k in (1, 2, 3)]
    for copy in planes:
        copy.wait_recv()
    small_c[pl.ds(zed, 1)] = (small_b[0:1] + small_b[1:2]) + (small_b[2:3] + small_b[3:4])
    columns = [send(small_c.at[zed], small_c.at[zed], line[k - 1]) for k in (1, 2, 3)]
    ends = []
    for a in range(many):
        ends.append(
            sum_line(send, lines[a], held[a], third[a], mine[a], outs[a], zed, core, sibling)
        )
    for copy in blocks + columns:
        copy.wait_recv()
    for z in range(4):
        for h in range(3):
            for part in range(3):
                start = part * width + (3 * z + h) * HEAD_DIM
                sum_qkv[:, start : start + HEAD_DIM] = gathered[
                    z, :, (3 * h + part) * HEAD_DIM : (3 * h + part + 1) * HEAD_DIM
                ]
    settle_small(small_c, vecs, rms, grp * 8 + seq)
    for copy in ends:
        copy.wait_recv()
    for copy in coming + swaps + sends + planes + blocks + columns + ends:
        copy.wait_send()
    for copies in lines:
        for copy in copies:
            copy.wait_send()
    for each in sums + [heads_sum]:
        each.drain()


def attend_back(gmix, saved, span, block_input, gain, w_qkv, grad_middle, small, terms):
    f32, bf16 = jnp.float32, jnp.bfloat16
    tokens, width = block_input.shape
    many = len(terms)
    vmem, smem = pl.BlockSpec(memory_space=pltpu.VMEM), pl.BlockSpec(memory_space=pltpu.SMEM)
    block = (HEAD_DIM, tokens)
    copies = 9 + 10 * many + 3 + 9 + 10 + 1 + 3 * many + 3 + 3 + 3 + many
    shapes = [t.shape for t in terms]
    own_rows, columns = width // 32, 10 * HEAD_DIM
    return pl.pallas_call(
        functools.partial(attend_back_kernel, many),
        out_shape=[
            jax.ShapeDtypeStruct((tokens, width), bf16),
            jax.ShapeDtypeStruct((own_rows, 3 * width), f32),
            jax.ShapeDtypeStruct((4, 1, own_rows), f32),
            jax.ShapeDtypeStruct((1, 3), f32),
        ]
        + [jax.ShapeDtypeStruct((r // 32, c), f32) for r, c in shapes],
        in_specs=[vmem] * 7 + [smem] + [vmem] * (5 + many),
        out_specs=[vmem] * (4 + many),
        scratch_shapes=[pltpu.VMEM((r, c // 2), bf16) for r, c in shapes]
        + [pltpu.VMEM((6, r // 8, c // 2), bf16) for r, c in shapes]
        + [pltpu.VMEM((r // 4, c // 2), bf16) for r, c in shapes]
        + [pltpu.VMEM((3, r // 16, c // 2), bf16) for r, c in shapes]
        + [pltpu.VMEM((r // 16, c // 2), f32) for r, c in shapes]
        + [
            pltpu.VMEM((3, 4) + block, bf16),
            pltpu.VMEM((3, 4, 2 * tokens, HEAD_DIM), bf16),
            pltpu.VMEM((3, 4, 2 * tokens, HEAD_DIM), bf16),
            pltpu.VMEM((4,) + block, bf16),
            pltpu.VMEM((4, 1, tokens), f32),
            pltpu.VMEM((3, 4, 2, 2) + block, f32),
            pltpu.VMEM((3, 4, 2) + block, bf16),
            pltpu.VMEM((3, 4, 2) + block, bf16),
            pltpu.VMEM((4, 10) + block, bf16),
            pltpu.VMEM((3, HEADS) + block, bf16),
            pltpu.VMEM((16, 2, own_rows, columns), f32),
            pltpu.VMEM((16, own_rows, columns), f32),
            pltpu.VMEM((16 * own_rows, columns), bf16),
            pltpu.VMEM((6, 2 * own_rows, columns), bf16),
            pltpu.VMEM((4, own_rows, columns), f32),
            pltpu.VMEM((4, own_rows, columns), f32),
            pltpu.VMEM((tokens, width), f32),
            pltpu.VMEM((2,) + small.shape, f32),
            pltpu.VMEM((4,) + small.shape, f32),
            pltpu.VMEM((4,) + small.shape, f32),
            pltpu.SemaphoreType.DMA((copies,)),
            pltpu.SemaphoreType.DMA((copies,)),
        ],
        compiler_params=pltpu.CompilerParams(
            collective_id=2, has_side_effects=True, vmem_limit_bytes=62 * 2**20
        ),
    )(gmix, *saved, span, block_input, gain, w_qkv, grad_middle, small, *terms)


def per_device_planned(
    block_input,
    out_grad,
    seq_span,
    ln1_gain,
    ln1_bias,
    w_qkv,
    w_out,
    ln2_gain,
    ln2_bias,
    w_up,
    w_down,
):
    tokens, width = block_input.shape
    mixed, *saved = attend(block_input, ln1_gain, ln1_bias, w_qkv, seq_span)
    mixed = mixed.reshape(width, tokens)
    block_output, grad_middle, grad_mixed, *terms, small = middle_part(
        mixed, block_input, out_grad, w_out, w_up, w_down, ln2_gain, ln2_bias, seq_span
    )
    input_grad, sum_qkv, vecs, rms_stats, sum_down, sum_up, sum_out = attend_back(
        grad_mixed.reshape(HEADS, HEAD_DIM, tokens),
        saved,
        seq_span,
        block_input,
        ln1_gain,
        w_qkv,
        grad_middle,
        small,
        terms,
    )
    vecs = vecs.reshape(4, -1)
    return (
        block_output,
        input_grad,
        vecs[0],
        vecs[1],
        sum_qkv,
        sum_out,
        vecs[2],
        vecs[3],
        sum_up,
        sum_down,
        rms_stats.reshape(3),
    )


def solution(mesh):
    placed = (
        P(("grp", "seq"), None),
        P(("grp", "seq"), None),
        P("grp", None),
        P(),
        P(),
        P(),
        P(),
        P(),
        P(),
        P(),
        P(),
    )
    planned = mesh.shape["grp"] == 4 and mesh.shape["seq"] == 8
    return jax.shard_map(
        per_device_planned if planned else per_device,
        mesh=mesh,
        in_specs=placed,
        out_specs=(
            P(("grp", "seq"), None),
            P(("grp", "seq"), None),
            P(("grp", "seq")),
            P(("grp", "seq")),
            P(("grp", "seq"), None),
            P(("grp", "seq"), None),
            P(("grp", "seq")),
            P(("grp", "seq")),
            P(("grp", "seq"), None),
            P(("grp", "seq"), None),
            P(),
        ),
        check_vma=False,
    )
```

```python
import functools

import jax
import jax.numpy as jnp
from jax import lax
from jax.experimental import pallas as pl
from jax.experimental.pallas import tpu as pltpu
from jax.sharding import PartitionSpec as P

D = 768
HEADS = 12
HEAD_DIM = 64
MESH = pl.DeviceIdType.MESH


epsilon = 1e-05


def passed_along(array, axis, by):
    devices = lax.axis_size(axis)
    pairs = [(i, i + by) for i in range(devices) if 0 <= i + by < devices]
    return lax.ppermute(array, axis, pairs)


def shifted(array, axis, by):
    devices = lax.axis_size(axis)
    return lax.ppermute(array, axis, [(i, (i + by) % devices) for i in range(devices)])


def layer_norm(vector, scale_vec, shift_vec):
    row_mean = jnp.mean(vector, axis=-1, keepdims=True)
    centered = vector - row_mean
    variance = jnp.mean(centered * centered, axis=-1, keepdims=True)
    return centered * lax.rsqrt(variance + epsilon) * scale_vec + shift_vec


def contract_rows(left, right):
    return lax.dot_general(
        left, right, (((0,), (0,)), ((), ())), preferred_element_type=jnp.float32
    )


def contract_cols(left, right):
    return lax.dot_general(
        left, right, (((1,), (1,)), ((), ())), preferred_element_type=jnp.float32
    )


def score_terms(queries, key_block, query_pos, key_pos, seq_first, seq_limit):
    scores = (
        jnp.einsum("qhd,khd->qhk", queries, key_block, preferred_element_type=jnp.float32) * 0.125
    )
    query_valid = (query_pos >= seq_first) & (query_pos < seq_limit)
    key_valid = (key_pos >= seq_first) & (key_pos < seq_limit)
    allowed = (key_pos[None, :] <= query_pos[:, None]) & (
        query_valid[:, None] & key_valid[None, :] | (key_pos[None, :] == query_pos[:, None])
    )
    magnitude = jnp.sqrt(scores * scores + 1.0)
    signed_part = scores / magnitude
    exp_terms = jnp.where(allowed[:, None, :], jnp.exp(magnitude), 0.0)
    return (magnitude, signed_part, exp_terms)


def split_pair(kv_pair):
    count_rows = kv_pair.shape[0]
    key_block = kv_pair[:, :D].reshape(count_rows, HEADS, HEAD_DIM)
    value_block = kv_pair[:, D:].reshape(count_rows, HEADS, HEAD_DIM)
    return (key_block, value_block)


def forward_block(running, kv_pair, key_start, queries, query_pos, seq_first, seq_limit):
    totals, unnorm = running
    key_block, value_block = split_pair(kv_pair)
    key_pos = key_start + jnp.arange(kv_pair.shape[0], dtype=jnp.int32)
    magnitude, signed_part, exp_terms = score_terms(
        queries, key_block, query_pos, key_pos, seq_first, seq_limit
    )
    weights = (signed_part * exp_terms).astype(jnp.bfloat16)
    totals = totals + jnp.sum(exp_terms, axis=-1)
    unnorm = unnorm + jnp.einsum(
        "qhk,khd->qhd", weights, value_block, preferred_element_type=jnp.float32
    )
    return (totals, unnorm)


def grad_core(
    kv_pair, key_start, queries, query_pos, seq_first, seq_limit, grad_unnorm, grad_totals
):
    key_block, value_block = split_pair(kv_pair)
    key_pos = key_start + jnp.arange(kv_pair.shape[0], dtype=jnp.int32)
    magnitude, signed_part, exp_terms = score_terms(
        queries, key_block, query_pos, key_pos, seq_first, seq_limit
    )
    weights = (signed_part * exp_terms).astype(jnp.bfloat16)
    grad_weights = jnp.einsum(
        "qhd,khd->qhk", grad_unnorm, value_block, preferred_element_type=jnp.float32
    )
    grad_scores = (
        grad_weights * exp_terms / (magnitude * magnitude * magnitude)
        + (grad_weights * signed_part + grad_totals[:, :, None]) * exp_terms * signed_part
    )
    return (key_block, weights, grad_scores.astype(jnp.bfloat16))


def backward_block(
    kv_pair, key_start, queries, query_pos, seq_first, seq_limit, grad_unnorm, grad_totals
):
    key_block, weights, grad_scores = grad_core(
        kv_pair, key_start, queries, query_pos, seq_first, seq_limit, grad_unnorm, grad_totals
    )
    count_rows = kv_pair.shape[0]
    grad_query = (
        jnp.einsum("qhk,khd->qhd", grad_scores, key_block, preferred_element_type=jnp.float32)
        * 0.125
    )
    grad_key = (
        jnp.einsum("qhk,qhd->khd", grad_scores, queries, preferred_element_type=jnp.float32) * 0.125
    )
    grad_value = jnp.einsum(
        "qhk,qhd->khd", weights, grad_unnorm, preferred_element_type=jnp.float32
    )
    grad_pair = jnp.concatenate(
        [grad_key.reshape(count_rows, D), grad_value.reshape(count_rows, D)], axis=1
    )
    return (grad_query, grad_pair)


def per_device(
    block_input,
    out_grad,
    seq_span,
    ln1_gain,
    ln1_bias,
    w_qkv,
    w_out,
    ln2_gain,
    ln2_bias,
    w_up,
    w_down,
):
    tok_rows = block_input.shape[0]
    feat_width = block_input.shape[1]
    seq_count = lax.axis_size("seq")
    seq_index = lax.axis_index("seq")
    query_pos = seq_index * tok_rows + jnp.arange(tok_rows, dtype=jnp.int32)
    query_last = query_pos[tok_rows - 1]
    seq_first = seq_span[0, 0]
    seq_limit = seq_span[0, 1]
    inputs = block_input.astype(jnp.float32)
    normed = layer_norm(inputs, ln1_gain, ln1_bias).astype(jnp.bfloat16)
    proj_qkv = jnp.dot(normed, w_qkv, preferred_element_type=jnp.float32).astype(jnp.bfloat16)
    queries = proj_qkv[:, :feat_width].reshape(tok_rows, HEADS, HEAD_DIM)
    kv_pair = proj_qkv[:, feat_width:]

    def visit_block(running, shard_rows, key_start):
        return lax.cond(
            key_start <= query_last,
            lambda state_in: forward_block(
                state_in, shard_rows, key_start, queries, query_pos, seq_first, seq_limit
            ),
            lambda state_in: state_in,
            running,
        )

    empty = (
        jnp.zeros((tok_rows, HEADS), jnp.float32),
        jnp.zeros((tok_rows, HEADS, HEAD_DIM), jnp.float32),
    )
    first_state = visit_block(empty, kv_pair, seq_index * tok_rows)

    def forward_hop(hop_count, loop_state):
        moving, running = loop_state
        moving = passed_along(moving, "seq", 1)
        source = (seq_index - hop_count) % seq_count
        return (moving, visit_block(running, moving, source * tok_rows))

    _, (totals, unnorm) = lax.fori_loop(1, seq_count, forward_hop, (kv_pair, first_state))
    mixed_heads = (unnorm / totals[:, :, None]).reshape(tok_rows, feat_width).astype(jnp.bfloat16)
    attn_out = jnp.dot(mixed_heads, w_out, preferred_element_type=jnp.float32)
    middle = inputs + attn_out
    normed_two = layer_norm(middle, ln2_gain, ln2_bias).astype(jnp.bfloat16)
    up_proj = jnp.dot(normed_two, w_up, preferred_element_type=jnp.float32)
    activated = jax.nn.gelu(up_proj, approximate=True).astype(jnp.bfloat16)
    mlp_out = jnp.dot(activated, w_down, preferred_element_type=jnp.float32)
    output = middle + mlp_out
    valid_rows = ((query_pos >= seq_first) & (query_pos < seq_limit)).astype(jnp.float32)[:, None]
    rms_parts = lax.psum(
        (
            jnp.sum(valid_rows * output * output),
            jnp.sum(valid_rows * attn_out * attn_out),
            jnp.sum(valid_rows * mlp_out * mlp_out),
            jnp.sum(valid_rows) * feat_width,
        ),
        ("grp", "seq"),
    )
    rms_stats = jnp.sqrt(jnp.stack([rms_parts[0], rms_parts[1], rms_parts[2]]) / rms_parts[3])
    grad_w_down = contract_rows(activated, out_grad)
    grad_activated = contract_cols(out_grad, w_down)
    _, gelu_pull = jax.vjp(lambda pre_act: jax.nn.gelu(pre_act, approximate=True), up_proj)
    grad_up = gelu_pull(grad_activated)[0].astype(jnp.bfloat16)
    grad_w_up = contract_rows(normed_two, grad_up)
    grad_norm_two = contract_cols(grad_up, w_up)
    _, norm_pull_two = jax.vjp(layer_norm, middle, ln2_gain, ln2_bias)
    grad_mid_norm, grad_gain_two, grad_bias_two = norm_pull_two(grad_norm_two)
    grad_middle = out_grad.astype(jnp.float32) + grad_mid_norm
    grad_attn = grad_middle.astype(jnp.bfloat16)
    grad_w_out = contract_rows(mixed_heads, grad_attn)
    grad_mixed = contract_cols(grad_attn, w_out).reshape(tok_rows, HEADS, HEAD_DIM)
    grad_unnorm = (grad_mixed / totals[:, :, None]).astype(jnp.bfloat16)
    grad_totals = -jnp.sum(grad_mixed * unnorm, axis=-1) / (totals * totals)

    def back_block(grad_run, shard_rows, key_start):

        def compute_block(grad_in):
            grad_query, grad_pair = backward_block(
                shard_rows,
                key_start,
                queries,
                query_pos,
                seq_first,
                seq_limit,
                grad_unnorm,
                grad_totals,
            )
            return (grad_in + grad_query, grad_pair)

        def skip_block(grad_in):
            return (grad_in, jnp.zeros((shard_rows.shape[0], 2 * feat_width), jnp.float32))

        return lax.cond(key_start <= query_last, compute_block, skip_block, grad_run)

    grad_start = jnp.zeros((tok_rows, HEADS, HEAD_DIM), jnp.float32)
    grad_queries, local_terms = back_block(grad_start, kv_pair, seq_index * tok_rows)

    def backward_hop(hop_count, loop_state):
        moving, grad_acc, grad_run = loop_state
        moving = passed_along(moving, "seq", 1)
        grad_acc = shifted(grad_acc.astype(jnp.bfloat16), "seq", 1).astype(grad_acc.dtype)
        source = (seq_index - hop_count) % seq_count
        grad_run, new_terms = back_block(grad_run, moving, source * tok_rows)
        return (moving, grad_acc + new_terms, grad_run)

    _, grad_acc, grad_queries = lax.fori_loop(
        1, seq_count, backward_hop, (kv_pair, local_terms, grad_queries)
    )
    grad_kv = shifted(grad_acc.astype(jnp.bfloat16), "seq", 1).astype(grad_acc.dtype)
    grad_qkv = jnp.concatenate(
        [grad_queries.reshape(tok_rows, feat_width), grad_kv], axis=1
    ).astype(jnp.bfloat16)
    grad_w_qkv = contract_rows(normed, grad_qkv)
    grad_norm_one = contract_cols(grad_qkv, w_qkv)
    _, norm_pull_one = jax.vjp(layer_norm, inputs, ln1_gain, ln1_bias)
    grad_in_norm, grad_gain_one, grad_bias_one = norm_pull_one(grad_norm_one)
    input_grad = (grad_middle + grad_in_norm).astype(jnp.bfloat16)
    summed = (
        lax.psum_scatter(grad_gain_one, ("grp", "seq"), scatter_dimension=0, tiled=True),
        lax.psum_scatter(grad_bias_one, ("grp", "seq"), scatter_dimension=0, tiled=True),
        lax.psum_scatter(grad_w_qkv, ("grp", "seq"), scatter_dimension=0, tiled=True),
        lax.psum_scatter(grad_w_out, ("grp", "seq"), scatter_dimension=0, tiled=True),
        lax.psum_scatter(grad_gain_two, ("grp", "seq"), scatter_dimension=0, tiled=True),
        lax.psum_scatter(grad_bias_two, ("grp", "seq"), scatter_dimension=0, tiled=True),
        lax.psum_scatter(grad_w_up, ("grp", "seq"), scatter_dimension=0, tiled=True),
        lax.psum_scatter(grad_w_down, ("grp", "seq"), scatter_dimension=0, tiled=True),
    )
    return (
        output.astype(jnp.bfloat16),
        input_grad,
        summed[0],
        summed[1],
        summed[2],
        summed[3],
        summed[4],
        summed[5],
        summed[6],
        summed[7],
        rms_stats,
    )


def rows_of(start, count):
    return pl.ds(pl.multiple_of(start, 16), count)


def matmul(left, right):
    return jnp.dot(left, right, preferred_element_type=jnp.float32)


def signed_terms(scores):
    square = scores * scores + 1.0
    inverse = lax.rsqrt(square)
    return inverse, scores * inverse, jnp.exp(square * inverse)


def valid_columns(span, start, count):
    pos = start + lax.broadcasted_iota(jnp.int32, (1, count), 1)
    return (pos >= span[0, 0]) & (pos < span[0, 1])


def greet_start(partners):
    for partner in partners:
        pl.semaphore_signal(
            pltpu.get_barrier_semaphore(), inc=1, device_id=partner, device_id_type=MESH
        )


def greet_end(partners):
    pl.semaphore_wait(pltpu.get_barrier_semaphore(), len(partners))


def sender(send_sems, recv_sems):
    count = [0]

    def send(src, dst, target):
        slot = count[0]
        count[0] += 1
        copy = pltpu.make_async_remote_copy(
            src_ref=src, dst_ref=dst, send_sem=send_sems.at[slot], recv_sem=recv_sems.at[slot],
            device_id=target, device_id_type=MESH,
        )
        copy.start()
        return copy

    return send


def place():
    grp, seq = lax.axis_index("grp"), lax.axis_index("seq")
    zed, core = seq // 2, seq % 2
    sibling = (grp, zed * 2 + 1 - core)
    along = [(zed + k) % 4 for k in range(4)]
    return grp, seq, zed, core, sibling, along


def alone_terms(raw):
    q, k, v = (raw[part].astype(jnp.float32) for part in range(3))
    inverse, signed, terms = signed_terms(jnp.sum(q * k, axis=0, keepdims=True))
    weight = (signed * terms).astype(jnp.bfloat16).astype(jnp.float32)
    return q, k, v, inverse, signed, terms, weight


def attend_kernel(
    x, gain, bias, w_qkv, span, mixed_out, q_all, kv_all, raw, mix_all, tot_all, norm_all,
    windows, weights, keys, mixes, totals, leaving, load, hop_send, hop_recv, swap_send, swap_recv, back_send, back_recv,
):
    tokens, width = x.shape
    f32, bf16 = jnp.float32, jnp.bfloat16
    grp, seq, zed, core, sibling, along = place()

    start = pl.multiple_of(zed * 192 // 128 * 128, 128)
    inside = pl.ds(pl.multiple_of(zed % 2 * HEAD_DIM, HEAD_DIM), 3 * HEAD_DIM)
    loads = []
    for part in range(3):
        window = w_qkv.at[:, pl.ds(pl.multiple_of(part * width + start, 128), 256)]
        loads.append(pltpu.make_async_copy(window, windows.at[part], load.at[part]))
        loads[-1].start()
    partners = [sibling] + [(grp, along[k] * 2 + core) for k in (1, 2, 3)]
    greet_start(partners)
    vector = x[...].astype(f32)
    centered = vector - jnp.mean(vector, axis=-1, keepdims=True)
    variance = jnp.mean(centered * centered, axis=-1, keepdims=True)
    normed = (
        centered * lax.rsqrt(variance + epsilon) * gain[...].reshape(1, width)
        + bias[...].reshape(1, width)
    ).astype(bf16)
    norm_all[zed] = normed.T
    greet_end(partners)

    def hop(step, side):
        towards = 1 - 2 * side
        block = zed - towards * step
        runs = (block >= 0) & (block < 4) & (zed + towards >= 0) & (zed + towards < 4)
        copy = pltpu.make_async_remote_copy(
            src_ref=norm_all.at[block], dst_ref=norm_all.at[block],
            send_sem=hop_send.at[side, step], recv_sem=hop_recv.at[side, step],
            device_id=(grp, (zed + towards) * 2 + core), device_id_type=MESH,
        )
        return runs, copy

    def hop_on(step):
        for side in range(2):
            runs, copy = hop(step, side)
            pl.when(runs)(copy.start)

    hop_on(0)
    for part in range(3):
        loads[part].wait()
        weights[part] = windows[part].T
    no_score = signed_terms(jnp.zeros((1, tokens), f32))[2]
    extra = span[0, 0].astype(f32) * no_score
    mixes[...] = jnp.zeros(mixes.shape, f32)
    totals[...] = jnp.zeros(totals.shape, f32)

    def swap(block, slot):
        return pltpu.make_async_remote_copy(
            src_ref=kv_all.at[:, block, core], dst_ref=kv_all.at[:, block, core],
            send_sem=swap_send.at[slot], recv_sem=swap_recv.at[slot],
            device_id=sibling, device_id_type=MESH,
        )

    def project(block, slot):
        keep = valid_columns(span, (2 * block + core) * tokens, tokens).astype(f32)
        for part in range(3):
            heads = matmul(weights[part, inside, :], norm_all[block])
            if part == 0:
                heads = heads * 0.125
            for h in range(3):
                one = heads[h * HEAD_DIM : (h + 1) * HEAD_DIM]
                raw[block, 3 * h + part] = one.astype(bf16)
                if part == 0:
                    q_all[h, block] = (one * keep).astype(bf16)
                else:
                    kv_all[h, block, core, part - 1] = (one * keep).astype(bf16)
        swap(block, slot).start()

    def turn(block, slot):
        swap(block, slot).wait_recv()
        for h in range(3):
            for side in range(2):
                keys[h, block, side * tokens : (side + 1) * tokens, :] = kv_all[h, block, side, 0].T

    def pair(block, other, last):
        tiles = [(h, side) for h in range(3) for side in range(2)]
        total = [totals[h, block] for h in range(3)]
        mixed = [mixes[h, block] for h in range(3)]
        scored, weights = {}, {}
        for step in range(len(tiles) + 2):
            if step < len(tiles):
                h, side = tiles[step]
                at = pl.ds(side * tokens, tokens)
                scored[step] = matmul(keys[h, other, at, :], q_all[h, block])
            if 0 <= step - 1 < len(tiles):
                h, side = tiles[step - 1]
                scores = scored.pop(step - 1)
                _, signed, terms = signed_terms(scores)
                if last:
                    key_pos = lax.broadcasted_iota(jnp.int32, scores.shape, 0)
                    query_pos = lax.broadcasted_iota(jnp.int32, scores.shape, 1)
                    seen = key_pos + side * tokens <= query_pos + core * tokens
                    terms = jnp.where(seen, terms, 0.0)
                total[h] = total[h] + jnp.sum(terms.reshape(tokens // 8, 8, tokens), axis=0)
                weights[step - 1] = (signed * terms).astype(bf16)
            if step - 2 >= 0:
                h, side = tiles[step - 2]
                mixed[h] = mixed[h] + matmul(kv_all[h, other, side, 1], weights.pop(step - 2))
        for h in range(3):
            totals[h, block], mixes[h, block] = total[h], mixed[h]

    def back(block):
        return pltpu.make_async_remote_copy(
            src_ref=leaving.at[block], dst_ref=mixed_out.at[pl.ds(3 * zed, 3)],
            send_sem=back_send.at[block], recv_sem=back_recv.at[zed],
            device_id=(grp, block * 2 + core), device_id_type=MESH,
        )

    def complete(block):
        fine = valid_columns(span, (2 * block + core) * tokens, tokens)
        for h in range(3):
            total = jnp.sum(totals[h, block], axis=0, keepdims=True) - extra
            total = jnp.where(fine, total, 1.0)
            mixed = mixes[h, block] / total
            mix_all[h, block] = mixed
            tot_all[h, block] = total
            _, _, v, _, _, terms, weight = alone_terms(raw.at[block, pl.ds(3 * h, 3)])
            leaving[block, h] = jnp.where(fine, mixed, weight * v / terms).astype(bf16)

        @pl.when(block != zed)
        def _():
            back(block).start()

        @pl.when(block == zed)
        def _():
            mixed_out[pl.ds(3 * zed, 3)] = leaving[zed]

    project(zed, 0)
    turn(zed, 0)
    pair(zed, zed, True)

    @pl.when(zed == 0)
    def _():
        complete(0)

    def step(d, _):
        low, high = zed - d, zed + d
        for side, block in ((0, low), (1, high)):

            @pl.when((block >= 0) & (block < 4))
            def _():
                towards = 1 - 2 * side
                pltpu.make_async_remote_copy(
                    src_ref=norm_all.at[block], dst_ref=norm_all.at[block],
                    send_sem=hop_send.at[side, d - 1], recv_sem=hop_recv.at[side, d - 1],
                    device_id=(grp, (zed - towards) * 2 + core), device_id_type=MESH,
                ).wait_recv()
                runs, copy = hop(d, side)
                pl.when(runs)(copy.start)
                project(block, 2 * d + side)

        @pl.when(high < 4)
        def _():
            lax.fori_loop(jnp.maximum(low + 1, 0), high, lambda j, _: (pair(high, j, False), 0)[1], 0)
            turn(high, 2 * d + 1)
            pair(high, high, True)

        @pl.when(low >= 0)
        def _():
            turn(low, 2 * d)
            pair(low, low, True)

            @pl.when(high < 4)
            def _():
                pair(high, low, False)

            pl.when(low == 0)(lambda: complete(low))

            def later(i, _):
                pair(i, low, False)
                pl.when(low == 0)(lambda: complete(i))
                return 0

            lax.fori_loop(low + 1, jnp.minimum(high, 4), later, 0)

        @pl.when((high < 4) & (low <= 0))
        def _():
            complete(high)

        return 0

    lax.fori_loop(1, 4, step, 0)

    for k in (1, 2, 3):
        back(along[k]).wait_send()
        pltpu.make_async_remote_copy(
            src_ref=leaving.at[zed], dst_ref=mixed_out.at[pl.ds(3 * along[k], 3)],
            send_sem=back_send.at[zed], recv_sem=back_recv.at[along[k]],
            device_id=(grp, along[k] * 2 + core), device_id_type=MESH,
        ).wait_recv()
    for d in range(4):
        for side in range(2):
            runs, copy = hop(d, side)
            pl.when(runs)(copy.wait_send)
            if d > 0 or side == 0:
                block = zed + (2 * side - 1) * d
                pl.when((block >= 0) & (block < 4))(swap(block, 2 * d + side).wait_send)


def attend(block_input, gain, bias, w_qkv, span):
    f32, bf16 = jnp.float32, jnp.bfloat16
    tokens, width = block_input.shape
    vmem, smem = pl.BlockSpec(memory_space=pltpu.VMEM), pl.BlockSpec(memory_space=pltpu.SMEM)
    block = (HEAD_DIM, tokens)
    dma = pltpu.SemaphoreType.DMA
    return pl.pallas_call(
        attend_kernel,
        out_shape=[
            jax.ShapeDtypeStruct((HEADS,) + block, bf16),
            jax.ShapeDtypeStruct((3, 4) + block, bf16),
            jax.ShapeDtypeStruct((3, 4, 2, 2) + block, bf16),
            jax.ShapeDtypeStruct((4, 9) + block, bf16),
            jax.ShapeDtypeStruct((3, 4) + block, f32),
            jax.ShapeDtypeStruct((3, 4, 1, tokens), f32),
            jax.ShapeDtypeStruct((4, width, tokens), bf16),
        ],
        in_specs=[vmem] * 3 + [pl.BlockSpec(memory_space=pl.ANY), smem],
        out_specs=[vmem] * 7,
        scratch_shapes=[
            pltpu.VMEM((3, width, 256), bf16),
            pltpu.VMEM((3, 256, width), bf16),
            pltpu.VMEM((3, 4, 2 * tokens, HEAD_DIM), bf16),
            pltpu.VMEM((3, 4) + block, f32),
            pltpu.VMEM((3, 4, 8, tokens), f32),
            pltpu.VMEM((4, 3) + block, bf16),
            dma((3,)),
            dma((2, 4)),
            dma((2, 4)),
            dma((8,)),
            dma((8,)),
            dma((4,)),
            dma((4,)),
        ],
        compiler_params=pltpu.CompilerParams(
            collective_id=1, has_side_effects=True, vmem_limit_bytes=48 * 2**20
        ),
    )(block_input, gain, bias, w_qkv, span)


def gelu_and_slope(u):
    root = 0.7978845608028654
    square = u * u
    bent = jnp.tanh(root * (u + 0.044715 * (square * u)))
    half = 0.5 * (1.0 + bent)
    slope = half + 0.5 * u * (1.0 - bent * bent) * (root * (1.0 + 0.134145 * square))
    return u * half, slope


def normal_parts(vector):
    centered = vector - jnp.mean(vector, axis=-1, keepdims=True)
    variance = jnp.mean(centered * centered, axis=-1, keepdims=True)
    inverse = lax.rsqrt(variance + epsilon)
    return centered * inverse, inverse


def norm_pull(normal, inverse, gain, grad):
    scaled = grad * gain
    along_normal = jnp.mean(scaled * normal, axis=-1, keepdims=True)
    return inverse * (scaled - jnp.mean(scaled, axis=-1, keepdims=True) - normal * along_normal)


def add_rows(into, base, count, *terms):
    chunk = 96 if count % 96 == 0 else 48

    def add(i, _):
        total = None
        for ref, start in terms:
            term = ref[rows_of(start + i * chunk, chunk), :].astype(jnp.float32)
            total = term if total is None else total + term
        into[rows_of(base + i * chunk, chunk), :] = total.astype(jnp.bfloat16)
        return 0

    lax.fori_loop(0, count // chunk, add, 0)


class GroupSum:
    whole = False

    def __init__(self, term, first, near, held, third, mine, out):
        self.term, self.first, self.near, self.held = term, first, near, held
        self.third, self.line_sum, self.out = third, mine, out
        self.rows, self.columns = term.shape[0] // 4, term.shape[1] // 2
        grp, seq, zed, core, sibling, along = place()
        self.place_in_plane(grp, seq)
        self.sibling, self.zed, self.core, self.along = sibling, zed, core, along
        self.line_targets = [(grp, along[n] * 2 + core) for n in (1, 2, 3)]
        self.halves = []
        self.mine = term.at[:, pl.ds(pl.multiple_of(core * self.columns, 128), self.columns)]
        self.away = pl.ds(pl.multiple_of((1 - core) * self.columns, 128), self.columns)
        self.copies = []

    def place_in_plane(self, grp, seq):
        y, x = grp // 2, grp % 2
        self.own, self.beside, self.above = grp, y * 2 + 1 - x, (1 - y) * 2 + x
        self.across = (1 - y) * 2 + 1 - x
        self.to_x, self.to_y = (self.beside, seq), (self.above, seq)

    def swap_quarter(self, send, quarter):
        at = rows_of(quarter * self.rows, self.rows)
        return send(self.term.at[at, self.away], self.first.at[at, :], self.sibling)

    def swap(self, send):
        for quarter in (self.across, self.beside, self.above, self.own):
            self.halves.append(self.swap_quarter(send, quarter))

    def part(self, quarter, half):
        return rows_of(quarter * self.rows + half * (self.rows // 2), self.rows // 2)

    def pass_on(self, send, quarter, half, slot, target):
        self.copies.append(
            send(self.first.at[self.part(quarter, half), :], self.near.at[slot], target)
        )

    def core_sum(self, quarter):
        base = quarter * self.rows
        add_rows(self.first, base, self.rows, (self.mine, base), (self.first, base))

    def step_one(self, send):
        steps = (
            (self.across, ((0, 0, self.to_x), (1, 2, self.to_y))),
            (self.beside, ((0, 1, self.to_x),)),
            (self.above, ((1, 3, self.to_y),)),
        )
        for i, (quarter, passes) in enumerate(steps):
            for copy in self.halves if self.whole else self.halves[i : i + 1]:
                if not self.whole or i == 0:
                    copy.wait_recv()
            self.core_sum(quarter)
            for half, slot, target in passes:
                self.pass_on(send, quarter, half, slot, target)
        self.copies = [self.copies[i] for i in (0, 2, 1, 3)]

    def step_two(self, send):
        half = self.rows // 2
        for slot, quarter, side, target in (
            (0, self.above, 0, self.to_y),
            (2, self.beside, 1, self.to_x),
        ):
            base = quarter * self.rows + side * half
            self.copies[slot].wait_recv()
            add_rows(self.first, base, half, (self.first, base), (self.near.at[slot], 0))
            self.pass_on(send, quarter, side, 4 + side, target)

    def total(self):
        half = self.rows // 2
        if not self.whole:
            self.halves[3].wait_recv()
        for slot in (1, 3, 4, 5):
            self.copies[slot].wait_recv()
        for side, one, two in ((0, 1, 4), (1, 3, 5)):
            base = self.own * self.rows + side * half
            add_rows(
                self.held, side * half, half, (self.mine, base), (self.first, base),
                (self.near.at[one], 0), (self.near.at[two], 0),
            )

    def along_line(self, send):
        self.total()
        rows = self.held.shape[0] // 4
        self.line = [
            send(self.held.at[rows_of(self.along[n] * rows, rows), :], self.third.at[n - 1], target)
            for n, target in zip((1, 2, 3), self.line_targets)
        ]

    def settle(self, send):
        rows = self.held.shape[0] // 4
        for copy in self.line:
            copy.wait_recv()
        total = self.held[rows_of(self.zed * rows, rows), :].astype(jnp.float32)
        for j in range(3):
            total = total + self.third[j].astype(jnp.float32)
        self.line_sum[...] = total
        column = pl.ds(pl.multiple_of(self.core * self.columns, 128), self.columns)
        half = rows // 2
        away = pl.ds(pl.multiple_of((1 - self.core) * half, 8), half)
        self.out[:, column] = self.line_sum[pl.ds(pl.multiple_of(self.core * half, 8), half), :]
        self.last = send(self.line_sum.at[away, :], self.out.at[:, column], self.sibling)

    def drain(self):
        for copy in self.halves + self.copies + self.line:
            copy.wait_send()
        self.last.wait()


class HeadsSum(GroupSum):
    def __init__(self, term, other, first, near, final):
        self.term, self.other, self.first, self.near, self.final = term, other, first, near, final
        self.rows = 4 * term.shape[2]
        grp, seq, zed, self.core, self.sibling, along = place()
        self.place_in_plane(grp, seq)
        self.copies, self.halves = [], []

    def swap_quarter(self, send, quarter):
        at = pl.ds(4 * quarter, 4)
        return send(self.term.at[at, 1 - self.core], self.other.at[at], self.sibling)

    def both_cores(self, quarter):
        at = pl.ds(4 * quarter, 4)
        return (self.term[at, self.core] + self.other[at]).reshape(self.rows, -1)

    def core_sum(self, quarter):
        self.first[rows_of(quarter * self.rows, self.rows), :] = self.both_cores(quarter).astype(
            jnp.bfloat16
        )

    def total(self):
        self.halves[3].wait_recv()
        for slot in (1, 3, 4, 5):
            self.copies[slot].wait_recv()
        near = [self.near[i].astype(jnp.float32) for i in range(6)]
        total = self.both_cores(self.own) + jnp.concatenate(
            [near[1] + near[4], near[3] + near[5]], axis=0
        )
        self.final[...] = total.reshape(self.final.shape)

    def drain(self):
        for copy in self.halves + self.copies:
            copy.wait_send()


def norm_back(x, gain, grad_norm, grad_out, into, chunk):
    f32 = jnp.float32
    tokens, width = x.shape
    gain_row = gain[...].reshape(1, width)

    def one(i, sums):
        at = rows_of(i * chunk, chunk)
        vector, grad = x[at, :].astype(f32), grad_norm[at, :]
        normal, inverse = normal_parts(vector)
        pulled = norm_pull(normal, inverse, gain_row, grad)
        into[at, :] = (grad_out[at, :] + pulled).astype(into.dtype)
        return (
            sums[0] + jnp.sum(grad * normal, axis=0, keepdims=True),
            sums[1] + jnp.sum(grad, axis=0, keepdims=True),
        )

    zero = jnp.zeros((1, width), f32)
    return lax.fori_loop(0, tokens // chunk, one, (zero, zero))


def settle_small(small, vecs, rms, owner):
    width, count = small.shape[-1], vecs.shape[-1]
    total = (small[0] + small[1]) + (small[2] + small[3])
    turned = pltpu.roll(total, (width - owner * count) % width, 1)
    for i in range(4):
        vecs[i] = turned[i : i + 1, :count]
    rms[...] = jnp.sqrt(total[4:5, :3] / total[4:5, 3:4])


def back_kernel(
    mixed_in, q_in, kv_in, raw_in, mix_in, tot_in, norm_in,
    x_in, out_grad_in, w_out_in, w_up_in, w_down_in, w_qkv_in,
    gain_one, gain_two, bias_two, span,
    block_output, input_grad, sum_qkv, vecs, rms, out_down, out_up, out_out,
    mixed, q_all, kv_all, raw, mix_all, tot_all, norm_all, x, out_grad, w_out, w_up, w_down, w_qkv,
    term_out, middle, normed, normed_t, mlp_out, grad_norm, grad_middle, gmix,
    first, near, held, third, mine, first_down, near_down, held_down, third_down, mine_down,
    gm_in, keys, values, g_all, gt_all, grad_kv, part_out, part_in, leaving, arrived,
    term, other, first_qkv, near_qkv, final, gathered, grad_query, small_a, small_b, small_c,
    load_sems, send_sems, recv_sems,
):
    tokens, width = x.shape
    f32, bf16 = jnp.float32, jnp.bfloat16
    grp, seq, zed, core, sibling, along = place()
    line = [(grp, along[k] * 2 + core) for k in (1, 2, 3)]
    chunks = w_up.shape[1] // width

    loads = {}

    def load(name, source, target):
        loads[name] = pltpu.make_async_copy(source, target, load_sems.at[len(loads)])
        loads[name].start()

    load("mixed", mixed_in, mixed)
    load("x", x_in, x)
    load("w_out", w_out_in, w_out)
    load("out_grad", out_grad_in, out_grad)
    for i in range(chunks):
        at = pl.ds(i * width, width)
        load(("up", i), w_up_in.at[:, at], w_up.at[:, at])
        load(("down", i), w_down_in.at[at, :], w_down.at[at, :])
    later = ((q_in, q_all), (kv_in, kv_all), (raw_in, raw), (mix_in, mix_all), (tot_in, tot_all),
             (norm_in, norm_all), (w_qkv_in, w_qkv))
    for i, (source, target) in enumerate(later):
        load(("later", i), source, target)

    ups = [
        GroupSum(
            w_up.at[:, pl.ds(i * width, width)], first.at[i], near.at[i], held.at[i], third.at[i],
            mine.at[i], out_up.at[:, pl.ds(i * width, width)],
        )
        for i in range(chunks)
    ]
    outs = GroupSum(
        term_out, first.at[chunks], near.at[chunks], held.at[chunks], third.at[chunks],
        mine.at[chunks], out_out,
    )
    downs = GroupSum(w_down, first_down, near_down, held_down, third_down, mine_down, out_down)
    downs.whole = True
    heads_sum = HeadsSum(term, other, first_qkv, near_qkv, final)
    across = [(k, seq) for k in (heads_sum.beside, heads_sum.above, heads_sum.across)]
    around = [(k, zed * 2 + 1 - core) for k in (heads_sum.beside, heads_sum.above, heads_sum.across)]
    partners = [sibling] + line + across + around
    greet_start(partners)
    send = sender(send_sems, recv_sems)

    pos = seq * tokens + lax.broadcasted_iota(jnp.int32, (tokens, 1), 0)
    keep = ((pos >= span[0, 0]) & (pos < span[0, 1])).astype(f32)
    gain_row, bias_row = gain_two[...].reshape(1, width), bias_two[...].reshape(1, width)

    def squares(value):
        return jnp.sum(keep * value * value)

    for name in ("mixed", "x", "w_out", "out_grad"):
        loads[name].wait()
    attn_out = matmul(mixed[...].reshape(width, tokens).T, w_out[...])
    attn_squares = squares(attn_out)
    middle[...] = x[...].astype(f32) + attn_out
    normed[...] = (normal_parts(middle[...])[0] * gain_row + bias_row).astype(bf16)
    normed_t[...] = normed[...].T
    mlp_out[...] = jnp.zeros((tokens, width), f32)
    grad_norm[...] = jnp.zeros((tokens, width), f32)
    for i in range(chunks):
        at = pl.ds(i * width, width)
        loads["up", i].wait()
        loads["down", i].wait()
        activated, slope = gelu_and_slope(matmul(normed[...], w_up[:, at]))
        activated = activated.astype(bf16)
        mlp_out[...] += matmul(activated, w_down[at, :])
        grad_up = (contract_cols(out_grad[...], w_down[at, :]) * slope).astype(bf16)
        grad_norm[...] += contract_cols(grad_up, w_up[:, at])
        w_up[:, at] = matmul(normed_t[...], grad_up).astype(bf16)
        if i == 0:
            greet_end(partners)
        ups[i].swap(send)
        w_down[at, :] = matmul(activated.T, out_grad[...]).astype(bf16)
        downs.halves.append(downs.swap_quarter(send, i))
        if i >= 2:
            ups[i - 2].step_one(send)
    normal, inverse = normal_parts(middle[...])
    grad = grad_norm[...]
    grad_middle[...] = out_grad[...].astype(f32) + norm_pull(normal, inverse, gain_row, grad)
    grad_attn = grad_middle[...].astype(bf16)
    gmix[...] = contract_cols(w_out[...], grad_attn).astype(bf16).reshape(gmix.shape)
    coming = []
    for h in range(3):
        for k in (1, 2, 3):
            coming.append(send(gmix.at[along[k] * 3 + h], gm_in.at[h, zed], line[k - 1]))
        gm_in[h, zed] = gmix[zed * 3 + h]
    term_out[...] = matmul(mixed[...].reshape(width, tokens), grad_attn).astype(bf16)
    ups[0].step_two(send)
    ups[2].step_one(send)
    outs.swap(send)
    ups[1].step_two(send)
    ups[3].step_one(send)
    small_a[0, 2:3] = jnp.sum(grad * normal, axis=0, keepdims=True)
    small_a[0, 3:4] = jnp.sum(grad, axis=0, keepdims=True)
    output = middle[...] + mlp_out[...]
    block_output[...] = output.astype(bf16)
    lane = lax.broadcasted_iota(jnp.int32, (4, width), 1)
    row = jnp.zeros((4, width), f32)
    squared = (squares(output), attn_squares, squares(mlp_out[...]), jnp.sum(keep) * width)
    for i, value in enumerate(squared):
        row = jnp.where(lane == i, value, row)
    small_a[0, 4:8] = row

    for i in range(len(later)):
        loads["later", i].wait()

    def turn(h):
        def one(z, _):
            for side in range(2):
                at = pl.ds(side * tokens, tokens)
                keys[h % 2, z, at, :] = kv_all[h, z, side, 0].T
                values[h % 2, z, at, :] = kv_all[h, z, side, 1].T
            return 0

        lax.fori_loop(0, 4, one, 0)

    turn(0)
    ups[0].along_line(send)
    for z in range(4):
        leaving[z, 9] = jnp.zeros((HEAD_DIM, tokens), bf16)
    downs.step_one(send)

    swaps, sends = [], []

    def finish(h):
        swaps[h].wait_recv()

        def merge(z, _):
            fine = valid_columns(span, (2 * z + core) * tokens, tokens)
            q, k, v, inverse, signed, terms, weight = alone_terms(raw.at[z, pl.ds(3 * h, 3)])
            g = gm_in[h, z].astype(f32)
            total = 1.0 / terms
            grad_total = -jnp.sum(g * (weight * v), axis=0, keepdims=True) * total * total
            g = (g * total).astype(bf16).astype(f32)
            grad_weight = jnp.sum(g * v, axis=0, keepdims=True)
            slope = 1.0 + (inverse * inverse) * (inverse - 1.0)
            grad_score = terms * (grad_weight * slope + grad_total * signed)
            grad_score = grad_score.astype(bf16).astype(f32)
            alone = (grad_score * k * 0.125, grad_score * q, weight * g)
            parts = [leaving[z, 3 * h].astype(f32)]
            for part in range(2):
                parts.append(grad_kv[h, z, core, part] + part_in[h, z, part].astype(f32))
            for part in range(3):
                leaving[z, 3 * h + part] = jnp.where(fine, parts[part], alone[part]).astype(bf16)
            return 0

        lax.fori_loop(0, 4, merge, 0)
        at = pl.ds(3 * h, 3)
        for k in (1, 2, 3):
            sends.append(
                send(leaving.at[along[k], at], arrived.at[:, zed * 3 + h], line[k - 1])
            )
        for part in range(3):
            arrived[part, zed * 3 + h] = leaving[zed, 3 * h + part]

    def tile_products(h, z, z_key, side):
        at = pl.ds(side * tokens, tokens)
        scores = matmul(keys[h % 2, z_key, at, :], q_all[h, z])
        return scores, matmul(values[h % 2, z_key, at, :], g_all[z])

    def tile_grads(tile, scores, grad_weights):
        z, z_key, side = tile
        inverse, signed, terms = signed_terms(scores)
        if z == z_key:
            key_pos = lax.broadcasted_iota(jnp.int32, scores.shape, 0)
            query_pos = lax.broadcasted_iota(jnp.int32, scores.shape, 1)
            seen = key_pos + side * tokens <= query_pos + core * tokens
            terms = jnp.where(seen, terms, 0.0)
        weights = (signed * terms).astype(bf16)
        slope = 1.0 + (inverse * inverse) * (inverse - 1.0)
        grad_scores = terms * (grad_weights * slope + gt_all[z] * signed)
        return weights, grad_scores.astype(bf16)

    def tile_sums(h, z, z_key, side, weights, grad_scores):
        for part, left, right in ((0, q_all[h, z], grad_scores), (1, g_all[z], weights)):
            grad = contract_cols(left, right)
            if z == z_key:
                grad_kv[h, z_key, side, part] = grad
            else:
                grad_kv[h, z_key, side, part] += grad
        grad = matmul(kv_all[h, z_key, side, 0], grad_scores)
        if z_key == 0 and side == 0:
            grad_query[...] = grad
        else:
            grad_query[...] += grad
        if z == z_key and side == 1:
            leaving[z, 3 * h] = (grad_query[...] * 0.125).astype(bf16)

    for h in range(3):
        for copy in coming[h * 3 : h * 3 + 3]:
            copy.wait_recv()

        def prepare(z, _):
            g = gm_in[h, z].astype(f32)
            total = 1.0 / tot_all[h, z]
            g_all[z] = (g * total).astype(bf16)
            gt_all[z] = -jnp.sum(g * mix_all[h, z], axis=0, keepdims=True) * total
            return 0

        lax.fori_loop(0, 4, prepare, 0)

        tiles = [(z, z_key, side) for z in range(4) for z_key in range(z + 1) for side in range(2)]
        scored, parts = {}, {}
        for step in range(len(tiles) + 2):
            if step < len(tiles):
                scored[step] = tile_products(h, *tiles[step])
            if 0 <= step - 1 < len(tiles):
                parts[step - 1] = tile_grads(tiles[step - 1], *scored.pop(step - 1))
            if step - 2 >= 0:
                tile_sums(h, *tiles[step - 2], *parts.pop(step - 2))

        def pack(z, _):
            for part in range(2):
                part_out[h, z, part] = grad_kv[h, z, 1 - core, part].astype(bf16)
            return 0

        lax.fori_loop(0, 4, pack, 0)
        swaps.append(send(part_out.at[h], part_in.at[h], sibling))
        if h == 0:
            turn(1)
            ups[1].along_line(send)
            outs.step_one(send)
        if h == 1:
            turn(2)
            ups[2].step_two(send)
            ups[3].step_two(send)
        finish(h)

    for quarter in (heads_sum.across, heads_sum.beside, heads_sum.above, heads_sum.own):
        total = None
        for z in range(4):
            rows = norm_all[z, rows_of(quarter * (width // 4), width // 4), :]
            part = contract_cols(rows, leaving[z].reshape(10 * HEAD_DIM, tokens))
            total = part if total is None else total + part
        term[pl.ds(4 * quarter, 4)] = total.reshape((4,) + term.shape[1:])
        heads_sum.halves.append(heads_sum.swap_quarter(send, quarter))
    ups[2].along_line(send)
    heads_sum.step_one(send)
    downs.step_two(send)
    outs.step_two(send)
    ups[3].along_line(send)
    heads_sum.step_two(send)
    downs.along_line(send)
    outs.along_line(send)

    for copy in sends:
        copy.wait_recv()
    grads = arrived[...].reshape(3 * width, tokens)
    for i in range(width // 256):
        columns = slice(i * 256, (i + 1) * 256)
        grad_norm[:, columns] = matmul(w_qkv[columns, :], grads).T
    gain_grad, bias_grad = norm_back(x, gain_one, grad_norm, grad_middle, input_grad, 64)
    small_a[0, 0:1] = gain_grad
    small_a[0, 1:2] = bias_grad
    whose = 2 * grp + core
    small_b[pl.ds(whose, 1)] = small_a[0:1]
    planes = [
        send(small_b.at[whose], small_b.at[whose], target)
        for target in [sibling] + across + around
    ]
    heads_sum.total()
    gathered[pl.ds(zed, 1)] = final[pl.ds(zed, 1)]
    blocks = [send(final.at[along[k]], gathered.at[zed], line[k - 1]) for k in (1, 2, 3)]
    for copy in planes:
        copy.wait_recv()
    total = small_b[0]
    for i in range(1, 8):
        total = total + small_b[i]
    small_c[pl.ds(zed, 1)] = total.reshape(1, 8, width)
    columns = [send(small_c.at[zed], small_c.at[zed], line[k - 1]) for k in (1, 2, 3)]
    sums = ups + [downs, outs]
    for each in sums:
        each.settle(send)
    for copy in blocks + columns:
        copy.wait_recv()
    for z in range(4):
        for h in range(3):
            for part in range(3):
                start = part * width + (3 * z + h) * HEAD_DIM
                sum_qkv[:, start : start + HEAD_DIM] = gathered[
                    z, :, (3 * h + part) * HEAD_DIM : (3 * h + part + 1) * HEAD_DIM
                ]
    settle_small(small_c, vecs, rms, grp * 8 + seq)
    for copy in coming + swaps + sends + planes + blocks + columns:
        copy.wait_send()
    for each in sums + [heads_sum]:
        each.drain()


def back(mixed, saved, block_input, out_grad, w_out, w_up, w_down, w_qkv, gain_one, gain_two, bias_two, span):
    f32, bf16 = jnp.float32, jnp.bfloat16
    tokens, width = block_input.shape
    hidden = w_up.shape[1]
    count = hidden // width + 1
    vmem, smem = pl.BlockSpec(memory_space=pltpu.VMEM), pl.BlockSpec(memory_space=pltpu.SMEM)
    block = (HEAD_DIM, tokens)
    own_rows, columns = width // 32, 10 * HEAD_DIM
    quarter, half = width // 4, width // 2
    copies = 14 * (count + 1) + 9 + 3 + 9 + 10 + 7 + 3 + 3
    in_hbm = [mixed, *saved, block_input, out_grad, w_out, w_up, w_down, w_qkv]

    def sum_scratch(lead, rows):
        return [
            pltpu.VMEM(lead + (4 * rows, half), bf16),
            pltpu.VMEM(lead + (6, rows // 2, half), bf16),
            pltpu.VMEM(lead + (rows, half), bf16),
            pltpu.VMEM(lead + (3, rows // 4, half), bf16),
            pltpu.VMEM(lead + (rows // 4, half), f32),
        ]

    return pl.pallas_call(
        back_kernel,
        out_shape=[
            jax.ShapeDtypeStruct((tokens, width), bf16),
            jax.ShapeDtypeStruct((tokens, width), bf16),
            jax.ShapeDtypeStruct((own_rows, 3 * width), f32),
            jax.ShapeDtypeStruct((4, 1, own_rows), f32),
            jax.ShapeDtypeStruct((1, 3), f32),
            jax.ShapeDtypeStruct((hidden // 32, width), f32),
            jax.ShapeDtypeStruct((own_rows, hidden), f32),
            jax.ShapeDtypeStruct((own_rows, width), f32),
        ],
        in_specs=[pl.BlockSpec(memory_space=pl.ANY)] * len(in_hbm) + [vmem] * 3 + [smem],
        out_specs=[vmem] * 8,
        scratch_shapes=[pltpu.VMEM(a.shape, a.dtype) for a in in_hbm]
        + [
            pltpu.VMEM((width, width), bf16),
            pltpu.VMEM((tokens, width), f32),
            pltpu.VMEM((tokens, width), bf16),
            pltpu.VMEM((width, tokens), bf16),
            pltpu.VMEM((tokens, width), f32),
            pltpu.VMEM((tokens, width), f32),
            pltpu.VMEM((tokens, width), f32),
            pltpu.VMEM((HEADS,) + block, bf16),
        ]
        + sum_scratch((count,), quarter)
        + sum_scratch((), hidden // 4)
        + [
            pltpu.VMEM((3, 4) + block, bf16),
            pltpu.VMEM((2, 4, 2 * tokens, HEAD_DIM), bf16),
            pltpu.VMEM((2, 4, 2 * tokens, HEAD_DIM), bf16),
            pltpu.VMEM((4,) + block, bf16),
            pltpu.VMEM((4, 1, tokens), f32),
            pltpu.VMEM((3, 4, 2, 2) + block, f32),
            pltpu.VMEM((3, 4, 2) + block, bf16),
            pltpu.VMEM((3, 4, 2) + block, bf16),
            pltpu.VMEM((4, 10) + block, bf16),
            pltpu.VMEM((3, HEADS) + block, bf16),
            pltpu.VMEM((16, 2, own_rows, columns), f32),
            pltpu.VMEM((16, own_rows, columns), f32),
            pltpu.VMEM((16 * own_rows, columns), bf16),
            pltpu.VMEM((6, 2 * own_rows, columns), bf16),
            pltpu.VMEM((4, own_rows, columns), f32),
            pltpu.VMEM((4, own_rows, columns), f32),
            pltpu.VMEM(block, f32),
            pltpu.VMEM((1, 8, width), f32),
            pltpu.VMEM((8, 8, width), f32),
            pltpu.VMEM((4, 8, width), f32),
            pltpu.SemaphoreType.DMA((11 + 2 * (count - 1),)),
            pltpu.SemaphoreType.DMA((copies,)),
            pltpu.SemaphoreType.DMA((copies,)),
        ],
        compiler_params=pltpu.CompilerParams(
            collective_id=2, has_side_effects=True, vmem_limit_bytes=63 * 2**20
        ),
    )(*in_hbm, gain_one, gain_two, bias_two, span)


def per_device_planned(
    block_input,
    out_grad,
    seq_span,
    ln1_gain,
    ln1_bias,
    w_qkv,
    w_out,
    ln2_gain,
    ln2_bias,
    w_up,
    w_down,
):
    mixed, *saved = attend(block_input, ln1_gain, ln1_bias, w_qkv, seq_span)
    block_output, input_grad, sum_qkv, vecs, rms_stats, sum_down, sum_up, sum_out = back(
        mixed, saved, block_input, out_grad, w_out, w_up, w_down, w_qkv, ln1_gain, ln2_gain,
        ln2_bias, seq_span,
    )
    vecs = vecs.reshape(4, -1)
    return (
        block_output,
        input_grad,
        vecs[0],
        vecs[1],
        sum_qkv,
        sum_out,
        vecs[2],
        vecs[3],
        sum_up,
        sum_down,
        rms_stats.reshape(3),
    )


def solution(mesh):
    placed = (
        P(("grp", "seq"), None),
        P(("grp", "seq"), None),
        P("grp", None),
        P(),
        P(),
        P(),
        P(),
        P(),
        P(),
        P(),
        P(),
    )
    planned = mesh.shape["grp"] == 4 and mesh.shape["seq"] == 8
    return jax.shard_map(
        per_device_planned if planned else per_device,
        mesh=mesh,
        in_specs=placed,
        out_specs=(
            P(("grp", "seq"), None),
            P(("grp", "seq"), None),
            P(("grp", "seq")),
            P(("grp", "seq")),
            P(("grp", "seq"), None),
            P(("grp", "seq"), None),
            P(("grp", "seq")),
            P(("grp", "seq")),
            P(("grp", "seq"), None),
            P(("grp", "seq"), None),
            P(),
        ),
        check_vma=False,
    )
```

```python
import functools

import jax
import jax.numpy as jnp
from jax import lax
from jax.experimental import pallas as pl
from jax.experimental.pallas import tpu as pltpu
from jax.sharding import PartitionSpec as P

D = 768
HEADS = 12
HEAD_DIM = 64
MESH = pl.DeviceIdType.MESH


epsilon = 1e-05


def passed_along(array, axis, by):
    devices = lax.axis_size(axis)
    pairs = [(i, i + by) for i in range(devices) if 0 <= i + by < devices]
    return lax.ppermute(array, axis, pairs)


def shifted(array, axis, by):
    devices = lax.axis_size(axis)
    return lax.ppermute(array, axis, [(i, (i + by) % devices) for i in range(devices)])


def layer_norm(vector, scale_vec, shift_vec):
    row_mean = jnp.mean(vector, axis=-1, keepdims=True)
    centered = vector - row_mean
    variance = jnp.mean(centered * centered, axis=-1, keepdims=True)
    return centered * lax.rsqrt(variance + epsilon) * scale_vec + shift_vec


def contract_rows(left, right):
    return lax.dot_general(
        left, right, (((0,), (0,)), ((), ())), preferred_element_type=jnp.float32
    )


def contract_cols(left, right):
    return lax.dot_general(
        left, right, (((1,), (1,)), ((), ())), preferred_element_type=jnp.float32
    )


def score_terms(queries, key_block, query_pos, key_pos, seq_first, seq_limit):
    scores = (
        jnp.einsum("qhd,khd->qhk", queries, key_block, preferred_element_type=jnp.float32) * 0.125
    )
    query_valid = (query_pos >= seq_first) & (query_pos < seq_limit)
    key_valid = (key_pos >= seq_first) & (key_pos < seq_limit)
    allowed = (key_pos[None, :] <= query_pos[:, None]) & (
        query_valid[:, None] & key_valid[None, :] | (key_pos[None, :] == query_pos[:, None])
    )
    magnitude = jnp.sqrt(scores * scores + 1.0)
    signed_part = scores / magnitude
    exp_terms = jnp.where(allowed[:, None, :], jnp.exp(magnitude), 0.0)
    return (magnitude, signed_part, exp_terms)


def split_pair(kv_pair):
    count_rows = kv_pair.shape[0]
    key_block = kv_pair[:, :D].reshape(count_rows, HEADS, HEAD_DIM)
    value_block = kv_pair[:, D:].reshape(count_rows, HEADS, HEAD_DIM)
    return (key_block, value_block)


def forward_block(running, kv_pair, key_start, queries, query_pos, seq_first, seq_limit):
    totals, unnorm = running
    key_block, value_block = split_pair(kv_pair)
    key_pos = key_start + jnp.arange(kv_pair.shape[0], dtype=jnp.int32)
    magnitude, signed_part, exp_terms = score_terms(
        queries, key_block, query_pos, key_pos, seq_first, seq_limit
    )
    weights = (signed_part * exp_terms).astype(jnp.bfloat16)
    totals = totals + jnp.sum(exp_terms, axis=-1)
    unnorm = unnorm + jnp.einsum(
        "qhk,khd->qhd", weights, value_block, preferred_element_type=jnp.float32
    )
    return (totals, unnorm)


def grad_core(
    kv_pair, key_start, queries, query_pos, seq_first, seq_limit, grad_unnorm, grad_totals
):
    key_block, value_block = split_pair(kv_pair)
    key_pos = key_start + jnp.arange(kv_pair.shape[0], dtype=jnp.int32)
    magnitude, signed_part, exp_terms = score_terms(
        queries, key_block, query_pos, key_pos, seq_first, seq_limit
    )
    weights = (signed_part * exp_terms).astype(jnp.bfloat16)
    grad_weights = jnp.einsum(
        "qhd,khd->qhk", grad_unnorm, value_block, preferred_element_type=jnp.float32
    )
    grad_scores = (
        grad_weights * exp_terms / (magnitude * magnitude * magnitude)
        + (grad_weights * signed_part + grad_totals[:, :, None]) * exp_terms * signed_part
    )
    return (key_block, weights, grad_scores.astype(jnp.bfloat16))


def backward_block(
    kv_pair, key_start, queries, query_pos, seq_first, seq_limit, grad_unnorm, grad_totals
):
    key_block, weights, grad_scores = grad_core(
        kv_pair, key_start, queries, query_pos, seq_first, seq_limit, grad_unnorm, grad_totals
    )
    count_rows = kv_pair.shape[0]
    grad_query = (
        jnp.einsum("qhk,khd->qhd", grad_scores, key_block, preferred_element_type=jnp.float32)
        * 0.125
    )
    grad_key = (
        jnp.einsum("qhk,qhd->khd", grad_scores, queries, preferred_element_type=jnp.float32) * 0.125
    )
    grad_value = jnp.einsum(
        "qhk,qhd->khd", weights, grad_unnorm, preferred_element_type=jnp.float32
    )
    grad_pair = jnp.concatenate(
        [grad_key.reshape(count_rows, D), grad_value.reshape(count_rows, D)], axis=1
    )
    return (grad_query, grad_pair)


def per_device(
    block_input,
    out_grad,
    seq_span,
    ln1_gain,
    ln1_bias,
    w_qkv,
    w_out,
    ln2_gain,
    ln2_bias,
    w_up,
    w_down,
):
    tok_rows = block_input.shape[0]
    feat_width = block_input.shape[1]
    seq_count = lax.axis_size("seq")
    seq_index = lax.axis_index("seq")
    query_pos = seq_index * tok_rows + jnp.arange(tok_rows, dtype=jnp.int32)
    query_last = query_pos[tok_rows - 1]
    seq_first = seq_span[0, 0]
    seq_limit = seq_span[0, 1]
    inputs = block_input.astype(jnp.float32)
    normed = layer_norm(inputs, ln1_gain, ln1_bias).astype(jnp.bfloat16)
    proj_qkv = jnp.dot(normed, w_qkv, preferred_element_type=jnp.float32).astype(jnp.bfloat16)
    queries = proj_qkv[:, :feat_width].reshape(tok_rows, HEADS, HEAD_DIM)
    kv_pair = proj_qkv[:, feat_width:]

    def visit_block(running, shard_rows, key_start):
        return lax.cond(
            key_start <= query_last,
            lambda state_in: forward_block(
                state_in, shard_rows, key_start, queries, query_pos, seq_first, seq_limit
            ),
            lambda state_in: state_in,
            running,
        )

    empty = (
        jnp.zeros((tok_rows, HEADS), jnp.float32),
        jnp.zeros((tok_rows, HEADS, HEAD_DIM), jnp.float32),
    )
    first_state = visit_block(empty, kv_pair, seq_index * tok_rows)

    def forward_hop(hop_count, loop_state):
        moving, running = loop_state
        moving = passed_along(moving, "seq", 1)
        source = (seq_index - hop_count) % seq_count
        return (moving, visit_block(running, moving, source * tok_rows))

    _, (totals, unnorm) = lax.fori_loop(1, seq_count, forward_hop, (kv_pair, first_state))
    mixed_heads = (unnorm / totals[:, :, None]).reshape(tok_rows, feat_width).astype(jnp.bfloat16)
    attn_out = jnp.dot(mixed_heads, w_out, preferred_element_type=jnp.float32)
    middle = inputs + attn_out
    normed_two = layer_norm(middle, ln2_gain, ln2_bias).astype(jnp.bfloat16)
    up_proj = jnp.dot(normed_two, w_up, preferred_element_type=jnp.float32)
    activated = jax.nn.gelu(up_proj, approximate=True).astype(jnp.bfloat16)
    mlp_out = jnp.dot(activated, w_down, preferred_element_type=jnp.float32)
    output = middle + mlp_out
    valid_rows = ((query_pos >= seq_first) & (query_pos < seq_limit)).astype(jnp.float32)[:, None]
    rms_parts = lax.psum(
        (
            jnp.sum(valid_rows * output * output),
            jnp.sum(valid_rows * attn_out * attn_out),
            jnp.sum(valid_rows * mlp_out * mlp_out),
            jnp.sum(valid_rows) * feat_width,
        ),
        ("grp", "seq"),
    )
    rms_stats = jnp.sqrt(jnp.stack([rms_parts[0], rms_parts[1], rms_parts[2]]) / rms_parts[3])
    grad_w_down = contract_rows(activated, out_grad)
    grad_activated = contract_cols(out_grad, w_down)
    _, gelu_pull = jax.vjp(lambda pre_act: jax.nn.gelu(pre_act, approximate=True), up_proj)
    grad_up = gelu_pull(grad_activated)[0].astype(jnp.bfloat16)
    grad_w_up = contract_rows(normed_two, grad_up)
    grad_norm_two = contract_cols(grad_up, w_up)
    _, norm_pull_two = jax.vjp(layer_norm, middle, ln2_gain, ln2_bias)
    grad_mid_norm, grad_gain_two, grad_bias_two = norm_pull_two(grad_norm_two)
    grad_middle = out_grad.astype(jnp.float32) + grad_mid_norm
    grad_attn = grad_middle.astype(jnp.bfloat16)
    grad_w_out = contract_rows(mixed_heads, grad_attn)
    grad_mixed = contract_cols(grad_attn, w_out).reshape(tok_rows, HEADS, HEAD_DIM)
    grad_unnorm = (grad_mixed / totals[:, :, None]).astype(jnp.bfloat16)
    grad_totals = -jnp.sum(grad_mixed * unnorm, axis=-1) / (totals * totals)

    def back_block(grad_run, shard_rows, key_start):

        def compute_block(grad_in):
            grad_query, grad_pair = backward_block(
                shard_rows,
                key_start,
                queries,
                query_pos,
                seq_first,
                seq_limit,
                grad_unnorm,
                grad_totals,
            )
            return (grad_in + grad_query, grad_pair)

        def skip_block(grad_in):
            return (grad_in, jnp.zeros((shard_rows.shape[0], 2 * feat_width), jnp.float32))

        return lax.cond(key_start <= query_last, compute_block, skip_block, grad_run)

    grad_start = jnp.zeros((tok_rows, HEADS, HEAD_DIM), jnp.float32)
    grad_queries, local_terms = back_block(grad_start, kv_pair, seq_index * tok_rows)

    def backward_hop(hop_count, loop_state):
        moving, grad_acc, grad_run = loop_state
        moving = passed_along(moving, "seq", 1)
        grad_acc = shifted(grad_acc.astype(jnp.bfloat16), "seq", 1).astype(grad_acc.dtype)
        source = (seq_index - hop_count) % seq_count
        grad_run, new_terms = back_block(grad_run, moving, source * tok_rows)
        return (moving, grad_acc + new_terms, grad_run)

    _, grad_acc, grad_queries = lax.fori_loop(
        1, seq_count, backward_hop, (kv_pair, local_terms, grad_queries)
    )
    grad_kv = shifted(grad_acc.astype(jnp.bfloat16), "seq", 1).astype(grad_acc.dtype)
    grad_qkv = jnp.concatenate(
        [grad_queries.reshape(tok_rows, feat_width), grad_kv], axis=1
    ).astype(jnp.bfloat16)
    grad_w_qkv = contract_rows(normed, grad_qkv)
    grad_norm_one = contract_cols(grad_qkv, w_qkv)
    _, norm_pull_one = jax.vjp(layer_norm, inputs, ln1_gain, ln1_bias)
    grad_in_norm, grad_gain_one, grad_bias_one = norm_pull_one(grad_norm_one)
    input_grad = (grad_middle + grad_in_norm).astype(jnp.bfloat16)
    summed = (
        lax.psum_scatter(grad_gain_one, ("grp", "seq"), scatter_dimension=0, tiled=True),
        lax.psum_scatter(grad_bias_one, ("grp", "seq"), scatter_dimension=0, tiled=True),
        lax.psum_scatter(grad_w_qkv, ("grp", "seq"), scatter_dimension=0, tiled=True),
        lax.psum_scatter(grad_w_out, ("grp", "seq"), scatter_dimension=0, tiled=True),
        lax.psum_scatter(grad_gain_two, ("grp", "seq"), scatter_dimension=0, tiled=True),
        lax.psum_scatter(grad_bias_two, ("grp", "seq"), scatter_dimension=0, tiled=True),
        lax.psum_scatter(grad_w_up, ("grp", "seq"), scatter_dimension=0, tiled=True),
        lax.psum_scatter(grad_w_down, ("grp", "seq"), scatter_dimension=0, tiled=True),
    )
    return (
        output.astype(jnp.bfloat16),
        input_grad,
        summed[0],
        summed[1],
        summed[2],
        summed[3],
        summed[4],
        summed[5],
        summed[6],
        summed[7],
        rms_stats,
    )


def rows_of(start, count):
    return pl.ds(pl.multiple_of(start, 16), count)


def matmul(left, right):
    return jnp.dot(left, right, preferred_element_type=jnp.float32)


def signed_terms(scores):
    square = scores * scores + 1.0
    inverse = lax.rsqrt(square)
    return inverse, scores * inverse, jnp.exp(square * inverse)


def valid_columns(span, start, count):
    pos = start + lax.broadcasted_iota(jnp.int32, (1, count), 1)
    return (pos >= span[0, 0]) & (pos < span[0, 1])


def greet_start(partners):
    for partner in partners:
        pl.semaphore_signal(
            pltpu.get_barrier_semaphore(), inc=1, device_id=partner, device_id_type=MESH
        )


def greet_end(partners):
    pl.semaphore_wait(pltpu.get_barrier_semaphore(), len(partners))


def sender(send_sems, recv_sems):
    count = [0]

    def send(src, dst, target):
        slot = count[0]
        count[0] += 1
        copy = pltpu.make_async_remote_copy(
            src_ref=src, dst_ref=dst, send_sem=send_sems.at[slot], recv_sem=recv_sems.at[slot],
            device_id=target, device_id_type=MESH,
        )
        copy.start()
        return copy

    return send


def place():
    grp, seq = lax.axis_index("grp"), lax.axis_index("seq")
    zed, core = seq // 2, seq % 2
    sibling = (grp, zed * 2 + 1 - core)
    along = [(zed + k) % 4 for k in range(4)]
    return grp, seq, zed, core, sibling, along


def alone_terms(raw):
    q, k, v = (raw[part].astype(jnp.float32) for part in range(3))
    inverse, signed, terms = signed_terms(jnp.sum(q * k, axis=0, keepdims=True))
    weight = (signed * terms).astype(jnp.bfloat16).astype(jnp.float32)
    return q, k, v, inverse, signed, terms, weight


def attend_part(
    x, gain_one, bias_one, w_qkv, span, mixed, q_all, kv_all, raw, mix_all, tot_all, norm_all,
    weights, keys, totals, leaving, hop_send, hop_recv, swap_send, swap_recv, back_send, back_recv,
    loads, greet_end,
):
    tokens, width = x.shape
    f32, bf16 = jnp.float32, jnp.bfloat16
    grp, seq, zed, core, sibling, along = place()

    start = pl.multiple_of(zed * 192 // 128 * 128, 128)
    inside = pl.ds(pl.multiple_of(zed % 2 * HEAD_DIM, HEAD_DIM), 3 * HEAD_DIM)
    loads["x"].wait()
    vector = x[...].astype(f32)
    centered = vector - jnp.mean(vector, axis=-1, keepdims=True)
    variance = jnp.mean(centered * centered, axis=-1, keepdims=True)
    normed = (
        centered * lax.rsqrt(variance + epsilon) * gain_one[...].reshape(1, width)
        + bias_one[...].reshape(1, width)
    ).astype(bf16)
    norm_all[zed] = normed.T
    greet_end()

    def hop(step, side):
        towards = 1 - 2 * side
        block = zed - towards * step
        runs = (block >= 0) & (block < 4) & (zed + towards >= 0) & (zed + towards < 4)
        copy = pltpu.make_async_remote_copy(
            src_ref=norm_all.at[block], dst_ref=norm_all.at[block],
            send_sem=hop_send.at[side, step], recv_sem=hop_recv.at[side, step],
            device_id=(grp, (zed + towards) * 2 + core), device_id_type=MESH,
        )
        return runs, copy

    def hop_on(step):
        for side in range(2):
            runs, copy = hop(step, side)
            pl.when(runs)(copy.start)

    hop_on(0)
    loads["w_qkv"].wait()
    for part in range(3):
        at = pl.ds(pl.multiple_of(part * width + start, 128), 256)
        weights[part] = w_qkv[:, at].T
    no_score = signed_terms(jnp.zeros((1, tokens), f32))[2]
    extra = span[0, 0].astype(f32) * no_score
    mix_all[...] = jnp.zeros(mix_all.shape, f32)
    totals[...] = jnp.zeros(totals.shape, f32)

    def swap(block, slot):
        return pltpu.make_async_remote_copy(
            src_ref=kv_all.at[:, block, core], dst_ref=kv_all.at[:, block, core],
            send_sem=swap_send.at[slot], recv_sem=swap_recv.at[slot],
            device_id=sibling, device_id_type=MESH,
        )

    def project(block, slot):
        keep = valid_columns(span, (2 * block + core) * tokens, tokens).astype(f32)
        for part in range(3):
            heads = matmul(weights[part, inside, :], norm_all[block])
            if part == 0:
                heads = heads * 0.125
            for h in range(3):
                one = heads[h * HEAD_DIM : (h + 1) * HEAD_DIM]
                raw[block, 3 * h + part] = one.astype(bf16)
                if part == 0:
                    q_all[h, block] = (one * keep).astype(bf16)
                else:
                    kv_all[h, block, core, part - 1] = (one * keep).astype(bf16)
        swap(block, slot).start()

    def turn(block, slot):
        swap(block, slot).wait_recv()
        for h in range(3):
            for side in range(2):
                keys[h, block, side * tokens : (side + 1) * tokens, :] = kv_all[h, block, side, 0].T

    def pair(block, other, last):
        tiles = [(h, side) for h in range(3) for side in range(2)]
        total = [totals[h, block] for h in range(3)]
        blend = [mix_all[h, block] for h in range(3)]
        scored, weights = {}, {}
        for step in range(len(tiles) + 2):
            if step < len(tiles):
                h, side = tiles[step]
                at = pl.ds(side * tokens, tokens)
                scored[step] = matmul(keys[h, other, at, :], q_all[h, block])
            if 0 <= step - 1 < len(tiles):
                h, side = tiles[step - 1]
                scores = scored.pop(step - 1)
                _, signed, terms = signed_terms(scores)
                if last:
                    key_pos = lax.broadcasted_iota(jnp.int32, scores.shape, 0)
                    query_pos = lax.broadcasted_iota(jnp.int32, scores.shape, 1)
                    seen = key_pos + side * tokens <= query_pos + core * tokens
                    terms = jnp.where(seen, terms, 0.0)
                total[h] = total[h] + jnp.sum(terms.reshape(tokens // 8, 8, tokens), axis=0)
                weights[step - 1] = (signed * terms).astype(bf16)
            if step - 2 >= 0:
                h, side = tiles[step - 2]
                blend[h] = blend[h] + matmul(kv_all[h, other, side, 1], weights.pop(step - 2))
        for h in range(3):
            totals[h, block], mix_all[h, block] = total[h], blend[h]

    def back(block):
        return pltpu.make_async_remote_copy(
            src_ref=leaving.at[block, pl.ds(0, 3)], dst_ref=mixed.at[pl.ds(3 * zed, 3)],
            send_sem=back_send.at[block], recv_sem=back_recv.at[zed],
            device_id=(grp, block * 2 + core), device_id_type=MESH,
        )

    def complete(block):
        fine = valid_columns(span, (2 * block + core) * tokens, tokens)
        for h in range(3):
            total = jnp.sum(totals[h, block], axis=0, keepdims=True) - extra
            total = jnp.where(fine, total, 1.0)
            blend = mix_all[h, block] / total
            mix_all[h, block] = blend
            tot_all[h, block] = total
            _, _, v, _, _, terms, weight = alone_terms(raw.at[block, pl.ds(3 * h, 3)])
            leaving[block, h] = jnp.where(fine, blend, weight * v / terms).astype(bf16)

        @pl.when(block != zed)
        def _():
            back(block).start()

        @pl.when(block == zed)
        def _():
            mixed[pl.ds(3 * zed, 3)] = leaving[zed, 0:3]

    project(zed, 0)
    turn(zed, 0)
    pair(zed, zed, True)

    @pl.when(zed == 0)
    def _():
        complete(0)

    def step(d, _):
        low, high = zed - d, zed + d
        for side, block in ((0, low), (1, high)):

            @pl.when((block >= 0) & (block < 4))
            def _():
                towards = 1 - 2 * side
                pltpu.make_async_remote_copy(
                    src_ref=norm_all.at[block], dst_ref=norm_all.at[block],
                    send_sem=hop_send.at[side, d - 1], recv_sem=hop_recv.at[side, d - 1],
                    device_id=(grp, (zed - towards) * 2 + core), device_id_type=MESH,
                ).wait_recv()
                runs, copy = hop(d, side)
                pl.when(runs)(copy.start)
                project(block, 2 * d + side)

        @pl.when(high < 4)
        def _():
            lax.fori_loop(jnp.maximum(low + 1, 0), high, lambda j, _: (pair(high, j, False), 0)[1], 0)
            turn(high, 2 * d + 1)
            pair(high, high, True)

        @pl.when(low >= 0)
        def _():
            turn(low, 2 * d)
            pair(low, low, True)

            @pl.when(high < 4)
            def _():
                pair(high, low, False)

            pl.when(low == 0)(lambda: complete(low))

            def later(i, _):
                pair(i, low, False)
                pl.when(low == 0)(lambda: complete(i))
                return 0

            lax.fori_loop(low + 1, jnp.minimum(high, 4), later, 0)

        @pl.when((high < 4) & (low <= 0))
        def _():
            complete(high)

        return 0

    lax.fori_loop(1, 4, step, 0)

    for k in (1, 2, 3):
        back(along[k]).wait_send()
        pltpu.make_async_remote_copy(
            src_ref=leaving.at[zed, pl.ds(0, 3)], dst_ref=mixed.at[pl.ds(3 * along[k], 3)],
            send_sem=back_send.at[zed], recv_sem=back_recv.at[along[k]],
            device_id=(grp, along[k] * 2 + core), device_id_type=MESH,
        ).wait_recv()
    for d in range(4):
        for side in range(2):
            runs, copy = hop(d, side)
            pl.when(runs)(copy.wait_send)
            if d > 0 or side == 0:
                block = zed + (2 * side - 1) * d
                pl.when((block >= 0) & (block < 4))(swap(block, 2 * d + side).wait_send)


def gelu_and_slope(u):
    root = 0.7978845608028654
    square = u * u
    bent = jnp.tanh(root * (u + 0.044715 * (square * u)))
    half = 0.5 * (1.0 + bent)
    slope = half + 0.5 * u * (1.0 - bent * bent) * (root * (1.0 + 0.134145 * square))
    return u * half, slope


def normal_parts(vector):
    centered = vector - jnp.mean(vector, axis=-1, keepdims=True)
    variance = jnp.mean(centered * centered, axis=-1, keepdims=True)
    inverse = lax.rsqrt(variance + epsilon)
    return centered * inverse, inverse


def norm_pull(normal, inverse, gain, grad):
    scaled = grad * gain
    along_normal = jnp.mean(scaled * normal, axis=-1, keepdims=True)
    return inverse * (scaled - jnp.mean(scaled, axis=-1, keepdims=True) - normal * along_normal)


def add_rows(into, base, count, *terms):
    chunk = 96 if count % 96 == 0 else 48

    def add(i, _):
        total = None
        for ref, start in terms:
            term = ref[rows_of(start + i * chunk, chunk), :].astype(jnp.float32)
            total = term if total is None else total + term
        into[rows_of(base + i * chunk, chunk), :] = total.astype(jnp.bfloat16)
        return 0

    lax.fori_loop(0, count // chunk, add, 0)


class GroupSum:
    whole = False

    def __init__(self, term, first, near, held, third, mine, out):
        self.term, self.first, self.near, self.held = term, first, near, held
        self.third, self.line_sum, self.out = third, mine, out
        self.rows, self.columns = term.shape[0] // 4, term.shape[1] // 2
        grp, seq, zed, core, sibling, along = place()
        self.place_in_plane(grp, seq)
        self.sibling, self.zed, self.core, self.along = sibling, zed, core, along
        self.line_targets = [(grp, along[n] * 2 + core) for n in (1, 2, 3)]
        self.halves = []
        self.mine = term.at[:, pl.ds(pl.multiple_of(core * self.columns, 128), self.columns)]
        self.away = pl.ds(pl.multiple_of((1 - core) * self.columns, 128), self.columns)
        self.copies = []

    def place_in_plane(self, grp, seq):
        y, x = grp // 2, grp % 2
        self.own, self.beside, self.above = grp, y * 2 + 1 - x, (1 - y) * 2 + x
        self.across = (1 - y) * 2 + 1 - x
        self.to_x, self.to_y = (self.beside, seq), (self.above, seq)

    def swap_quarter(self, send, quarter):
        at = rows_of(quarter * self.rows, self.rows)
        return send(self.term.at[at, self.away], self.first.at[at, :], self.sibling)

    def swap(self, send):
        for quarter in (self.across, self.beside, self.above, self.own):
            self.halves.append(self.swap_quarter(send, quarter))

    def part(self, quarter, half):
        return rows_of(quarter * self.rows + half * (self.rows // 2), self.rows // 2)

    def pass_on(self, send, quarter, half, slot, target):
        self.copies.append(
            send(self.first.at[self.part(quarter, half), :], self.near.at[slot], target)
        )

    def core_sum(self, quarter):
        base = quarter * self.rows
        add_rows(self.first, base, self.rows, (self.mine, base), (self.first, base))

    def step_one(self, send):
        steps = (
            (self.across, ((0, 0, self.to_x), (1, 2, self.to_y))),
            (self.beside, ((0, 1, self.to_x),)),
            (self.above, ((1, 3, self.to_y),)),
        )
        for i, (quarter, passes) in enumerate(steps):
            for copy in self.halves if self.whole else self.halves[i : i + 1]:
                if not self.whole or i == 0:
                    copy.wait_recv()
            self.core_sum(quarter)
            for half, slot, target in passes:
                self.pass_on(send, quarter, half, slot, target)
        self.copies = [self.copies[i] for i in (0, 2, 1, 3)]

    def step_two(self, send):
        half = self.rows // 2
        for slot, quarter, side, target in (
            (0, self.above, 0, self.to_y),
            (2, self.beside, 1, self.to_x),
        ):
            base = quarter * self.rows + side * half
            self.copies[slot].wait_recv()
            add_rows(self.first, base, half, (self.first, base), (self.near.at[slot], 0))
            self.pass_on(send, quarter, side, 4 + side, target)

    def total(self):
        half = self.rows // 2
        if not self.whole:
            self.halves[3].wait_recv()
        for slot in (1, 3, 4, 5):
            self.copies[slot].wait_recv()
        for side, one, two in ((0, 1, 4), (1, 3, 5)):
            base = self.own * self.rows + side * half
            add_rows(
                self.held, side * half, half, (self.mine, base), (self.first, base),
                (self.near.at[one], 0), (self.near.at[two], 0),
            )

    def along_line(self, send):
        self.total()
        rows = self.held.shape[0] // 4
        self.line = [
            send(self.held.at[rows_of(self.along[n] * rows, rows), :], self.third.at[n - 1], target)
            for n, target in zip((1, 2, 3), self.line_targets)
        ]

    def settle(self, send):
        rows = self.held.shape[0] // 4
        for copy in self.line:
            copy.wait_recv()
        total = self.held[rows_of(self.zed * rows, rows), :].astype(jnp.float32)
        for j in range(3):
            total = total + self.third[j].astype(jnp.float32)
        self.line_sum[...] = total
        column = pl.ds(pl.multiple_of(self.core * self.columns, 128), self.columns)
        half = rows // 2
        away = pl.ds(pl.multiple_of((1 - self.core) * half, 8), half)
        self.out[:, column] = self.line_sum[pl.ds(pl.multiple_of(self.core * half, 8), half), :]
        self.last = send(self.line_sum.at[away, :], self.out.at[:, column], self.sibling)

    def drain(self):
        for copy in self.halves + self.copies + self.line:
            copy.wait_send()
        self.last.wait()


class HeadsSum(GroupSum):
    def __init__(self, term, other, first, near, final):
        self.term, self.other, self.first, self.near, self.final = term, other, first, near, final
        self.rows = 4 * term.shape[2]
        grp, seq, zed, self.core, self.sibling, along = place()
        self.place_in_plane(grp, seq)
        self.copies, self.halves = [], []

    def swap_quarter(self, send, quarter):
        at = pl.ds(4 * quarter, 4)
        return send(self.term.at[at, 1 - self.core], self.other.at[at], self.sibling)

    def both_cores(self, quarter):
        at = pl.ds(4 * quarter, 4)
        return (self.term[at, self.core] + self.other[at]).reshape(self.rows, -1)

    def core_sum(self, quarter):
        self.first[rows_of(quarter * self.rows, self.rows), :] = self.both_cores(quarter).astype(
            jnp.bfloat16
        )

    def total(self):
        self.halves[3].wait_recv()
        for slot in (1, 3, 4, 5):
            self.copies[slot].wait_recv()
        near = [self.near[i].astype(jnp.float32) for i in range(6)]
        total = self.both_cores(self.own) + jnp.concatenate(
            [near[1] + near[4], near[3] + near[5]], axis=0
        )
        self.final[...] = total.reshape(self.final.shape)

    def drain(self):
        for copy in self.halves + self.copies:
            copy.wait_send()


def norm_back(x, gain, grad_norm, grad_out, into, chunk):
    f32 = jnp.float32
    tokens, width = x.shape
    gain_row = gain[...].reshape(1, width)

    def one(i, sums):
        at = rows_of(i * chunk, chunk)
        vector, grad = x[at, :].astype(f32), grad_norm[at, :]
        normal, inverse = normal_parts(vector)
        pulled = norm_pull(normal, inverse, gain_row, grad)
        into[at, :] = (grad_out[at, :] + pulled).astype(into.dtype)
        return (
            sums[0] + jnp.sum(grad * normal, axis=0, keepdims=True),
            sums[1] + jnp.sum(grad, axis=0, keepdims=True),
        )

    zero = jnp.zeros((1, width), f32)
    return lax.fori_loop(0, tokens // chunk, one, (zero, zero))


def settle_small(small, vecs, rms, owner):
    width, count = small.shape[-1], vecs.shape[-1]
    total = (small[0] + small[1]) + (small[2] + small[3])
    turned = pltpu.roll(total, (width - owner * count) % width, 1)
    for i in range(4):
        vecs[i] = turned[i : i + 1, :count]
    rms[...] = jnp.sqrt(total[4:5, :3] / total[4:5, 3:4])


def layer_kernel(
    x_in, out_grad_in, w_qkv_in, w_out_in, w_up_in, w_down_in,
    gain_one, bias_one, gain_two, bias_two, span,
    block_output, input_grad, sum_qkv, vecs, rms, out_down, out_up, out_out,
    x, out_grad, w_qkv, w_out, w_up, w_down,
    mixed, q_all, kv_all, raw, mix_all, tot_all, norm_all, weights, totals,
    term_out, middle, normed, normed_t, mlp_out, grad_norm, grad_middle, gmix,
    first, near, held, third, mine, first_down, near_down, held_down, third_down, mine_down,
    gm_in, turned, g_all, gt_all, grad_kv, part_out, part_in, leaving, arrived,
    term, other, first_qkv, near_qkv, final, gathered, grad_query, small_a, small_b, small_c,
    load_sems, send_sems, recv_sems,
    hop_send, hop_recv, swap_send, swap_recv, back_send, back_recv,
):
    tokens, width = x.shape
    f32, bf16 = jnp.float32, jnp.bfloat16
    grp, seq, zed, core, sibling, along = place()
    line = [(grp, along[k] * 2 + core) for k in (1, 2, 3)]
    chunks = w_up.shape[1] // width

    loads = {}

    def load(name, source, target):
        loads[name] = pltpu.make_async_copy(source, target, load_sems.at[len(loads)])
        loads[name].start()

    load("x", x_in, x)
    load("w_qkv", w_qkv_in, w_qkv)
    load("w_out", w_out_in, w_out)
    load("out_grad", out_grad_in, out_grad)
    for i in range(chunks):
        at = pl.ds(i * width, width)
        load(("up", i), w_up_in.at[:, at], w_up.at[:, at])
        load(("down", i), w_down_in.at[at, :], w_down.at[at, :])

    ups = [
        GroupSum(
            w_up.at[:, pl.ds(i * width, width)], first.at[i], near.at[i], held.at[i], third.at[i],
            mine.at[i], out_up.at[:, pl.ds(i * width, width)],
        )
        for i in range(chunks)
    ]
    outs = GroupSum(
        term_out, first.at[chunks], near.at[chunks], held.at[chunks], third.at[chunks],
        mine.at[chunks], out_out,
    )
    downs = GroupSum(w_down, first_down, near_down, held_down, third_down, mine_down, out_down)
    downs.whole = True
    heads_sum = HeadsSum(term, other, first_qkv, near_qkv, final)
    across = [(k, seq) for k in (heads_sum.beside, heads_sum.above, heads_sum.across)]
    around = [(k, zed * 2 + 1 - core) for k in (heads_sum.beside, heads_sum.above, heads_sum.across)]
    partners = [sibling] + line + across + around
    greet_start(partners)
    send = sender(send_sems, recv_sems)
    attend_part(
        x, gain_one, bias_one, w_qkv, span, mixed, q_all, kv_all, raw, mix_all, tot_all, norm_all,
        weights, turned, totals, leaving, hop_send, hop_recv, swap_send, swap_recv, back_send,
        back_recv, loads, functools.partial(greet_end, partners),
    )

    pos = seq * tokens + lax.broadcasted_iota(jnp.int32, (tokens, 1), 0)
    keep = ((pos >= span[0, 0]) & (pos < span[0, 1])).astype(f32)
    gain_row, bias_row = gain_two[...].reshape(1, width), bias_two[...].reshape(1, width)

    def squares(value):
        return jnp.sum(keep * value * value)

    for name in ("w_out", "out_grad"):
        loads[name].wait()
    attn_out = matmul(mixed[...].reshape(width, tokens).T, w_out[...])
    attn_squares = squares(attn_out)
    middle[...] = x[...].astype(f32) + attn_out
    normed[...] = (normal_parts(middle[...])[0] * gain_row + bias_row).astype(bf16)
    normed_t[...] = normed[...].T
    mlp_out[...] = jnp.zeros((tokens, width), f32)
    grad_norm[...] = jnp.zeros((tokens, width), f32)
    for i in range(chunks):
        at = pl.ds(i * width, width)
        loads["up", i].wait()
        loads["down", i].wait()
        activated, slope = gelu_and_slope(matmul(normed[...], w_up[:, at]))
        activated = activated.astype(bf16)
        mlp_out[...] += matmul(activated, w_down[at, :])
        grad_up = (contract_cols(out_grad[...], w_down[at, :]) * slope).astype(bf16)
        grad_norm[...] += contract_cols(grad_up, w_up[:, at])
        w_up[:, at] = matmul(normed_t[...], grad_up).astype(bf16)
        ups[i].swap(send)
        w_down[at, :] = matmul(activated.T, out_grad[...]).astype(bf16)
        downs.halves.append(downs.swap_quarter(send, i))
        if i >= 2:
            ups[i - 2].step_one(send)
    normal, inverse = normal_parts(middle[...])
    grad = grad_norm[...]
    grad_middle[...] = out_grad[...].astype(f32) + norm_pull(normal, inverse, gain_row, grad)
    grad_attn = grad_middle[...].astype(bf16)
    gmix[...] = contract_cols(w_out[...], grad_attn).astype(bf16).reshape(gmix.shape)
    coming = []
    for h in range(3):
        for k in (1, 2, 3):
            coming.append(send(gmix.at[along[k] * 3 + h], gm_in.at[h, zed], line[k - 1]))
        gm_in[h, zed] = gmix[zed * 3 + h]
    term_out[...] = matmul(mixed[...].reshape(width, tokens), grad_attn).astype(bf16)
    ups[0].step_two(send)
    ups[2].step_one(send)
    outs.swap(send)
    ups[1].step_two(send)
    ups[3].step_one(send)
    small_a[0, 2:3] = jnp.sum(grad * normal, axis=0, keepdims=True)
    small_a[0, 3:4] = jnp.sum(grad, axis=0, keepdims=True)
    output = middle[...] + mlp_out[...]
    block_output[...] = output.astype(bf16)
    lane = lax.broadcasted_iota(jnp.int32, (4, width), 1)
    row = jnp.zeros((4, width), f32)
    squared = (squares(output), attn_squares, squares(mlp_out[...]), jnp.sum(keep) * width)
    for i, value in enumerate(squared):
        row = jnp.where(lane == i, value, row)
    small_a[0, 4:8] = row


    def turn(h):
        def one(z, _):
            for side in range(2):
                at = pl.ds(side * tokens, tokens)
                turned[h % 2, z, at, :] = kv_all[h, z, side, 0].T
                turned[2 + h % 2, z, at, :] = kv_all[h, z, side, 1].T
            return 0

        lax.fori_loop(0, 4, one, 0)

    turn(0)
    ups[0].along_line(send)
    for z in range(4):
        leaving[z, 9] = jnp.zeros((HEAD_DIM, tokens), bf16)
    downs.step_one(send)

    swaps, sends = [], []

    def finish(h):
        swaps[h].wait_recv()

        def merge(z, _):
            fine = valid_columns(span, (2 * z + core) * tokens, tokens)
            q, k, v, inverse, signed, terms, weight = alone_terms(raw.at[z, pl.ds(3 * h, 3)])
            g = gm_in[h, z].astype(f32)
            total = 1.0 / terms
            grad_total = -jnp.sum(g * (weight * v), axis=0, keepdims=True) * total * total
            g = (g * total).astype(bf16).astype(f32)
            grad_weight = jnp.sum(g * v, axis=0, keepdims=True)
            slope = 1.0 + (inverse * inverse) * (inverse - 1.0)
            grad_score = terms * (grad_weight * slope + grad_total * signed)
            grad_score = grad_score.astype(bf16).astype(f32)
            alone = (grad_score * k * 0.125, grad_score * q, weight * g)
            parts = [leaving[z, 3 * h].astype(f32)]
            for part in range(2):
                parts.append(grad_kv[h, z, core, part] + part_in[h, z, part].astype(f32))
            for part in range(3):
                leaving[z, 3 * h + part] = jnp.where(fine, parts[part], alone[part]).astype(bf16)
            return 0

        lax.fori_loop(0, 4, merge, 0)
        at = pl.ds(3 * h, 3)
        for k in (1, 2, 3):
            sends.append(
                send(leaving.at[along[k], at], arrived.at[:, zed * 3 + h], line[k - 1])
            )
        for part in range(3):
            arrived[part, zed * 3 + h] = leaving[zed, 3 * h + part]

    def tile_products(h, z, z_key, side):
        at = pl.ds(side * tokens, tokens)
        scores = matmul(turned[h % 2, z_key, at, :], q_all[h, z])
        return scores, matmul(turned[2 + h % 2, z_key, at, :], g_all[z])

    def tile_grads(tile, scores, grad_weights):
        z, z_key, side = tile
        inverse, signed, terms = signed_terms(scores)
        if z == z_key:
            key_pos = lax.broadcasted_iota(jnp.int32, scores.shape, 0)
            query_pos = lax.broadcasted_iota(jnp.int32, scores.shape, 1)
            seen = key_pos + side * tokens <= query_pos + core * tokens
            terms = jnp.where(seen, terms, 0.0)
        weights = (signed * terms).astype(bf16)
        slope = 1.0 + (inverse * inverse) * (inverse - 1.0)
        grad_scores = terms * (grad_weights * slope + gt_all[z] * signed)
        return weights, grad_scores.astype(bf16)

    def tile_sums(h, z, z_key, side, weights, grad_scores):
        for part, left, right in ((0, q_all[h, z], grad_scores), (1, g_all[z], weights)):
            grad = contract_cols(left, right)
            if z == z_key:
                grad_kv[h, z_key, side, part] = grad
            else:
                grad_kv[h, z_key, side, part] += grad
        grad = matmul(kv_all[h, z_key, side, 0], grad_scores)
        if z_key == 0 and side == 0:
            grad_query[...] = grad
        else:
            grad_query[...] += grad
        if z == z_key and side == 1:
            leaving[z, 3 * h] = (grad_query[...] * 0.125).astype(bf16)

    for h in range(3):
        for copy in coming[h * 3 : h * 3 + 3]:
            copy.wait_recv()

        def prepare(z, _):
            g = gm_in[h, z].astype(f32)
            total = 1.0 / tot_all[h, z]
            g_all[z] = (g * total).astype(bf16)
            gt_all[z] = -jnp.sum(g * mix_all[h, z], axis=0, keepdims=True) * total
            return 0

        lax.fori_loop(0, 4, prepare, 0)

        tiles = [(z, z_key, side) for z in range(4) for z_key in range(z + 1) for side in range(2)]
        scored, parts = {}, {}
        for step in range(len(tiles) + 2):
            if step < len(tiles):
                scored[step] = tile_products(h, *tiles[step])
            if 0 <= step - 1 < len(tiles):
                parts[step - 1] = tile_grads(tiles[step - 1], *scored.pop(step - 1))
            if step - 2 >= 0:
                tile_sums(h, *tiles[step - 2], *parts.pop(step - 2))

        def pack(z, _):
            for part in range(2):
                part_out[h, z, part] = grad_kv[h, z, 1 - core, part].astype(bf16)
            return 0

        lax.fori_loop(0, 4, pack, 0)
        swaps.append(send(part_out.at[h], part_in.at[h], sibling))
        if h == 0:
            turn(1)
            ups[1].along_line(send)
            outs.step_one(send)
        if h == 1:
            turn(2)
            ups[2].step_two(send)
            ups[3].step_two(send)
        finish(h)

    for quarter in (heads_sum.across, heads_sum.beside, heads_sum.above, heads_sum.own):
        total = None
        for z in range(4):
            rows = norm_all[z, rows_of(quarter * (width // 4), width // 4), :]
            part = contract_cols(rows, leaving[z].reshape(10 * HEAD_DIM, tokens))
            total = part if total is None else total + part
        term[pl.ds(4 * quarter, 4)] = total.reshape((4,) + term.shape[1:])
        heads_sum.halves.append(heads_sum.swap_quarter(send, quarter))
    ups[2].along_line(send)
    heads_sum.step_one(send)
    downs.step_two(send)
    outs.step_two(send)
    ups[3].along_line(send)
    heads_sum.step_two(send)
    downs.along_line(send)
    outs.along_line(send)

    for copy in sends:
        copy.wait_recv()
    grads = arrived[...].reshape(3 * width, tokens)
    for i in range(width // 256):
        columns = slice(i * 256, (i + 1) * 256)
        grad_norm[:, columns] = matmul(w_qkv[columns, :], grads).T
    gain_grad, bias_grad = norm_back(x, gain_one, grad_norm, grad_middle, input_grad, 64)
    small_a[0, 0:1] = gain_grad
    small_a[0, 1:2] = bias_grad
    whose = 2 * grp + core
    small_b[pl.ds(whose, 1)] = small_a[0:1]
    planes = [
        send(small_b.at[whose], small_b.at[whose], target)
        for target in [sibling] + across + around
    ]
    heads_sum.total()
    gathered[pl.ds(zed, 1)] = final[pl.ds(zed, 1)]
    blocks = [send(final.at[along[k]], gathered.at[zed], line[k - 1]) for k in (1, 2, 3)]
    for copy in planes:
        copy.wait_recv()
    total = small_b[0]
    for i in range(1, 8):
        total = total + small_b[i]
    small_c[pl.ds(zed, 1)] = total.reshape(1, 8, width)
    columns = [send(small_c.at[zed], small_c.at[zed], line[k - 1]) for k in (1, 2, 3)]
    sums = ups + [downs, outs]
    for each in sums:
        each.settle(send)
    for copy in blocks + columns:
        copy.wait_recv()
    for z in range(4):
        for h in range(3):
            for part in range(3):
                start = part * width + (3 * z + h) * HEAD_DIM
                sum_qkv[:, start : start + HEAD_DIM] = gathered[
                    z, :, (3 * h + part) * HEAD_DIM : (3 * h + part + 1) * HEAD_DIM
                ]
    settle_small(small_c, vecs, rms, grp * 8 + seq)
    for copy in coming + swaps + sends + planes + blocks + columns:
        copy.wait_send()
    for each in sums + [heads_sum]:
        each.drain()


def layer(block_input, out_grad, w_qkv, w_out, w_up, w_down, vectors, span):
    f32, bf16 = jnp.float32, jnp.bfloat16
    tokens, width = block_input.shape
    hidden = w_up.shape[1]
    count = hidden // width + 1
    vmem, smem = pl.BlockSpec(memory_space=pltpu.VMEM), pl.BlockSpec(memory_space=pltpu.SMEM)
    block = (HEAD_DIM, tokens)
    own_rows, columns = width // 32, 10 * HEAD_DIM
    quarter, half = width // 4, width // 2
    copies = 14 * (count + 1) + 9 + 3 + 9 + 10 + 7 + 3 + 3
    dma = pltpu.SemaphoreType.DMA
    in_hbm = [block_input, out_grad, w_qkv, w_out, w_up, w_down]

    def sum_scratch(lead, rows):
        return [
            pltpu.VMEM(lead + (4 * rows, half), bf16),
            pltpu.VMEM(lead + (6, rows // 2, half), bf16),
            pltpu.VMEM(lead + (rows, half), bf16),
            pltpu.VMEM(lead + (3, rows // 4, half), bf16),
            pltpu.VMEM(lead + (rows // 4, half), f32),
        ]

    return pl.pallas_call(
        layer_kernel,
        out_shape=[
            jax.ShapeDtypeStruct((tokens, width), bf16),
            jax.ShapeDtypeStruct((tokens, width), bf16),
            jax.ShapeDtypeStruct((own_rows, 3 * width), f32),
            jax.ShapeDtypeStruct((4, 1, own_rows), f32),
            jax.ShapeDtypeStruct((1, 3), f32),
            jax.ShapeDtypeStruct((hidden // 32, width), f32),
            jax.ShapeDtypeStruct((own_rows, hidden), f32),
            jax.ShapeDtypeStruct((own_rows, width), f32),
        ],
        in_specs=[pl.BlockSpec(memory_space=pl.ANY)] * len(in_hbm) + [vmem] * 4 + [smem],
        out_specs=[vmem] * 8,
        scratch_shapes=[pltpu.VMEM(a.shape, a.dtype) for a in in_hbm]
        + [
            pltpu.VMEM((HEADS,) + block, bf16),
            pltpu.VMEM((3, 4) + block, bf16),
            pltpu.VMEM((3, 4, 2, 2) + block, bf16),
            pltpu.VMEM((4, 9) + block, bf16),
            pltpu.VMEM((3, 4) + block, f32),
            pltpu.VMEM((3, 4, 1, tokens), f32),
            pltpu.VMEM((4, width, tokens), bf16),
            pltpu.VMEM((3, 256, width), bf16),
            pltpu.VMEM((3, 4, 8, tokens), f32),
            pltpu.VMEM((width, width), bf16),
            pltpu.VMEM((tokens, width), f32),
            pltpu.VMEM((tokens, width), bf16),
            pltpu.VMEM((width, tokens), bf16),
            pltpu.VMEM((tokens, width), f32),
            pltpu.VMEM((tokens, width), f32),
            pltpu.VMEM((tokens, width), f32),
            pltpu.VMEM((HEADS,) + block, bf16),
        ]
        + sum_scratch((count,), quarter)
        + sum_scratch((), hidden // 4)
        + [
            pltpu.VMEM((3, 4) + block, bf16),
            pltpu.VMEM((4, 4, 2 * tokens, HEAD_DIM), bf16),
            pltpu.VMEM((4,) + block, bf16),
            pltpu.VMEM((4, 1, tokens), f32),
            pltpu.VMEM((3, 4, 2, 2) + block, f32),
            pltpu.VMEM((3, 4, 2) + block, bf16),
            pltpu.VMEM((3, 4, 2) + block, bf16),
            pltpu.VMEM((4, 10) + block, bf16),
            pltpu.VMEM((3, HEADS) + block, bf16),
            pltpu.VMEM((16, 2, own_rows, columns), f32),
            pltpu.VMEM((16, own_rows, columns), f32),
            pltpu.VMEM((16 * own_rows, columns), bf16),
            pltpu.VMEM((6, 2 * own_rows, columns), bf16),
            pltpu.VMEM((4, own_rows, columns), f32),
            pltpu.VMEM((4, own_rows, columns), f32),
            pltpu.VMEM(block, f32),
            pltpu.VMEM((1, 8, width), f32),
            pltpu.VMEM((8, 8, width), f32),
            pltpu.VMEM((4, 8, width), f32),
            dma((4 + 2 * (count - 1),)),
            dma((copies,)),
            dma((copies,)),
            dma((2, 4)),
            dma((2, 4)),
            dma((8,)),
            dma((8,)),
            dma((4,)),
            dma((4,)),
        ],
        compiler_params=pltpu.CompilerParams(
            collective_id=0, has_side_effects=True, vmem_limit_bytes=63 * 2**20
        ),
    )(*in_hbm, *vectors, span)


def hand_over_kernel(many, *refs):
    vecs, rms, arrays = refs[0], refs[1], refs[2 : 2 + many]
    outs, rest = refs[2 + many : 7 + 2 * many], refs[7 + 2 * many :]
    held, sems = rest[:many], rest[many]
    loads = [
        pltpu.make_async_copy(arrays[i], held[i], sems.at[0, i]) for i in range(many)
    ]
    stores = [
        pltpu.make_async_copy(held[i], outs[5 + i], sems.at[1, i]) for i in range(many)
    ]
    for load in loads:
        load.start()
    for i in range(4):
        outs[i][...] = vecs[i, 0]
    outs[4][...] = rms[0]
    for load, store in zip(loads, stores):
        load.wait()
        store.start()
    for store in stores:
        store.wait()


def hand_over(vecs, rms, arrays):
    vmem, hbm = pl.BlockSpec(memory_space=pltpu.VMEM), pl.BlockSpec(memory_space=pl.ANY)
    many, f32 = len(arrays), jnp.float32
    return pl.pallas_call(
        functools.partial(hand_over_kernel, many),
        out_shape=[jax.ShapeDtypeStruct(vecs.shape[2:], f32)] * 4
        + [jax.ShapeDtypeStruct(rms.shape[1:], f32)]
        + [jax.ShapeDtypeStruct(a.shape, a.dtype) for a in arrays],
        in_specs=[vmem] * 2 + [hbm] * many,
        out_specs=[vmem] * 5 + [hbm] * many,
        scratch_shapes=[pltpu.VMEM(a.shape, a.dtype) for a in arrays]
        + [pltpu.SemaphoreType.DMA((2, many))],
    )(vecs, rms, *arrays)


def per_device_planned(
    block_input,
    out_grad,
    seq_span,
    ln1_gain,
    ln1_bias,
    w_qkv,
    w_out,
    ln2_gain,
    ln2_bias,
    w_up,
    w_down,
):
    block_output, input_grad, sum_qkv, vecs, rms, sum_down, sum_up, sum_out = layer(
        block_input, out_grad, w_qkv, w_out, w_up, w_down,
        (ln1_gain, ln1_bias, ln2_gain, ln2_bias), seq_span,
    )
    arrays = (block_output, input_grad, sum_qkv, sum_out, sum_up, sum_down)
    gain_one, bias_one, gain_two, bias_two, rms, *arrays = hand_over(vecs, rms, arrays)
    block_output, input_grad, sum_qkv, sum_out, sum_up, sum_down = arrays
    return (
        block_output,
        input_grad,
        gain_one,
        bias_one,
        sum_qkv,
        sum_out,
        gain_two,
        bias_two,
        sum_up,
        sum_down,
        rms,
    )


def solution(mesh):
    placed = (
        P(("grp", "seq"), None),
        P(("grp", "seq"), None),
        P("grp", None),
        P(),
        P(),
        P(),
        P(),
        P(),
        P(),
        P(),
        P(),
    )
    planned = mesh.shape["grp"] == 4 and mesh.shape["seq"] == 8
    return jax.shard_map(
        per_device_planned if planned else per_device,
        mesh=mesh,
        in_specs=placed,
        out_specs=(
            P(("grp", "seq"), None),
            P(("grp", "seq"), None),
            P(("grp", "seq")),
            P(("grp", "seq")),
            P(("grp", "seq"), None),
            P(("grp", "seq"), None),
            P(("grp", "seq")),
            P(("grp", "seq")),
            P(("grp", "seq"), None),
            P(("grp", "seq"), None),
            P(),
        ),
        check_vma=False,
    )
```

```python
import functools

import jax
import jax.numpy as jnp
from jax import lax
from jax.experimental import pallas as pl
from jax.experimental.pallas import tpu as pltpu
from jax.sharding import PartitionSpec as P

D = 768
HEADS = 12
HEAD_DIM = 64
MESH = pl.DeviceIdType.MESH


epsilon = 1e-05


def passed_along(array, axis, by):
    devices = lax.axis_size(axis)
    pairs = [(i, i + by) for i in range(devices) if 0 <= i + by < devices]
    return lax.ppermute(array, axis, pairs)


def shifted(array, axis, by):
    devices = lax.axis_size(axis)
    return lax.ppermute(array, axis, [(i, (i + by) % devices) for i in range(devices)])


def layer_norm(vector, scale_vec, shift_vec):
    row_mean = jnp.mean(vector, axis=-1, keepdims=True)
    centered = vector - row_mean
    variance = jnp.mean(centered * centered, axis=-1, keepdims=True)
    return centered * lax.rsqrt(variance + epsilon) * scale_vec + shift_vec


def contract_rows(left, right):
    return lax.dot_general(
        left, right, (((0,), (0,)), ((), ())), preferred_element_type=jnp.float32
    )


def contract_cols(left, right):
    return lax.dot_general(
        left, right, (((1,), (1,)), ((), ())), preferred_element_type=jnp.float32
    )


def score_terms(queries, key_block, query_pos, key_pos, seq_first, seq_limit):
    scores = (
        jnp.einsum("qhd,khd->qhk", queries, key_block, preferred_element_type=jnp.float32) * 0.125
    )
    query_valid = (query_pos >= seq_first) & (query_pos < seq_limit)
    key_valid = (key_pos >= seq_first) & (key_pos < seq_limit)
    allowed = (key_pos[None, :] <= query_pos[:, None]) & (
        query_valid[:, None] & key_valid[None, :] | (key_pos[None, :] == query_pos[:, None])
    )
    magnitude = jnp.sqrt(scores * scores + 1.0)
    signed_part = scores / magnitude
    exp_terms = jnp.where(allowed[:, None, :], jnp.exp(magnitude), 0.0)
    return (magnitude, signed_part, exp_terms)


def split_pair(kv_pair):
    count_rows = kv_pair.shape[0]
    key_block = kv_pair[:, :D].reshape(count_rows, HEADS, HEAD_DIM)
    value_block = kv_pair[:, D:].reshape(count_rows, HEADS, HEAD_DIM)
    return (key_block, value_block)


def forward_block(running, kv_pair, key_start, queries, query_pos, seq_first, seq_limit):
    totals, unnorm = running
    key_block, value_block = split_pair(kv_pair)
    key_pos = key_start + jnp.arange(kv_pair.shape[0], dtype=jnp.int32)
    magnitude, signed_part, exp_terms = score_terms(
        queries, key_block, query_pos, key_pos, seq_first, seq_limit
    )
    weights = (signed_part * exp_terms).astype(jnp.bfloat16)
    totals = totals + jnp.sum(exp_terms, axis=-1)
    unnorm = unnorm + jnp.einsum(
        "qhk,khd->qhd", weights, value_block, preferred_element_type=jnp.float32
    )
    return (totals, unnorm)


def grad_core(
    kv_pair, key_start, queries, query_pos, seq_first, seq_limit, grad_unnorm, grad_totals
):
    key_block, value_block = split_pair(kv_pair)
    key_pos = key_start + jnp.arange(kv_pair.shape[0], dtype=jnp.int32)
    magnitude, signed_part, exp_terms = score_terms(
        queries, key_block, query_pos, key_pos, seq_first, seq_limit
    )
    weights = (signed_part * exp_terms).astype(jnp.bfloat16)
    grad_weights = jnp.einsum(
        "qhd,khd->qhk", grad_unnorm, value_block, preferred_element_type=jnp.float32
    )
    grad_scores = (
        grad_weights * exp_terms / (magnitude * magnitude * magnitude)
        + (grad_weights * signed_part + grad_totals[:, :, None]) * exp_terms * signed_part
    )
    return (key_block, weights, grad_scores.astype(jnp.bfloat16))


def backward_block(
    kv_pair, key_start, queries, query_pos, seq_first, seq_limit, grad_unnorm, grad_totals
):
    key_block, weights, grad_scores = grad_core(
        kv_pair, key_start, queries, query_pos, seq_first, seq_limit, grad_unnorm, grad_totals
    )
    count_rows = kv_pair.shape[0]
    grad_query = (
        jnp.einsum("qhk,khd->qhd", grad_scores, key_block, preferred_element_type=jnp.float32)
        * 0.125
    )
    grad_key = (
        jnp.einsum("qhk,qhd->khd", grad_scores, queries, preferred_element_type=jnp.float32) * 0.125
    )
    grad_value = jnp.einsum(
        "qhk,qhd->khd", weights, grad_unnorm, preferred_element_type=jnp.float32
    )
    grad_pair = jnp.concatenate(
        [grad_key.reshape(count_rows, D), grad_value.reshape(count_rows, D)], axis=1
    )
    return (grad_query, grad_pair)


def per_device(
    block_input,
    out_grad,
    seq_span,
    ln1_gain,
    ln1_bias,
    w_qkv,
    w_out,
    ln2_gain,
    ln2_bias,
    w_up,
    w_down,
):
    tok_rows = block_input.shape[0]
    feat_width = block_input.shape[1]
    seq_count = lax.axis_size("seq")
    seq_index = lax.axis_index("seq")
    query_pos = seq_index * tok_rows + jnp.arange(tok_rows, dtype=jnp.int32)
    query_last = query_pos[tok_rows - 1]
    seq_first = seq_span[0, 0]
    seq_limit = seq_span[0, 1]
    inputs = block_input.astype(jnp.float32)
    normed = layer_norm(inputs, ln1_gain, ln1_bias).astype(jnp.bfloat16)
    proj_qkv = jnp.dot(normed, w_qkv, preferred_element_type=jnp.float32).astype(jnp.bfloat16)
    queries = proj_qkv[:, :feat_width].reshape(tok_rows, HEADS, HEAD_DIM)
    kv_pair = proj_qkv[:, feat_width:]

    def visit_block(running, shard_rows, key_start):
        return lax.cond(
            key_start <= query_last,
            lambda state_in: forward_block(
                state_in, shard_rows, key_start, queries, query_pos, seq_first, seq_limit
            ),
            lambda state_in: state_in,
            running,
        )

    empty = (
        jnp.zeros((tok_rows, HEADS), jnp.float32),
        jnp.zeros((tok_rows, HEADS, HEAD_DIM), jnp.float32),
    )
    first_state = visit_block(empty, kv_pair, seq_index * tok_rows)

    def forward_hop(hop_count, loop_state):
        moving, running = loop_state
        moving = passed_along(moving, "seq", 1)
        source = (seq_index - hop_count) % seq_count
        return (moving, visit_block(running, moving, source * tok_rows))

    _, (totals, unnorm) = lax.fori_loop(1, seq_count, forward_hop, (kv_pair, first_state))
    mixed_heads = (unnorm / totals[:, :, None]).reshape(tok_rows, feat_width).astype(jnp.bfloat16)
    attn_out = jnp.dot(mixed_heads, w_out, preferred_element_type=jnp.float32)
    middle = inputs + attn_out
    normed_two = layer_norm(middle, ln2_gain, ln2_bias).astype(jnp.bfloat16)
    up_proj = jnp.dot(normed_two, w_up, preferred_element_type=jnp.float32)
    activated = jax.nn.gelu(up_proj, approximate=True).astype(jnp.bfloat16)
    mlp_out = jnp.dot(activated, w_down, preferred_element_type=jnp.float32)
    output = middle + mlp_out
    valid_rows = ((query_pos >= seq_first) & (query_pos < seq_limit)).astype(jnp.float32)[:, None]
    rms_parts = lax.psum(
        (
            jnp.sum(valid_rows * output * output),
            jnp.sum(valid_rows * attn_out * attn_out),
            jnp.sum(valid_rows * mlp_out * mlp_out),
            jnp.sum(valid_rows) * feat_width,
        ),
        ("grp", "seq"),
    )
    rms_stats = jnp.sqrt(jnp.stack([rms_parts[0], rms_parts[1], rms_parts[2]]) / rms_parts[3])
    grad_w_down = contract_rows(activated, out_grad)
    grad_activated = contract_cols(out_grad, w_down)
    _, gelu_pull = jax.vjp(lambda pre_act: jax.nn.gelu(pre_act, approximate=True), up_proj)
    grad_up = gelu_pull(grad_activated)[0].astype(jnp.bfloat16)
    grad_w_up = contract_rows(normed_two, grad_up)
    grad_norm_two = contract_cols(grad_up, w_up)
    _, norm_pull_two = jax.vjp(layer_norm, middle, ln2_gain, ln2_bias)
    grad_mid_norm, grad_gain_two, grad_bias_two = norm_pull_two(grad_norm_two)
    grad_middle = out_grad.astype(jnp.float32) + grad_mid_norm
    grad_attn = grad_middle.astype(jnp.bfloat16)
    grad_w_out = contract_rows(mixed_heads, grad_attn)
    grad_mixed = contract_cols(grad_attn, w_out).reshape(tok_rows, HEADS, HEAD_DIM)
    grad_unnorm = (grad_mixed / totals[:, :, None]).astype(jnp.bfloat16)
    grad_totals = -jnp.sum(grad_mixed * unnorm, axis=-1) / (totals * totals)

    def back_block(grad_run, shard_rows, key_start):

        def compute_block(grad_in):
            grad_query, grad_pair = backward_block(
                shard_rows,
                key_start,
                queries,
                query_pos,
                seq_first,
                seq_limit,
                grad_unnorm,
                grad_totals,
            )
            return (grad_in + grad_query, grad_pair)

        def skip_block(grad_in):
            return (grad_in, jnp.zeros((shard_rows.shape[0], 2 * feat_width), jnp.float32))

        return lax.cond(key_start <= query_last, compute_block, skip_block, grad_run)

    grad_start = jnp.zeros((tok_rows, HEADS, HEAD_DIM), jnp.float32)
    grad_queries, local_terms = back_block(grad_start, kv_pair, seq_index * tok_rows)

    def backward_hop(hop_count, loop_state):
        moving, grad_acc, grad_run = loop_state
        moving = passed_along(moving, "seq", 1)
        grad_acc = shifted(grad_acc.astype(jnp.bfloat16), "seq", 1).astype(grad_acc.dtype)
        source = (seq_index - hop_count) % seq_count
        grad_run, new_terms = back_block(grad_run, moving, source * tok_rows)
        return (moving, grad_acc + new_terms, grad_run)

    _, grad_acc, grad_queries = lax.fori_loop(
        1, seq_count, backward_hop, (kv_pair, local_terms, grad_queries)
    )
    grad_kv = shifted(grad_acc.astype(jnp.bfloat16), "seq", 1).astype(grad_acc.dtype)
    grad_qkv = jnp.concatenate(
        [grad_queries.reshape(tok_rows, feat_width), grad_kv], axis=1
    ).astype(jnp.bfloat16)
    grad_w_qkv = contract_rows(normed, grad_qkv)
    grad_norm_one = contract_cols(grad_qkv, w_qkv)
    _, norm_pull_one = jax.vjp(layer_norm, inputs, ln1_gain, ln1_bias)
    grad_in_norm, grad_gain_one, grad_bias_one = norm_pull_one(grad_norm_one)
    input_grad = (grad_middle + grad_in_norm).astype(jnp.bfloat16)
    summed = (
        lax.psum_scatter(grad_gain_one, ("grp", "seq"), scatter_dimension=0, tiled=True),
        lax.psum_scatter(grad_bias_one, ("grp", "seq"), scatter_dimension=0, tiled=True),
        lax.psum_scatter(grad_w_qkv, ("grp", "seq"), scatter_dimension=0, tiled=True),
        lax.psum_scatter(grad_w_out, ("grp", "seq"), scatter_dimension=0, tiled=True),
        lax.psum_scatter(grad_gain_two, ("grp", "seq"), scatter_dimension=0, tiled=True),
        lax.psum_scatter(grad_bias_two, ("grp", "seq"), scatter_dimension=0, tiled=True),
        lax.psum_scatter(grad_w_up, ("grp", "seq"), scatter_dimension=0, tiled=True),
        lax.psum_scatter(grad_w_down, ("grp", "seq"), scatter_dimension=0, tiled=True),
    )
    return (
        output.astype(jnp.bfloat16),
        input_grad,
        summed[0],
        summed[1],
        summed[2],
        summed[3],
        summed[4],
        summed[5],
        summed[6],
        summed[7],
        rms_stats,
    )


def rows_of(start, count):
    return pl.ds(pl.multiple_of(start, 16), count)


def matmul(left, right):
    return jnp.dot(left, right, preferred_element_type=jnp.float32)


def signed_terms(scores):
    square = scores * scores + 1.0
    inverse = lax.rsqrt(square)
    return inverse, scores * inverse, jnp.exp(square * inverse)


def valid_columns(span, start, count):
    pos = start + lax.broadcasted_iota(jnp.int32, (1, count), 1)
    return (pos >= span[0, 0]) & (pos < span[0, 1])


def greet_start(partners):
    for partner in partners:
        pl.semaphore_signal(
            pltpu.get_barrier_semaphore(), inc=1, device_id=partner, device_id_type=MESH
        )


def greet_end(partners):
    pl.semaphore_wait(pltpu.get_barrier_semaphore(), len(partners))


def sender(send_sems, recv_sems):
    count = [0]

    def send(src, dst, target, only=None, arrives=None):
        slot = count[0]
        count[0] += 1
        copy = pltpu.make_async_remote_copy(
            src_ref=src, dst_ref=dst, send_sem=send_sems.at[slot],
            recv_sem=recv_sems.at[slot if arrives is None else arrives],
            device_id=target, device_id_type=MESH,
        )
        if only is None:
            copy.start()
        else:
            pl.when(only)(copy.start)
        return copy

    send.count = count
    return send


def place():
    grp, seq = lax.axis_index("grp"), lax.axis_index("seq")
    zed, core = seq // 2, seq % 2
    sibling = (grp, zed * 2 + 1 - core)
    along = [(zed + k) % 4 for k in range(4)]
    return grp, seq, zed, core, sibling, along


def alone_terms(raw):
    q, k, v = (raw[part].astype(jnp.float32) for part in range(3))
    inverse, signed, terms = signed_terms(jnp.sum(q * k, axis=0, keepdims=True))
    weight = (signed * terms).astype(jnp.bfloat16).astype(jnp.float32)
    return q, k, v, inverse, signed, terms, weight


def attend_part(
    x, gain_one, bias_one, w_qkv, span, mixed, q_all, kv_all, raw, mix_all, tot_all, norm_all,
    weights, keys, totals, leaving, hop_send, hop_recv, swap_send, swap_recv, back_send, back_recv,
    loads, greet_end,
):
    tokens, width = x.shape
    f32, bf16 = jnp.float32, jnp.bfloat16
    grp, seq, zed, core, sibling, along = place()

    start = pl.multiple_of(zed * 192 // 128 * 128, 128)
    inside = pl.ds(pl.multiple_of(zed % 2 * HEAD_DIM, HEAD_DIM), 3 * HEAD_DIM)
    loads["x"].wait()
    vector = x[...].astype(f32)
    centered = vector - jnp.mean(vector, axis=-1, keepdims=True)
    variance = jnp.mean(centered * centered, axis=-1, keepdims=True)
    normed = (
        centered * lax.rsqrt(variance + epsilon) * gain_one[...].reshape(1, width)
        + bias_one[...].reshape(1, width)
    ).astype(bf16)
    norm_all[zed] = normed.T
    greet_end()

    halves = [pl.ds(half * (width // 2), width // 2) for half in range(2)]

    def hop(step, side, half):
        towards = 1 - 2 * side
        block = zed - towards * step
        runs = (block >= 0) & (block < 4) & (zed + towards >= 0) & (zed + towards < 4)
        copy = pltpu.make_async_remote_copy(
            src_ref=norm_all.at[block, halves[half]], dst_ref=norm_all.at[block, halves[half]],
            send_sem=hop_send.at[side, step, half], recv_sem=hop_recv.at[side, step, half],
            device_id=(grp, (zed + towards) * 2 + core), device_id_type=MESH,
        )
        return runs, copy

    for half in range(2):
        for side in range(2):
            runs, copy = hop(0, side, half)
            pl.when(runs)(copy.start)
    loads["w_qkv"].wait()
    for part in range(3):
        at = pl.ds(pl.multiple_of(part * width + start, 128), 256)
        weights[part] = w_qkv[:, at].T
    no_score = signed_terms(jnp.zeros((1, tokens), f32))[2]
    extra = span[0, 0].astype(f32) * no_score
    mix_all[...] = jnp.zeros(mix_all.shape, f32)
    totals[...] = jnp.zeros(totals.shape, f32)

    def swap(block, slot):
        return pltpu.make_async_remote_copy(
            src_ref=kv_all.at[:, block, core], dst_ref=kv_all.at[:, block, core],
            send_sem=swap_send.at[slot], recv_sem=swap_recv.at[slot],
            device_id=sibling, device_id_type=MESH,
        )

    def project(block, slot):
        keep = valid_columns(span, (2 * block + core) * tokens, tokens).astype(f32)
        for part in range(3):
            heads = matmul(weights[part, inside, :], norm_all[block])
            if part == 0:
                heads = heads * 0.125
            for h in range(3):
                one = heads[h * HEAD_DIM : (h + 1) * HEAD_DIM]
                raw[block, 3 * h + part] = one.astype(bf16)
                if part == 0:
                    q_all[h, block] = (one * keep).astype(bf16)
                else:
                    kv_all[h, block, core, part - 1] = (one * keep).astype(bf16)
        swap(block, slot).start()

    def turn(block, slot):
        swap(block, slot).wait_recv()
        for h in range(3):
            for side in range(2):
                keys[h, block, side * tokens : (side + 1) * tokens, :] = kv_all[h, block, side, 0].T

    def pair(block, other, last):
        tiles = [(h, side) for h in range(3) for side in range(2)]
        total = [totals[h, block] for h in range(3)]
        blend = [mix_all[h, block] for h in range(3)]
        scored, weights = {}, {}
        for step in range(len(tiles) + 2):
            if step < len(tiles):
                h, side = tiles[step]
                at = pl.ds(side * tokens, tokens)
                scored[step] = matmul(keys[h, other, at, :], q_all[h, block])
            if 0 <= step - 1 < len(tiles):
                h, side = tiles[step - 1]
                scores = scored.pop(step - 1)
                _, signed, terms = signed_terms(scores)
                if last:
                    key_pos = lax.broadcasted_iota(jnp.int32, scores.shape, 0)
                    query_pos = lax.broadcasted_iota(jnp.int32, scores.shape, 1)
                    seen = key_pos + side * tokens <= query_pos + core * tokens
                    terms = jnp.where(seen, terms, 0.0)
                total[h] = total[h] + jnp.sum(terms.reshape(tokens // 8, 8, tokens), axis=0)
                weights[step - 1] = (signed * terms).astype(bf16)
            if step - 2 >= 0:
                h, side = tiles[step - 2]
                blend[h] = blend[h] + matmul(kv_all[h, other, side, 1], weights.pop(step - 2))
        for h in range(3):
            totals[h, block], mix_all[h, block] = total[h], blend[h]

    def back(block):
        return pltpu.make_async_remote_copy(
            src_ref=leaving.at[block, pl.ds(0, 3)], dst_ref=mixed.at[pl.ds(3 * zed, 3)],
            send_sem=back_send.at[block], recv_sem=back_recv.at[zed],
            device_id=(grp, block * 2 + core), device_id_type=MESH,
        )

    def complete(block):
        fine = valid_columns(span, (2 * block + core) * tokens, tokens)
        for h in range(3):
            total = jnp.sum(totals[h, block], axis=0, keepdims=True) - extra
            total = jnp.where(fine, total, 1.0)
            blend = mix_all[h, block] / total
            mix_all[h, block] = blend
            tot_all[h, block] = total
            _, _, v, _, _, terms, weight = alone_terms(raw.at[block, pl.ds(3 * h, 3)])
            leaving[block, h] = jnp.where(fine, blend, weight * v / terms).astype(bf16)

        @pl.when(block != zed)
        def _():
            back(block).start()

        @pl.when(block == zed)
        def _():
            mixed[pl.ds(3 * zed, 3)] = leaving[zed, 0:3]

    project(zed, 0)
    turn(zed, 0)
    pair(zed, zed, True)

    @pl.when(zed == 0)
    def _():
        complete(0)

    def step(d, _):
        low, high = zed - d, zed + d
        for half in range(2):
            for side, block in ((0, low), (1, high)):

                @pl.when((block >= 0) & (block < 4))
                def _():
                    towards = 1 - 2 * side
                    part = norm_all.at[block, halves[half]]
                    pltpu.make_async_remote_copy(
                        src_ref=part, dst_ref=part, send_sem=hop_send.at[side, d - 1, half],
                        recv_sem=hop_recv.at[side, d - 1, half],
                        device_id=(grp, (zed - towards) * 2 + core), device_id_type=MESH,
                    ).wait_recv()
                    runs, copy = hop(d, side, half)
                    pl.when(runs)(copy.start)
                    if half == 1:
                        project(block, 2 * d + side)

        @pl.when(high < 4)
        def _():
            lax.fori_loop(jnp.maximum(low + 1, 0), high, lambda j, _: (pair(high, j, False), 0)[1], 0)
            turn(high, 2 * d + 1)
            pair(high, high, True)

        @pl.when(low >= 0)
        def _():
            turn(low, 2 * d)
            pair(low, low, True)

            @pl.when(high < 4)
            def _():
                pair(high, low, False)

            pl.when(low == 0)(lambda: complete(low))

            def later(i, _):
                pair(i, low, False)
                pl.when(low == 0)(lambda: complete(i))
                return 0

            lax.fori_loop(low + 1, jnp.minimum(high, 4), later, 0)

        @pl.when((high < 4) & (low <= 0))
        def _():
            complete(high)

        return 0

    lax.fori_loop(1, 4, step, 0)

    for k in (1, 2, 3):
        back(along[k]).wait_send()
        pltpu.make_async_remote_copy(
            src_ref=leaving.at[zed, pl.ds(0, 3)], dst_ref=mixed.at[pl.ds(3 * along[k], 3)],
            send_sem=back_send.at[zed], recv_sem=back_recv.at[along[k]],
            device_id=(grp, along[k] * 2 + core), device_id_type=MESH,
        ).wait_recv()
    for d in range(4):
        for side in range(2):
            for half in range(2):
                runs, copy = hop(d, side, half)
                pl.when(runs)(copy.wait_send)
            if d > 0 or side == 0:
                block = zed + (2 * side - 1) * d
                pl.when((block >= 0) & (block < 4))(swap(block, 2 * d + side).wait_send)


def gelu_and_slope(u):
    root = 0.7978845608028654
    square = u * u
    bent = jnp.tanh(root * (u + 0.044715 * (square * u)))
    half = 0.5 * (1.0 + bent)
    slope = half + 0.5 * u * (1.0 - bent * bent) * (root * (1.0 + 0.134145 * square))
    return u * half, slope


def normal_parts(vector):
    centered = vector - jnp.mean(vector, axis=-1, keepdims=True)
    variance = jnp.mean(centered * centered, axis=-1, keepdims=True)
    inverse = lax.rsqrt(variance + epsilon)
    return centered * inverse, inverse


def norm_pull(normal, inverse, gain, grad):
    scaled = grad * gain
    along_normal = jnp.mean(scaled * normal, axis=-1, keepdims=True)
    return inverse * (scaled - jnp.mean(scaled, axis=-1, keepdims=True) - normal * along_normal)


def add_rows(into, base, count, *terms):
    chunk = 96 if count % 96 == 0 else 48

    def add(i, _):
        total = None
        for ref, start in terms:
            term = ref[rows_of(start + i * chunk, chunk), :].astype(jnp.float32)
            total = term if total is None else total + term
        into[rows_of(base + i * chunk, chunk), :] = total.astype(jnp.bfloat16)
        return 0

    lax.fori_loop(0, count // chunk, add, 0)


class GroupSum:
    whole = False

    def __init__(self, term, first, near, held, third, mine, out):
        self.term, self.first, self.near, self.held = term, first, near, held
        self.third, self.line_sum, self.out = third, mine, out
        self.rows, self.columns = term.shape[0] // 4, term.shape[1] // 2
        grp, seq, zed, core, sibling, along = place()
        self.place_in_plane(grp, seq)
        self.sibling, self.grp, self.zed, self.core = sibling, grp, zed, core
        self.halves = []
        self.mine = term.at[:, pl.ds(pl.multiple_of(core * self.columns, 128), self.columns)]
        self.away = pl.ds(pl.multiple_of((1 - core) * self.columns, 128), self.columns)
        self.copies = []

    def place_in_plane(self, grp, seq):
        y, x = grp // 2, grp % 2
        self.own, self.beside, self.above = grp, y * 2 + 1 - x, (1 - y) * 2 + x
        self.across = (1 - y) * 2 + 1 - x
        self.to_x, self.to_y = (self.beside, seq), (self.above, seq)

    def swap_quarter(self, send, quarter):
        at = rows_of(quarter * self.rows, self.rows)
        return send(self.term.at[at, self.away], self.first.at[at, :], self.sibling)

    def swap(self, send):
        for quarter in (self.across, self.beside, self.above, self.own):
            self.halves.append(self.swap_quarter(send, quarter))

    def part(self, quarter, half):
        return rows_of(quarter * self.rows + half * (self.rows // 2), self.rows // 2)

    def pass_on(self, send, quarter, half, slot, target):
        self.copies.append(
            send(self.first.at[self.part(quarter, half), :], self.near.at[slot], target)
        )

    def core_sum(self, quarter):
        base = quarter * self.rows
        add_rows(self.first, base, self.rows, (self.mine, base), (self.first, base))

    def step_one(self, send):
        steps = (
            (self.across, ((0, 0, self.to_x), (1, 2, self.to_y))),
            (self.beside, ((0, 1, self.to_x),)),
            (self.above, ((1, 3, self.to_y),)),
        )
        for i, (quarter, passes) in enumerate(steps):
            for copy in self.halves if self.whole else self.halves[i : i + 1]:
                if not self.whole or i == 0:
                    copy.wait_recv()
            self.core_sum(quarter)
            for half, slot, target in passes:
                self.pass_on(send, quarter, half, slot, target)
        self.copies = [self.copies[i] for i in (0, 2, 1, 3)]

    def step_two(self, send):
        half = self.rows // 2
        for slot, quarter, side, target in (
            (0, self.above, 0, self.to_y),
            (2, self.beside, 1, self.to_x),
        ):
            base = quarter * self.rows + side * half
            self.copies[slot].wait_recv()
            add_rows(self.first, base, half, (self.first, base), (self.near.at[slot], 0))
            self.pass_on(send, quarter, side, 4 + side, target)

    def total(self):
        half = self.rows // 2
        if not self.whole:
            self.halves[3].wait_recv()
        for slot in (1, 3, 4, 5):
            self.copies[slot].wait_recv()
        for side, one, two in ((0, 1, 4), (1, 3, 5)):
            base = self.own * self.rows + side * half
            add_rows(
                self.held, side * half, half, (self.mine, base), (self.first, base),
                (self.near.at[one], 0), (self.near.at[two], 0),
            )

    def along_line(self, send):
        self.total()
        rows = self.held.shape[0] // 4
        self.inner = (self.zed == 1) | (self.zed == 2)
        mate = self.zed + 1 - 2 * (self.zed % 2)
        self.far = (1 - self.zed // 2) * 2
        target = (self.grp, mate * 2 + self.core)
        far_rows = rows_of(self.far * rows, 2 * rows)
        self.outward = send(
            self.held.at[far_rows, :], self.third.at[pl.ds(2 * rows, 2 * rows), :], target,
            only=jnp.logical_not(self.inner),
        )
        self.beside_copy = send(
            self.held.at[rows_of(mate * rows, rows), :], self.third.at[pl.ds(0, rows), :], target
        )

    def pass_line(self, send):
        rows = self.held.shape[0] // 4

        @pl.when(self.inner)
        def _():
            self.outward.wait_recv()
            base = self.far * rows
            add_rows(
                self.third, 2 * rows, 2 * rows, (self.third, 2 * rows), (self.held, base)
            )

        self.passed = []
        arrives = send.count[0]
        for i in range(2):
            self.passed.append(
                send(
                    self.third.at[pl.ds((2 + i) * rows, rows), :],
                    self.third.at[pl.ds(rows, rows), :],
                    (self.grp, (self.far + i) * 2 + self.core),
                    only=self.inner,
                    arrives=arrives,
                )
            )

    def settle(self, send):
        rows = self.held.shape[0] // 4
        self.beside_copy.wait_recv()
        self.passed[0].wait_recv()
        total = self.held[rows_of(self.zed * rows, rows), :].astype(jnp.float32)
        for j in range(2):
            total = total + self.third[j * rows : (j + 1) * rows, :].astype(jnp.float32)
        self.line_sum[...] = total
        column = pl.ds(pl.multiple_of(self.core * self.columns, 128), self.columns)
        half = rows // 2
        away = pl.ds(pl.multiple_of((1 - self.core) * half, 8), half)
        self.out[:, column] = self.line_sum[pl.ds(pl.multiple_of(self.core * half, 8), half), :]
        self.last = send(self.line_sum.at[away, :], self.out.at[:, column], self.sibling)

    def drain(self):
        for copy in self.halves + self.copies + [self.beside_copy]:
            copy.wait_send()
        pl.when(jnp.logical_not(self.inner))(self.outward.wait_send)
        for copy in self.passed:
            pl.when(self.inner)(copy.wait_send)
        self.last.wait()


class HeadsSum(GroupSum):
    def __init__(self, term, other, first, near, final):
        self.term, self.other, self.first, self.near, self.final = term, other, first, near, final
        self.rows = 4 * term.shape[2]
        grp, seq, zed, self.core, self.sibling, along = place()
        self.place_in_plane(grp, seq)
        self.copies, self.halves = [], []

    def swap_quarter(self, send, quarter):
        at = pl.ds(4 * quarter, 4)
        return send(self.term.at[at, 1 - self.core], self.other.at[at], self.sibling)

    def both_cores(self, quarter):
        at = pl.ds(4 * quarter, 4)
        return (self.term[at, self.core] + self.other[at]).reshape(self.rows, -1)

    def core_sum(self, quarter):
        self.first[rows_of(quarter * self.rows, self.rows), :] = self.both_cores(quarter).astype(
            jnp.bfloat16
        )

    def total(self):
        self.halves[3].wait_recv()
        for slot in (1, 3, 4, 5):
            self.copies[slot].wait_recv()
        near = [self.near[i].astype(jnp.float32) for i in range(6)]
        total = self.both_cores(self.own) + jnp.concatenate(
            [near[1] + near[4], near[3] + near[5]], axis=0
        )
        self.final[...] = total.reshape(self.final.shape)

    def drain(self):
        for copy in self.halves + self.copies:
            copy.wait_send()


def norm_back(x, gain, grad_norm, grad_out, into, chunk):
    f32 = jnp.float32
    tokens, width = x.shape
    gain_row = gain[...].reshape(1, width)

    def one(i, sums):
        at = rows_of(i * chunk, chunk)
        vector, grad = x[at, :].astype(f32), grad_norm[at, :]
        normal, inverse = normal_parts(vector)
        pulled = norm_pull(normal, inverse, gain_row, grad)
        into[at, :] = (grad_out[at, :] + pulled).astype(into.dtype)
        return (
            sums[0] + jnp.sum(grad * normal, axis=0, keepdims=True),
            sums[1] + jnp.sum(grad, axis=0, keepdims=True),
        )

    zero = jnp.zeros((1, width), f32)
    return lax.fori_loop(0, tokens // chunk, one, (zero, zero))


def settle_small(small, vecs, rms, owner):
    width, count = small.shape[-1], vecs.shape[-1]
    total = (small[0] + small[1]) + (small[2] + small[3])
    turned = pltpu.roll(total, (width - owner * count) % width, 1)
    for i in range(4):
        vecs[i] = turned[i : i + 1, :count]
    rms[...] = jnp.sqrt(total[4:5, :3] / total[4:5, 3:4])


def layer_kernel(
    x_in, out_grad_in, w_qkv_in, w_out_in, w_up_in, w_down_in,
    gain_one, bias_one, gain_two, bias_two, span,
    block_output, input_grad, sum_qkv, vecs, rms, out_down, out_up, out_out,
    x, out_grad, w_qkv, w_out, w_up, w_down,
    mixed, q_all, kv_all, raw, mix_all, tot_all, norm_all, weights, totals,
    term_out, middle, normed, normed_t, mlp_out, grad_norm, grad_middle, gmix,
    first, near, held, third, mine, first_down, near_down, held_down, third_down, mine_down,
    gm_in, turned, g_all, gt_all, grad_kv, part_out, part_in, leaving, arrived,
    term, other, first_qkv, near_qkv, final, gathered, grad_query, small_a, small_b, small_c,
    load_sems, send_sems, recv_sems,
    hop_send, hop_recv, swap_send, swap_recv, back_send, back_recv,
):
    tokens, width = x.shape
    f32, bf16 = jnp.float32, jnp.bfloat16
    grp, seq, zed, core, sibling, along = place()
    line = [(grp, along[k] * 2 + core) for k in (1, 2, 3)]
    chunks = w_up.shape[1] // width

    loads = {}

    def load(name, source, target):
        loads[name] = pltpu.make_async_copy(source, target, load_sems.at[len(loads)])
        loads[name].start()

    load("x", x_in, x)
    load("w_qkv", w_qkv_in, w_qkv)
    load("w_out", w_out_in, w_out)
    load("out_grad", out_grad_in, out_grad)
    for i in range(chunks):
        at = pl.ds(i * width, width)
        load(("up", i), w_up_in.at[:, at], w_up.at[:, at])
        load(("down", i), w_down_in.at[at, :], w_down.at[at, :])

    ups = [
        GroupSum(
            w_up.at[:, pl.ds(i * width, width)], first.at[i], near.at[i], held.at[i], third.at[i],
            mine.at[i], out_up.at[:, pl.ds(i * width, width)],
        )
        for i in range(chunks)
    ]
    outs = GroupSum(
        term_out, first.at[chunks], near.at[chunks], held.at[chunks], third.at[chunks],
        mine.at[chunks], out_out,
    )
    downs = GroupSum(w_down, first_down, near_down, held_down, third_down, mine_down, out_down)
    downs.whole = True
    heads_sum = HeadsSum(term, other, first_qkv, near_qkv, final)
    across = [(k, seq) for k in (heads_sum.beside, heads_sum.above, heads_sum.across)]
    around = [(k, zed * 2 + 1 - core) for k in (heads_sum.beside, heads_sum.above, heads_sum.across)]
    partners = [sibling] + line + across + around
    greet_start(partners)
    send = sender(send_sems, recv_sems)
    attend_part(
        x, gain_one, bias_one, w_qkv, span, mixed, q_all, kv_all, raw, mix_all, tot_all, norm_all,
        weights, turned, totals, leaving, hop_send, hop_recv, swap_send, swap_recv, back_send,
        back_recv, loads, functools.partial(greet_end, partners),
    )

    pos = seq * tokens + lax.broadcasted_iota(jnp.int32, (tokens, 1), 0)
    keep = ((pos >= span[0, 0]) & (pos < span[0, 1])).astype(f32)
    gain_row, bias_row = gain_two[...].reshape(1, width), bias_two[...].reshape(1, width)

    def squares(value):
        return jnp.sum(keep * value * value)

    for name in ("w_out", "out_grad"):
        loads[name].wait()
    attn_out = matmul(mixed[...].reshape(width, tokens).T, w_out[...])
    attn_squares = squares(attn_out)
    middle[...] = x[...].astype(f32) + attn_out
    normed[...] = (normal_parts(middle[...])[0] * gain_row + bias_row).astype(bf16)
    normed_t[...] = normed[...].T
    mlp_out[...] = jnp.zeros((tokens, width), f32)
    grad_norm[...] = jnp.zeros((tokens, width), f32)
    for i in range(chunks):
        at = pl.ds(i * width, width)
        loads["up", i].wait()
        loads["down", i].wait()
        activated, slope = gelu_and_slope(matmul(normed[...], w_up[:, at]))
        activated = activated.astype(bf16)
        mlp_out[...] += matmul(activated, w_down[at, :])
        grad_up = (contract_cols(out_grad[...], w_down[at, :]) * slope).astype(bf16)
        grad_norm[...] += contract_cols(grad_up, w_up[:, at])
        w_up[:, at] = matmul(normed_t[...], grad_up).astype(bf16)
        ups[i].swap(send)
        w_down[at, :] = matmul(activated.T, out_grad[...]).astype(bf16)
        downs.halves.append(downs.swap_quarter(send, i))
        if i >= 2:
            ups[i - 2].step_one(send)
    normal, inverse = normal_parts(middle[...])
    grad = grad_norm[...]
    grad_middle[...] = out_grad[...].astype(f32) + norm_pull(normal, inverse, gain_row, grad)
    grad_attn = grad_middle[...].astype(bf16)
    gmix[...] = contract_cols(w_out[...], grad_attn).astype(bf16).reshape(gmix.shape)
    coming = []
    for h in range(3):
        for k in (1, 2, 3):
            coming.append(send(gmix.at[along[k] * 3 + h], gm_in.at[h, zed], line[k - 1]))
        gm_in[h, zed] = gmix[zed * 3 + h]
    term_out[...] = matmul(mixed[...].reshape(width, tokens), grad_attn).astype(bf16)
    ups[0].step_two(send)
    ups[2].step_one(send)
    outs.swap(send)
    ups[1].step_two(send)
    ups[3].step_one(send)
    small_a[0, 2:3] = jnp.sum(grad * normal, axis=0, keepdims=True)
    small_a[0, 3:4] = jnp.sum(grad, axis=0, keepdims=True)
    output = middle[...] + mlp_out[...]
    block_output[...] = output.astype(bf16)
    lane = lax.broadcasted_iota(jnp.int32, (4, width), 1)
    row = jnp.zeros((4, width), f32)
    squared = (squares(output), attn_squares, squares(mlp_out[...]), jnp.sum(keep) * width)
    for i, value in enumerate(squared):
        row = jnp.where(lane == i, value, row)
    small_a[0, 4:8] = row


    def turn(h):
        def one(z, _):
            for side in range(2):
                at = pl.ds(side * tokens, tokens)
                turned[h % 2, z, at, :] = kv_all[h, z, side, 0].T
                turned[2 + h % 2, z, at, :] = kv_all[h, z, side, 1].T
            return 0

        lax.fori_loop(0, 4, one, 0)

    turn(0)
    ups[0].along_line(send)
    for z in range(4):
        leaving[z, 9] = jnp.zeros((HEAD_DIM, tokens), bf16)
    downs.step_one(send)

    swaps, sends = [], []

    def finish(h):
        swaps[h].wait_recv()

        def merge(z, _):
            fine = valid_columns(span, (2 * z + core) * tokens, tokens)
            q, k, v, inverse, signed, terms, weight = alone_terms(raw.at[z, pl.ds(3 * h, 3)])
            g = gm_in[h, z].astype(f32)
            total = 1.0 / terms
            grad_total = -jnp.sum(g * (weight * v), axis=0, keepdims=True) * total * total
            g = (g * total).astype(bf16).astype(f32)
            grad_weight = jnp.sum(g * v, axis=0, keepdims=True)
            slope = 1.0 + (inverse * inverse) * (inverse - 1.0)
            grad_score = terms * (grad_weight * slope + grad_total * signed)
            grad_score = grad_score.astype(bf16).astype(f32)
            alone = (grad_score * k * 0.125, grad_score * q, weight * g)
            parts = [leaving[z, 3 * h].astype(f32)]
            for part in range(2):
                parts.append(grad_kv[h, z, core, part] + part_in[h, z, part].astype(f32))
            for part in range(3):
                leaving[z, 3 * h + part] = jnp.where(fine, parts[part], alone[part]).astype(bf16)
            return 0

        lax.fori_loop(0, 4, merge, 0)
        at = pl.ds(3 * h, 3)
        for k in (1, 2, 3):
            sends.append(
                send(leaving.at[along[k], at], arrived.at[:, zed * 3 + h], line[k - 1])
            )
        for part in range(3):
            arrived[part, zed * 3 + h] = leaving[zed, 3 * h + part]

    def tile_products(h, z, z_key, side):
        at = pl.ds(side * tokens, tokens)
        scores = matmul(turned[h % 2, z_key, at, :], q_all[h, z])
        return scores, matmul(turned[2 + h % 2, z_key, at, :], g_all[z])

    def tile_grads(tile, scores, grad_weights):
        z, z_key, side = tile
        inverse, signed, terms = signed_terms(scores)
        if z == z_key:
            key_pos = lax.broadcasted_iota(jnp.int32, scores.shape, 0)
            query_pos = lax.broadcasted_iota(jnp.int32, scores.shape, 1)
            seen = key_pos + side * tokens <= query_pos + core * tokens
            terms = jnp.where(seen, terms, 0.0)
        weights = (signed * terms).astype(bf16)
        slope = 1.0 + (inverse * inverse) * (inverse - 1.0)
        grad_scores = terms * (grad_weights * slope + gt_all[z] * signed)
        return weights, grad_scores.astype(bf16)

    def tile_sums(h, z, z_key, side, weights, grad_scores):
        for part, left, right in ((0, q_all[h, z], grad_scores), (1, g_all[z], weights)):
            grad = contract_cols(left, right)
            if z == z_key:
                grad_kv[h, z_key, side, part] = grad
            else:
                grad_kv[h, z_key, side, part] += grad
        grad = matmul(kv_all[h, z_key, side, 0], grad_scores)
        if z_key == 0 and side == 0:
            grad_query[...] = grad
        else:
            grad_query[...] += grad
        if z == z_key and side == 1:
            leaving[z, 3 * h] = (grad_query[...] * 0.125).astype(bf16)

    for h in range(3):
        for copy in coming[h * 3 : h * 3 + 3]:
            copy.wait_recv()

        def prepare(z, _):
            g = gm_in[h, z].astype(f32)
            total = 1.0 / tot_all[h, z]
            g_all[z] = (g * total).astype(bf16)
            gt_all[z] = -jnp.sum(g * mix_all[h, z], axis=0, keepdims=True) * total
            return 0

        lax.fori_loop(0, 4, prepare, 0)

        tiles = [(z, z_key, side) for z in range(4) for z_key in range(z + 1) for side in range(2)]
        scored, parts = {}, {}
        for step in range(len(tiles) + 2):
            if step < len(tiles):
                scored[step] = tile_products(h, *tiles[step])
            if 0 <= step - 1 < len(tiles):
                parts[step - 1] = tile_grads(tiles[step - 1], *scored.pop(step - 1))
            if step - 2 >= 0:
                tile_sums(h, *tiles[step - 2], *parts.pop(step - 2))

        def pack(z, _):
            for part in range(2):
                part_out[h, z, part] = grad_kv[h, z, 1 - core, part].astype(bf16)
            return 0

        lax.fori_loop(0, 4, pack, 0)
        swaps.append(send(part_out.at[h], part_in.at[h], sibling))
        if h == 0:
            turn(1)
            ups[1].along_line(send)
            outs.step_one(send)
            ups[0].pass_line(send)
        if h == 1:
            turn(2)
            ups[2].step_two(send)
            ups[3].step_two(send)
            ups[1].pass_line(send)
        finish(h)

    for quarter in (heads_sum.across, heads_sum.beside, heads_sum.above, heads_sum.own):
        total = None
        for z in range(4):
            rows = norm_all[z, rows_of(quarter * (width // 4), width // 4), :]
            part = contract_cols(rows, leaving[z].reshape(10 * HEAD_DIM, tokens))
            total = part if total is None else total + part
        term[pl.ds(4 * quarter, 4)] = total.reshape((4,) + term.shape[1:])
        heads_sum.halves.append(heads_sum.swap_quarter(send, quarter))
    ups[2].along_line(send)
    heads_sum.step_one(send)
    downs.step_two(send)
    outs.step_two(send)
    ups[3].along_line(send)
    downs.along_line(send)
    outs.along_line(send)
    ups[2].pass_line(send)
    heads_sum.step_two(send)
    ups[3].pass_line(send)

    for copy in sends:
        copy.wait_recv()
    grads = arrived[...].reshape(3 * width, tokens)
    for i in range(width // 256):
        columns = slice(i * 256, (i + 1) * 256)
        grad_norm[:, columns] = matmul(w_qkv[columns, :], grads).T
    downs.pass_line(send)
    outs.pass_line(send)
    gain_grad, bias_grad = norm_back(x, gain_one, grad_norm, grad_middle, input_grad, 64)
    small_a[0, 0:1] = gain_grad
    small_a[0, 1:2] = bias_grad
    whose = 2 * grp + core
    small_b[pl.ds(whose, 1)] = small_a[0:1]
    planes = [
        send(small_b.at[whose], small_b.at[whose], target)
        for target in [sibling] + across + around
    ]
    heads_sum.total()
    gathered[pl.ds(zed, 1)] = final[pl.ds(zed, 1)]
    blocks = [send(final.at[along[k]], gathered.at[zed], line[k - 1]) for k in (1, 2, 3)]
    for copy in planes:
        copy.wait_recv()
    total = small_b[0]
    for i in range(1, 8):
        total = total + small_b[i]
    small_c[pl.ds(zed, 1)] = total.reshape(1, 8, width)
    columns = [send(small_c.at[zed], small_c.at[zed], line[k - 1]) for k in (1, 2, 3)]
    sums = ups + [downs, outs]
    for each in sums:
        each.settle(send)
    for copy in blocks + columns:
        copy.wait_recv()
    for z in range(4):
        for h in range(3):
            for part in range(3):
                start = part * width + (3 * z + h) * HEAD_DIM
                sum_qkv[:, start : start + HEAD_DIM] = gathered[
                    z, :, (3 * h + part) * HEAD_DIM : (3 * h + part + 1) * HEAD_DIM
                ]
    settle_small(small_c, vecs, rms, grp * 8 + seq)
    for copy in coming + swaps + sends + planes + blocks + columns:
        copy.wait_send()
    for each in sums + [heads_sum]:
        each.drain()


def layer(block_input, out_grad, w_qkv, w_out, w_up, w_down, vectors, span):
    f32, bf16 = jnp.float32, jnp.bfloat16
    tokens, width = block_input.shape
    hidden = w_up.shape[1]
    count = hidden // width + 1
    vmem, smem = pl.BlockSpec(memory_space=pltpu.VMEM), pl.BlockSpec(memory_space=pltpu.SMEM)
    block = (HEAD_DIM, tokens)
    own_rows, columns = width // 32, 10 * HEAD_DIM
    quarter, half = width // 4, width // 2
    copies = 15 * (count + 1) + 9 + 3 + 9 + 10 + 7 + 3 + 3
    dma = pltpu.SemaphoreType.DMA
    in_hbm = [block_input, out_grad, w_qkv, w_out, w_up, w_down]

    def sum_scratch(lead, rows):
        return [
            pltpu.VMEM(lead + (4 * rows, half), bf16),
            pltpu.VMEM(lead + (6, rows // 2, half), bf16),
            pltpu.VMEM(lead + (rows, half), bf16),
            pltpu.VMEM(lead + (rows, half), bf16),
            pltpu.VMEM(lead + (rows // 4, half), f32),
        ]

    return pl.pallas_call(
        layer_kernel,
        out_shape=[
            jax.ShapeDtypeStruct((tokens, width), bf16),
            jax.ShapeDtypeStruct((tokens, width), bf16),
            jax.ShapeDtypeStruct((own_rows, 3 * width), f32),
            jax.ShapeDtypeStruct((4, 1, own_rows), f32),
            jax.ShapeDtypeStruct((1, 3), f32),
            jax.ShapeDtypeStruct((hidden // 32, width), f32),
            jax.ShapeDtypeStruct((own_rows, hidden), f32),
            jax.ShapeDtypeStruct((own_rows, width), f32),
        ],
        in_specs=[pl.BlockSpec(memory_space=pl.ANY)] * len(in_hbm) + [vmem] * 4 + [smem],
        out_specs=[vmem] * 8,
        scratch_shapes=[pltpu.VMEM(a.shape, a.dtype) for a in in_hbm]
        + [
            pltpu.VMEM((HEADS,) + block, bf16),
            pltpu.VMEM((3, 4) + block, bf16),
            pltpu.VMEM((3, 4, 2, 2) + block, bf16),
            pltpu.VMEM((4, 9) + block, bf16),
            pltpu.VMEM((3, 4) + block, f32),
            pltpu.VMEM((3, 4, 1, tokens), f32),
            pltpu.VMEM((4, width, tokens), bf16),
            pltpu.VMEM((3, 256, width), bf16),
            pltpu.VMEM((3, 4, 8, tokens), f32),
            pltpu.VMEM((width, width), bf16),
            pltpu.VMEM((tokens, width), f32),
            pltpu.VMEM((tokens, width), bf16),
            pltpu.VMEM((width, tokens), bf16),
            pltpu.VMEM((tokens, width), f32),
            pltpu.VMEM((tokens, width), f32),
            pltpu.VMEM((tokens, width), f32),
            pltpu.VMEM((HEADS,) + block, bf16),
        ]
        + sum_scratch((count,), quarter)
        + sum_scratch((), hidden // 4)
        + [
            pltpu.VMEM((3, 4) + block, bf16),
            pltpu.VMEM((4, 4, 2 * tokens, HEAD_DIM), bf16),
            pltpu.VMEM((4,) + block, bf16),
            pltpu.VMEM((4, 1, tokens), f32),
            pltpu.VMEM((3, 4, 2, 2) + block, f32),
            pltpu.VMEM((3, 4, 2) + block, bf16),
            pltpu.VMEM((3, 4, 2) + block, bf16),
            pltpu.VMEM((4, 10) + block, bf16),
            pltpu.VMEM((3, HEADS) + block, bf16),
            pltpu.VMEM((16, 2, own_rows, columns), f32),
            pltpu.VMEM((16, own_rows, columns), f32),
            pltpu.VMEM((16 * own_rows, columns), bf16),
            pltpu.VMEM((6, 2 * own_rows, columns), bf16),
            pltpu.VMEM((4, own_rows, columns), f32),
            pltpu.VMEM((4, own_rows, columns), f32),
            pltpu.VMEM(block, f32),
            pltpu.VMEM((1, 8, width), f32),
            pltpu.VMEM((8, 8, width), f32),
            pltpu.VMEM((4, 8, width), f32),
            dma((4 + 2 * (count - 1),)),
            dma((copies,)),
            dma((copies,)),
            dma((2, 4, 2)),
            dma((2, 4, 2)),
            dma((8,)),
            dma((8,)),
            dma((4,)),
            dma((4,)),
        ],
        compiler_params=pltpu.CompilerParams(
            collective_id=0, has_side_effects=True, vmem_limit_bytes=63 * 2**20
        ),
    )(*in_hbm, *vectors, span)


def hand_over_kernel(many, *refs):
    vecs, rms, arrays = refs[0], refs[1], refs[2 : 2 + many]
    outs, rest = refs[2 + many : 7 + 2 * many], refs[7 + 2 * many :]
    held, sems = rest[:many], rest[many]
    loads = [
        pltpu.make_async_copy(arrays[i], held[i], sems.at[0, i]) for i in range(many)
    ]
    stores = [
        pltpu.make_async_copy(held[i], outs[5 + i], sems.at[1, i]) for i in range(many)
    ]
    for load in loads:
        load.start()
    for i in range(4):
        outs[i][...] = vecs[i, 0]
    outs[4][...] = rms[0]
    for load, store in zip(loads, stores):
        load.wait()
        store.start()
    for store in stores:
        store.wait()


def hand_over(vecs, rms, arrays):
    vmem, hbm = pl.BlockSpec(memory_space=pltpu.VMEM), pl.BlockSpec(memory_space=pl.ANY)
    many, f32 = len(arrays), jnp.float32
    return pl.pallas_call(
        functools.partial(hand_over_kernel, many),
        out_shape=[jax.ShapeDtypeStruct(vecs.shape[2:], f32)] * 4
        + [jax.ShapeDtypeStruct(rms.shape[1:], f32)]
        + [jax.ShapeDtypeStruct(a.shape, a.dtype) for a in arrays],
        in_specs=[vmem] * 2 + [hbm] * many,
        out_specs=[vmem] * 5 + [hbm] * many,
        scratch_shapes=[pltpu.VMEM(a.shape, a.dtype) for a in arrays]
        + [pltpu.SemaphoreType.DMA((2, many))],
    )(vecs, rms, *arrays)


def per_device_planned(
    block_input,
    out_grad,
    seq_span,
    ln1_gain,
    ln1_bias,
    w_qkv,
    w_out,
    ln2_gain,
    ln2_bias,
    w_up,
    w_down,
):
    block_output, input_grad, sum_qkv, vecs, rms, sum_down, sum_up, sum_out = layer(
        block_input, out_grad, w_qkv, w_out, w_up, w_down,
        (ln1_gain, ln1_bias, ln2_gain, ln2_bias), seq_span,
    )
    arrays = (block_output, input_grad, sum_qkv, sum_out, sum_up, sum_down)
    gain_one, bias_one, gain_two, bias_two, rms, *arrays = hand_over(vecs, rms, arrays)
    block_output, input_grad, sum_qkv, sum_out, sum_up, sum_down = arrays
    return (
        block_output,
        input_grad,
        gain_one,
        bias_one,
        sum_qkv,
        sum_out,
        gain_two,
        bias_two,
        sum_up,
        sum_down,
        rms,
    )


def solution(mesh):
    placed = (
        P(("grp", "seq"), None),
        P(("grp", "seq"), None),
        P("grp", None),
        P(),
        P(),
        P(),
        P(),
        P(),
        P(),
        P(),
        P(),
    )
    planned = mesh.shape["grp"] == 4 and mesh.shape["seq"] == 8
    return jax.shard_map(
        per_device_planned if planned else per_device,
        mesh=mesh,
        in_specs=placed,
        out_specs=(
            P(("grp", "seq"), None),
            P(("grp", "seq"), None),
            P(("grp", "seq")),
            P(("grp", "seq")),
            P(("grp", "seq"), None),
            P(("grp", "seq"), None),
            P(("grp", "seq")),
            P(("grp", "seq")),
            P(("grp", "seq"), None),
            P(("grp", "seq"), None),
            P(),
        ),
        check_vma=False,
    )
```

```python
import functools

import jax
import jax.numpy as jnp
from jax import lax
from jax.experimental import pallas as pl
from jax.experimental.pallas import tpu as pltpu
from jax.sharding import PartitionSpec as P

D = 768
HEADS = 12
HEAD_DIM = 64
MESH = pl.DeviceIdType.MESH


epsilon = 1e-05


def passed_along(array, axis, by):
    devices = lax.axis_size(axis)
    pairs = [(i, i + by) for i in range(devices) if 0 <= i + by < devices]
    return lax.ppermute(array, axis, pairs)


def shifted(array, axis, by):
    devices = lax.axis_size(axis)
    return lax.ppermute(array, axis, [(i, (i + by) % devices) for i in range(devices)])


def layer_norm(vector, scale_vec, shift_vec):
    row_mean = jnp.mean(vector, axis=-1, keepdims=True)
    centered = vector - row_mean
    variance = jnp.mean(centered * centered, axis=-1, keepdims=True)
    return centered * lax.rsqrt(variance + epsilon) * scale_vec + shift_vec


def contract_rows(left, right):
    return lax.dot_general(
        left, right, (((0,), (0,)), ((), ())), preferred_element_type=jnp.float32
    )


def contract_cols(left, right):
    return lax.dot_general(
        left, right, (((1,), (1,)), ((), ())), preferred_element_type=jnp.float32
    )


def score_terms(queries, key_block, query_pos, key_pos, seq_first, seq_limit):
    scores = (
        jnp.einsum("qhd,khd->qhk", queries, key_block, preferred_element_type=jnp.float32) * 0.125
    )
    query_valid = (query_pos >= seq_first) & (query_pos < seq_limit)
    key_valid = (key_pos >= seq_first) & (key_pos < seq_limit)
    allowed = (key_pos[None, :] <= query_pos[:, None]) & (
        query_valid[:, None] & key_valid[None, :] | (key_pos[None, :] == query_pos[:, None])
    )
    magnitude = jnp.sqrt(scores * scores + 1.0)
    signed_part = scores / magnitude
    exp_terms = jnp.where(allowed[:, None, :], jnp.exp(magnitude), 0.0)
    return (magnitude, signed_part, exp_terms)


def split_pair(kv_pair):
    count_rows = kv_pair.shape[0]
    key_block = kv_pair[:, :D].reshape(count_rows, HEADS, HEAD_DIM)
    value_block = kv_pair[:, D:].reshape(count_rows, HEADS, HEAD_DIM)
    return (key_block, value_block)


def forward_block(running, kv_pair, key_start, queries, query_pos, seq_first, seq_limit):
    totals, unnorm = running
    key_block, value_block = split_pair(kv_pair)
    key_pos = key_start + jnp.arange(kv_pair.shape[0], dtype=jnp.int32)
    magnitude, signed_part, exp_terms = score_terms(
        queries, key_block, query_pos, key_pos, seq_first, seq_limit
    )
    weights = (signed_part * exp_terms).astype(jnp.bfloat16)
    totals = totals + jnp.sum(exp_terms, axis=-1)
    unnorm = unnorm + jnp.einsum(
        "qhk,khd->qhd", weights, value_block, preferred_element_type=jnp.float32
    )
    return (totals, unnorm)


def grad_core(
    kv_pair, key_start, queries, query_pos, seq_first, seq_limit, grad_unnorm, grad_totals
):
    key_block, value_block = split_pair(kv_pair)
    key_pos = key_start + jnp.arange(kv_pair.shape[0], dtype=jnp.int32)
    magnitude, signed_part, exp_terms = score_terms(
        queries, key_block, query_pos, key_pos, seq_first, seq_limit
    )
    weights = (signed_part * exp_terms).astype(jnp.bfloat16)
    grad_weights = jnp.einsum(
        "qhd,khd->qhk", grad_unnorm, value_block, preferred_element_type=jnp.float32
    )
    grad_scores = (
        grad_weights * exp_terms / (magnitude * magnitude * magnitude)
        + (grad_weights * signed_part + grad_totals[:, :, None]) * exp_terms * signed_part
    )
    return (key_block, weights, grad_scores.astype(jnp.bfloat16))


def backward_block(
    kv_pair, key_start, queries, query_pos, seq_first, seq_limit, grad_unnorm, grad_totals
):
    key_block, weights, grad_scores = grad_core(
        kv_pair, key_start, queries, query_pos, seq_first, seq_limit, grad_unnorm, grad_totals
    )
    count_rows = kv_pair.shape[0]
    grad_query = (
        jnp.einsum("qhk,khd->qhd", grad_scores, key_block, preferred_element_type=jnp.float32)
        * 0.125
    )
    grad_key = (
        jnp.einsum("qhk,qhd->khd", grad_scores, queries, preferred_element_type=jnp.float32) * 0.125
    )
    grad_value = jnp.einsum(
        "qhk,qhd->khd", weights, grad_unnorm, preferred_element_type=jnp.float32
    )
    grad_pair = jnp.concatenate(
        [grad_key.reshape(count_rows, D), grad_value.reshape(count_rows, D)], axis=1
    )
    return (grad_query, grad_pair)


def per_device(
    block_input,
    out_grad,
    seq_span,
    ln1_gain,
    ln1_bias,
    w_qkv,
    w_out,
    ln2_gain,
    ln2_bias,
    w_up,
    w_down,
):
    tok_rows = block_input.shape[0]
    feat_width = block_input.shape[1]
    seq_count = lax.axis_size("seq")
    seq_index = lax.axis_index("seq")
    query_pos = seq_index * tok_rows + jnp.arange(tok_rows, dtype=jnp.int32)
    query_last = query_pos[tok_rows - 1]
    seq_first = seq_span[0, 0]
    seq_limit = seq_span[0, 1]
    inputs = block_input.astype(jnp.float32)
    normed = layer_norm(inputs, ln1_gain, ln1_bias).astype(jnp.bfloat16)
    proj_qkv = jnp.dot(normed, w_qkv, preferred_element_type=jnp.float32).astype(jnp.bfloat16)
    queries = proj_qkv[:, :feat_width].reshape(tok_rows, HEADS, HEAD_DIM)
    kv_pair = proj_qkv[:, feat_width:]

    def visit_block(running, shard_rows, key_start):
        return lax.cond(
            key_start <= query_last,
            lambda state_in: forward_block(
                state_in, shard_rows, key_start, queries, query_pos, seq_first, seq_limit
            ),
            lambda state_in: state_in,
            running,
        )

    empty = (
        jnp.zeros((tok_rows, HEADS), jnp.float32),
        jnp.zeros((tok_rows, HEADS, HEAD_DIM), jnp.float32),
    )
    first_state = visit_block(empty, kv_pair, seq_index * tok_rows)

    def forward_hop(hop_count, loop_state):
        moving, running = loop_state
        moving = passed_along(moving, "seq", 1)
        source = (seq_index - hop_count) % seq_count
        return (moving, visit_block(running, moving, source * tok_rows))

    _, (totals, unnorm) = lax.fori_loop(1, seq_count, forward_hop, (kv_pair, first_state))
    mixed_heads = (unnorm / totals[:, :, None]).reshape(tok_rows, feat_width).astype(jnp.bfloat16)
    attn_out = jnp.dot(mixed_heads, w_out, preferred_element_type=jnp.float32)
    middle = inputs + attn_out
    normed_two = layer_norm(middle, ln2_gain, ln2_bias).astype(jnp.bfloat16)
    up_proj = jnp.dot(normed_two, w_up, preferred_element_type=jnp.float32)
    activated = jax.nn.gelu(up_proj, approximate=True).astype(jnp.bfloat16)
    mlp_out = jnp.dot(activated, w_down, preferred_element_type=jnp.float32)
    output = middle + mlp_out
    valid_rows = ((query_pos >= seq_first) & (query_pos < seq_limit)).astype(jnp.float32)[:, None]
    rms_parts = lax.psum(
        (
            jnp.sum(valid_rows * output * output),
            jnp.sum(valid_rows * attn_out * attn_out),
            jnp.sum(valid_rows * mlp_out * mlp_out),
            jnp.sum(valid_rows) * feat_width,
        ),
        ("grp", "seq"),
    )
    rms_stats = jnp.sqrt(jnp.stack([rms_parts[0], rms_parts[1], rms_parts[2]]) / rms_parts[3])
    grad_w_down = contract_rows(activated, out_grad)
    grad_activated = contract_cols(out_grad, w_down)
    _, gelu_pull = jax.vjp(lambda pre_act: jax.nn.gelu(pre_act, approximate=True), up_proj)
    grad_up = gelu_pull(grad_activated)[0].astype(jnp.bfloat16)
    grad_w_up = contract_rows(normed_two, grad_up)
    grad_norm_two = contract_cols(grad_up, w_up)
    _, norm_pull_two = jax.vjp(layer_norm, middle, ln2_gain, ln2_bias)
    grad_mid_norm, grad_gain_two, grad_bias_two = norm_pull_two(grad_norm_two)
    grad_middle = out_grad.astype(jnp.float32) + grad_mid_norm
    grad_attn = grad_middle.astype(jnp.bfloat16)
    grad_w_out = contract_rows(mixed_heads, grad_attn)
    grad_mixed = contract_cols(grad_attn, w_out).reshape(tok_rows, HEADS, HEAD_DIM)
    grad_unnorm = (grad_mixed / totals[:, :, None]).astype(jnp.bfloat16)
    grad_totals = -jnp.sum(grad_mixed * unnorm, axis=-1) / (totals * totals)

    def back_block(grad_run, shard_rows, key_start):

        def compute_block(grad_in):
            grad_query, grad_pair = backward_block(
                shard_rows,
                key_start,
                queries,
                query_pos,
                seq_first,
                seq_limit,
                grad_unnorm,
                grad_totals,
            )
            return (grad_in + grad_query, grad_pair)

        def skip_block(grad_in):
            return (grad_in, jnp.zeros((shard_rows.shape[0], 2 * feat_width), jnp.float32))

        return lax.cond(key_start <= query_last, compute_block, skip_block, grad_run)

    grad_start = jnp.zeros((tok_rows, HEADS, HEAD_DIM), jnp.float32)
    grad_queries, local_terms = back_block(grad_start, kv_pair, seq_index * tok_rows)

    def backward_hop(hop_count, loop_state):
        moving, grad_acc, grad_run = loop_state
        moving = passed_along(moving, "seq", 1)
        grad_acc = shifted(grad_acc.astype(jnp.bfloat16), "seq", 1).astype(grad_acc.dtype)
        source = (seq_index - hop_count) % seq_count
        grad_run, new_terms = back_block(grad_run, moving, source * tok_rows)
        return (moving, grad_acc + new_terms, grad_run)

    _, grad_acc, grad_queries = lax.fori_loop(
        1, seq_count, backward_hop, (kv_pair, local_terms, grad_queries)
    )
    grad_kv = shifted(grad_acc.astype(jnp.bfloat16), "seq", 1).astype(grad_acc.dtype)
    grad_qkv = jnp.concatenate(
        [grad_queries.reshape(tok_rows, feat_width), grad_kv], axis=1
    ).astype(jnp.bfloat16)
    grad_w_qkv = contract_rows(normed, grad_qkv)
    grad_norm_one = contract_cols(grad_qkv, w_qkv)
    _, norm_pull_one = jax.vjp(layer_norm, inputs, ln1_gain, ln1_bias)
    grad_in_norm, grad_gain_one, grad_bias_one = norm_pull_one(grad_norm_one)
    input_grad = (grad_middle + grad_in_norm).astype(jnp.bfloat16)
    summed = (
        lax.psum_scatter(grad_gain_one, ("grp", "seq"), scatter_dimension=0, tiled=True),
        lax.psum_scatter(grad_bias_one, ("grp", "seq"), scatter_dimension=0, tiled=True),
        lax.psum_scatter(grad_w_qkv, ("grp", "seq"), scatter_dimension=0, tiled=True),
        lax.psum_scatter(grad_w_out, ("grp", "seq"), scatter_dimension=0, tiled=True),
        lax.psum_scatter(grad_gain_two, ("grp", "seq"), scatter_dimension=0, tiled=True),
        lax.psum_scatter(grad_bias_two, ("grp", "seq"), scatter_dimension=0, tiled=True),
        lax.psum_scatter(grad_w_up, ("grp", "seq"), scatter_dimension=0, tiled=True),
        lax.psum_scatter(grad_w_down, ("grp", "seq"), scatter_dimension=0, tiled=True),
    )
    return (
        output.astype(jnp.bfloat16),
        input_grad,
        summed[0],
        summed[1],
        summed[2],
        summed[3],
        summed[4],
        summed[5],
        summed[6],
        summed[7],
        rms_stats,
    )


def rows_of(start, count):
    return pl.ds(pl.multiple_of(start, 16), count)


def matmul(left, right):
    return jnp.dot(left, right, preferred_element_type=jnp.float32)


def signed_terms(scores):
    square = scores * scores + 1.0
    inverse = lax.rsqrt(square)
    return inverse, scores * inverse, jnp.exp(square * inverse)


def valid_columns(span, start, count):
    pos = start + lax.broadcasted_iota(jnp.int32, (1, count), 1)
    return (pos >= span[0, 0]) & (pos < span[0, 1])


def greet_start(partners):
    for partner in partners:
        pl.semaphore_signal(
            pltpu.get_barrier_semaphore(), inc=1, device_id=partner, device_id_type=MESH
        )


def greet_end(partners):
    pl.semaphore_wait(pltpu.get_barrier_semaphore(), len(partners))


def sender(send_sems, recv_sems):
    count = [0]

    def send(src, dst, target, only=None, arrives=None):
        slot = count[0]
        count[0] += 1
        copy = pltpu.make_async_remote_copy(
            src_ref=src, dst_ref=dst, send_sem=send_sems.at[slot],
            recv_sem=recv_sems.at[slot if arrives is None else arrives],
            device_id=target, device_id_type=MESH,
        )
        if only is None:
            copy.start()
        else:
            pl.when(only)(copy.start)
        return copy

    send.count = count
    return send


def place():
    grp, seq = lax.axis_index("grp"), lax.axis_index("seq")
    zed, core = seq // 2, seq % 2
    sibling = (grp, zed * 2 + 1 - core)
    along = [(zed + k) % 4 for k in range(4)]
    return grp, seq, zed, core, sibling, along


def alone_terms(raw):
    q, k, v = (raw[part].astype(jnp.float32) for part in range(3))
    inverse, signed, terms = signed_terms(jnp.sum(q * k, axis=0, keepdims=True))
    weight = (signed * terms).astype(jnp.bfloat16).astype(jnp.float32)
    return q, k, v, inverse, signed, terms, weight


def attend_part(
    x, gain_one, bias_one, w_qkv, span, mixed, q_all, kv_all, raw, mix_all, tot_all, norm_all,
    weights, keys, totals, leaving, hop_send, hop_recv, swap_send, swap_recv, back_send, back_recv,
    loads, greet_end,
):
    tokens, width = x.shape
    f32, bf16 = jnp.float32, jnp.bfloat16
    grp, seq, zed, core, sibling, along = place()

    start = pl.multiple_of(zed * 192 // 128 * 128, 128)
    inside = pl.ds(pl.multiple_of(zed % 2 * HEAD_DIM, HEAD_DIM), 3 * HEAD_DIM)
    for name in ("x", ("small", 0), ("small", 1)):
        loads[name].wait()
    vector = x[...].astype(f32)
    centered = vector - jnp.mean(vector, axis=-1, keepdims=True)
    variance = jnp.mean(centered * centered, axis=-1, keepdims=True)
    normed = (
        centered * lax.rsqrt(variance + epsilon) * gain_one[...].reshape(1, width)
        + bias_one[...].reshape(1, width)
    ).astype(bf16)
    norm_all[zed] = normed.T
    greet_end()

    halves = [pl.ds(half * (width // 2), width // 2) for half in range(2)]

    def hop(step, side, half):
        towards = 1 - 2 * side
        block = zed - towards * step
        runs = (block >= 0) & (block < 4) & (zed + towards >= 0) & (zed + towards < 4)
        copy = pltpu.make_async_remote_copy(
            src_ref=norm_all.at[block, halves[half]], dst_ref=norm_all.at[block, halves[half]],
            send_sem=hop_send.at[side, step, half], recv_sem=hop_recv.at[side, step, half],
            device_id=(grp, (zed + towards) * 2 + core), device_id_type=MESH,
        )
        return runs, copy

    for half in range(2):
        for side in range(2):
            runs, copy = hop(0, side, half)
            pl.when(runs)(copy.start)
    loads["w_qkv"].wait()
    for part in range(3):
        at = pl.ds(pl.multiple_of(part * width + start, 128), 256)
        weights[part] = w_qkv[:, at].T
    no_score = signed_terms(jnp.zeros((1, tokens), f32))[2]
    extra = span[0, 0].astype(f32) * no_score
    mix_all[...] = jnp.zeros(mix_all.shape, f32)
    totals[...] = jnp.zeros(totals.shape, f32)

    def swap(block, slot):
        return pltpu.make_async_remote_copy(
            src_ref=kv_all.at[:, block, core], dst_ref=kv_all.at[:, block, core],
            send_sem=swap_send.at[slot], recv_sem=swap_recv.at[slot],
            device_id=sibling, device_id_type=MESH,
        )

    def project(block, slot):
        keep = valid_columns(span, (2 * block + core) * tokens, tokens).astype(f32)
        for part in range(3):
            heads = matmul(weights[part, inside, :], norm_all[block])
            if part == 0:
                heads = heads * 0.125
            for h in range(3):
                one = heads[h * HEAD_DIM : (h + 1) * HEAD_DIM]
                raw[block, 3 * h + part] = one.astype(bf16)
                if part == 0:
                    q_all[h, block] = (one * keep).astype(bf16)
                else:
                    kv_all[h, block, core, part - 1] = (one * keep).astype(bf16)
        swap(block, slot).start()

    def turn(block, side):
        for h in range(3):
            keys[h, block, rows_of(side * tokens, tokens), :] = kv_all[h, block, side, 0].T

    def pair(block, other, last, sides=(0, 1)):
        tiles = [(h, side) for h in range(3) for side in sides]
        total = [totals[h, block] for h in range(3)]
        blend = [mix_all[h, block] for h in range(3)]
        scored, weights = {}, {}
        for step in range(len(tiles) + 2):
            if step < len(tiles):
                h, side = tiles[step]
                at = rows_of(side * tokens, tokens)
                scored[step] = matmul(keys[h, other, at, :], q_all[h, block])
            if 0 <= step - 1 < len(tiles):
                h, side = tiles[step - 1]
                scores = scored.pop(step - 1)
                _, signed, terms = signed_terms(scores)
                if last:
                    key_pos = lax.broadcasted_iota(jnp.int32, scores.shape, 0)
                    query_pos = lax.broadcasted_iota(jnp.int32, scores.shape, 1)
                    seen = key_pos + side * tokens <= query_pos + core * tokens
                    terms = jnp.where(seen, terms, 0.0)
                total[h] = total[h] + jnp.sum(terms.reshape(tokens // 8, 8, tokens), axis=0)
                weights[step - 1] = (signed * terms).astype(bf16)
            if step - 2 >= 0:
                h, side = tiles[step - 2]
                blend[h] = blend[h] + matmul(kv_all[h, other, side, 1], weights.pop(step - 2))
        for h in range(3):
            totals[h, block], mix_all[h, block] = total[h], blend[h]

    def back(block):
        return pltpu.make_async_remote_copy(
            src_ref=leaving.at[block, pl.ds(0, 3)], dst_ref=mixed.at[pl.ds(3 * zed, 3)],
            send_sem=back_send.at[block], recv_sem=back_recv.at[zed],
            device_id=(grp, block * 2 + core), device_id_type=MESH,
        )

    def complete(block):
        fine = valid_columns(span, (2 * block + core) * tokens, tokens)
        for h in range(3):
            total = jnp.sum(totals[h, block], axis=0, keepdims=True) - extra
            total = jnp.where(fine, total, 1.0)
            blend = mix_all[h, block] / total
            mix_all[h, block] = blend
            tot_all[h, block] = total
            _, _, v, _, _, terms, weight = alone_terms(raw.at[block, pl.ds(3 * h, 3)])
            leaving[block, h] = jnp.where(fine, blend, weight * v / terms).astype(bf16)

        @pl.when(block != zed)
        def _():
            back(block).start()

        @pl.when(block == zed)
        def _():
            mixed[pl.ds(3 * zed, 3)] = leaving[zed, 0:3]

    project(zed, 0)
    turn(zed, core)
    pair(zed, zed, True, (core,))
    swap(zed, 0).wait_recv()
    turn(zed, 1 - core)
    pair(zed, zed, True, (1 - core,))

    @pl.when(zed == 0)
    def _():
        complete(0)

    def step(d, _):
        low, high = zed - d, zed + d
        for half in range(2):
            for side, block in ((0, low), (1, high)):

                @pl.when((block >= 0) & (block < 4))
                def _():
                    towards = 1 - 2 * side
                    part = norm_all.at[block, halves[half]]
                    pltpu.make_async_remote_copy(
                        src_ref=part, dst_ref=part, send_sem=hop_send.at[side, d - 1, half],
                        recv_sem=hop_recv.at[side, d - 1, half],
                        device_id=(grp, (zed - towards) * 2 + core), device_id_type=MESH,
                    ).wait_recv()
                    runs, copy = hop(d, side, half)
                    pl.when(runs)(copy.start)
                    if half == 1:
                        project(block, 2 * d + side)

        @pl.when(high < 4)
        def _():
            lax.fori_loop(jnp.maximum(low + 1, 0), high, lambda j, _: (pair(high, j, False), 0)[1], 0)
            turn(high, core)
            pair(high, high, True, (core,))
            swap(high, 2 * d + 1).wait_recv()
            turn(high, 1 - core)
            pair(high, high, True, (1 - core,))

        @pl.when(low >= 0)
        def _():
            last = jnp.minimum(high + 1, 4)
            turn(low, core)
            pair(low, low, True, (core,))
            lax.fori_loop(low + 1, last, lambda i, _: (pair(i, low, False, (core,)), 0)[1], 0)
            swap(low, 2 * d).wait_recv()
            turn(low, 1 - core)
            pair(low, low, True, (1 - core,))
            pl.when(low == 0)(lambda: complete(low))

            def later(i, _):
                pair(i, low, False, (1 - core,))
                pl.when((low == 0) & (i != high))(lambda: complete(i))
                return 0

            lax.fori_loop(low + 1, last, later, 0)

        @pl.when((high < 4) & (low <= 0))
        def _():
            complete(high)

        return 0

    lax.fori_loop(1, 4, step, 0)

    for k in (1, 2, 3):
        back(along[k]).wait_send()
        pltpu.make_async_remote_copy(
            src_ref=leaving.at[zed, pl.ds(0, 3)], dst_ref=mixed.at[pl.ds(3 * along[k], 3)],
            send_sem=back_send.at[zed], recv_sem=back_recv.at[along[k]],
            device_id=(grp, along[k] * 2 + core), device_id_type=MESH,
        ).wait_recv()
    for d in range(4):
        for side in range(2):
            for half in range(2):
                runs, copy = hop(d, side, half)
                pl.when(runs)(copy.wait_send)
            if d > 0 or side == 0:
                block = zed + (2 * side - 1) * d
                pl.when((block >= 0) & (block < 4))(swap(block, 2 * d + side).wait_send)


def gelu_and_slope(u):
    root = 0.7978845608028654
    square = u * u
    bent = jnp.tanh(root * (u + 0.044715 * (square * u)))
    half = 0.5 * (1.0 + bent)
    slope = half + 0.5 * u * (1.0 - bent * bent) * (root * (1.0 + 0.134145 * square))
    return u * half, slope


def normal_parts(vector):
    centered = vector - jnp.mean(vector, axis=-1, keepdims=True)
    variance = jnp.mean(centered * centered, axis=-1, keepdims=True)
    inverse = lax.rsqrt(variance + epsilon)
    return centered * inverse, inverse


def norm_pull(normal, inverse, gain, grad):
    scaled = grad * gain
    along_normal = jnp.mean(scaled * normal, axis=-1, keepdims=True)
    return inverse * (scaled - jnp.mean(scaled, axis=-1, keepdims=True) - normal * along_normal)


def add_rows(into, base, count, *terms):
    chunk = 96 if count % 96 == 0 else 48

    def add(i, _):
        total = None
        for ref, start in terms:
            term = ref[rows_of(start + i * chunk, chunk), :].astype(jnp.float32)
            total = term if total is None else total + term
        into[rows_of(base + i * chunk, chunk), :] = total.astype(jnp.bfloat16)
        return 0

    lax.fori_loop(0, count // chunk, add, 0)


class GroupSum:
    def __init__(self, term, first, near, held, third, mine, out, part=None):
        self.term, self.first, self.near, self.held = term, first, near, held
        self.third, self.line_sum, self.out = third, mine, out
        self.rows, half = term.shape[0] // 4, term.shape[1] // 2
        start, count = part or (0, half)
        grp, seq, zed, core, sibling, along = place()
        self.place_in_plane(grp, seq)
        self.sibling, self.grp, self.zed, self.core = sibling, grp, zed, core
        self.column = pl.ds(pl.multiple_of(core * half + start, 128), count)
        self.mine = term.at[:, self.column]
        self.away = pl.ds(pl.multiple_of((1 - core) * half, 128), half)
        self.halves, self.copies = [], []

    def place_in_plane(self, grp, seq):
        y, x = grp // 2, grp % 2
        self.own, self.beside, self.above = grp, y * 2 + 1 - x, (1 - y) * 2 + x
        self.across = (1 - y) * 2 + 1 - x
        self.to_x, self.to_y = (self.beside, seq), (self.above, seq)

    def swap_quarter(self, send, quarter):
        at = rows_of(quarter * self.rows, self.rows)
        return send(self.term.at[at, self.away], self.first.at[at, :], self.sibling)

    def swap(self, send):
        for quarter in (self.across, self.beside, self.above, self.own):
            self.halves.append(self.swap_quarter(send, quarter))

    def part(self, quarter, half):
        return rows_of(quarter * self.rows + half * (self.rows // 2), self.rows // 2)

    def pass_on(self, send, quarter, half, slot, target):
        self.copies.append(
            send(self.first.at[self.part(quarter, half), :], self.near.at[slot], target)
        )

    def core_sum(self, quarter):
        base = quarter * self.rows
        add_rows(self.first, base, self.rows, (self.mine, base), (self.first, base))

    def step_one(self, send):
        steps = (
            (self.across, ((0, 0, self.to_x), (1, 2, self.to_y))),
            (self.beside, ((0, 1, self.to_x),)),
            (self.above, ((1, 3, self.to_y),)),
        )
        for i, (quarter, passes) in enumerate(steps):
            if self.halves:
                self.halves[i].wait_recv()
            self.core_sum(quarter)
            for half, slot, target in passes:
                self.pass_on(send, quarter, half, slot, target)
        self.copies = [self.copies[i] for i in (0, 2, 1, 3)]

    def step_two(self, send):
        half = self.rows // 2
        for slot, quarter, side, target in (
            (0, self.above, 0, self.to_y),
            (2, self.beside, 1, self.to_x),
        ):
            base = quarter * self.rows + side * half
            self.copies[slot].wait_recv()
            add_rows(self.first, base, half, (self.first, base), (self.near.at[slot], 0))
            self.pass_on(send, quarter, side, 4 + side, target)

    def total(self):
        half = self.rows // 2
        if self.halves:
            self.halves[3].wait_recv()
        for slot in (1, 3, 4, 5):
            self.copies[slot].wait_recv()
        for side, one, two in ((0, 1, 4), (1, 3, 5)):
            base = self.own * self.rows + side * half
            add_rows(
                self.held, side * half, half, (self.mine, base), (self.first, base),
                (self.near.at[one], 0), (self.near.at[two], 0),
            )

    def along_line(self, send):
        self.total()
        rows = self.held.shape[0] // 4
        self.inner = (self.zed == 1) | (self.zed == 2)
        mate = self.zed + 1 - 2 * (self.zed % 2)
        self.far = (1 - self.zed // 2) * 2
        target = (self.grp, mate * 2 + self.core)
        far_rows = rows_of(self.far * rows, 2 * rows)
        self.outward = send(
            self.held.at[far_rows, :], self.third.at[pl.ds(2 * rows, 2 * rows), :], target,
            only=jnp.logical_not(self.inner),
        )
        self.beside_copy = send(
            self.held.at[rows_of(mate * rows, rows), :], self.third.at[pl.ds(0, rows), :], target
        )

    def pass_line(self, send):
        rows = self.held.shape[0] // 4

        @pl.when(self.inner)
        def _():
            self.outward.wait_recv()
            base = self.far * rows
            add_rows(
                self.third, 2 * rows, 2 * rows, (self.third, 2 * rows), (self.held, base)
            )

        self.passed = []
        arrives = send.count[0]
        for i in range(2):
            self.passed.append(
                send(
                    self.third.at[pl.ds((2 + i) * rows, rows), :],
                    self.third.at[pl.ds(rows, rows), :],
                    (self.grp, (self.far + i) * 2 + self.core),
                    only=self.inner,
                    arrives=arrives,
                )
            )

    def settle(self, send):
        rows = self.held.shape[0] // 4
        self.beside_copy.wait_recv()
        self.passed[0].wait_recv()
        total = self.held[rows_of(self.zed * rows, rows), :].astype(jnp.float32)
        for j in range(2):
            total = total + self.third[j * rows : (j + 1) * rows, :].astype(jnp.float32)
        self.line_sum[...] = total
        half = rows // 2
        away = pl.ds(pl.multiple_of((1 - self.core) * half, 8), half)
        self.out[:, self.column] = self.line_sum[pl.ds(pl.multiple_of(self.core * half, 8), half), :]
        self.last = send(self.line_sum.at[away, :], self.out.at[:, self.column], self.sibling)

    def drain(self):
        for copy in self.halves + self.copies + [self.beside_copy]:
            copy.wait_send()
        pl.when(jnp.logical_not(self.inner))(self.outward.wait_send)
        for copy in self.passed:
            pl.when(self.inner)(copy.wait_send)
        self.last.wait()


class HeadsSum(GroupSum):
    def __init__(self, term, other, first, near, final):
        self.term, self.other, self.first, self.near, self.final = term, other, first, near, final
        self.rows = 4 * term.shape[2]
        grp, seq, zed, self.core, self.sibling, along = place()
        self.place_in_plane(grp, seq)
        self.copies, self.halves = [], []

    def swap_quarter(self, send, quarter):
        at = pl.ds(4 * quarter, 4)
        return send(self.term.at[at, 1 - self.core], self.other.at[at], self.sibling)

    def both_cores(self, quarter):
        at = pl.ds(4 * quarter, 4)
        return (self.term[at, self.core] + self.other[at]).reshape(self.rows, -1)

    def core_sum(self, quarter):
        self.first[rows_of(quarter * self.rows, self.rows), :] = self.both_cores(quarter).astype(
            jnp.bfloat16
        )

    def total(self):
        self.halves[3].wait_recv()
        for slot in (1, 3, 4, 5):
            self.copies[slot].wait_recv()
        near = [self.near[i].astype(jnp.float32) for i in range(6)]
        total = self.both_cores(self.own) + jnp.concatenate(
            [near[1] + near[4], near[3] + near[5]], axis=0
        )
        self.final[...] = total.reshape(self.final.shape)

    def drain(self):
        for copy in self.halves + self.copies:
            copy.wait_send()


def norm_back(x, gain, grad_norm, grad_out, into, chunk):
    f32 = jnp.float32
    tokens, width = x.shape
    gain_row = gain[...].reshape(1, width)

    def one(i, sums):
        at = rows_of(i * chunk, chunk)
        vector, grad = x[at, :].astype(f32), grad_norm[at, :]
        normal, inverse = normal_parts(vector)
        pulled = norm_pull(normal, inverse, gain_row, grad)
        into[at, :] = (grad_out[at, :] + pulled).astype(into.dtype)
        return (
            sums[0] + jnp.sum(grad * normal, axis=0, keepdims=True),
            sums[1] + jnp.sum(grad, axis=0, keepdims=True),
        )

    zero = jnp.zeros((1, width), f32)
    return lax.fori_loop(0, tokens // chunk, one, (zero, zero))


def settle_small(small, vecs, rms, owner):
    width, count = small.shape[-1], vecs.shape[-1]
    total = (small[0] + small[1]) + (small[2] + small[3])
    turned = pltpu.roll(total, (width - owner * count) % width, 1)
    for i in range(4):
        vecs[i] = turned[i : i + 1, :count]
    rms[...] = jnp.sqrt(total[4:5, :3] / total[4:5, 3:4])


def layer_kernel(
    x_in, out_grad_in, w_qkv_in, w_out_in, w_up_in, w_down_in,
    gain_one_in, bias_one_in, gain_two_in, bias_two_in, span,
    block_output_out, input_grad_out, sum_qkv_out, vecs, rms, out_down_out, out_up_out, out_out_out,
    x, out_grad, w_qkv, w_out, w_up, w_down, gain_one, bias_one, gain_two, bias_two,
    block_output, input_grad, sum_qkv, out_down, out_up, out_out,
    mixed, q_all, kv_all, raw, mix_all, tot_all, norm_all, weights, totals,
    term_out, middle, normed, normed_t, mlp_out, grad_norm, grad_middle, gmix,
    first, near, held, third, mine, first_down, near_down, held_down, third_down, mine_down,
    gm_in, turned, g_all, gt_all, grad_kv, part_out, part_in, leaving, arrived,
    term, other, first_qkv, near_qkv, final, gathered, grad_query, small_a, small_b, small_c,
    load_sems, store_sems, send_sems, recv_sems,
    hop_send, hop_recv, swap_send, swap_recv, back_send, back_recv,
):
    tokens, width = x.shape
    f32, bf16 = jnp.float32, jnp.bfloat16
    grp, seq, zed, core, sibling, along = place()
    line = [(grp, along[k] * 2 + core) for k in (1, 2, 3)]
    chunks = w_up.shape[1] // width

    loads, stores = {}, []

    def store(source, target):
        stores.append(pltpu.make_async_copy(source, target, store_sems.at[len(stores)]))
        stores[-1].start()

    def load(name, source, target):
        loads[name] = pltpu.make_async_copy(source, target, load_sems.at[len(loads)])
        loads[name].start()

    load("x", x_in, x)
    small_in = (gain_one_in, bias_one_in, gain_two_in, bias_two_in)
    for i, (source, target) in enumerate(zip(small_in, (gain_one, bias_one, gain_two, bias_two))):
        load(("small", i), source, target)
    load("w_qkv", w_qkv_in, w_qkv)
    load("w_out", w_out_in, w_out)
    load("out_grad", out_grad_in, out_grad)
    for i in range(chunks):
        at = pl.ds(i * width, width)
        load(("up", i), w_up_in.at[:, at], w_up.at[:, at])
        load(("down", i), w_down_in.at[at, :], w_down.at[at, :])

    ups = [
        GroupSum(
            w_up.at[:, pl.ds(i * width, width)], first.at[i], near.at[i], held.at[i], third.at[i],
            mine.at[i], out_up.at[:, pl.ds(i * width, width)],
        )
        for i in range(chunks)
    ]
    outs = GroupSum(
        term_out, first.at[chunks], near.at[chunks], held.at[chunks], third.at[chunks],
        mine.at[chunks], out_out,
    )
    downs = [
        GroupSum(
            w_down, first_down.at[:, pl.ds(i * 128, 128)], near_down.at[i], held_down.at[i],
            third_down.at[i], mine_down.at[i], out_down, (i * 128, 128),
        )
        for i in range(width // 256)
    ]
    whole_down = GroupSum(w_down, first_down, None, None, None, None, None)
    down_swaps = []
    heads_sum = HeadsSum(term, other, first_qkv, near_qkv, final)
    across = [(k, seq) for k in (heads_sum.beside, heads_sum.above, heads_sum.across)]
    around = [(k, zed * 2 + 1 - core) for k in (heads_sum.beside, heads_sum.above, heads_sum.across)]
    partners = [sibling] + line + across + around
    greet_start(partners)
    send = sender(send_sems, recv_sems)
    attend_part(
        x, gain_one, bias_one, w_qkv, span, mixed, q_all, kv_all, raw, mix_all, tot_all, norm_all,
        weights, turned, totals, leaving, hop_send, hop_recv, swap_send, swap_recv, back_send,
        back_recv, loads, functools.partial(greet_end, partners),
    )

    pos = seq * tokens + lax.broadcasted_iota(jnp.int32, (tokens, 1), 0)
    keep = ((pos >= span[0, 0]) & (pos < span[0, 1])).astype(f32)
    loads["small", 2].wait()
    loads["small", 3].wait()
    gain_row, bias_row = gain_two[...].reshape(1, width), bias_two[...].reshape(1, width)

    def squares(value):
        return jnp.sum(keep * value * value)

    for name in ("w_out", "out_grad"):
        loads[name].wait()
    attn_out = matmul(mixed[...].reshape(width, tokens).T, w_out[...])
    attn_squares = squares(attn_out)
    middle[...] = x[...].astype(f32) + attn_out
    normed[...] = (normal_parts(middle[...])[0] * gain_row + bias_row).astype(bf16)
    normed_t[...] = normed[...].T
    mlp_out[...] = jnp.zeros((tokens, width), f32)
    grad_norm[...] = jnp.zeros((tokens, width), f32)
    for i in range(chunks):
        at = pl.ds(i * width, width)
        loads["up", i].wait()
        loads["down", i].wait()
        activated, slope = gelu_and_slope(matmul(normed[...], w_up[:, at]))
        activated = activated.astype(bf16)
        mlp_out[...] += matmul(activated, w_down[at, :])
        grad_up = (contract_cols(out_grad[...], w_down[at, :]) * slope).astype(bf16)
        grad_norm[...] += contract_cols(grad_up, w_up[:, at])
        w_up[:, at] = matmul(normed_t[...], grad_up).astype(bf16)
        ups[i].swap(send)
        w_down[at, :] = matmul(activated.T, out_grad[...]).astype(bf16)
        down_swaps.append(whole_down.swap_quarter(send, i))
        if i >= 2:
            ups[i - 2].step_one(send)
    normal, inverse = normal_parts(middle[...])
    grad = grad_norm[...]
    grad_middle[...] = out_grad[...].astype(f32) + norm_pull(normal, inverse, gain_row, grad)
    grad_attn = grad_middle[...].astype(bf16)
    gmix[...] = contract_cols(w_out[...], grad_attn).astype(bf16).reshape(gmix.shape)
    coming = []
    for h in range(3):
        for k in (1, 2, 3):
            coming.append(send(gmix.at[along[k] * 3 + h], gm_in.at[h, zed], line[k - 1]))
        gm_in[h, zed] = gmix[zed * 3 + h]
    term_out[...] = matmul(mixed[...].reshape(width, tokens), grad_attn).astype(bf16)
    outs.swap(send)
    ups[0].step_two(send)
    for copy in down_swaps:
        copy.wait_recv()
    downs[0].step_one(send)
    ups[1].step_two(send)
    downs[1].step_one(send)
    small_a[0, 2:3] = jnp.sum(grad * normal, axis=0, keepdims=True)
    small_a[0, 3:4] = jnp.sum(grad, axis=0, keepdims=True)
    output = middle[...] + mlp_out[...]
    block_output[...] = output.astype(bf16)
    store(block_output, block_output_out)
    lane = lax.broadcasted_iota(jnp.int32, (4, width), 1)
    row = jnp.zeros((4, width), f32)
    squared = (squares(output), attn_squares, squares(mlp_out[...]), jnp.sum(keep) * width)
    for i, value in enumerate(squared):
        row = jnp.where(lane == i, value, row)
    small_a[0, 4:8] = row


    def turn(h):
        def one(z, _):
            for side in range(2):
                at = pl.ds(side * tokens, tokens)
                turned[h % 2, z, at, :] = kv_all[h, z, side, 0].T
                turned[2 + h % 2, z, at, :] = kv_all[h, z, side, 1].T
            return 0

        lax.fori_loop(0, 4, one, 0)

    turn(0)
    ups[0].along_line(send)
    for z in range(4):
        leaving[z, 9] = jnp.zeros((HEAD_DIM, tokens), bf16)
    swaps, sends = [], []

    def finish(h):
        swaps[h].wait_recv()

        def merge(z, _):
            fine = valid_columns(span, (2 * z + core) * tokens, tokens)
            q, k, v, inverse, signed, terms, weight = alone_terms(raw.at[z, pl.ds(3 * h, 3)])
            g = gm_in[h, z].astype(f32)
            total = 1.0 / terms
            grad_total = -jnp.sum(g * (weight * v), axis=0, keepdims=True) * total * total
            g = (g * total).astype(bf16).astype(f32)
            grad_weight = jnp.sum(g * v, axis=0, keepdims=True)
            slope = 1.0 + (inverse * inverse) * (inverse - 1.0)
            grad_score = terms * (grad_weight * slope + grad_total * signed)
            grad_score = grad_score.astype(bf16).astype(f32)
            alone = (grad_score * k * 0.125, grad_score * q, weight * g)
            parts = [leaving[z, 3 * h].astype(f32)]
            for part in range(2):
                parts.append(grad_kv[h, z, core, part] + part_in[h, z, part].astype(f32))
            for part in range(3):
                leaving[z, 3 * h + part] = jnp.where(fine, parts[part], alone[part]).astype(bf16)
            return 0

        lax.fori_loop(0, 4, merge, 0)
        at = pl.ds(3 * h, 3)
        for k in (1, 2, 3):
            sends.append(
                send(leaving.at[along[k], at], arrived.at[:, zed * 3 + h], line[k - 1])
            )
        for part in range(3):
            arrived[part, zed * 3 + h] = leaving[zed, 3 * h + part]

    def tile_products(h, z, z_key, side):
        at = pl.ds(side * tokens, tokens)
        scores = matmul(turned[h % 2, z_key, at, :], q_all[h, z])
        return scores, matmul(turned[2 + h % 2, z_key, at, :], g_all[z])

    def tile_grads(tile, scores, grad_weights):
        z, z_key, side = tile
        inverse, signed, terms = signed_terms(scores)
        if z == z_key:
            key_pos = lax.broadcasted_iota(jnp.int32, scores.shape, 0)
            query_pos = lax.broadcasted_iota(jnp.int32, scores.shape, 1)
            seen = key_pos + side * tokens <= query_pos + core * tokens
            terms = jnp.where(seen, terms, 0.0)
        weights = (signed * terms).astype(bf16)
        slope = 1.0 + (inverse * inverse) * (inverse - 1.0)
        grad_scores = terms * (grad_weights * slope + gt_all[z] * signed)
        return weights, grad_scores.astype(bf16)

    def tile_sums(h, z, z_key, side, weights, grad_scores):
        for part, left, right in ((0, q_all[h, z], grad_scores), (1, g_all[z], weights)):
            grad = contract_cols(left, right)
            if z == z_key:
                grad_kv[h, z_key, side, part] = grad
            else:
                grad_kv[h, z_key, side, part] += grad
        grad = matmul(kv_all[h, z_key, side, 0], grad_scores)
        if z_key == 0 and side == 0:
            grad_query[...] = grad
        else:
            grad_query[...] += grad
        if z == z_key and side == 1:
            leaving[z, 3 * h] = (grad_query[...] * 0.125).astype(bf16)

    for h in range(3):
        for copy in coming[h * 3 : h * 3 + 3]:
            copy.wait_recv()

        def prepare(z, _):
            g = gm_in[h, z].astype(f32)
            total = 1.0 / tot_all[h, z]
            g_all[z] = (g * total).astype(bf16)
            gt_all[z] = -jnp.sum(g * mix_all[h, z], axis=0, keepdims=True) * total
            return 0

        lax.fori_loop(0, 4, prepare, 0)

        tiles = [(z, z_key, side) for z in range(4) for z_key in range(z + 1) for side in range(2)]
        scored, parts = {}, {}
        for step in range(len(tiles) + 2):
            if step < len(tiles):
                scored[step] = tile_products(h, *tiles[step])
            if 0 <= step - 1 < len(tiles):
                parts[step - 1] = tile_grads(tiles[step - 1], *scored.pop(step - 1))
            if step - 2 >= 0:
                tile_sums(h, *tiles[step - 2], *parts.pop(step - 2))

        def pack(z, _):
            for part in range(2):
                part_out[h, z, part] = grad_kv[h, z, 1 - core, part].astype(bf16)
            return 0

        lax.fori_loop(0, 4, pack, 0)
        swaps.append(send(part_out.at[h], part_in.at[h], sibling))
        if h == 0:
            turn(1)
            ups[1].along_line(send)
            downs[0].step_two(send)
            downs[2].step_one(send)
            ups[0].pass_line(send)
            ups[2].step_one(send)
        if h == 1:
            turn(2)
            downs[1].step_two(send)
            downs[0].along_line(send)
            ups[1].pass_line(send)
            ups[3].step_one(send)
        finish(h)

    downs[2].step_two(send)
    downs[1].along_line(send)
    outs.step_one(send)
    downs[0].pass_line(send)
    ups[2].step_two(send)

    for quarter in (heads_sum.across, heads_sum.beside, heads_sum.above, heads_sum.own):
        total = None
        for z in range(4):
            rows = norm_all[z, rows_of(quarter * (width // 4), width // 4), :]
            part = contract_cols(rows, leaving[z].reshape(10 * HEAD_DIM, tokens))
            total = part if total is None else total + part
        term[pl.ds(4 * quarter, 4)] = total.reshape((4,) + term.shape[1:])
        heads_sum.halves.append(heads_sum.swap_quarter(send, quarter))
    heads_sum.step_one(send)
    downs[2].along_line(send)
    ups[3].step_two(send)
    downs[1].pass_line(send)
    outs.step_two(send)
    ups[2].along_line(send)
    heads_sum.step_two(send)

    for copy in sends:
        copy.wait_recv()
    grads = arrived[...].reshape(3 * width, tokens)
    for i in range(width // 256):
        columns = slice(i * 256, (i + 1) * 256)
        grad_norm[:, columns] = matmul(w_qkv[columns, :], grads).T
    downs[2].pass_line(send)
    ups[3].along_line(send)
    outs.along_line(send)
    ups[2].pass_line(send)
    gain_grad, bias_grad = norm_back(x, gain_one, grad_norm, grad_middle, input_grad, 64)
    store(input_grad, input_grad_out)
    small_a[0, 0:1] = gain_grad
    small_a[0, 1:2] = bias_grad
    whose = 2 * grp + core
    small_b[pl.ds(whose, 1)] = small_a[0:1]
    planes = [
        send(small_b.at[whose], small_b.at[whose], target)
        for target in [sibling] + across + around
    ]
    ups[3].pass_line(send)
    outs.pass_line(send)
    heads_sum.total()
    gathered[pl.ds(zed, 1)] = final[pl.ds(zed, 1)]
    blocks = [send(final.at[along[k]], gathered.at[zed], line[k - 1]) for k in (1, 2, 3)]
    for copy in planes:
        copy.wait_recv()
    total = small_b[0]
    for i in range(1, 8):
        total = total + small_b[i]
    small_c[pl.ds(zed, 1)] = total.reshape(1, 8, width)
    columns = [send(small_c.at[zed], small_c.at[zed], line[k - 1]) for k in (1, 2, 3)]
    sums = ups[:2] + downs + ups[2:] + [outs]
    for each in sums:
        each.settle(send)
    for copy in blocks + columns:
        copy.wait_recv()
    for z in range(4):
        for h in range(3):
            for part in range(3):
                start = part * width + (3 * z + h) * HEAD_DIM
                sum_qkv[:, start : start + HEAD_DIM] = gathered[
                    z, :, (3 * h + part) * HEAD_DIM : (3 * h + part + 1) * HEAD_DIM
                ]
    store(sum_qkv, sum_qkv_out)
    settle_small(small_c, vecs, rms, grp * 8 + seq)
    for copy in down_swaps + coming + swaps + sends + planes + blocks + columns:
        copy.wait_send()
    for each in sums + [heads_sum]:
        each.drain()
    store(out_down, out_down_out)
    store(out_up, out_up_out)
    store(out_out, out_out_out)
    for copy in stores:
        copy.wait()


def layer(block_input, out_grad, w_qkv, w_out, w_up, w_down, vectors, span):
    f32, bf16 = jnp.float32, jnp.bfloat16
    tokens, width = block_input.shape
    hidden = w_up.shape[1]
    count = hidden // width + 1
    vmem, smem = pl.BlockSpec(memory_space=pltpu.VMEM), pl.BlockSpec(memory_space=pltpu.SMEM)
    block = (HEAD_DIM, tokens)
    own_rows, columns = width // 32, 10 * HEAD_DIM
    quarter, half = width // 4, width // 2
    copies = 11 * 3 + 4 + 15 * count + 9 + 3 + 9 + 10 + 7 + 3 + 3
    dma = pltpu.SemaphoreType.DMA
    hbm = pl.BlockSpec(memory_space=pl.ANY)
    in_hbm = [block_input, out_grad, w_qkv, w_out, w_up, w_down, *vectors]

    def sum_scratch(lead, rows):
        return [
            pltpu.VMEM(lead + (4 * rows, half), bf16),
            pltpu.VMEM(lead + (6, rows // 2, half), bf16),
            pltpu.VMEM(lead + (rows, half), bf16),
            pltpu.VMEM(lead + (rows, half), bf16),
            pltpu.VMEM(lead + (rows // 4, half), f32),
        ]

    return pl.pallas_call(
        layer_kernel,
        out_shape=[
            jax.ShapeDtypeStruct((tokens, width), bf16),
            jax.ShapeDtypeStruct((tokens, width), bf16),
            jax.ShapeDtypeStruct((own_rows, 3 * width), f32),
            jax.ShapeDtypeStruct((4, 1, own_rows), f32),
            jax.ShapeDtypeStruct((1, 3), f32),
            jax.ShapeDtypeStruct((hidden // 32, width), f32),
            jax.ShapeDtypeStruct((own_rows, hidden), f32),
            jax.ShapeDtypeStruct((own_rows, width), f32),
        ],
        in_specs=[hbm] * len(in_hbm) + [smem],
        out_specs=[hbm] * 3 + [vmem] * 2 + [hbm] * 3,
        scratch_shapes=[pltpu.VMEM(a.shape, a.dtype) for a in in_hbm]
        + [
            pltpu.VMEM((tokens, width), bf16),
            pltpu.VMEM((tokens, width), bf16),
            pltpu.VMEM((own_rows, 3 * width), f32),
            pltpu.VMEM((hidden // 32, width), f32),
            pltpu.VMEM((own_rows, hidden), f32),
            pltpu.VMEM((own_rows, width), f32),
            pltpu.VMEM((HEADS,) + block, bf16),
            pltpu.VMEM((3, 4) + block, bf16),
            pltpu.VMEM((3, 4, 2, 2) + block, bf16),
            pltpu.VMEM((4, 9) + block, bf16),
            pltpu.VMEM((3, 4) + block, f32),
            pltpu.VMEM((3, 4, 1, tokens), f32),
            pltpu.VMEM((4, width, tokens), bf16),
            pltpu.VMEM((3, 256, width), bf16),
            pltpu.VMEM((3, 4, 8, tokens), f32),
            pltpu.VMEM((width, width), bf16),
            pltpu.VMEM((tokens, width), f32),
            pltpu.VMEM((tokens, width), bf16),
            pltpu.VMEM((width, tokens), bf16),
            pltpu.VMEM((tokens, width), f32),
            pltpu.VMEM((tokens, width), f32),
            pltpu.VMEM((tokens, width), f32),
            pltpu.VMEM((HEADS,) + block, bf16),
        ]
        + sum_scratch((count,), quarter)
        + [
            pltpu.VMEM((hidden, half), bf16),
            pltpu.VMEM((3, 6, hidden // 8, 128), bf16),
            pltpu.VMEM((3, hidden // 4, 128), bf16),
            pltpu.VMEM((3, hidden // 4, 128), bf16),
            pltpu.VMEM((3, hidden // 16, 128), f32),
        ]
        + [
            pltpu.VMEM((3, 4) + block, bf16),
            pltpu.VMEM((4, 4, 2 * tokens, HEAD_DIM), bf16),
            pltpu.VMEM((4,) + block, bf16),
            pltpu.VMEM((4, 1, tokens), f32),
            pltpu.VMEM((3, 4, 2, 2) + block, f32),
            pltpu.VMEM((3, 4, 2) + block, bf16),
            pltpu.VMEM((3, 4, 2) + block, bf16),
            pltpu.VMEM((4, 10) + block, bf16),
            pltpu.VMEM((3, HEADS) + block, bf16),
            pltpu.VMEM((16, 2, own_rows, columns), f32),
            pltpu.VMEM((16, own_rows, columns), f32),
            pltpu.VMEM((16 * own_rows, columns), bf16),
            pltpu.VMEM((6, 2 * own_rows, columns), bf16),
            pltpu.VMEM((4, own_rows, columns), f32),
            pltpu.VMEM((4, own_rows, columns), f32),
            pltpu.VMEM(block, f32),
            pltpu.VMEM((1, 8, width), f32),
            pltpu.VMEM((8, 8, width), f32),
            pltpu.VMEM((4, 8, width), f32),
            dma((8 + 2 * (count - 1),)),
            dma((6,)),
            dma((copies,)),
            dma((copies,)),
            dma((2, 4, 2)),
            dma((2, 4, 2)),
            dma((8,)),
            dma((8,)),
            dma((4,)),
            dma((4,)),
        ],
        compiler_params=pltpu.CompilerParams(
            collective_id=0, has_side_effects=True, vmem_limit_bytes=63 * 2**20
        ),
    )(*in_hbm, span)


def hand_over_kernel(many, *refs):
    vecs, rms, arrays = refs[0], refs[1], refs[2 : 2 + many]
    outs, rest = refs[2 + many : 7 + 2 * many], refs[7 + 2 * many :]
    held, sems = rest[:many], rest[many]
    loads = [
        pltpu.make_async_copy(arrays[i], held[i], sems.at[0, i]) for i in range(many)
    ]
    stores = [
        pltpu.make_async_copy(held[i], outs[5 + i], sems.at[1, i]) for i in range(many)
    ]
    for load in loads:
        load.start()
    for i in range(4):
        outs[i][...] = vecs[i, 0]
    outs[4][...] = rms[0]
    for load, store in zip(loads, stores):
        load.wait()
        store.start()
    for store in stores:
        store.wait()


def hand_over(vecs, rms, arrays):
    vmem, hbm = pl.BlockSpec(memory_space=pltpu.VMEM), pl.BlockSpec(memory_space=pl.ANY)
    many, f32 = len(arrays), jnp.float32
    return pl.pallas_call(
        functools.partial(hand_over_kernel, many),
        out_shape=[jax.ShapeDtypeStruct(vecs.shape[2:], f32)] * 4
        + [jax.ShapeDtypeStruct(rms.shape[1:], f32)]
        + [jax.ShapeDtypeStruct(a.shape, a.dtype) for a in arrays],
        in_specs=[vmem] * 2 + [hbm] * many,
        out_specs=[vmem] * 5 + [hbm] * many,
        scratch_shapes=[pltpu.VMEM(a.shape, a.dtype) for a in arrays]
        + [pltpu.SemaphoreType.DMA((2, many))],
    )(vecs, rms, *arrays)


def per_device_planned(
    block_input,
    out_grad,
    seq_span,
    ln1_gain,
    ln1_bias,
    w_qkv,
    w_out,
    ln2_gain,
    ln2_bias,
    w_up,
    w_down,
):
    block_output, input_grad, sum_qkv, vecs, rms, sum_down, sum_up, sum_out = layer(
        block_input, out_grad, w_qkv, w_out, w_up, w_down,
        (ln1_gain, ln1_bias, ln2_gain, ln2_bias), seq_span,
    )
    arrays = (block_output, input_grad, sum_qkv, sum_out, sum_up, sum_down)
    gain_one, bias_one, gain_two, bias_two, rms, *arrays = hand_over(vecs, rms, arrays)
    block_output, input_grad, sum_qkv, sum_out, sum_up, sum_down = arrays
    return (
        block_output,
        input_grad,
        gain_one,
        bias_one,
        sum_qkv,
        sum_out,
        gain_two,
        bias_two,
        sum_up,
        sum_down,
        rms,
    )


def solution(mesh):
    placed = (
        P(("grp", "seq"), None),
        P(("grp", "seq"), None),
        P("grp", None),
        P(),
        P(),
        P(),
        P(),
        P(),
        P(),
        P(),
        P(),
    )
    planned = mesh.shape["grp"] == 4 and mesh.shape["seq"] == 8
    return jax.shard_map(
        per_device_planned if planned else per_device,
        mesh=mesh,
        in_specs=placed,
        out_specs=(
            P(("grp", "seq"), None),
            P(("grp", "seq"), None),
            P(("grp", "seq")),
            P(("grp", "seq")),
            P(("grp", "seq"), None),
            P(("grp", "seq"), None),
            P(("grp", "seq")),
            P(("grp", "seq")),
            P(("grp", "seq"), None),
            P(("grp", "seq"), None),
            P(),
        ),
        check_vma=False,
    )
```

```python
import functools

import jax
import jax.numpy as jnp
from jax import lax
from jax.experimental import pallas as pl
from jax.experimental.pallas import tpu as pltpu
from jax.sharding import PartitionSpec as P

D = 768
HEADS = 12
HEAD_DIM = 64
MESH = pl.DeviceIdType.MESH


epsilon = 1e-05


def passed_along(array, axis, by):
    devices = lax.axis_size(axis)
    pairs = [(i, i + by) for i in range(devices) if 0 <= i + by < devices]
    return lax.ppermute(array, axis, pairs)


def shifted(array, axis, by):
    devices = lax.axis_size(axis)
    return lax.ppermute(array, axis, [(i, (i + by) % devices) for i in range(devices)])


def layer_norm(vector, scale_vec, shift_vec):
    row_mean = jnp.mean(vector, axis=-1, keepdims=True)
    centered = vector - row_mean
    variance = jnp.mean(centered * centered, axis=-1, keepdims=True)
    return centered * lax.rsqrt(variance + epsilon) * scale_vec + shift_vec


def contract_rows(left, right):
    return lax.dot_general(
        left, right, (((0,), (0,)), ((), ())), preferred_element_type=jnp.float32
    )


def contract_cols(left, right):
    return lax.dot_general(
        left, right, (((1,), (1,)), ((), ())), preferred_element_type=jnp.float32
    )


def score_terms(queries, key_block, query_pos, key_pos, seq_first, seq_limit):
    scores = (
        jnp.einsum("qhd,khd->qhk", queries, key_block, preferred_element_type=jnp.float32) * 0.125
    )
    query_valid = (query_pos >= seq_first) & (query_pos < seq_limit)
    key_valid = (key_pos >= seq_first) & (key_pos < seq_limit)
    allowed = (key_pos[None, :] <= query_pos[:, None]) & (
        query_valid[:, None] & key_valid[None, :] | (key_pos[None, :] == query_pos[:, None])
    )
    magnitude = jnp.sqrt(scores * scores + 1.0)
    signed_part = scores / magnitude
    exp_terms = jnp.where(allowed[:, None, :], jnp.exp(magnitude), 0.0)
    return (magnitude, signed_part, exp_terms)


def split_pair(kv_pair):
    count_rows = kv_pair.shape[0]
    key_block = kv_pair[:, :D].reshape(count_rows, HEADS, HEAD_DIM)
    value_block = kv_pair[:, D:].reshape(count_rows, HEADS, HEAD_DIM)
    return (key_block, value_block)


def forward_block(running, kv_pair, key_start, queries, query_pos, seq_first, seq_limit):
    totals, unnorm = running
    key_block, value_block = split_pair(kv_pair)
    key_pos = key_start + jnp.arange(kv_pair.shape[0], dtype=jnp.int32)
    magnitude, signed_part, exp_terms = score_terms(
        queries, key_block, query_pos, key_pos, seq_first, seq_limit
    )
    weights = (signed_part * exp_terms).astype(jnp.bfloat16)
    totals = totals + jnp.sum(exp_terms, axis=-1)
    unnorm = unnorm + jnp.einsum(
        "qhk,khd->qhd", weights, value_block, preferred_element_type=jnp.float32
    )
    return (totals, unnorm)


def grad_core(
    kv_pair, key_start, queries, query_pos, seq_first, seq_limit, grad_unnorm, grad_totals
):
    key_block, value_block = split_pair(kv_pair)
    key_pos = key_start + jnp.arange(kv_pair.shape[0], dtype=jnp.int32)
    magnitude, signed_part, exp_terms = score_terms(
        queries, key_block, query_pos, key_pos, seq_first, seq_limit
    )
    weights = (signed_part * exp_terms).astype(jnp.bfloat16)
    grad_weights = jnp.einsum(
        "qhd,khd->qhk", grad_unnorm, value_block, preferred_element_type=jnp.float32
    )
    grad_scores = (
        grad_weights * exp_terms / (magnitude * magnitude * magnitude)
        + (grad_weights * signed_part + grad_totals[:, :, None]) * exp_terms * signed_part
    )
    return (key_block, weights, grad_scores.astype(jnp.bfloat16))


def backward_block(
    kv_pair, key_start, queries, query_pos, seq_first, seq_limit, grad_unnorm, grad_totals
):
    key_block, weights, grad_scores = grad_core(
        kv_pair, key_start, queries, query_pos, seq_first, seq_limit, grad_unnorm, grad_totals
    )
    count_rows = kv_pair.shape[0]
    grad_query = (
        jnp.einsum("qhk,khd->qhd", grad_scores, key_block, preferred_element_type=jnp.float32)
        * 0.125
    )
    grad_key = (
        jnp.einsum("qhk,qhd->khd", grad_scores, queries, preferred_element_type=jnp.float32) * 0.125
    )
    grad_value = jnp.einsum(
        "qhk,qhd->khd", weights, grad_unnorm, preferred_element_type=jnp.float32
    )
    grad_pair = jnp.concatenate(
        [grad_key.reshape(count_rows, D), grad_value.reshape(count_rows, D)], axis=1
    )
    return (grad_query, grad_pair)


def per_device(
    block_input,
    out_grad,
    seq_span,
    ln1_gain,
    ln1_bias,
    w_qkv,
    w_out,
    ln2_gain,
    ln2_bias,
    w_up,
    w_down,
):
    tok_rows = block_input.shape[0]
    feat_width = block_input.shape[1]
    seq_count = lax.axis_size("seq")
    seq_index = lax.axis_index("seq")
    query_pos = seq_index * tok_rows + jnp.arange(tok_rows, dtype=jnp.int32)
    query_last = query_pos[tok_rows - 1]
    seq_first = seq_span[0, 0]
    seq_limit = seq_span[0, 1]
    inputs = block_input.astype(jnp.float32)
    normed = layer_norm(inputs, ln1_gain, ln1_bias).astype(jnp.bfloat16)
    proj_qkv = jnp.dot(normed, w_qkv, preferred_element_type=jnp.float32).astype(jnp.bfloat16)
    queries = proj_qkv[:, :feat_width].reshape(tok_rows, HEADS, HEAD_DIM)
    kv_pair = proj_qkv[:, feat_width:]

    def visit_block(running, shard_rows, key_start):
        return lax.cond(
            key_start <= query_last,
            lambda state_in: forward_block(
                state_in, shard_rows, key_start, queries, query_pos, seq_first, seq_limit
            ),
            lambda state_in: state_in,
            running,
        )

    empty = (
        jnp.zeros((tok_rows, HEADS), jnp.float32),
        jnp.zeros((tok_rows, HEADS, HEAD_DIM), jnp.float32),
    )
    first_state = visit_block(empty, kv_pair, seq_index * tok_rows)

    def forward_hop(hop_count, loop_state):
        moving, running = loop_state
        moving = passed_along(moving, "seq", 1)
        source = (seq_index - hop_count) % seq_count
        return (moving, visit_block(running, moving, source * tok_rows))

    _, (totals, unnorm) = lax.fori_loop(1, seq_count, forward_hop, (kv_pair, first_state))
    mixed_heads = (unnorm / totals[:, :, None]).reshape(tok_rows, feat_width).astype(jnp.bfloat16)
    attn_out = jnp.dot(mixed_heads, w_out, preferred_element_type=jnp.float32)
    middle = inputs + attn_out
    normed_two = layer_norm(middle, ln2_gain, ln2_bias).astype(jnp.bfloat16)
    up_proj = jnp.dot(normed_two, w_up, preferred_element_type=jnp.float32)
    activated = jax.nn.gelu(up_proj, approximate=True).astype(jnp.bfloat16)
    mlp_out = jnp.dot(activated, w_down, preferred_element_type=jnp.float32)
    output = middle + mlp_out
    valid_rows = ((query_pos >= seq_first) & (query_pos < seq_limit)).astype(jnp.float32)[:, None]
    rms_parts = lax.psum(
        (
            jnp.sum(valid_rows * output * output),
            jnp.sum(valid_rows * attn_out * attn_out),
            jnp.sum(valid_rows * mlp_out * mlp_out),
            jnp.sum(valid_rows) * feat_width,
        ),
        ("grp", "seq"),
    )
    rms_stats = jnp.sqrt(jnp.stack([rms_parts[0], rms_parts[1], rms_parts[2]]) / rms_parts[3])
    grad_w_down = contract_rows(activated, out_grad)
    grad_activated = contract_cols(out_grad, w_down)
    _, gelu_pull = jax.vjp(lambda pre_act: jax.nn.gelu(pre_act, approximate=True), up_proj)
    grad_up = gelu_pull(grad_activated)[0].astype(jnp.bfloat16)
    grad_w_up = contract_rows(normed_two, grad_up)
    grad_norm_two = contract_cols(grad_up, w_up)
    _, norm_pull_two = jax.vjp(layer_norm, middle, ln2_gain, ln2_bias)
    grad_mid_norm, grad_gain_two, grad_bias_two = norm_pull_two(grad_norm_two)
    grad_middle = out_grad.astype(jnp.float32) + grad_mid_norm
    grad_attn = grad_middle.astype(jnp.bfloat16)
    grad_w_out = contract_rows(mixed_heads, grad_attn)
    grad_mixed = contract_cols(grad_attn, w_out).reshape(tok_rows, HEADS, HEAD_DIM)
    grad_unnorm = (grad_mixed / totals[:, :, None]).astype(jnp.bfloat16)
    grad_totals = -jnp.sum(grad_mixed * unnorm, axis=-1) / (totals * totals)

    def back_block(grad_run, shard_rows, key_start):

        def compute_block(grad_in):
            grad_query, grad_pair = backward_block(
                shard_rows,
                key_start,
                queries,
                query_pos,
                seq_first,
                seq_limit,
                grad_unnorm,
                grad_totals,
            )
            return (grad_in + grad_query, grad_pair)

        def skip_block(grad_in):
            return (grad_in, jnp.zeros((shard_rows.shape[0], 2 * feat_width), jnp.float32))

        return lax.cond(key_start <= query_last, compute_block, skip_block, grad_run)

    grad_start = jnp.zeros((tok_rows, HEADS, HEAD_DIM), jnp.float32)
    grad_queries, local_terms = back_block(grad_start, kv_pair, seq_index * tok_rows)

    def backward_hop(hop_count, loop_state):
        moving, grad_acc, grad_run = loop_state
        moving = passed_along(moving, "seq", 1)
        grad_acc = shifted(grad_acc.astype(jnp.bfloat16), "seq", 1).astype(grad_acc.dtype)
        source = (seq_index - hop_count) % seq_count
        grad_run, new_terms = back_block(grad_run, moving, source * tok_rows)
        return (moving, grad_acc + new_terms, grad_run)

    _, grad_acc, grad_queries = lax.fori_loop(
        1, seq_count, backward_hop, (kv_pair, local_terms, grad_queries)
    )
    grad_kv = shifted(grad_acc.astype(jnp.bfloat16), "seq", 1).astype(grad_acc.dtype)
    grad_qkv = jnp.concatenate(
        [grad_queries.reshape(tok_rows, feat_width), grad_kv], axis=1
    ).astype(jnp.bfloat16)
    grad_w_qkv = contract_rows(normed, grad_qkv)
    grad_norm_one = contract_cols(grad_qkv, w_qkv)
    _, norm_pull_one = jax.vjp(layer_norm, inputs, ln1_gain, ln1_bias)
    grad_in_norm, grad_gain_one, grad_bias_one = norm_pull_one(grad_norm_one)
    input_grad = (grad_middle + grad_in_norm).astype(jnp.bfloat16)
    summed = (
        lax.psum_scatter(grad_gain_one, ("grp", "seq"), scatter_dimension=0, tiled=True),
        lax.psum_scatter(grad_bias_one, ("grp", "seq"), scatter_dimension=0, tiled=True),
        lax.psum_scatter(grad_w_qkv, ("grp", "seq"), scatter_dimension=0, tiled=True),
        lax.psum_scatter(grad_w_out, ("grp", "seq"), scatter_dimension=0, tiled=True),
        lax.psum_scatter(grad_gain_two, ("grp", "seq"), scatter_dimension=0, tiled=True),
        lax.psum_scatter(grad_bias_two, ("grp", "seq"), scatter_dimension=0, tiled=True),
        lax.psum_scatter(grad_w_up, ("grp", "seq"), scatter_dimension=0, tiled=True),
        lax.psum_scatter(grad_w_down, ("grp", "seq"), scatter_dimension=0, tiled=True),
    )
    return (
        output.astype(jnp.bfloat16),
        input_grad,
        summed[0],
        summed[1],
        summed[2],
        summed[3],
        summed[4],
        summed[5],
        summed[6],
        summed[7],
        rms_stats,
    )


def rows_of(start, count):
    return pl.ds(pl.multiple_of(start, 16), count)


def matmul(left, right):
    return jnp.dot(left, right, preferred_element_type=jnp.float32)


def signed_terms(scores):
    square = scores * scores + 1.0
    inverse = lax.rsqrt(square)
    return inverse, scores * inverse, jnp.exp(square * inverse)


def valid_columns(span, start, count):
    pos = start + lax.broadcasted_iota(jnp.int32, (1, count), 1)
    return (pos >= span[0, 0]) & (pos < span[0, 1])


def greet_start(partners):
    for partner in partners:
        pl.semaphore_signal(
            pltpu.get_barrier_semaphore(), inc=1, device_id=partner, device_id_type=MESH
        )


def greet_end(partners):
    pl.semaphore_wait(pltpu.get_barrier_semaphore(), len(partners))


def sender(send_sems, recv_sems):
    count = [0]

    def send(src, dst, target, only=None, arrives=None):
        slot = count[0]
        count[0] += 1
        copy = pltpu.make_async_remote_copy(
            src_ref=src, dst_ref=dst, send_sem=send_sems.at[slot],
            recv_sem=recv_sems.at[slot if arrives is None else arrives],
            device_id=target, device_id_type=MESH,
        )
        if only is None:
            copy.start()
        else:
            pl.when(only)(copy.start)
        return copy

    send.count = count
    return send


def place():
    grp, seq = lax.axis_index("grp"), lax.axis_index("seq")
    zed, core = seq // 2, seq % 2
    sibling = (grp, zed * 2 + 1 - core)
    along = [(zed + k) % 4 for k in range(4)]
    return grp, seq, zed, core, sibling, along


def alone_terms(raw):
    q, k, v = (raw[part].astype(jnp.float32) for part in range(3))
    inverse, signed, terms = signed_terms(jnp.sum(q * k, axis=0, keepdims=True))
    weight = (signed * terms).astype(jnp.bfloat16).astype(jnp.float32)
    return q, k, v, inverse, signed, terms, weight


def attend_part(
    x, gain_one, bias_one, w_qkv, span, mixed, q_all, kv_all, raw, mix_all, tot_all, norm_all,
    weights, keys, totals, leaving, hop_send, hop_recv, swap_send, swap_recv, back_send, back_recv,
    loads, greet_end,
):
    tokens, width = x.shape
    f32, bf16 = jnp.float32, jnp.bfloat16
    grp, seq, zed, core, sibling, along = place()

    start = pl.multiple_of(zed * 192 // 128 * 128, 128)
    inside = pl.ds(pl.multiple_of(zed % 2 * HEAD_DIM, HEAD_DIM), 3 * HEAD_DIM)
    loads["x"].wait()
    vector = x[...].astype(f32)
    centered = vector - jnp.mean(vector, axis=-1, keepdims=True)
    variance = jnp.mean(centered * centered, axis=-1, keepdims=True)
    normed = (
        centered * lax.rsqrt(variance + epsilon) * gain_one[...].reshape(1, width)
        + bias_one[...].reshape(1, width)
    ).astype(bf16)
    norm_all[zed] = normed.T
    greet_end()

    halves = [pl.ds(half * (width // 2), width // 2) for half in range(2)]

    def hop(step, side, half):
        towards = 1 - 2 * side
        block = zed - towards * step
        runs = (block >= 0) & (block < 4) & (zed + towards >= 0) & (zed + towards < 4)
        copy = pltpu.make_async_remote_copy(
            src_ref=norm_all.at[block, halves[half]], dst_ref=norm_all.at[block, halves[half]],
            send_sem=hop_send.at[side, step, half], recv_sem=hop_recv.at[side, step, half],
            device_id=(grp, (zed + towards) * 2 + core), device_id_type=MESH,
        )
        return runs, copy

    for half in range(2):
        for side in range(2):
            runs, copy = hop(0, side, half)
            pl.when(runs)(copy.start)
    loads["w_qkv"].wait()
    for part in range(3):
        at = pl.ds(pl.multiple_of(part * width + start, 128), 256)
        weights[part] = w_qkv[:, at].T
    no_score = signed_terms(jnp.zeros((1, tokens), f32))[2]
    extra = span[0, 0].astype(f32) * no_score
    mix_all[...] = jnp.zeros(mix_all.shape, f32)
    totals[...] = jnp.zeros(totals.shape, f32)

    def swap(block, slot):
        return pltpu.make_async_remote_copy(
            src_ref=kv_all.at[:, block, core], dst_ref=kv_all.at[:, block, core],
            send_sem=swap_send.at[slot], recv_sem=swap_recv.at[slot],
            device_id=sibling, device_id_type=MESH,
        )

    def project(block, slot):
        keep = valid_columns(span, (2 * block + core) * tokens, tokens).astype(f32)
        for part in range(3):
            heads = matmul(weights[part, inside, :], norm_all[block])
            if part == 0:
                heads = heads * 0.125
            for h in range(3):
                one = heads[h * HEAD_DIM : (h + 1) * HEAD_DIM]
                raw[block, 3 * h + part] = one.astype(bf16)
                if part == 0:
                    q_all[h, block] = (one * keep).astype(bf16)
                else:
                    kv_all[h, block, core, part - 1] = (one * keep).astype(bf16)
        swap(block, slot).start()

    def turn(block, slot):
        swap(block, slot).wait_recv()
        for h in range(3):
            for side in range(2):
                keys[h, block, side * tokens : (side + 1) * tokens, :] = kv_all[h, block, side, 0].T

    def pair(block, other, last):
        tiles = [(h, side) for h in range(3) for side in range(2)]
        total = [totals[h, block] for h in range(3)]
        blend = [mix_all[h, block] for h in range(3)]
        scored, weights = {}, {}
        for step in range(len(tiles) + 2):
            if step < len(tiles):
                h, side = tiles[step]
                at = pl.ds(side * tokens, tokens)
                scored[step] = matmul(keys[h, other, at, :], q_all[h, block])
            if 0 <= step - 1 < len(tiles):
                h, side = tiles[step - 1]
                scores = scored.pop(step - 1)
                _, signed, terms = signed_terms(scores)
                if last:
                    key_pos = lax.broadcasted_iota(jnp.int32, scores.shape, 0)
                    query_pos = lax.broadcasted_iota(jnp.int32, scores.shape, 1)
                    seen = key_pos + side * tokens <= query_pos + core * tokens
                    terms = jnp.where(seen, terms, 0.0)
                total[h] = total[h] + jnp.sum(terms.reshape(tokens // 8, 8, tokens), axis=0)
                weights[step - 1] = (signed * terms).astype(bf16)
            if step - 2 >= 0:
                h, side = tiles[step - 2]
                blend[h] = blend[h] + matmul(kv_all[h, other, side, 1], weights.pop(step - 2))
        for h in range(3):
            totals[h, block], mix_all[h, block] = total[h], blend[h]

    def back(block):
        return pltpu.make_async_remote_copy(
            src_ref=leaving.at[block, pl.ds(0, 3)], dst_ref=mixed.at[pl.ds(3 * zed, 3)],
            send_sem=back_send.at[block], recv_sem=back_recv.at[zed],
            device_id=(grp, block * 2 + core), device_id_type=MESH,
        )

    def complete(block):
        fine = valid_columns(span, (2 * block + core) * tokens, tokens)
        for h in range(3):
            total = jnp.sum(totals[h, block], axis=0, keepdims=True) - extra
            total = jnp.where(fine, total, 1.0)
            blend = mix_all[h, block] / total
            mix_all[h, block] = blend
            tot_all[h, block] = total
            _, _, v, _, _, terms, weight = alone_terms(raw.at[block, pl.ds(3 * h, 3)])
            leaving[block, h] = jnp.where(fine, blend, weight * v / terms).astype(bf16)

        @pl.when(block != zed)
        def _():
            back(block).start()

        @pl.when(block == zed)
        def _():
            mixed[pl.ds(3 * zed, 3)] = leaving[zed, 0:3]

    project(zed, 0)
    turn(zed, 0)
    pair(zed, zed, True)

    @pl.when(zed == 0)
    def _():
        complete(0)

    def step(d, _):
        low, high = zed - d, zed + d
        for half in range(2):
            for side, block in ((0, low), (1, high)):

                @pl.when((block >= 0) & (block < 4))
                def _():
                    towards = 1 - 2 * side
                    part = norm_all.at[block, halves[half]]
                    pltpu.make_async_remote_copy(
                        src_ref=part, dst_ref=part, send_sem=hop_send.at[side, d - 1, half],
                        recv_sem=hop_recv.at[side, d - 1, half],
                        device_id=(grp, (zed - towards) * 2 + core), device_id_type=MESH,
                    ).wait_recv()
                    runs, copy = hop(d, side, half)
                    pl.when(runs)(copy.start)
                    if half == 1:
                        project(block, 2 * d + side)

        @pl.when(high < 4)
        def _():
            lax.fori_loop(jnp.maximum(low + 1, 0), high, lambda j, _: (pair(high, j, False), 0)[1], 0)
            turn(high, 2 * d + 1)
            pair(high, high, True)

        @pl.when(low >= 0)
        def _():
            turn(low, 2 * d)
            pair(low, low, True)

            @pl.when(high < 4)
            def _():
                pair(high, low, False)

            pl.when(low == 0)(lambda: complete(low))

            def later(i, _):
                pair(i, low, False)
                pl.when(low == 0)(lambda: complete(i))
                return 0

            lax.fori_loop(low + 1, jnp.minimum(high, 4), later, 0)

        @pl.when((high < 4) & (low <= 0))
        def _():
            complete(high)

        return 0

    lax.fori_loop(1, 4, step, 0)

    for k in (1, 2, 3):
        back(along[k]).wait_send()
        pltpu.make_async_remote_copy(
            src_ref=leaving.at[zed, pl.ds(0, 3)], dst_ref=mixed.at[pl.ds(3 * along[k], 3)],
            send_sem=back_send.at[zed], recv_sem=back_recv.at[along[k]],
            device_id=(grp, along[k] * 2 + core), device_id_type=MESH,
        ).wait_recv()
    for d in range(4):
        for side in range(2):
            for half in range(2):
                runs, copy = hop(d, side, half)
                pl.when(runs)(copy.wait_send)
            if d > 0 or side == 0:
                block = zed + (2 * side - 1) * d
                pl.when((block >= 0) & (block < 4))(swap(block, 2 * d + side).wait_send)


def gelu_and_slope(u):
    root = 0.7978845608028654
    square = u * u
    bent = jnp.tanh(root * (u + 0.044715 * (square * u)))
    half = 0.5 * (1.0 + bent)
    slope = half + 0.5 * u * (1.0 - bent * bent) * (root * (1.0 + 0.134145 * square))
    return u * half, slope


def normal_parts(vector):
    centered = vector - jnp.mean(vector, axis=-1, keepdims=True)
    variance = jnp.mean(centered * centered, axis=-1, keepdims=True)
    inverse = lax.rsqrt(variance + epsilon)
    return centered * inverse, inverse


def norm_pull(normal, inverse, gain, grad):
    scaled = grad * gain
    along_normal = jnp.mean(scaled * normal, axis=-1, keepdims=True)
    return inverse * (scaled - jnp.mean(scaled, axis=-1, keepdims=True) - normal * along_normal)


def add_rows(into, base, count, *terms):
    chunk = 96 if count % 96 == 0 else 48

    def add(i, _):
        total = None
        for ref, start in terms:
            term = ref[rows_of(start + i * chunk, chunk), :].astype(jnp.float32)
            total = term if total is None else total + term
        into[rows_of(base + i * chunk, chunk), :] = total.astype(jnp.bfloat16)
        return 0

    lax.fori_loop(0, count // chunk, add, 0)


class GroupSum:
    def __init__(self, term, first, near, held, third, mine, out, part=None):
        self.term, self.first, self.near, self.held = term, first, near, held
        self.third, self.line_sum, self.out = third, mine, out
        self.rows, half = term.shape[0] // 4, term.shape[1] // 2
        start, count = part or (0, half)
        grp, seq, zed, core, sibling, along = place()
        self.place_in_plane(grp, seq)
        self.sibling, self.grp, self.zed, self.core = sibling, grp, zed, core
        self.column = pl.ds(pl.multiple_of(core * half + start, 128), count)
        self.mine = term.at[:, self.column]
        self.away = pl.ds(pl.multiple_of((1 - core) * half, 128), half)
        self.halves, self.copies = [], []

    def place_in_plane(self, grp, seq):
        y, x = grp // 2, grp % 2
        self.own, self.beside, self.above = grp, y * 2 + 1 - x, (1 - y) * 2 + x
        self.across = (1 - y) * 2 + 1 - x
        self.to_x, self.to_y = (self.beside, seq), (self.above, seq)

    def swap_quarter(self, send, quarter):
        at = rows_of(quarter * self.rows, self.rows)
        return send(self.term.at[at, self.away], self.first.at[at, :], self.sibling)

    def swap(self, send):
        for quarter in (self.across, self.beside, self.above, self.own):
            self.halves.append(self.swap_quarter(send, quarter))

    def part(self, quarter, half):
        return rows_of(quarter * self.rows + half * (self.rows // 2), self.rows // 2)

    def pass_on(self, send, quarter, half, slot, target):
        self.copies.append(
            send(self.first.at[self.part(quarter, half), :], self.near.at[slot], target)
        )

    def core_sum(self, quarter):
        base = quarter * self.rows
        add_rows(self.first, base, self.rows, (self.mine, base), (self.first, base))

    def step_one(self, send):
        steps = (
            (self.across, ((0, 0, self.to_x), (1, 2, self.to_y))),
            (self.beside, ((0, 1, self.to_x),)),
            (self.above, ((1, 3, self.to_y),)),
        )
        for i, (quarter, passes) in enumerate(steps):
            if self.halves:
                self.halves[i].wait_recv()
            self.core_sum(quarter)
            for half, slot, target in passes:
                self.pass_on(send, quarter, half, slot, target)
        self.copies = [self.copies[i] for i in (0, 2, 1, 3)]

    def step_two(self, send):
        half = self.rows // 2
        for slot, quarter, side, target in (
            (0, self.above, 0, self.to_y),
            (2, self.beside, 1, self.to_x),
        ):
            base = quarter * self.rows + side * half
            self.copies[slot].wait_recv()
            add_rows(self.first, base, half, (self.first, base), (self.near.at[slot], 0))
            self.pass_on(send, quarter, side, 4 + side, target)

    def total(self):
        half = self.rows // 2
        if self.halves:
            self.halves[3].wait_recv()
        for slot in (1, 3, 4, 5):
            self.copies[slot].wait_recv()
        for side, one, two in ((0, 1, 4), (1, 3, 5)):
            base = self.own * self.rows + side * half
            add_rows(
                self.held, side * half, half, (self.mine, base), (self.first, base),
                (self.near.at[one], 0), (self.near.at[two], 0),
            )

    def along_line(self, send):
        self.total()
        rows = self.held.shape[0] // 4
        self.inner = (self.zed == 1) | (self.zed == 2)
        mate = self.zed + 1 - 2 * (self.zed % 2)
        self.far = (1 - self.zed // 2) * 2
        target = (self.grp, mate * 2 + self.core)
        far_rows = rows_of(self.far * rows, 2 * rows)
        self.outward = send(
            self.held.at[far_rows, :], self.third.at[pl.ds(2 * rows, 2 * rows), :], target,
            only=jnp.logical_not(self.inner),
        )
        self.beside_copy = send(
            self.held.at[rows_of(mate * rows, rows), :], self.third.at[pl.ds(0, rows), :], target
        )

    def pass_line(self, send):
        rows = self.held.shape[0] // 4

        @pl.when(self.inner)
        def _():
            self.outward.wait_recv()
            base = self.far * rows
            add_rows(
                self.third, 2 * rows, 2 * rows, (self.third, 2 * rows), (self.held, base)
            )

        self.passed = []
        arrives = send.count[0]
        for i in range(2):
            self.passed.append(
                send(
                    self.third.at[pl.ds((2 + i) * rows, rows), :],
                    self.third.at[pl.ds(rows, rows), :],
                    (self.grp, (self.far + i) * 2 + self.core),
                    only=self.inner,
                    arrives=arrives,
                )
            )

    def settle(self, send):
        rows = self.held.shape[0] // 4
        self.beside_copy.wait_recv()
        self.passed[0].wait_recv()
        total = self.held[rows_of(self.zed * rows, rows), :].astype(jnp.float32)
        for j in range(2):
            total = total + self.third[j * rows : (j + 1) * rows, :].astype(jnp.float32)
        self.line_sum[...] = total
        half = rows // 2
        away = pl.ds(pl.multiple_of((1 - self.core) * half, 8), half)
        self.out[:, self.column] = self.line_sum[pl.ds(pl.multiple_of(self.core * half, 8), half), :]
        self.last = send(self.line_sum.at[away, :], self.out.at[:, self.column], self.sibling)

    def drain(self):
        for copy in self.halves + self.copies + [self.beside_copy]:
            copy.wait_send()
        pl.when(jnp.logical_not(self.inner))(self.outward.wait_send)
        for copy in self.passed:
            pl.when(self.inner)(copy.wait_send)
        self.last.wait()


class HeadsSum(GroupSum):
    def __init__(self, term, other, first, near, final):
        self.term, self.other, self.first, self.near, self.final = term, other, first, near, final
        self.rows = 4 * term.shape[2]
        grp, seq, zed, self.core, self.sibling, along = place()
        self.place_in_plane(grp, seq)
        self.copies, self.halves = [], []

    def swap_quarter(self, send, quarter):
        at = pl.ds(4 * quarter, 4)
        return send(self.term.at[at, 1 - self.core], self.other.at[at], self.sibling)

    def both_cores(self, quarter):
        at = pl.ds(4 * quarter, 4)
        return (self.term[at, self.core] + self.other[at]).reshape(self.rows, -1)

    def core_sum(self, quarter):
        self.first[rows_of(quarter * self.rows, self.rows), :] = self.both_cores(quarter).astype(
            jnp.bfloat16
        )

    def total(self):
        self.halves[3].wait_recv()
        for slot in (1, 3, 4, 5):
            self.copies[slot].wait_recv()
        near = [self.near[i].astype(jnp.float32) for i in range(6)]
        total = self.both_cores(self.own) + jnp.concatenate(
            [near[1] + near[4], near[3] + near[5]], axis=0
        )
        self.final[...] = total.reshape(self.final.shape)

    def drain(self):
        for copy in self.halves + self.copies:
            copy.wait_send()


def norm_back(x, gain, grad_norm, grad_out, into, chunk):
    f32 = jnp.float32
    tokens, width = x.shape
    gain_row = gain[...].reshape(1, width)

    def one(i, sums):
        at = rows_of(i * chunk, chunk)
        vector, grad = x[at, :].astype(f32), grad_norm[at, :]
        normal, inverse = normal_parts(vector)
        pulled = norm_pull(normal, inverse, gain_row, grad)
        into[at, :] = (grad_out[at, :] + pulled).astype(into.dtype)
        return (
            sums[0] + jnp.sum(grad * normal, axis=0, keepdims=True),
            sums[1] + jnp.sum(grad, axis=0, keepdims=True),
        )

    zero = jnp.zeros((1, width), f32)
    return lax.fori_loop(0, tokens // chunk, one, (zero, zero))


def settle_small(small, vecs, rms, owner):
    width, count = small.shape[-1], vecs.shape[-1]
    total = (small[0] + small[1]) + (small[2] + small[3])
    turned = pltpu.roll(total, (width - owner * count) % width, 1)
    for i in range(4):
        vecs[i] = turned[i : i + 1, :count]
    rms[...] = jnp.sqrt(total[4:5, :3] / total[4:5, 3:4])


def layer_kernel(
    x_in, out_grad_in, w_qkv_in, w_out_in, w_up_in, w_down_in,
    gain_one, bias_one, gain_two, bias_two, span,
    block_output, input_grad, sum_qkv, vecs, rms, out_down, out_up, out_out,
    x, out_grad, w_qkv, w_out, w_up, w_down,
    mixed, q_all, kv_all, raw, mix_all, tot_all, norm_all, weights, totals,
    term_out, middle, normed, normed_t, mlp_out, grad_norm, grad_middle, gmix,
    first, near, held, third, mine, first_down, near_down, held_down, third_down, mine_down,
    gm_in, turned, g_all, gt_all, grad_kv, part_out, part_in, leaving, arrived,
    term, other, first_qkv, near_qkv, final, gathered, grad_query, small_a, small_b, small_c,
    load_sems, send_sems, recv_sems,
    hop_send, hop_recv, swap_send, swap_recv, back_send, back_recv,
):
    tokens, width = x.shape
    f32, bf16 = jnp.float32, jnp.bfloat16
    grp, seq, zed, core, sibling, along = place()
    line = [(grp, along[k] * 2 + core) for k in (1, 2, 3)]
    chunks = w_up.shape[1] // width

    loads = {}

    def load(name, source, target):
        loads[name] = pltpu.make_async_copy(source, target, load_sems.at[len(loads)])
        loads[name].start()

    load("x", x_in, x)
    load("w_qkv", w_qkv_in, w_qkv)
    load("w_out", w_out_in, w_out)
    load("out_grad", out_grad_in, out_grad)
    for i in range(chunks):
        at = pl.ds(i * width, width)
        load(("up", i), w_up_in.at[:, at], w_up.at[:, at])
        load(("down", i), w_down_in.at[at, :], w_down.at[at, :])

    ups = [
        GroupSum(
            w_up.at[:, pl.ds(i * width, width)], first.at[i], near.at[i], held.at[i], third.at[i],
            mine.at[i], out_up.at[:, pl.ds(i * width, width)],
        )
        for i in range(chunks)
    ]
    outs = GroupSum(
        term_out, first.at[chunks], near.at[chunks], held.at[chunks], third.at[chunks],
        mine.at[chunks], out_out,
    )
    downs = [
        GroupSum(
            w_down, first_down.at[:, pl.ds(i * 128, 128)], near_down.at[i], held_down.at[i],
            third_down.at[i], mine_down.at[i], out_down, (i * 128, 128),
        )
        for i in range(width // 256)
    ]
    whole_down = GroupSum(w_down, first_down, None, None, None, None, None)
    down_swaps = []
    heads_sum = HeadsSum(term, other, first_qkv, near_qkv, final)
    across = [(k, seq) for k in (heads_sum.beside, heads_sum.above, heads_sum.across)]
    around = [(k, zed * 2 + 1 - core) for k in (heads_sum.beside, heads_sum.above, heads_sum.across)]
    partners = [sibling] + line + across + around
    greet_start(partners)
    send = sender(send_sems, recv_sems)
    attend_part(
        x, gain_one, bias_one, w_qkv, span, mixed, q_all, kv_all, raw, mix_all, tot_all, norm_all,
        weights, turned, totals, leaving, hop_send, hop_recv, swap_send, swap_recv, back_send,
        back_recv, loads, functools.partial(greet_end, partners),
    )

    pos = seq * tokens + lax.broadcasted_iota(jnp.int32, (tokens, 1), 0)
    keep = ((pos >= span[0, 0]) & (pos < span[0, 1])).astype(f32)
    gain_row, bias_row = gain_two[...].reshape(1, width), bias_two[...].reshape(1, width)

    def squares(value):
        return jnp.sum(keep * value * value)

    for name in ("w_out", "out_grad"):
        loads[name].wait()
    attn_out = matmul(mixed[...].reshape(width, tokens).T, w_out[...])
    attn_squares = squares(attn_out)
    middle[...] = x[...].astype(f32) + attn_out
    normed[...] = (normal_parts(middle[...])[0] * gain_row + bias_row).astype(bf16)
    normed_t[...] = normed[...].T
    mlp_out[...] = jnp.zeros((tokens, width), f32)
    grad_norm[...] = jnp.zeros((tokens, width), f32)
    for i in range(chunks):
        at = pl.ds(i * width, width)
        loads["up", i].wait()
        loads["down", i].wait()
        activated, slope = gelu_and_slope(matmul(normed[...], w_up[:, at]))
        activated = activated.astype(bf16)
        mlp_out[...] += matmul(activated, w_down[at, :])
        grad_up = (contract_cols(out_grad[...], w_down[at, :]) * slope).astype(bf16)
        grad_norm[...] += contract_cols(grad_up, w_up[:, at])
        w_up[:, at] = matmul(normed_t[...], grad_up).astype(bf16)
        ups[i].swap(send)
        w_down[at, :] = matmul(activated.T, out_grad[...]).astype(bf16)
        down_swaps.append(whole_down.swap_quarter(send, i))
        if i >= 2:
            ups[i - 2].step_one(send)
    normal, inverse = normal_parts(middle[...])
    grad = grad_norm[...]
    grad_middle[...] = out_grad[...].astype(f32) + norm_pull(normal, inverse, gain_row, grad)
    grad_attn = grad_middle[...].astype(bf16)
    gmix[...] = contract_cols(w_out[...], grad_attn).astype(bf16).reshape(gmix.shape)
    coming = []
    for h in range(3):
        for k in (1, 2, 3):
            coming.append(send(gmix.at[along[k] * 3 + h], gm_in.at[h, zed], line[k - 1]))
        gm_in[h, zed] = gmix[zed * 3 + h]
    term_out[...] = matmul(mixed[...].reshape(width, tokens), grad_attn).astype(bf16)
    outs.swap(send)
    ups[0].step_two(send)
    for copy in down_swaps:
        copy.wait_recv()
    downs[0].step_one(send)
    ups[1].step_two(send)
    downs[1].step_one(send)
    small_a[0, 2:3] = jnp.sum(grad * normal, axis=0, keepdims=True)
    small_a[0, 3:4] = jnp.sum(grad, axis=0, keepdims=True)
    output = middle[...] + mlp_out[...]
    block_output[...] = output.astype(bf16)
    lane = lax.broadcasted_iota(jnp.int32, (4, width), 1)
    row = jnp.zeros((4, width), f32)
    squared = (squares(output), attn_squares, squares(mlp_out[...]), jnp.sum(keep) * width)
    for i, value in enumerate(squared):
        row = jnp.where(lane == i, value, row)
    small_a[0, 4:8] = row


    def turn(h):
        def one(z, _):
            for side in range(2):
                at = pl.ds(side * tokens, tokens)
                turned[h % 2, z, at, :] = kv_all[h, z, side, 0].T
                turned[2 + h % 2, z, at, :] = kv_all[h, z, side, 1].T
            return 0

        lax.fori_loop(0, 4, one, 0)

    turn(0)
    ups[0].along_line(send)
    for z in range(4):
        leaving[z, 9] = jnp.zeros((HEAD_DIM, tokens), bf16)
    swaps, sends = [], []

    def finish(h):
        swaps[h].wait_recv()

        def merge(z, _):
            fine = valid_columns(span, (2 * z + core) * tokens, tokens)
            q, k, v, inverse, signed, terms, weight = alone_terms(raw.at[z, pl.ds(3 * h, 3)])
            g = gm_in[h, z].astype(f32)
            total = 1.0 / terms
            grad_total = -jnp.sum(g * (weight * v), axis=0, keepdims=True) * total * total
            g = (g * total).astype(bf16).astype(f32)
            grad_weight = jnp.sum(g * v, axis=0, keepdims=True)
            slope = 1.0 + (inverse * inverse) * (inverse - 1.0)
            grad_score = terms * (grad_weight * slope + grad_total * signed)
            grad_score = grad_score.astype(bf16).astype(f32)
            alone = (grad_score * k * 0.125, grad_score * q, weight * g)
            parts = [leaving[z, 3 * h].astype(f32)]
            for part in range(2):
                parts.append(grad_kv[h, z, core, part] + part_in[h, z, part].astype(f32))
            for part in range(3):
                leaving[z, 3 * h + part] = jnp.where(fine, parts[part], alone[part]).astype(bf16)
            return 0

        lax.fori_loop(0, 4, merge, 0)
        at = pl.ds(3 * h, 3)
        for k in (1, 2, 3):
            sends.append(
                send(leaving.at[along[k], at], arrived.at[:, zed * 3 + h], line[k - 1])
            )
        for part in range(3):
            arrived[part, zed * 3 + h] = leaving[zed, 3 * h + part]

    def tile_products(h, z, z_key, side):
        at = pl.ds(side * tokens, tokens)
        scores = matmul(turned[h % 2, z_key, at, :], q_all[h, z])
        return scores, matmul(turned[2 + h % 2, z_key, at, :], g_all[z])

    def tile_grads(tile, scores, grad_weights):
        z, z_key, side = tile
        inverse, signed, terms = signed_terms(scores)
        if z == z_key:
            key_pos = lax.broadcasted_iota(jnp.int32, scores.shape, 0)
            query_pos = lax.broadcasted_iota(jnp.int32, scores.shape, 1)
            seen = key_pos + side * tokens <= query_pos + core * tokens
            terms = jnp.where(seen, terms, 0.0)
        weights = (signed * terms).astype(bf16)
        slope = 1.0 + (inverse * inverse) * (inverse - 1.0)
        grad_scores = terms * (grad_weights * slope + gt_all[z] * signed)
        return weights, grad_scores.astype(bf16)

    def tile_sums(h, z, z_key, side, weights, grad_scores):
        for part, left, right in ((0, q_all[h, z], grad_scores), (1, g_all[z], weights)):
            grad = contract_cols(left, right)
            if z == z_key:
                grad_kv[h, z_key, side, part] = grad
            else:
                grad_kv[h, z_key, side, part] += grad
        grad = matmul(kv_all[h, z_key, side, 0], grad_scores)
        if z_key == 0 and side == 0:
            grad_query[...] = grad
        else:
            grad_query[...] += grad
        if z == z_key and side == 1:
            leaving[z, 3 * h] = (grad_query[...] * 0.125).astype(bf16)

    for h in range(3):
        for copy in coming[h * 3 : h * 3 + 3]:
            copy.wait_recv()

        def prepare(z, _):
            g = gm_in[h, z].astype(f32)
            total = 1.0 / tot_all[h, z]
            g_all[z] = (g * total).astype(bf16)
            gt_all[z] = -jnp.sum(g * mix_all[h, z], axis=0, keepdims=True) * total
            return 0

        lax.fori_loop(0, 4, prepare, 0)

        tiles = [(z, z_key, side) for z in range(4) for z_key in range(z + 1) for side in range(2)]
        scored, parts = {}, {}
        for step in range(len(tiles) + 2):
            if step < len(tiles):
                scored[step] = tile_products(h, *tiles[step])
            if 0 <= step - 1 < len(tiles):
                parts[step - 1] = tile_grads(tiles[step - 1], *scored.pop(step - 1))
            if step - 2 >= 0:
                tile_sums(h, *tiles[step - 2], *parts.pop(step - 2))

        def pack(z, _):
            for part in range(2):
                part_out[h, z, part] = grad_kv[h, z, 1 - core, part].astype(bf16)
            return 0

        lax.fori_loop(0, 4, pack, 0)
        swaps.append(send(part_out.at[h], part_in.at[h], sibling))
        if h == 0:
            turn(1)
            ups[1].along_line(send)
            downs[0].step_two(send)
            downs[2].step_one(send)
            ups[0].pass_line(send)
            ups[2].step_one(send)
        if h == 1:
            turn(2)
            downs[1].step_two(send)
            downs[0].along_line(send)
            ups[1].pass_line(send)
            ups[3].step_one(send)
        finish(h)

    downs[2].step_two(send)
    downs[1].along_line(send)
    outs.step_one(send)
    downs[0].pass_line(send)
    ups[2].step_two(send)

    for quarter in (heads_sum.across, heads_sum.beside, heads_sum.above, heads_sum.own):
        total = None
        for z in range(4):
            rows = norm_all[z, rows_of(quarter * (width // 4), width // 4), :]
            part = contract_cols(rows, leaving[z].reshape(10 * HEAD_DIM, tokens))
            total = part if total is None else total + part
        term[pl.ds(4 * quarter, 4)] = total.reshape((4,) + term.shape[1:])
        heads_sum.halves.append(heads_sum.swap_quarter(send, quarter))
    heads_sum.step_one(send)
    downs[2].along_line(send)
    ups[3].step_two(send)
    downs[1].pass_line(send)
    outs.step_two(send)
    ups[2].along_line(send)
    heads_sum.step_two(send)

    for copy in sends:
        copy.wait_recv()
    grads = arrived[...].reshape(3 * width, tokens)
    for i in range(width // 256):
        columns = slice(i * 256, (i + 1) * 256)
        grad_norm[:, columns] = matmul(w_qkv[columns, :], grads).T
    downs[2].pass_line(send)
    ups[3].along_line(send)
    outs.along_line(send)
    ups[2].pass_line(send)
    gain_grad, bias_grad = norm_back(x, gain_one, grad_norm, grad_middle, input_grad, 64)
    small_a[0, 0:1] = gain_grad
    small_a[0, 1:2] = bias_grad
    whose = 2 * grp + core
    small_b[pl.ds(whose, 1)] = small_a[0:1]
    planes = [
        send(small_b.at[whose], small_b.at[whose], target)
        for target in [sibling] + across + around
    ]
    ups[3].pass_line(send)
    outs.pass_line(send)
    heads_sum.total()
    gathered[pl.ds(zed, 1)] = final[pl.ds(zed, 1)]
    blocks = [send(final.at[along[k]], gathered.at[zed], line[k - 1]) for k in (1, 2, 3)]
    for copy in planes:
        copy.wait_recv()
    total = small_b[0]
    for i in range(1, 8):
        total = total + small_b[i]
    small_c[pl.ds(zed, 1)] = total.reshape(1, 8, width)
    columns = [send(small_c.at[zed], small_c.at[zed], line[k - 1]) for k in (1, 2, 3)]
    sums = ups[:2] + downs + ups[2:] + [outs]
    for each in sums:
        each.settle(send)
    for copy in blocks + columns:
        copy.wait_recv()
    for z in range(4):
        for h in range(3):
            for part in range(3):
                start = part * width + (3 * z + h) * HEAD_DIM
                sum_qkv[:, start : start + HEAD_DIM] = gathered[
                    z, :, (3 * h + part) * HEAD_DIM : (3 * h + part + 1) * HEAD_DIM
                ]
    settle_small(small_c, vecs, rms, grp * 8 + seq)
    for copy in down_swaps + coming + swaps + sends + planes + blocks + columns:
        copy.wait_send()
    for each in sums + [heads_sum]:
        each.drain()


def layer(block_input, out_grad, w_qkv, w_out, w_up, w_down, vectors, span):
    f32, bf16 = jnp.float32, jnp.bfloat16
    tokens, width = block_input.shape
    hidden = w_up.shape[1]
    count = hidden // width + 1
    vmem, smem = pl.BlockSpec(memory_space=pltpu.VMEM), pl.BlockSpec(memory_space=pltpu.SMEM)
    block = (HEAD_DIM, tokens)
    own_rows, columns = width // 32, 10 * HEAD_DIM
    quarter, half = width // 4, width // 2
    copies = 11 * 3 + 4 + 15 * count + 9 + 3 + 9 + 10 + 7 + 3 + 3
    dma = pltpu.SemaphoreType.DMA
    in_hbm = [block_input, out_grad, w_qkv, w_out, w_up, w_down]

    def sum_scratch(lead, rows):
        return [
            pltpu.VMEM(lead + (4 * rows, half), bf16),
            pltpu.VMEM(lead + (6, rows // 2, half), bf16),
            pltpu.VMEM(lead + (rows, half), bf16),
            pltpu.VMEM(lead + (rows, half), bf16),
            pltpu.VMEM(lead + (rows // 4, half), f32),
        ]

    return pl.pallas_call(
        layer_kernel,
        out_shape=[
            jax.ShapeDtypeStruct((tokens, width), bf16),
            jax.ShapeDtypeStruct((tokens, width), bf16),
            jax.ShapeDtypeStruct((own_rows, 3 * width), f32),
            jax.ShapeDtypeStruct((4, 1, own_rows), f32),
            jax.ShapeDtypeStruct((1, 3), f32),
            jax.ShapeDtypeStruct((hidden // 32, width), f32),
            jax.ShapeDtypeStruct((own_rows, hidden), f32),
            jax.ShapeDtypeStruct((own_rows, width), f32),
        ],
        in_specs=[pl.BlockSpec(memory_space=pl.ANY)] * len(in_hbm) + [vmem] * 4 + [smem],
        out_specs=[vmem] * 8,
        scratch_shapes=[pltpu.VMEM(a.shape, a.dtype) for a in in_hbm]
        + [
            pltpu.VMEM((HEADS,) + block, bf16),
            pltpu.VMEM((3, 4) + block, bf16),
            pltpu.VMEM((3, 4, 2, 2) + block, bf16),
            pltpu.VMEM((4, 9) + block, bf16),
            pltpu.VMEM((3, 4) + block, f32),
            pltpu.VMEM((3, 4, 1, tokens), f32),
            pltpu.VMEM((4, width, tokens), bf16),
            pltpu.VMEM((3, 256, width), bf16),
            pltpu.VMEM((3, 4, 8, tokens), f32),
            pltpu.VMEM((width, width), bf16),
            pltpu.VMEM((tokens, width), f32),
            pltpu.VMEM((tokens, width), bf16),
            pltpu.VMEM((width, tokens), bf16),
            pltpu.VMEM((tokens, width), f32),
            pltpu.VMEM((tokens, width), f32),
            pltpu.VMEM((tokens, width), f32),
            pltpu.VMEM((HEADS,) + block, bf16),
        ]
        + sum_scratch((count,), quarter)
        + [
            pltpu.VMEM((hidden, half), bf16),
            pltpu.VMEM((3, 6, hidden // 8, 128), bf16),
            pltpu.VMEM((3, hidden // 4, 128), bf16),
            pltpu.VMEM((3, hidden // 4, 128), bf16),
            pltpu.VMEM((3, hidden // 16, 128), f32),
        ]
        + [
            pltpu.VMEM((3, 4) + block, bf16),
            pltpu.VMEM((4, 4, 2 * tokens, HEAD_DIM), bf16),
            pltpu.VMEM((4,) + block, bf16),
            pltpu.VMEM((4, 1, tokens), f32),
            pltpu.VMEM((3, 4, 2, 2) + block, f32),
            pltpu.VMEM((3, 4, 2) + block, bf16),
            pltpu.VMEM((3, 4, 2) + block, bf16),
            pltpu.VMEM((4, 10) + block, bf16),
            pltpu.VMEM((3, HEADS) + block, bf16),
            pltpu.VMEM((16, 2, own_rows, columns), f32),
            pltpu.VMEM((16, own_rows, columns), f32),
            pltpu.VMEM((16 * own_rows, columns), bf16),
            pltpu.VMEM((6, 2 * own_rows, columns), bf16),
            pltpu.VMEM((4, own_rows, columns), f32),
            pltpu.VMEM((4, own_rows, columns), f32),
            pltpu.VMEM(block, f32),
            pltpu.VMEM((1, 8, width), f32),
            pltpu.VMEM((8, 8, width), f32),
            pltpu.VMEM((4, 8, width), f32),
            dma((4 + 2 * (count - 1),)),
            dma((copies,)),
            dma((copies,)),
            dma((2, 4, 2)),
            dma((2, 4, 2)),
            dma((8,)),
            dma((8,)),
            dma((4,)),
            dma((4,)),
        ],
        compiler_params=pltpu.CompilerParams(
            collective_id=0, has_side_effects=True, vmem_limit_bytes=63 * 2**20
        ),
    )(*in_hbm, *vectors, span)


def hand_over_kernel(many, *refs):
    vecs, rms, arrays = refs[0], refs[1], refs[2 : 2 + many]
    outs, rest = refs[2 + many : 7 + 2 * many], refs[7 + 2 * many :]
    held, sems = rest[:many], rest[many]
    loads = [
        pltpu.make_async_copy(arrays[i], held[i], sems.at[0, i]) for i in range(many)
    ]
    stores = [
        pltpu.make_async_copy(held[i], outs[5 + i], sems.at[1, i]) for i in range(many)
    ]
    for load in loads:
        load.start()
    for i in range(4):
        outs[i][...] = vecs[i, 0]
    outs[4][...] = rms[0]
    for load, store in zip(loads, stores):
        load.wait()
        store.start()
    for store in stores:
        store.wait()


def hand_over(vecs, rms, arrays):
    vmem, hbm = pl.BlockSpec(memory_space=pltpu.VMEM), pl.BlockSpec(memory_space=pl.ANY)
    many, f32 = len(arrays), jnp.float32
    return pl.pallas_call(
        functools.partial(hand_over_kernel, many),
        out_shape=[jax.ShapeDtypeStruct(vecs.shape[2:], f32)] * 4
        + [jax.ShapeDtypeStruct(rms.shape[1:], f32)]
        + [jax.ShapeDtypeStruct(a.shape, a.dtype) for a in arrays],
        in_specs=[vmem] * 2 + [hbm] * many,
        out_specs=[vmem] * 5 + [hbm] * many,
        scratch_shapes=[pltpu.VMEM(a.shape, a.dtype) for a in arrays]
        + [pltpu.SemaphoreType.DMA((2, many))],
    )(vecs, rms, *arrays)


def per_device_planned(
    block_input,
    out_grad,
    seq_span,
    ln1_gain,
    ln1_bias,
    w_qkv,
    w_out,
    ln2_gain,
    ln2_bias,
    w_up,
    w_down,
):
    block_output, input_grad, sum_qkv, vecs, rms, sum_down, sum_up, sum_out = layer(
        block_input, out_grad, w_qkv, w_out, w_up, w_down,
        (ln1_gain, ln1_bias, ln2_gain, ln2_bias), seq_span,
    )
    arrays = (block_output, input_grad, sum_qkv, sum_out, sum_up, sum_down)
    gain_one, bias_one, gain_two, bias_two, rms, *arrays = hand_over(vecs, rms, arrays)
    block_output, input_grad, sum_qkv, sum_out, sum_up, sum_down = arrays
    return (
        block_output,
        input_grad,
        gain_one,
        bias_one,
        sum_qkv,
        sum_out,
        gain_two,
        bias_two,
        sum_up,
        sum_down,
        rms,
    )


def solution(mesh):
    placed = (
        P(("grp", "seq"), None),
        P(("grp", "seq"), None),
        P("grp", None),
        P(),
        P(),
        P(),
        P(),
        P(),
        P(),
        P(),
        P(),
    )
    planned = mesh.shape["grp"] == 4 and mesh.shape["seq"] == 8
    return jax.shard_map(
        per_device_planned if planned else per_device,
        mesh=mesh,
        in_specs=placed,
        out_specs=(
            P(("grp", "seq"), None),
            P(("grp", "seq"), None),
            P(("grp", "seq")),
            P(("grp", "seq")),
            P(("grp", "seq"), None),
            P(("grp", "seq"), None),
            P(("grp", "seq")),
            P(("grp", "seq")),
            P(("grp", "seq"), None),
            P(("grp", "seq"), None),
            P(),
        ),
        check_vma=False,
    )
```

```python
import functools

import jax
import jax.numpy as jnp
from jax import lax
from jax.experimental import pallas as pl
from jax.experimental.pallas import tpu as pltpu
from jax.sharding import PartitionSpec as P

D = 768
HEADS = 12
HEAD_DIM = 64
MESH = pl.DeviceIdType.MESH


epsilon = 1e-05


def passed_along(array, axis, by):
    devices = lax.axis_size(axis)
    pairs = [(i, i + by) for i in range(devices) if 0 <= i + by < devices]
    return lax.ppermute(array, axis, pairs)


def shifted(array, axis, by):
    devices = lax.axis_size(axis)
    return lax.ppermute(array, axis, [(i, (i + by) % devices) for i in range(devices)])


def layer_norm(vector, scale_vec, shift_vec):
    row_mean = jnp.mean(vector, axis=-1, keepdims=True)
    centered = vector - row_mean
    variance = jnp.mean(centered * centered, axis=-1, keepdims=True)
    return centered * lax.rsqrt(variance + epsilon) * scale_vec + shift_vec


def contract_rows(left, right):
    return lax.dot_general(
        left, right, (((0,), (0,)), ((), ())), preferred_element_type=jnp.float32
    )


def contract_cols(left, right):
    return lax.dot_general(
        left, right, (((1,), (1,)), ((), ())), preferred_element_type=jnp.float32
    )


def score_terms(queries, key_block, query_pos, key_pos, seq_first, seq_limit):
    scores = (
        jnp.einsum("qhd,khd->qhk", queries, key_block, preferred_element_type=jnp.float32) * 0.125
    )
    query_valid = (query_pos >= seq_first) & (query_pos < seq_limit)
    key_valid = (key_pos >= seq_first) & (key_pos < seq_limit)
    allowed = (key_pos[None, :] <= query_pos[:, None]) & (
        query_valid[:, None] & key_valid[None, :] | (key_pos[None, :] == query_pos[:, None])
    )
    magnitude = jnp.sqrt(scores * scores + 1.0)
    signed_part = scores / magnitude
    exp_terms = jnp.where(allowed[:, None, :], jnp.exp(magnitude), 0.0)
    return (magnitude, signed_part, exp_terms)


def split_pair(kv_pair):
    count_rows = kv_pair.shape[0]
    key_block = kv_pair[:, :D].reshape(count_rows, HEADS, HEAD_DIM)
    value_block = kv_pair[:, D:].reshape(count_rows, HEADS, HEAD_DIM)
    return (key_block, value_block)


def forward_block(running, kv_pair, key_start, queries, query_pos, seq_first, seq_limit):
    totals, unnorm = running
    key_block, value_block = split_pair(kv_pair)
    key_pos = key_start + jnp.arange(kv_pair.shape[0], dtype=jnp.int32)
    magnitude, signed_part, exp_terms = score_terms(
        queries, key_block, query_pos, key_pos, seq_first, seq_limit
    )
    weights = (signed_part * exp_terms).astype(jnp.bfloat16)
    totals = totals + jnp.sum(exp_terms, axis=-1)
    unnorm = unnorm + jnp.einsum(
        "qhk,khd->qhd", weights, value_block, preferred_element_type=jnp.float32
    )
    return (totals, unnorm)


def grad_core(
    kv_pair, key_start, queries, query_pos, seq_first, seq_limit, grad_unnorm, grad_totals
):
    key_block, value_block = split_pair(kv_pair)
    key_pos = key_start + jnp.arange(kv_pair.shape[0], dtype=jnp.int32)
    magnitude, signed_part, exp_terms = score_terms(
        queries, key_block, query_pos, key_pos, seq_first, seq_limit
    )
    weights = (signed_part * exp_terms).astype(jnp.bfloat16)
    grad_weights = jnp.einsum(
        "qhd,khd->qhk", grad_unnorm, value_block, preferred_element_type=jnp.float32
    )
    grad_scores = (
        grad_weights * exp_terms / (magnitude * magnitude * magnitude)
        + (grad_weights * signed_part + grad_totals[:, :, None]) * exp_terms * signed_part
    )
    return (key_block, weights, grad_scores.astype(jnp.bfloat16))


def backward_block(
    kv_pair, key_start, queries, query_pos, seq_first, seq_limit, grad_unnorm, grad_totals
):
    key_block, weights, grad_scores = grad_core(
        kv_pair, key_start, queries, query_pos, seq_first, seq_limit, grad_unnorm, grad_totals
    )
    count_rows = kv_pair.shape[0]
    grad_query = (
        jnp.einsum("qhk,khd->qhd", grad_scores, key_block, preferred_element_type=jnp.float32)
        * 0.125
    )
    grad_key = (
        jnp.einsum("qhk,qhd->khd", grad_scores, queries, preferred_element_type=jnp.float32) * 0.125
    )
    grad_value = jnp.einsum(
        "qhk,qhd->khd", weights, grad_unnorm, preferred_element_type=jnp.float32
    )
    grad_pair = jnp.concatenate(
        [grad_key.reshape(count_rows, D), grad_value.reshape(count_rows, D)], axis=1
    )
    return (grad_query, grad_pair)


def per_device(
    block_input,
    out_grad,
    seq_span,
    ln1_gain,
    ln1_bias,
    w_qkv,
    w_out,
    ln2_gain,
    ln2_bias,
    w_up,
    w_down,
):
    tok_rows = block_input.shape[0]
    feat_width = block_input.shape[1]
    seq_count = lax.axis_size("seq")
    seq_index = lax.axis_index("seq")
    query_pos = seq_index * tok_rows + jnp.arange(tok_rows, dtype=jnp.int32)
    query_last = query_pos[tok_rows - 1]
    seq_first = seq_span[0, 0]
    seq_limit = seq_span[0, 1]
    inputs = block_input.astype(jnp.float32)
    normed = layer_norm(inputs, ln1_gain, ln1_bias).astype(jnp.bfloat16)
    proj_qkv = jnp.dot(normed, w_qkv, preferred_element_type=jnp.float32).astype(jnp.bfloat16)
    queries = proj_qkv[:, :feat_width].reshape(tok_rows, HEADS, HEAD_DIM)
    kv_pair = proj_qkv[:, feat_width:]

    def visit_block(running, shard_rows, key_start):
        return lax.cond(
            key_start <= query_last,
            lambda state_in: forward_block(
                state_in, shard_rows, key_start, queries, query_pos, seq_first, seq_limit
            ),
            lambda state_in: state_in,
            running,
        )

    empty = (
        jnp.zeros((tok_rows, HEADS), jnp.float32),
        jnp.zeros((tok_rows, HEADS, HEAD_DIM), jnp.float32),
    )
    first_state = visit_block(empty, kv_pair, seq_index * tok_rows)

    def forward_hop(hop_count, loop_state):
        moving, running = loop_state
        moving = passed_along(moving, "seq", 1)
        source = (seq_index - hop_count) % seq_count
        return (moving, visit_block(running, moving, source * tok_rows))

    _, (totals, unnorm) = lax.fori_loop(1, seq_count, forward_hop, (kv_pair, first_state))
    mixed_heads = (unnorm / totals[:, :, None]).reshape(tok_rows, feat_width).astype(jnp.bfloat16)
    attn_out = jnp.dot(mixed_heads, w_out, preferred_element_type=jnp.float32)
    middle = inputs + attn_out
    normed_two = layer_norm(middle, ln2_gain, ln2_bias).astype(jnp.bfloat16)
    up_proj = jnp.dot(normed_two, w_up, preferred_element_type=jnp.float32)
    activated = jax.nn.gelu(up_proj, approximate=True).astype(jnp.bfloat16)
    mlp_out = jnp.dot(activated, w_down, preferred_element_type=jnp.float32)
    output = middle + mlp_out
    valid_rows = ((query_pos >= seq_first) & (query_pos < seq_limit)).astype(jnp.float32)[:, None]
    rms_parts = lax.psum(
        (
            jnp.sum(valid_rows * output * output),
            jnp.sum(valid_rows * attn_out * attn_out),
            jnp.sum(valid_rows * mlp_out * mlp_out),
            jnp.sum(valid_rows) * feat_width,
        ),
        ("grp", "seq"),
    )
    rms_stats = jnp.sqrt(jnp.stack([rms_parts[0], rms_parts[1], rms_parts[2]]) / rms_parts[3])
    grad_w_down = contract_rows(activated, out_grad)
    grad_activated = contract_cols(out_grad, w_down)
    _, gelu_pull = jax.vjp(lambda pre_act: jax.nn.gelu(pre_act, approximate=True), up_proj)
    grad_up = gelu_pull(grad_activated)[0].astype(jnp.bfloat16)
    grad_w_up = contract_rows(normed_two, grad_up)
    grad_norm_two = contract_cols(grad_up, w_up)
    _, norm_pull_two = jax.vjp(layer_norm, middle, ln2_gain, ln2_bias)
    grad_mid_norm, grad_gain_two, grad_bias_two = norm_pull_two(grad_norm_two)
    grad_middle = out_grad.astype(jnp.float32) + grad_mid_norm
    grad_attn = grad_middle.astype(jnp.bfloat16)
    grad_w_out = contract_rows(mixed_heads, grad_attn)
    grad_mixed = contract_cols(grad_attn, w_out).reshape(tok_rows, HEADS, HEAD_DIM)
    grad_unnorm = (grad_mixed / totals[:, :, None]).astype(jnp.bfloat16)
    grad_totals = -jnp.sum(grad_mixed * unnorm, axis=-1) / (totals * totals)

    def back_block(grad_run, shard_rows, key_start):

        def compute_block(grad_in):
            grad_query, grad_pair = backward_block(
                shard_rows,
                key_start,
                queries,
                query_pos,
                seq_first,
                seq_limit,
                grad_unnorm,
                grad_totals,
            )
            return (grad_in + grad_query, grad_pair)

        def skip_block(grad_in):
            return (grad_in, jnp.zeros((shard_rows.shape[0], 2 * feat_width), jnp.float32))

        return lax.cond(key_start <= query_last, compute_block, skip_block, grad_run)

    grad_start = jnp.zeros((tok_rows, HEADS, HEAD_DIM), jnp.float32)
    grad_queries, local_terms = back_block(grad_start, kv_pair, seq_index * tok_rows)

    def backward_hop(hop_count, loop_state):
        moving, grad_acc, grad_run = loop_state
        moving = passed_along(moving, "seq", 1)
        grad_acc = shifted(grad_acc.astype(jnp.bfloat16), "seq", 1).astype(grad_acc.dtype)
        source = (seq_index - hop_count) % seq_count
        grad_run, new_terms = back_block(grad_run, moving, source * tok_rows)
        return (moving, grad_acc + new_terms, grad_run)

    _, grad_acc, grad_queries = lax.fori_loop(
        1, seq_count, backward_hop, (kv_pair, local_terms, grad_queries)
    )
    grad_kv = shifted(grad_acc.astype(jnp.bfloat16), "seq", 1).astype(grad_acc.dtype)
    grad_qkv = jnp.concatenate(
        [grad_queries.reshape(tok_rows, feat_width), grad_kv], axis=1
    ).astype(jnp.bfloat16)
    grad_w_qkv = contract_rows(normed, grad_qkv)
    grad_norm_one = contract_cols(grad_qkv, w_qkv)
    _, norm_pull_one = jax.vjp(layer_norm, inputs, ln1_gain, ln1_bias)
    grad_in_norm, grad_gain_one, grad_bias_one = norm_pull_one(grad_norm_one)
    input_grad = (grad_middle + grad_in_norm).astype(jnp.bfloat16)
    summed = (
        lax.psum_scatter(grad_gain_one, ("grp", "seq"), scatter_dimension=0, tiled=True),
        lax.psum_scatter(grad_bias_one, ("grp", "seq"), scatter_dimension=0, tiled=True),
        lax.psum_scatter(grad_w_qkv, ("grp", "seq"), scatter_dimension=0, tiled=True),
        lax.psum_scatter(grad_w_out, ("grp", "seq"), scatter_dimension=0, tiled=True),
        lax.psum_scatter(grad_gain_two, ("grp", "seq"), scatter_dimension=0, tiled=True),
        lax.psum_scatter(grad_bias_two, ("grp", "seq"), scatter_dimension=0, tiled=True),
        lax.psum_scatter(grad_w_up, ("grp", "seq"), scatter_dimension=0, tiled=True),
        lax.psum_scatter(grad_w_down, ("grp", "seq"), scatter_dimension=0, tiled=True),
    )
    return (
        output.astype(jnp.bfloat16),
        input_grad,
        summed[0],
        summed[1],
        summed[2],
        summed[3],
        summed[4],
        summed[5],
        summed[6],
        summed[7],
        rms_stats,
    )


def rows_of(start, count):
    return pl.ds(pl.multiple_of(start, 16), count)


def matmul(left, right):
    return jnp.dot(left, right, preferred_element_type=jnp.float32)


def signed_terms(scores):
    square = scores * scores + 1.0
    inverse = lax.rsqrt(square)
    return inverse, scores * inverse, jnp.exp(square * inverse)


def valid_columns(span, start, count):
    pos = start + lax.broadcasted_iota(jnp.int32, (1, count), 1)
    return (pos >= span[0, 0]) & (pos < span[0, 1])


def greet_start(partners):
    for partner in partners:
        pl.semaphore_signal(
            pltpu.get_barrier_semaphore(), inc=1, device_id=partner, device_id_type=MESH
        )


def greet_end(partners):
    pl.semaphore_wait(pltpu.get_barrier_semaphore(), len(partners))


def sender(send_sems, recv_sems):
    count = [0]

    def send(src, dst, target, only=None, arrives=None):
        slot = count[0]
        count[0] += 1
        copy = pltpu.make_async_remote_copy(
            src_ref=src, dst_ref=dst, send_sem=send_sems.at[slot],
            recv_sem=recv_sems.at[slot if arrives is None else arrives],
            device_id=target, device_id_type=MESH,
        )
        if only is None:
            copy.start()
        else:
            pl.when(only)(copy.start)
        return copy

    send.count = count
    return send


def place():
    grp, seq = lax.axis_index("grp"), lax.axis_index("seq")
    zed, core = seq // 2, seq % 2
    sibling = (grp, zed * 2 + 1 - core)
    along = [(zed + k) % 4 for k in range(4)]
    return grp, seq, zed, core, sibling, along


def alone_terms(raw):
    q, k, v = (raw[part].astype(jnp.float32) for part in range(3))
    inverse, signed, terms = signed_terms(jnp.sum(q * k, axis=0, keepdims=True))
    weight = (signed * terms).astype(jnp.bfloat16).astype(jnp.float32)
    return q, k, v, inverse, signed, terms, weight


def attend_part(
    x, gain_one, bias_one, w_qkv, span, mixed, q_all, kv_all, raw, mix_all, tot_all, norm_all,
    weights, keys, totals, leaving, hop_send, hop_recv, swap_send, swap_recv, back_send, back_recv,
    loads, greet_end,
):
    tokens, width = x.shape
    f32, bf16 = jnp.float32, jnp.bfloat16
    grp, seq, zed, core, sibling, along = place()

    start = pl.multiple_of(zed * 192 // 128 * 128, 128)
    inside = pl.ds(pl.multiple_of(zed % 2 * HEAD_DIM, HEAD_DIM), 3 * HEAD_DIM)
    loads["x"].wait()
    vector = x[...].astype(f32)
    centered = vector - jnp.mean(vector, axis=-1, keepdims=True)
    variance = jnp.mean(centered * centered, axis=-1, keepdims=True)
    normed = (
        centered * lax.rsqrt(variance + epsilon) * gain_one[...].reshape(1, width)
        + bias_one[...].reshape(1, width)
    ).astype(bf16)
    norm_all[zed] = normed.T
    greet_end()

    halves = [pl.ds(half * (width // 2), width // 2) for half in range(2)]

    def hop(step, side, half):
        towards = 1 - 2 * side
        block = zed - towards * step
        runs = (block >= 0) & (block < 4) & (zed + towards >= 0) & (zed + towards < 4)
        copy = pltpu.make_async_remote_copy(
            src_ref=norm_all.at[block, halves[half]], dst_ref=norm_all.at[block, halves[half]],
            send_sem=hop_send.at[side, step, half], recv_sem=hop_recv.at[side, step, half],
            device_id=(grp, (zed + towards) * 2 + core), device_id_type=MESH,
        )
        return runs, copy

    for half in range(2):
        for side in range(2):
            runs, copy = hop(0, side, half)
            pl.when(runs)(copy.start)
    loads["w_qkv"].wait()
    for part in range(3):
        at = pl.ds(pl.multiple_of(part * width + start, 128), 256)
        weights[part] = w_qkv[:, at].T
    no_score = signed_terms(jnp.zeros((1, tokens), f32))[2]
    extra = span[0, 0].astype(f32) * no_score
    mix_all[...] = jnp.zeros(mix_all.shape, f32)
    totals[...] = jnp.zeros(totals.shape, f32)

    def swap(block, slot):
        return pltpu.make_async_remote_copy(
            src_ref=kv_all.at[:, block, core], dst_ref=kv_all.at[:, block, core],
            send_sem=swap_send.at[slot], recv_sem=swap_recv.at[slot],
            device_id=sibling, device_id_type=MESH,
        )

    def project(block, slot):
        keep = valid_columns(span, (2 * block + core) * tokens, tokens).astype(f32)
        for part in range(3):
            heads = matmul(weights[part, inside, :], norm_all[block])
            if part == 0:
                heads = heads * 0.125
            for h in range(3):
                one = heads[h * HEAD_DIM : (h + 1) * HEAD_DIM]
                raw[block, 3 * h + part] = one.astype(bf16)
                if part == 0:
                    q_all[h, block] = (one * keep).astype(bf16)
                else:
                    kv_all[h, block, core, part - 1] = (one * keep).astype(bf16)
        swap(block, slot).start()

    def turn(block, side):
        for h in range(3):
            keys[h, block, rows_of(side * tokens, tokens), :] = kv_all[h, block, side, 0].T

    def pair(block, other, last, sides=(0, 1)):
        tiles = [(h, side) for h in range(3) for side in sides]
        total = [totals[h, block] for h in range(3)]
        blend = [mix_all[h, block] for h in range(3)]
        scored, weights = {}, {}
        for step in range(len(tiles) + 2):
            if step < len(tiles):
                h, side = tiles[step]
                at = rows_of(side * tokens, tokens)
                scored[step] = matmul(keys[h, other, at, :], q_all[h, block])
            if 0 <= step - 1 < len(tiles):
                h, side = tiles[step - 1]
                scores = scored.pop(step - 1)
                _, signed, terms = signed_terms(scores)
                if last:
                    key_pos = lax.broadcasted_iota(jnp.int32, scores.shape, 0)
                    query_pos = lax.broadcasted_iota(jnp.int32, scores.shape, 1)
                    seen = key_pos + side * tokens <= query_pos + core * tokens
                    terms = jnp.where(seen, terms, 0.0)
                total[h] = total[h] + jnp.sum(terms.reshape(tokens // 8, 8, tokens), axis=0)
                weights[step - 1] = (signed * terms).astype(bf16)
            if step - 2 >= 0:
                h, side = tiles[step - 2]
                blend[h] = blend[h] + matmul(kv_all[h, other, side, 1], weights.pop(step - 2))
        for h in range(3):
            totals[h, block], mix_all[h, block] = total[h], blend[h]

    def back(block):
        return pltpu.make_async_remote_copy(
            src_ref=leaving.at[block, pl.ds(0, 3)], dst_ref=mixed.at[pl.ds(3 * zed, 3)],
            send_sem=back_send.at[block], recv_sem=back_recv.at[zed],
            device_id=(grp, block * 2 + core), device_id_type=MESH,
        )

    def complete(block):
        fine = valid_columns(span, (2 * block + core) * tokens, tokens)
        for h in range(3):
            total = jnp.sum(totals[h, block], axis=0, keepdims=True) - extra
            total = jnp.where(fine, total, 1.0)
            blend = mix_all[h, block] / total
            mix_all[h, block] = blend
            tot_all[h, block] = total
            _, _, v, _, _, terms, weight = alone_terms(raw.at[block, pl.ds(3 * h, 3)])
            leaving[block, h] = jnp.where(fine, blend, weight * v / terms).astype(bf16)

        @pl.when(block != zed)
        def _():
            back(block).start()

        @pl.when(block == zed)
        def _():
            mixed[pl.ds(3 * zed, 3)] = leaving[zed, 0:3]

    project(zed, 0)
    turn(zed, core)
    pair(zed, zed, True, (core,))
    swap(zed, 0).wait_recv()
    turn(zed, 1 - core)
    pair(zed, zed, True, (1 - core,))

    @pl.when(zed == 0)
    def _():
        complete(0)

    def step(d, _):
        low, high = zed - d, zed + d
        for half in range(2):
            for side, block in ((0, low), (1, high)):

                @pl.when((block >= 0) & (block < 4))
                def _():
                    towards = 1 - 2 * side
                    part = norm_all.at[block, halves[half]]
                    pltpu.make_async_remote_copy(
                        src_ref=part, dst_ref=part, send_sem=hop_send.at[side, d - 1, half],
                        recv_sem=hop_recv.at[side, d - 1, half],
                        device_id=(grp, (zed - towards) * 2 + core), device_id_type=MESH,
                    ).wait_recv()
                    runs, copy = hop(d, side, half)
                    pl.when(runs)(copy.start)
                    if half == 1:
                        project(block, 2 * d + side)

        @pl.when(high < 4)
        def _():
            lax.fori_loop(jnp.maximum(low + 1, 0), high, lambda j, _: (pair(high, j, False), 0)[1], 0)
            turn(high, core)
            pair(high, high, True, (core,))
            swap(high, 2 * d + 1).wait_recv()
            turn(high, 1 - core)
            pair(high, high, True, (1 - core,))

        @pl.when(low >= 0)
        def _():
            last = jnp.minimum(high + 1, 4)
            turn(low, core)
            pair(low, low, True, (core,))
            lax.fori_loop(low + 1, last, lambda i, _: (pair(i, low, False, (core,)), 0)[1], 0)
            swap(low, 2 * d).wait_recv()
            turn(low, 1 - core)
            pair(low, low, True, (1 - core,))
            pl.when(low == 0)(lambda: complete(low))

            def later(i, _):
                pair(i, low, False, (1 - core,))
                pl.when((low == 0) & (i != high))(lambda: complete(i))
                return 0

            lax.fori_loop(low + 1, last, later, 0)

        @pl.when((high < 4) & (low <= 0))
        def _():
            complete(high)

        return 0

    lax.fori_loop(1, 4, step, 0)

    for k in (1, 2, 3):
        back(along[k]).wait_send()
        pltpu.make_async_remote_copy(
            src_ref=leaving.at[zed, pl.ds(0, 3)], dst_ref=mixed.at[pl.ds(3 * along[k], 3)],
            send_sem=back_send.at[zed], recv_sem=back_recv.at[along[k]],
            device_id=(grp, along[k] * 2 + core), device_id_type=MESH,
        ).wait_recv()
    for d in range(4):
        for side in range(2):
            for half in range(2):
                runs, copy = hop(d, side, half)
                pl.when(runs)(copy.wait_send)
            if d > 0 or side == 0:
                block = zed + (2 * side - 1) * d
                pl.when((block >= 0) & (block < 4))(swap(block, 2 * d + side).wait_send)


def gelu_and_slope(u):
    root = 0.7978845608028654
    square = u * u
    bent = jnp.tanh(root * (u + 0.044715 * (square * u)))
    half = 0.5 * (1.0 + bent)
    slope = half + 0.5 * u * (1.0 - bent * bent) * (root * (1.0 + 0.134145 * square))
    return u * half, slope


def normal_parts(vector):
    centered = vector - jnp.mean(vector, axis=-1, keepdims=True)
    variance = jnp.mean(centered * centered, axis=-1, keepdims=True)
    inverse = lax.rsqrt(variance + epsilon)
    return centered * inverse, inverse


def norm_pull(normal, inverse, gain, grad):
    scaled = grad * gain
    along_normal = jnp.mean(scaled * normal, axis=-1, keepdims=True)
    return inverse * (scaled - jnp.mean(scaled, axis=-1, keepdims=True) - normal * along_normal)


def add_rows(into, base, count, *terms):
    chunk = 96 if count % 96 == 0 else 48

    def add(i, _):
        total = None
        for ref, start in terms:
            term = ref[rows_of(start + i * chunk, chunk), :].astype(jnp.float32)
            total = term if total is None else total + term
        into[rows_of(base + i * chunk, chunk), :] = total.astype(jnp.bfloat16)
        return 0

    lax.fori_loop(0, count // chunk, add, 0)


class GroupSum:
    def __init__(self, term, first, near, held, third, mine, out, part=None):
        self.term, self.first, self.near, self.held = term, first, near, held
        self.third, self.line_sum, self.out = third, mine, out
        self.rows, half = term.shape[0] // 4, term.shape[1] // 2
        start, count = part or (0, half)
        grp, seq, zed, core, sibling, along = place()
        self.place_in_plane(grp, seq)
        self.sibling, self.grp, self.zed, self.core = sibling, grp, zed, core
        self.column = pl.ds(pl.multiple_of(core * half + start, 128), count)
        self.mine = term.at[:, self.column]
        self.away = pl.ds(pl.multiple_of((1 - core) * half, 128), half)
        self.halves, self.copies = [], []

    def place_in_plane(self, grp, seq):
        y, x = grp // 2, grp % 2
        self.own, self.beside, self.above = grp, y * 2 + 1 - x, (1 - y) * 2 + x
        self.across = (1 - y) * 2 + 1 - x
        self.to_x, self.to_y = (self.beside, seq), (self.above, seq)

    def swap_quarter(self, send, quarter):
        at = rows_of(quarter * self.rows, self.rows)
        return send(self.term.at[at, self.away], self.first.at[at, :], self.sibling)

    def swap(self, send):
        for quarter in (self.across, self.beside, self.above, self.own):
            self.halves.append(self.swap_quarter(send, quarter))

    def part(self, quarter, half):
        return rows_of(quarter * self.rows + half * (self.rows // 2), self.rows // 2)

    def pass_on(self, send, quarter, half, slot, target):
        self.copies.append(
            send(self.first.at[self.part(quarter, half), :], self.near.at[slot], target)
        )

    def core_sum(self, quarter):
        base = quarter * self.rows
        add_rows(self.first, base, self.rows, (self.mine, base), (self.first, base))

    def step_one(self, send):
        steps = (
            (self.across, ((0, 0, self.to_x), (1, 2, self.to_y))),
            (self.beside, ((0, 1, self.to_x),)),
            (self.above, ((1, 3, self.to_y),)),
        )
        for i, (quarter, passes) in enumerate(steps):
            if self.halves:
                self.halves[i].wait_recv()
            self.core_sum(quarter)
            for half, slot, target in passes:
                self.pass_on(send, quarter, half, slot, target)
        self.copies = [self.copies[i] for i in (0, 2, 1, 3)]

    def step_two(self, send):
        half = self.rows // 2
        for slot, quarter, side, target in (
            (0, self.above, 0, self.to_y),
            (2, self.beside, 1, self.to_x),
        ):
            base = quarter * self.rows + side * half
            self.copies[slot].wait_recv()
            add_rows(self.first, base, half, (self.first, base), (self.near.at[slot], 0))
            self.pass_on(send, quarter, side, 4 + side, target)

    def total(self):
        half = self.rows // 2
        if self.halves:
            self.halves[3].wait_recv()
        for slot in (1, 3, 4, 5):
            self.copies[slot].wait_recv()
        for side, one, two in ((0, 1, 4), (1, 3, 5)):
            base = self.own * self.rows + side * half
            add_rows(
                self.held, side * half, half, (self.mine, base), (self.first, base),
                (self.near.at[one], 0), (self.near.at[two], 0),
            )

    def along_line(self, send):
        self.total()
        rows = self.held.shape[0] // 4
        self.inner = (self.zed == 1) | (self.zed == 2)
        mate = self.zed + 1 - 2 * (self.zed % 2)
        self.far = (1 - self.zed // 2) * 2
        target = (self.grp, mate * 2 + self.core)
        far_rows = rows_of(self.far * rows, 2 * rows)
        self.outward = send(
            self.held.at[far_rows, :], self.third.at[pl.ds(2 * rows, 2 * rows), :], target,
            only=jnp.logical_not(self.inner),
        )
        self.beside_copy = send(
            self.held.at[rows_of(mate * rows, rows), :], self.third.at[pl.ds(0, rows), :], target
        )

    def pass_line(self, send):
        rows = self.held.shape[0] // 4

        @pl.when(self.inner)
        def _():
            self.outward.wait_recv()
            base = self.far * rows
            add_rows(
                self.third, 2 * rows, 2 * rows, (self.third, 2 * rows), (self.held, base)
            )

        self.passed = []
        arrives = send.count[0]
        for i in range(2):
            self.passed.append(
                send(
                    self.third.at[pl.ds((2 + i) * rows, rows), :],
                    self.third.at[pl.ds(rows, rows), :],
                    (self.grp, (self.far + i) * 2 + self.core),
                    only=self.inner,
                    arrives=arrives,
                )
            )

    def settle(self, send):
        rows = self.held.shape[0] // 4
        self.beside_copy.wait_recv()
        self.passed[0].wait_recv()
        total = self.held[rows_of(self.zed * rows, rows), :].astype(jnp.float32)
        for j in range(2):
            total = total + self.third[j * rows : (j + 1) * rows, :].astype(jnp.float32)
        self.line_sum[...] = total
        half = rows // 2
        away = pl.ds(pl.multiple_of((1 - self.core) * half, 8), half)
        self.out[:, self.column] = self.line_sum[pl.ds(pl.multiple_of(self.core * half, 8), half), :]
        self.last = send(self.line_sum.at[away, :], self.out.at[:, self.column], self.sibling)

    def drain(self):
        for copy in self.halves + self.copies + [self.beside_copy]:
            copy.wait_send()
        pl.when(jnp.logical_not(self.inner))(self.outward.wait_send)
        for copy in self.passed:
            pl.when(self.inner)(copy.wait_send)
        self.last.wait()


class HeadsSum(GroupSum):
    def __init__(self, term, other, first, near, final):
        self.term, self.other, self.first, self.near, self.final = term, other, first, near, final
        self.rows = 4 * term.shape[2]
        grp, seq, zed, self.core, self.sibling, along = place()
        self.place_in_plane(grp, seq)
        self.copies, self.halves = [], []

    def swap_quarter(self, send, quarter):
        at = pl.ds(4 * quarter, 4)
        return send(self.term.at[at, 1 - self.core], self.other.at[at], self.sibling)

    def both_cores(self, quarter):
        at = pl.ds(4 * quarter, 4)
        return (self.term[at, self.core] + self.other[at]).reshape(self.rows, -1)

    def core_sum(self, quarter):
        self.first[rows_of(quarter * self.rows, self.rows), :] = self.both_cores(quarter).astype(
            jnp.bfloat16
        )

    def total(self):
        self.halves[3].wait_recv()
        for slot in (1, 3, 4, 5):
            self.copies[slot].wait_recv()
        near = [self.near[i].astype(jnp.float32) for i in range(6)]
        total = self.both_cores(self.own) + jnp.concatenate(
            [near[1] + near[4], near[3] + near[5]], axis=0
        )
        self.final[...] = total.reshape(self.final.shape)

    def drain(self):
        for copy in self.halves + self.copies:
            copy.wait_send()


def norm_back(x, gain, grad_norm, grad_out, into, chunk):
    f32 = jnp.float32
    tokens, width = x.shape
    gain_row = gain[...].reshape(1, width)

    def one(i, sums):
        at = rows_of(i * chunk, chunk)
        vector, grad = x[at, :].astype(f32), grad_norm[at, :]
        normal, inverse = normal_parts(vector)
        pulled = norm_pull(normal, inverse, gain_row, grad)
        into[at, :] = (grad_out[at, :] + pulled).astype(into.dtype)
        return (
            sums[0] + jnp.sum(grad * normal, axis=0, keepdims=True),
            sums[1] + jnp.sum(grad, axis=0, keepdims=True),
        )

    zero = jnp.zeros((1, width), f32)
    return lax.fori_loop(0, tokens // chunk, one, (zero, zero))


def settle_small(small, vecs, rms, owner):
    width, count = small.shape[-1], vecs.shape[-1]
    total = (small[0] + small[1]) + (small[2] + small[3])
    turned = pltpu.roll(total, (width - owner * count) % width, 1)
    for i in range(4):
        vecs[i] = turned[i : i + 1, :count]
    rms[...] = jnp.sqrt(total[4:5, :3] / total[4:5, 3:4])


def layer_kernel(
    x_in, out_grad_in, w_qkv_in, w_out_in, w_up_in, w_down_in,
    gain_one, bias_one, gain_two, bias_two, span,
    block_output, input_grad, sum_qkv, vecs, rms, out_down, out_up, out_out,
    x, out_grad, w_qkv, w_out, w_up, w_down,
    mixed, q_all, kv_all, raw, mix_all, tot_all, norm_all, weights, totals,
    term_out, middle, normed, normed_t, mlp_out, grad_norm, grad_middle, gmix,
    first, near, held, third, mine, first_down, near_down, held_down, third_down, mine_down,
    gm_in, turned, g_all, gt_all, grad_kv, part_out, part_in, leaving, arrived,
    term, other, first_qkv, near_qkv, final, gathered, grad_query, small_a, small_b, small_c,
    load_sems, send_sems, recv_sems,
    hop_send, hop_recv, swap_send, swap_recv, back_send, back_recv,
):
    tokens, width = x.shape
    f32, bf16 = jnp.float32, jnp.bfloat16
    grp, seq, zed, core, sibling, along = place()
    line = [(grp, along[k] * 2 + core) for k in (1, 2, 3)]
    chunks = w_up.shape[1] // width

    loads = {}

    def load(name, source, target):
        loads[name] = pltpu.make_async_copy(source, target, load_sems.at[len(loads)])
        loads[name].start()

    load("x", x_in, x)
    load("w_qkv", w_qkv_in, w_qkv)
    load("w_out", w_out_in, w_out)
    load("out_grad", out_grad_in, out_grad)
    for i in range(chunks):
        at = pl.ds(i * width, width)
        load(("up", i), w_up_in.at[:, at], w_up.at[:, at])
        load(("down", i), w_down_in.at[at, :], w_down.at[at, :])

    ups = [
        GroupSum(
            w_up.at[:, pl.ds(i * width, width)], first.at[i], near.at[i], held.at[i], third.at[i],
            mine.at[i], out_up.at[:, pl.ds(i * width, width)],
        )
        for i in range(chunks)
    ]
    outs = GroupSum(
        term_out, first.at[chunks], near.at[chunks], held.at[chunks], third.at[chunks],
        mine.at[chunks], out_out,
    )
    downs = [
        GroupSum(
            w_down, first_down.at[:, pl.ds(i * 128, 128)], near_down.at[i], held_down.at[i],
            third_down.at[i], mine_down.at[i], out_down, (i * 128, 128),
        )
        for i in range(width // 256)
    ]
    whole_down = GroupSum(w_down, first_down, None, None, None, None, None)
    down_swaps = []
    heads_sum = HeadsSum(term, other, first_qkv, near_qkv, final)
    across = [(k, seq) for k in (heads_sum.beside, heads_sum.above, heads_sum.across)]
    around = [(k, zed * 2 + 1 - core) for k in (heads_sum.beside, heads_sum.above, heads_sum.across)]
    partners = [sibling] + line + across + around
    greet_start(partners)
    send = sender(send_sems, recv_sems)
    attend_part(
        x, gain_one, bias_one, w_qkv, span, mixed, q_all, kv_all, raw, mix_all, tot_all, norm_all,
        weights, turned, totals, leaving, hop_send, hop_recv, swap_send, swap_recv, back_send,
        back_recv, loads, functools.partial(greet_end, partners),
    )

    pos = seq * tokens + lax.broadcasted_iota(jnp.int32, (tokens, 1), 0)
    keep = ((pos >= span[0, 0]) & (pos < span[0, 1])).astype(f32)
    gain_row, bias_row = gain_two[...].reshape(1, width), bias_two[...].reshape(1, width)

    def squares(value):
        return jnp.sum(keep * value * value)

    for name in ("w_out", "out_grad"):
        loads[name].wait()
    attn_out = matmul(mixed[...].reshape(width, tokens).T, w_out[...])
    attn_squares = squares(attn_out)
    middle[...] = x[...].astype(f32) + attn_out
    normed[...] = (normal_parts(middle[...])[0] * gain_row + bias_row).astype(bf16)
    normed_t[...] = normed[...].T
    mlp_out[...] = jnp.zeros((tokens, width), f32)
    grad_norm[...] = jnp.zeros((tokens, width), f32)
    for i in range(chunks):
        at = pl.ds(i * width, width)
        loads["up", i].wait()
        loads["down", i].wait()
        activated, slope = gelu_and_slope(matmul(normed[...], w_up[:, at]))
        activated = activated.astype(bf16)
        mlp_out[...] += matmul(activated, w_down[at, :])
        grad_up = (contract_cols(out_grad[...], w_down[at, :]) * slope).astype(bf16)
        grad_norm[...] += contract_cols(grad_up, w_up[:, at])
        w_up[:, at] = matmul(normed_t[...], grad_up).astype(bf16)
        ups[i].swap(send)
        w_down[at, :] = matmul(activated.T, out_grad[...]).astype(bf16)
        down_swaps.append(whole_down.swap_quarter(send, i))
        if i >= 2:
            ups[i - 2].step_one(send)
    normal, inverse = normal_parts(middle[...])
    grad = grad_norm[...]
    grad_middle[...] = out_grad[...].astype(f32) + norm_pull(normal, inverse, gain_row, grad)
    grad_attn = grad_middle[...].astype(bf16)
    gmix[...] = contract_cols(w_out[...], grad_attn).astype(bf16).reshape(gmix.shape)
    coming = []
    for h in range(3):
        for k in (1, 2, 3):
            coming.append(send(gmix.at[along[k] * 3 + h], gm_in.at[h, zed], line[k - 1]))
        gm_in[h, zed] = gmix[zed * 3 + h]
    term_out[...] = matmul(mixed[...].reshape(width, tokens), grad_attn).astype(bf16)
    outs.swap(send)
    ups[0].step_two(send)
    for copy in down_swaps:
        copy.wait_recv()
    downs[0].step_one(send)
    ups[1].step_two(send)
    downs[1].step_one(send)
    small_a[0, 2:3] = jnp.sum(grad * normal, axis=0, keepdims=True)
    small_a[0, 3:4] = jnp.sum(grad, axis=0, keepdims=True)
    output = middle[...] + mlp_out[...]
    block_output[...] = output.astype(bf16)
    lane = lax.broadcasted_iota(jnp.int32, (4, width), 1)
    row = jnp.zeros((4, width), f32)
    squared = (squares(output), attn_squares, squares(mlp_out[...]), jnp.sum(keep) * width)
    for i, value in enumerate(squared):
        row = jnp.where(lane == i, value, row)
    small_a[0, 4:8] = row


    def turn(h):
        def one(z, _):
            for side in range(2):
                at = pl.ds(side * tokens, tokens)
                turned[h % 2, z, at, :] = kv_all[h, z, side, 0].T
                turned[2 + h % 2, z, at, :] = kv_all[h, z, side, 1].T
            return 0

        lax.fori_loop(0, 4, one, 0)

    turn(0)
    ups[0].along_line(send)
    for z in range(4):
        leaving[z, 9] = jnp.zeros((HEAD_DIM, tokens), bf16)
    swaps, sends = [], []

    def finish(h):
        swaps[h].wait_recv()

        def merge(z, _):
            fine = valid_columns(span, (2 * z + core) * tokens, tokens)
            q, k, v, inverse, signed, terms, weight = alone_terms(raw.at[z, pl.ds(3 * h, 3)])
            g = gm_in[h, z].astype(f32)
            total = 1.0 / terms
            grad_total = -jnp.sum(g * (weight * v), axis=0, keepdims=True) * total * total
            g = (g * total).astype(bf16).astype(f32)
            grad_weight = jnp.sum(g * v, axis=0, keepdims=True)
            slope = 1.0 + (inverse * inverse) * (inverse - 1.0)
            grad_score = terms * (grad_weight * slope + grad_total * signed)
            grad_score = grad_score.astype(bf16).astype(f32)
            alone = (grad_score * k * 0.125, grad_score * q, weight * g)
            parts = [leaving[z, 3 * h].astype(f32)]
            for part in range(2):
                parts.append(grad_kv[h, z, core, part] + part_in[h, z, part].astype(f32))
            for part in range(3):
                leaving[z, 3 * h + part] = jnp.where(fine, parts[part], alone[part]).astype(bf16)
            return 0

        lax.fori_loop(0, 4, merge, 0)
        at = pl.ds(3 * h, 3)
        for k in (1, 2, 3):
            sends.append(
                send(leaving.at[along[k], at], arrived.at[:, zed * 3 + h], line[k - 1])
            )
        for part in range(3):
            arrived[part, zed * 3 + h] = leaving[zed, 3 * h + part]

    def tile_products(h, z, z_key, side):
        at = pl.ds(side * tokens, tokens)
        scores = matmul(turned[h % 2, z_key, at, :], q_all[h, z])
        return scores, matmul(turned[2 + h % 2, z_key, at, :], g_all[z])

    def tile_grads(tile, scores, grad_weights):
        z, z_key, side = tile
        inverse, signed, terms = signed_terms(scores)
        if z == z_key:
            key_pos = lax.broadcasted_iota(jnp.int32, scores.shape, 0)
            query_pos = lax.broadcasted_iota(jnp.int32, scores.shape, 1)
            seen = key_pos + side * tokens <= query_pos + core * tokens
            terms = jnp.where(seen, terms, 0.0)
        weights = (signed * terms).astype(bf16)
        slope = 1.0 + (inverse * inverse) * (inverse - 1.0)
        grad_scores = terms * (grad_weights * slope + gt_all[z] * signed)
        return weights, grad_scores.astype(bf16)

    def tile_sums(h, z, z_key, side, weights, grad_scores):
        for part, left, right in ((0, q_all[h, z], grad_scores), (1, g_all[z], weights)):
            grad = contract_cols(left, right)
            if z == z_key:
                grad_kv[h, z_key, side, part] = grad
            else:
                grad_kv[h, z_key, side, part] += grad
        grad = matmul(kv_all[h, z_key, side, 0], grad_scores)
        if z_key == 0 and side == 0:
            grad_query[...] = grad
        else:
            grad_query[...] += grad
        if z == z_key and side == 1:
            leaving[z, 3 * h] = (grad_query[...] * 0.125).astype(bf16)

    for h in range(3):
        for copy in coming[h * 3 : h * 3 + 3]:
            copy.wait_recv()

        def prepare(z, _):
            g = gm_in[h, z].astype(f32)
            total = 1.0 / tot_all[h, z]
            g_all[z] = (g * total).astype(bf16)
            gt_all[z] = -jnp.sum(g * mix_all[h, z], axis=0, keepdims=True) * total
            return 0

        lax.fori_loop(0, 4, prepare, 0)

        tiles = [(z, z_key, side) for z in range(4) for z_key in range(z + 1) for side in range(2)]
        scored, parts = {}, {}
        for step in range(len(tiles) + 2):
            if step < len(tiles):
                scored[step] = tile_products(h, *tiles[step])
            if 0 <= step - 1 < len(tiles):
                parts[step - 1] = tile_grads(tiles[step - 1], *scored.pop(step - 1))
            if step - 2 >= 0:
                tile_sums(h, *tiles[step - 2], *parts.pop(step - 2))

        def pack(z, _):
            for part in range(2):
                part_out[h, z, part] = grad_kv[h, z, 1 - core, part].astype(bf16)
            return 0

        lax.fori_loop(0, 4, pack, 0)
        swaps.append(send(part_out.at[h], part_in.at[h], sibling))
        if h == 0:
            turn(1)
            ups[1].along_line(send)
            downs[0].step_two(send)
            downs[2].step_one(send)
            ups[0].pass_line(send)
            ups[2].step_one(send)
        if h == 1:
            turn(2)
            downs[1].step_two(send)
            downs[0].along_line(send)
            ups[1].pass_line(send)
            ups[3].step_one(send)
        finish(h)

    downs[2].step_two(send)
    downs[1].along_line(send)
    outs.step_one(send)
    downs[0].pass_line(send)
    ups[2].step_two(send)

    for quarter in (heads_sum.across, heads_sum.beside, heads_sum.above, heads_sum.own):
        total = None
        for z in range(4):
            rows = norm_all[z, rows_of(quarter * (width // 4), width // 4), :]
            part = contract_cols(rows, leaving[z].reshape(10 * HEAD_DIM, tokens))
            total = part if total is None else total + part
        term[pl.ds(4 * quarter, 4)] = total.reshape((4,) + term.shape[1:])
        heads_sum.halves.append(heads_sum.swap_quarter(send, quarter))
    heads_sum.step_one(send)
    downs[2].along_line(send)
    ups[3].step_two(send)
    downs[1].pass_line(send)
    outs.step_two(send)
    ups[2].along_line(send)
    heads_sum.step_two(send)

    for copy in sends:
        copy.wait_recv()
    grads = arrived[...].reshape(3 * width, tokens)
    for i in range(width // 256):
        columns = slice(i * 256, (i + 1) * 256)
        grad_norm[:, columns] = matmul(w_qkv[columns, :], grads).T
    downs[2].pass_line(send)
    ups[3].along_line(send)
    outs.along_line(send)
    ups[2].pass_line(send)
    gain_grad, bias_grad = norm_back(x, gain_one, grad_norm, grad_middle, input_grad, 64)
    small_a[0, 0:1] = gain_grad
    small_a[0, 1:2] = bias_grad
    whose = 2 * grp + core
    small_b[pl.ds(whose, 1)] = small_a[0:1]
    planes = [
        send(small_b.at[whose], small_b.at[whose], target)
        for target in [sibling] + across + around
    ]
    ups[3].pass_line(send)
    outs.pass_line(send)
    heads_sum.total()
    gathered[pl.ds(zed, 1)] = final[pl.ds(zed, 1)]
    blocks = [send(final.at[along[k]], gathered.at[zed], line[k - 1]) for k in (1, 2, 3)]
    for copy in planes:
        copy.wait_recv()
    total = small_b[0]
    for i in range(1, 8):
        total = total + small_b[i]
    small_c[pl.ds(zed, 1)] = total.reshape(1, 8, width)
    columns = [send(small_c.at[zed], small_c.at[zed], line[k - 1]) for k in (1, 2, 3)]
    sums = ups[:2] + downs + ups[2:] + [outs]
    for each in sums:
        each.settle(send)
    for copy in blocks + columns:
        copy.wait_recv()
    for z in range(4):
        for h in range(3):
            for part in range(3):
                start = part * width + (3 * z + h) * HEAD_DIM
                sum_qkv[:, start : start + HEAD_DIM] = gathered[
                    z, :, (3 * h + part) * HEAD_DIM : (3 * h + part + 1) * HEAD_DIM
                ]
    settle_small(small_c, vecs, rms, grp * 8 + seq)
    for copy in down_swaps + coming + swaps + sends + planes + blocks + columns:
        copy.wait_send()
    for each in sums + [heads_sum]:
        each.drain()


def layer(block_input, out_grad, w_qkv, w_out, w_up, w_down, vectors, span):
    f32, bf16 = jnp.float32, jnp.bfloat16
    tokens, width = block_input.shape
    hidden = w_up.shape[1]
    count = hidden // width + 1
    vmem, smem = pl.BlockSpec(memory_space=pltpu.VMEM), pl.BlockSpec(memory_space=pltpu.SMEM)
    block = (HEAD_DIM, tokens)
    own_rows, columns = width // 32, 10 * HEAD_DIM
    quarter, half = width // 4, width // 2
    copies = 11 * 3 + 4 + 15 * count + 9 + 3 + 9 + 10 + 7 + 3 + 3
    dma = pltpu.SemaphoreType.DMA
    in_hbm = [block_input, out_grad, w_qkv, w_out, w_up, w_down]

    def sum_scratch(lead, rows):
        return [
            pltpu.VMEM(lead + (4 * rows, half), bf16),
            pltpu.VMEM(lead + (6, rows // 2, half), bf16),
            pltpu.VMEM(lead + (rows, half), bf16),
            pltpu.VMEM(lead + (rows, half), bf16),
            pltpu.VMEM(lead + (rows // 4, half), f32),
        ]

    return pl.pallas_call(
        layer_kernel,
        out_shape=[
            jax.ShapeDtypeStruct((tokens, width), bf16),
            jax.ShapeDtypeStruct((tokens, width), bf16),
            jax.ShapeDtypeStruct((own_rows, 3 * width), f32),
            jax.ShapeDtypeStruct((4, 1, own_rows), f32),
            jax.ShapeDtypeStruct((1, 3), f32),
            jax.ShapeDtypeStruct((hidden // 32, width), f32),
            jax.ShapeDtypeStruct((own_rows, hidden), f32),
            jax.ShapeDtypeStruct((own_rows, width), f32),
        ],
        in_specs=[pl.BlockSpec(memory_space=pl.ANY)] * len(in_hbm) + [vmem] * 4 + [smem],
        out_specs=[vmem] * 8,
        scratch_shapes=[pltpu.VMEM(a.shape, a.dtype) for a in in_hbm]
        + [
            pltpu.VMEM((HEADS,) + block, bf16),
            pltpu.VMEM((3, 4) + block, bf16),
            pltpu.VMEM((3, 4, 2, 2) + block, bf16),
            pltpu.VMEM((4, 9) + block, bf16),
            pltpu.VMEM((3, 4) + block, f32),
            pltpu.VMEM((3, 4, 1, tokens), f32),
            pltpu.VMEM((4, width, tokens), bf16),
            pltpu.VMEM((3, 256, width), bf16),
            pltpu.VMEM((3, 4, 8, tokens), f32),
            pltpu.VMEM((width, width), bf16),
            pltpu.VMEM((tokens, width), f32),
            pltpu.VMEM((tokens, width), bf16),
            pltpu.VMEM((width, tokens), bf16),
            pltpu.VMEM((tokens, width), f32),
            pltpu.VMEM((tokens, width), f32),
            pltpu.VMEM((tokens, width), f32),
            pltpu.VMEM((HEADS,) + block, bf16),
        ]
        + sum_scratch((count,), quarter)
        + [
            pltpu.VMEM((hidden, half), bf16),
            pltpu.VMEM((3, 6, hidden // 8, 128), bf16),
            pltpu.VMEM((3, hidden // 4, 128), bf16),
            pltpu.VMEM((3, hidden // 4, 128), bf16),
            pltpu.VMEM((3, hidden // 16, 128), f32),
        ]
        + [
            pltpu.VMEM((3, 4) + block, bf16),
            pltpu.VMEM((4, 4, 2 * tokens, HEAD_DIM), bf16),
            pltpu.VMEM((4,) + block, bf16),
            pltpu.VMEM((4, 1, tokens), f32),
            pltpu.VMEM((3, 4, 2, 2) + block, f32),
            pltpu.VMEM((3, 4, 2) + block, bf16),
            pltpu.VMEM((3, 4, 2) + block, bf16),
            pltpu.VMEM((4, 10) + block, bf16),
            pltpu.VMEM((3, HEADS) + block, bf16),
            pltpu.VMEM((16, 2, own_rows, columns), f32),
            pltpu.VMEM((16, own_rows, columns), f32),
            pltpu.VMEM((16 * own_rows, columns), bf16),
            pltpu.VMEM((6, 2 * own_rows, columns), bf16),
            pltpu.VMEM((4, own_rows, columns), f32),
            pltpu.VMEM((4, own_rows, columns), f32),
            pltpu.VMEM(block, f32),
            pltpu.VMEM((1, 8, width), f32),
            pltpu.VMEM((8, 8, width), f32),
            pltpu.VMEM((4, 8, width), f32),
            dma((4 + 2 * (count - 1),)),
            dma((copies,)),
            dma((copies,)),
            dma((2, 4, 2)),
            dma((2, 4, 2)),
            dma((8,)),
            dma((8,)),
            dma((4,)),
            dma((4,)),
        ],
        compiler_params=pltpu.CompilerParams(
            collective_id=0, has_side_effects=True, vmem_limit_bytes=63 * 2**20
        ),
    )(*in_hbm, *vectors, span)


def hand_over_kernel(many, *refs):
    vecs, rms, arrays = refs[0], refs[1], refs[2 : 2 + many]
    outs, rest = refs[2 + many : 7 + 2 * many], refs[7 + 2 * many :]
    held, sems = rest[:many], rest[many]
    loads = [
        pltpu.make_async_copy(arrays[i], held[i], sems.at[0, i]) for i in range(many)
    ]
    stores = [
        pltpu.make_async_copy(held[i], outs[5 + i], sems.at[1, i]) for i in range(many)
    ]
    for load in loads:
        load.start()
    for i in range(4):
        outs[i][...] = vecs[i, 0]
    outs[4][...] = rms[0]
    for load, store in zip(loads, stores):
        load.wait()
        store.start()
    for store in stores:
        store.wait()


def hand_over(vecs, rms, arrays):
    vmem, hbm = pl.BlockSpec(memory_space=pltpu.VMEM), pl.BlockSpec(memory_space=pl.ANY)
    many, f32 = len(arrays), jnp.float32
    return pl.pallas_call(
        functools.partial(hand_over_kernel, many),
        out_shape=[jax.ShapeDtypeStruct(vecs.shape[2:], f32)] * 4
        + [jax.ShapeDtypeStruct(rms.shape[1:], f32)]
        + [jax.ShapeDtypeStruct(a.shape, a.dtype) for a in arrays],
        in_specs=[vmem] * 2 + [hbm] * many,
        out_specs=[vmem] * 5 + [hbm] * many,
        scratch_shapes=[pltpu.VMEM(a.shape, a.dtype) for a in arrays]
        + [pltpu.SemaphoreType.DMA((2, many))],
    )(vecs, rms, *arrays)


def per_device_planned(
    block_input,
    out_grad,
    seq_span,
    ln1_gain,
    ln1_bias,
    w_qkv,
    w_out,
    ln2_gain,
    ln2_bias,
    w_up,
    w_down,
):
    block_output, input_grad, sum_qkv, vecs, rms, sum_down, sum_up, sum_out = layer(
        block_input, out_grad, w_qkv, w_out, w_up, w_down,
        (ln1_gain, ln1_bias, ln2_gain, ln2_bias), seq_span,
    )
    arrays = (block_output, input_grad, sum_qkv, sum_out, sum_up, sum_down)
    gain_one, bias_one, gain_two, bias_two, rms, *arrays = hand_over(vecs, rms, arrays)
    block_output, input_grad, sum_qkv, sum_out, sum_up, sum_down = arrays
    return (
        block_output,
        input_grad,
        gain_one,
        bias_one,
        sum_qkv,
        sum_out,
        gain_two,
        bias_two,
        sum_up,
        sum_down,
        rms,
    )


def solution(mesh):
    placed = (
        P(("grp", "seq"), None),
        P(("grp", "seq"), None),
        P("grp", None),
        P(),
        P(),
        P(),
        P(),
        P(),
        P(),
        P(),
        P(),
    )
    planned = mesh.shape["grp"] == 4 and mesh.shape["seq"] == 8
    return jax.shard_map(
        per_device_planned if planned else per_device,
        mesh=mesh,
        in_specs=placed,
        out_specs=(
            P(("grp", "seq"), None),
            P(("grp", "seq"), None),
            P(("grp", "seq")),
            P(("grp", "seq")),
            P(("grp", "seq"), None),
            P(("grp", "seq"), None),
            P(("grp", "seq")),
            P(("grp", "seq")),
            P(("grp", "seq"), None),
            P(("grp", "seq"), None),
            P(),
        ),
        check_vma=False,
    )
```
